32 devices in a mesh: slides: 2 (over y), seq: 16 (over z, x, core), mp: 1.
Axes of the slice: x: 2, y: 2, z: 4, core: 2. Of those that a mesh axis runs over, the one named last changes fastest.
Arguments:
- tokens: bfloat16 [32768, 768], P(('slides', 'seq', 'mp')), parts along dimension 0, may hold values from -6 to 6
- attn_gain: float32 [768], replicated, may hold values from 0.25 to 1.75
- query_first: bfloat16 [768, 768], P(None, 'mp'), may hold values from -4 to 4
- key_first: bfloat16 [768, 768], P(None, 'mp'), may hold values from -4 to 4
- segment_value: bfloat16 [768, 768], P(None, 'mp'), may hold values from -0.21875 to 0.21875
- output_first: bfloat16 [768, 768], P('mp'), may hold values from -0.875 to 0.875
- mlp_gain: float32 [768], replicated, may hold values from 0.25 to 1.75
- up_weight: bfloat16 [768, 3072], P(None, 'mp'), may hold values from -0.21875 to 0.21875
- down_weight: bfloat16 [3072, 768], P('mp'), may hold values from -0.109375 to 0.109375
- second_gain: float32 [768], replicated, may hold values from 0.25 to 1.75
- query_second: bfloat16 [768, 768], P(None, 'mp'), may hold values from -4 to 4
- key_second: bfloat16 [768, 768], P(None, 'mp'), may hold values from -4 to 4
- value_second: bfloat16 [768, 768], P(None, 'mp'), may hold values from -0.21875 to 0.21875
- output_second: bfloat16 [768, 768], P('mp'), may hold values from -0.875 to 0.875
- segment_offset: int32 [16], P('mp'), may hold values from 0 to 63
- global_offset: int32 [16], P('mp'), may hold values from 0 to 63
Outputs:
- encoded: bfloat16 [32768, 768], P(('slides', 'seq', 'mp')), parts along dimension 0
The draws below stay inside these ranges and needn't reach their ends.
There are 2 independent parts, one for each index of `slides`. The reference program is written for one: setup_inputs(seed, part) draws one part's arguments, and reference() takes and returns one part's arrays. A program takes and returns all parts, laid end to end along the dimension named above; an argument that names none is the same for every part. Nothing has to cross between parts.
All inputs are finite; a program needn't handle non-finite values.
Results may differ from the reference program's by a relative error of at most 0.03.
The reference program's roundings to bfloat16 on the way count: a program that leaves them out, or rounds other values in their place, can miss the bound.
Values may be sent and summed in bfloat16 or wider, within the bound.
No kernel may reach another device: no remote copies, remote signals or barrier semaphores. Data moves between devices by JAX's collectives and lax.ppermute only.
A program may use at most 128 MiB of HBM per device.

```python
import math
import jax
import jax.numpy as jnp
from jax import lax

D = 768
HEADS = 16
FF = 3072
HEAD_DIM = 48
KEYS = 256
TOK_DEV = 1024
SEG_DEV = 16
TOKENS = 16384
N_SEQ = 16


def weight_pair(key, layer):
    base_key = jax.random.fold_in(key, 7100 + layer)
    first_key, whole_sequence_key = jax.random.split(base_key, 2)
    common = jax.random.truncated_normal(first_key, -4.0, 4.0, (D, D), jnp.float32)
    spare = jax.random.truncated_normal(whole_sequence_key, -4.0, 4.0, (D, D), jnp.float32)
    query_part = common / math.sqrt(D)
    key_part = spare / math.sqrt(D)
    return (jnp.clip(query_part, -4.0, 4.0), jnp.clip(key_part, -4.0, 4.0))


def draw_query_first(key, part):
    return weight_pair(key, 1)[0].astype(jnp.bfloat16)


def draw_key_first(key, part):
    return weight_pair(key, 1)[1].astype(jnp.bfloat16)


def draw_query_second(key, part):
    return weight_pair(key, 2)[0].astype(jnp.bfloat16)


def draw_key_second(key, part):
    return weight_pair(key, 2)[1].astype(jnp.bfloat16)


def touch_ends(values, key, low, top_value):
    extent = values.shape
    spot = [jax.random.randint(jax.random.fold_in(key, axis), (), 0, extent[axis]) for axis in range(len(extent))]
    values = values.at[tuple(spot)].set(low)
    longest = extent.index(max(extent))
    spot[longest] = (spot[longest] + 1) % extent[longest]
    return values.at[tuple(spot)].set(top_value)


def levels(stream_key, dims, cuts, smallest, high):
    def one(dim, shards_of):
        steps = jax.random.uniform(jax.random.fold_in(jax.random.fold_in(stream_key, 6), dim), (shards_of,), jnp.float32, smallest / len(cuts), high / len(cuts))
        return jnp.repeat(jnp.exp(steps), dims[dim] // shards_of).reshape((-1,) + (1,) * (len(dims) - dim - 1))

    level = one(*cuts[0])
    for cut in cuts[1:]:
        level = level * one(*cut)
    return level


def gaussian(own_key, shape, scale, bound, shards=(), held_as=jnp.bfloat16):
    factor_of = levels(own_key, shape, shards, -0.22, 0.18) if shards else 1.0
    drawn = jax.random.normal(own_key, shape, jnp.float32) * scale * factor_of
    return jnp.minimum(jnp.maximum(drawn, -bound), bound).astype(held_as)


def setup_inputs(seed: int = 0, part: int = 0) -> dict:
    key_list = jax.random.split(jax.random.key(seed), 17)
    part_splits = jax.random.split(jax.random.fold_in(key_list[16], part), 17)
    tokens = gaussian(part_splits[0], (TOKENS, D), 1.0, 6.0, ((0, 16),))
    attn_gain = jnp.clip(1.0 + 0.15 * jax.random.normal(key_list[1], (D,), jnp.float32), 0.25, 1.75)
    query_first = draw_query_first(jax.random.fold_in(key_list[16], 71), part)
    key_first = draw_key_first(jax.random.fold_in(key_list[16], 71), part)
    segment_value = gaussian(key_list[4], (D, D), D ** -0.5, 0.21875)
    output_first = gaussian(key_list[5], (D, D), HEAD_DIM ** -0.5, 0.875)
    mlp_gain = jnp.clip(1.0 + 0.15 * jax.random.normal(key_list[6], (D,), jnp.float32), 0.25, 1.75)
    up_weight = gaussian(key_list[7], (D, FF), D ** -0.5, 0.21875)
    down_weight = gaussian(key_list[8], (FF, D), FF ** -0.5, 0.109375)
    second_gain = jnp.clip(1.0 + 0.15 * jax.random.normal(key_list[9], (D,), jnp.float32), 0.25, 1.75)
    query_second = draw_query_second(jax.random.fold_in(key_list[16], 71), part)
    key_second = draw_key_second(jax.random.fold_in(key_list[16], 71), part)
    value_second = gaussian(key_list[12], (D, D), D ** -0.5, 0.21875)
    output_second = gaussian(key_list[13], (D, D), HEAD_DIM ** -0.5, 0.875)
    segment_offset = touch_ends(jax.random.randint(key_list[14], (HEADS,), 0, SEG_DEV * TOK_DEV // KEYS), jax.random.fold_in(key_list[14], 1), 0, (SEG_DEV * TOK_DEV // KEYS) - 1).astype(jnp.int32)
    global_offset = touch_ends(jax.random.randint(key_list[15], (HEADS,), 0, N_SEQ * TOK_DEV // KEYS), jax.random.fold_in(key_list[15], 1), 0, (N_SEQ * TOK_DEV // KEYS) - 1).astype(jnp.int32)
    return {"tokens": tokens, "attn_gain": attn_gain, "query_first": query_first, "key_first": key_first, "segment_value": segment_value, "output_first": output_first, "mlp_gain": mlp_gain, "up_weight": up_weight, "down_weight": down_weight, "second_gain": second_gain, "query_second": query_second, "key_second": key_second, "value_second": value_second, "output_second": output_second, "segment_offset": segment_offset, "global_offset": global_offset}


def norm_rows(values, gain):
    center = values - lax.optimization_barrier(jnp.mean(values, axis=-1, keepdims=True))
    spread = lax.optimization_barrier(jnp.mean(center * center, axis=-1, keepdims=True))
    return (center * lax.rsqrt(spread + 1e-05) * gain).astype(jnp.bfloat16)

def attend(query, keys, values):
    scores = jnp.einsum('thd,khd->htk', query.astype(jnp.float32), keys.astype(jnp.float32)) * HEAD_DIM ** (-0.5)
    highest = lax.optimization_barrier(jnp.max(scores, axis=-1, keepdims=True))
    weights = jnp.exp(scores - highest)
    weights = (weights / lax.optimization_barrier(jnp.sum(weights, axis=-1, keepdims=True))).astype(jnp.bfloat16)
    return jnp.einsum('htk,khd->thd', weights.astype(jnp.float32), values.astype(jnp.float32)).astype(jnp.bfloat16)

def project(chosen, weight):
    shaped = weight.astype(jnp.float32).reshape(D, HEADS, HEAD_DIM)
    return jnp.einsum('...hd,dhe->...he', chosen.astype(jnp.float32), shaped).astype(jnp.bfloat16)

def reference(tokens, attn_gain, query_first, key_first, segment_value, output_first, mlp_gain, up_weight, down_weight, second_gain, query_second, key_second, value_second, output_second, segment_offset, global_offset):
    seg_len = SEG_DEV * TOK_DEV
    segment_count = TOKENS // seg_len
    seg_rate = seg_len // KEYS
    hidden = norm_rows(tokens.astype(jnp.float32), attn_gain)
    query = jnp.dot(hidden, query_first, preferred_element_type=jnp.float32).astype(jnp.bfloat16)
    query = query.reshape(segment_count, seg_len, HEADS, HEAD_DIM)
    positions = (jnp.arange(segment_count, dtype=jnp.int32)[:, None, None] * seg_len + jnp.arange(KEYS, dtype=jnp.int32)[None, :, None] * seg_rate + segment_offset.astype(jnp.int32)[None, None, :]).astype(jnp.int32)
    chosen = hidden[positions]
    keys = project(chosen, key_first)
    values = project(chosen, segment_value)
    mixed = lax.map(lambda items: attend(items[0], items[1], items[2]), (query, keys, values)).reshape(TOKENS, D)
    first = (tokens.astype(jnp.float32) + jnp.dot(mixed, output_first, preferred_element_type=jnp.float32)).astype(jnp.bfloat16)
    normed = norm_rows(first.astype(jnp.float32), mlp_gain)
    inner = jax.nn.gelu(jnp.dot(normed, up_weight, preferred_element_type=jnp.float32), approximate=True).astype(jnp.bfloat16)
    second_branch = (first.astype(jnp.float32) + jnp.dot(inner, down_weight, preferred_element_type=jnp.float32)).astype(jnp.bfloat16)
    hidden_two = norm_rows(second_branch.astype(jnp.float32), second_gain)
    query_two = jnp.dot(hidden_two, query_second, preferred_element_type=jnp.float32).astype(jnp.bfloat16)
    query_two = query_two.reshape(segment_count, seg_len, HEADS, HEAD_DIM)
    glob_rate = TOKENS // KEYS
    positions_two = (jnp.arange(KEYS, dtype=jnp.int32)[:, None] * glob_rate + global_offset.astype(jnp.int32)[None, :]).astype(jnp.int32)
    chosen_two = hidden_two[positions_two]
    keys_two = project(chosen_two, key_second)
    values_two = project(chosen_two, value_second)
    mixed_two = lax.map(lambda block: attend(block, keys_two, values_two), query_two).reshape(TOKENS, D)
    return (second_branch.astype(jnp.float32) + jnp.dot(mixed_two, output_second, preferred_element_type=jnp.float32)).astype(jnp.bfloat16)
```

```python
import functools

import jax
import jax.numpy as jnp
from jax import lax
from jax.experimental import pallas as pl
from jax.experimental.pallas import tpu as pltpu
from jax.sharding import PartitionSpec as P

KEYS = 256
SEG_MAX = 16
ROWS = 256
LOG2E = 1.4426950408889634
BF16 = jnp.bfloat16
F32 = jnp.float32
VMEM_LIMIT = 56 * 1024 * 1024


def swapped(x, axis, apart):
    return lax.ppermute(x, axis, [(i, i ^ 1 << apart) for i in range(lax.axis_size(axis))])


def norm_rows(values, gain):
    center = values - jnp.mean(values, axis=-1, keepdims=True)
    spread = jnp.mean(center * center, axis=-1, keepdims=True)
    return (center * lax.rsqrt(spread + 1e-05) * gain).astype(jnp.bfloat16)


def pick_keys(hidden, offsets, stride, key_weight, value_weight):
    token_count, width = hidden.shape
    head_count = offsets.shape[0]
    head_size = key_weight.shape[1] // head_count
    grouped_rows = hidden.reshape(token_count // stride, stride, width)
    dilation_selector = (
        lax.broadcasted_iota(jnp.int32, (stride, head_count), 0) == offsets[None, :]
    ).astype(jnp.bfloat16)
    chosen = jnp.einsum(
        "nof,oj->njf", grouped_rows, dilation_selector, preferred_element_type=jnp.float32
    ).astype(jnp.bfloat16)
    key_heads = jnp.einsum(
        "xkr,rkf->xkf",
        chosen,
        key_weight.reshape(width, head_count, head_size),
        preferred_element_type=jnp.float32,
    ).astype(jnp.bfloat16)
    value_heads = jnp.einsum(
        "xkr,rkf->xkf",
        chosen,
        value_weight.reshape(width, head_count, head_size),
        preferred_element_type=jnp.float32,
    ).astype(jnp.bfloat16)
    picked = token_count // stride
    return jnp.stack(
        [
            key_heads.reshape(picked, head_count * head_size),
            value_heads.reshape(picked, head_count * head_size),
        ]
    )


def attend_local(query, keyval, head_count):
    token_count, width = query.shape
    head_size = width // head_count
    query_heads = query.reshape(token_count, head_count, head_size)
    key_heads = keyval[0].reshape(-1, head_count, head_size)
    value_heads = keyval[1].reshape(-1, head_count, head_size)
    scores = jnp.einsum(
        "thd,khd->htk", query_heads, key_heads, preferred_element_type=jnp.float32
    ) * head_size ** (-0.5)
    highest = jnp.max(scores, axis=-1, keepdims=True)
    weights = jnp.exp(scores - highest)
    weights = (weights / jnp.sum(weights, axis=-1, keepdims=True)).astype(jnp.bfloat16)
    mixed = jnp.einsum(
        "htk,khd->thd", weights, value_heads, preferred_element_type=jnp.float32
    ).astype(jnp.bfloat16)
    return mixed.reshape(token_count, width)


def merge_branch_pair(mine, other, level, token_position):
    lower = token_position >> level & 1 == 0
    return jnp.where(
        lower, jnp.concatenate((mine, other), axis=1), jnp.concatenate((other, mine), axis=1)
    )


def spread_segment(keyval, seg_span, token_position):
    for level in range(seg_span.bit_length() - 1):
        partner = swapped(keyval, "seq", level)
        keyval = merge_branch_pair(keyval, partner, level, token_position)
    return keyval


def spread_global(keyval_two):
    keyval_two = lax.all_gather(keyval_two, "seq", axis=1, tiled=True)
    return keyval_two


def combine(partial_value, residual_full, need_full):
    row_count = residual_full.shape[0] // lax.axis_size("mp")
    row_start = lax.axis_index("mp") * row_count
    share = lax.psum_scatter(partial_value, "mp", scatter_dimension=0, tiled=True)
    own_rows = lax.dynamic_slice_in_dim(residual_full, row_start, row_count, 0)
    own_rows = (own_rows.astype(jnp.float32) + share).astype(jnp.bfloat16)
    full_rows = lax.all_gather(own_rows, "mp", axis=0, tiled=True) if need_full else own_rows
    return (own_rows, full_rows)


def split_body(
    tokens,
    attn_gain,
    query_first,
    key_first,
    segment_value,
    output_first,
    mlp_gain,
    up_weight,
    down_weight,
    second_gain,
    query_second,
    key_second,
    value_second,
    output_second,
    segment_offset,
    global_offset,
):
    seq_count = lax.axis_size("seq")
    token_position = lax.axis_index("seq")
    seg_span = min(SEG_MAX, seq_count)
    head_count = segment_offset.shape[0]
    full_rows = lax.all_gather(tokens, "mp", axis=0, tiled=True)
    token_count = full_rows.shape[0]
    hidden = norm_rows(full_rows.astype(jnp.float32), attn_gain)
    query = jnp.dot(hidden, query_first, preferred_element_type=jnp.float32).astype(jnp.bfloat16)
    seg_stride = token_count // (KEYS // seg_span)
    keyval = pick_keys(hidden, segment_offset, seg_stride, key_first, segment_value)
    keyval = spread_segment(keyval, seg_span, token_position)
    mixed = attend_local(query, keyval, head_count)
    partial_value = jnp.dot(mixed, output_first, preferred_element_type=jnp.float32)
    own_rows, first_rows = combine(partial_value, full_rows, True)
    normed = norm_rows(first_rows.astype(jnp.float32), mlp_gain)
    inner = jax.nn.gelu(
        jnp.dot(normed, up_weight, preferred_element_type=jnp.float32), approximate=True
    ).astype(jnp.bfloat16)
    partial_value = jnp.dot(inner, down_weight, preferred_element_type=jnp.float32)
    own_rows, second_rows = combine(partial_value, first_rows, True)
    hidden_two = norm_rows(second_rows.astype(jnp.float32), second_gain)
    query_two = jnp.dot(hidden_two, query_second, preferred_element_type=jnp.float32).astype(
        jnp.bfloat16
    )
    glob_stride = token_count // (KEYS // seq_count)
    keyval_two = pick_keys(hidden_two, global_offset, glob_stride, key_second, value_second)
    keyval_two = spread_global(keyval_two)
    mixed_two = attend_local(query_two, keyval_two, head_count)
    partial_value = jnp.dot(mixed_two, output_second, preferred_element_type=jnp.float32)
    own_rows, unused_rows = combine(partial_value, second_rows, False)
    return own_rows


def one_hot(condition):
    return jnp.where(condition, 1.0, 0.0).astype(BF16)


def contract(left, right, left_dim, right_dim):
    return lax.dot_general(
        left, right, (((left_dim,), (right_dim,)), ((), ())), preferred_element_type=F32
    )


def keys_values(rows, stride, offsets, gain, key_weight, value_weight, keyval_ref, normed):
    count, width = rows.shape
    heads = offsets.shape[0]
    groups = count // stride
    head_size = width // heads
    place = lax.broadcasted_iota(jnp.int32, (groups, count), 1)
    place = place - lax.broadcasted_iota(jnp.int32, (groups, count), 0) * stride
    chooser = jnp.concatenate([one_hot(place == offsets[h]) for h in range(heads)], axis=0)
    chosen = contract(chooser, rows, 1, 0)
    chosen = chosen.astype(BF16) if normed else norm_rows(chosen, gain)
    column = lax.broadcasted_iota(jnp.int32, (groups, width), 1)
    for slot, weight in enumerate((key_weight, value_weight)):
        wide = contract(chosen, weight[...], 1, 0)
        total = jnp.zeros((groups, width), F32)
        for h in range(heads):
            own = (column >= h * head_size) & (column < (h + 1) * head_size)
            total = jnp.where(own, wide[h * groups : (h + 1) * groups], total)
        keyval_ref[slot] = total.astype(BF16)


def first_keys_kernel(offsets, tokens, gain, key_weight, value_weight, keyval, *, stride):
    keys_values(tokens[...], stride, offsets, gain[...], key_weight, value_weight, keyval, False)


def query_kernel(
    target, tokens, gain, weight, picked_rows, rest_rows, picked_query, rest_query, *, share
):
    chunk = target.shape[1]
    width = tokens.shape[1]
    mover = one_hot(
        lax.broadcasted_iota(jnp.int32, (chunk, chunk), 0)
        == jnp.broadcast_to(target[...], (chunk, chunk))
    )
    rest = chunk - share
    for c in range(tokens.shape[0] // chunk):
        moved = contract(mover, tokens[c * chunk : (c + 1) * chunk, :], 1, 0)
        query = contract(norm_rows(moved, gain[...]), weight[...], 1, 0).astype(BF16)
        moved = moved.astype(BF16)
        picked_rows[c * share : (c + 1) * share, :] = moved[:share]
        rest_rows[c * rest : (c + 1) * rest, :] = moved[share:]
        picked_query[c * share : (c + 1) * share, :] = query[:share]
        rest_query[c * rest : (c + 1) * rest, :] = query[share:]


def head_window(h, head_size, width):
    start = h * head_size // 128 * 128
    return min(start, width - 256) if width >= 256 else 0


def load_keys(keyvals, heads, keys_ref, values_ref):
    keys = jnp.concatenate([keyval[0] for keyval in keyvals], axis=0)
    values = jnp.concatenate([keyval[1] for keyval in keyvals], axis=0)
    key_count, width = keys.shape
    head_size = width // heads
    column = lax.broadcasted_iota(jnp.int32, (key_count, 256), 1)
    turned = values.T
    for h in range(heads):
        start = head_window(h, head_size, width)
        own = (column >= h * head_size - start) & (column < (h + 1) * head_size - start)
        keys_ref[h] = jnp.where(own, keys[:, start : start + 256], jnp.zeros((), BF16))
        values_ref[h, :head_size, :] = turned[h * head_size : (h + 1) * head_size]
        values_ref[h, head_size:, :] = jnp.ones(
            (values_ref.shape[1] - head_size, key_count), BF16
        )


def attend_rows(query, heads, keys_ref, values_ref, mixed_ref):
    width = query.shape[1]
    head_size = width // heads
    factor = head_size ** (-0.5) * LOG2E
    for h in range(heads):
        start = head_window(h, head_size, width)
        scores = contract(keys_ref[h], query[:, start : start + 256], 1, 1)
        highest = jnp.max(scores, axis=0, keepdims=True)
        weights = jnp.exp2((scores - highest) * factor).astype(BF16)
        mixed = contract(values_ref[h], weights, 1, 0)
        total = mixed[head_size : head_size + 1, :]
        mixed_ref[h * head_size : (h + 1) * head_size, :] = (
            mixed[:head_size, :] * (1.0 / total)
        ).astype(BF16)


def gelu(x):
    half = 0.5 * x
    return half + half * jnp.tanh(x * (0.7978845608028654 + 0.035677408136300125 * (x * x)))


def layer_rows(
    rows, query, heads, keys_ref, values_ref, mixed_ref, out_weight, gain, up_weight, down_weight
):
    attend_rows(query, heads, keys_ref, values_ref, mixed_ref)
    first = (rows.astype(F32) + contract(mixed_ref[...], out_weight[...], 0, 0)).astype(BF16)
    first = first.astype(F32)
    normed = norm_rows(first, gain[...])
    hidden = up_weight.shape[1]
    part = hidden // 4 if hidden % 512 == 0 else hidden
    total = first
    for start in range(0, hidden, part):
        inner = gelu(contract(normed, up_weight[:, start : start + part], 1, 0)).astype(BF16)
        total = total + contract(inner, down_weight[start : start + part, :], 1, 0)
    return total.astype(BF16)


def picked_kernel(
    slots,
    rows,
    query,
    keyval,
    keyval_far,
    out_weight,
    mlp_gain,
    up_weight,
    down_weight,
    gain,
    key_weight,
    value_weight,
    second,
    keyval_two,
    keys_ref,
    values_ref,
    mixed_ref,
    *,
    heads,
):
    load_keys((keyval, keyval_far), heads, keys_ref, values_ref)
    result = layer_rows(
        rows[...],
        query[...],
        heads,
        keys_ref,
        values_ref,
        mixed_ref,
        out_weight,
        mlp_gain,
        up_weight,
        down_weight,
    )
    second[...] = result
    hidden = norm_rows(result.astype(F32), gain[...])
    keys_values(hidden, heads, slots, None, key_weight, value_weight, keyval_two, True)


def rest_kernel(
    rows,
    query,
    keyval,
    keyval_far,
    out_weight,
    mlp_gain,
    up_weight,
    down_weight,
    second,
    keys_ref,
    values_ref,
    mixed_ref,
    *,
    heads,
):
    load_keys((keyval, keyval_far), heads, keys_ref, values_ref)
    size = mixed_ref.shape[1]

    @pl.loop(0, rows.shape[0] // size)
    def _(step):
        span = pl.ds(pl.multiple_of(step * size, size), size)
        second[span, :] = layer_rows(
            rows[span, :],
            query[span, :],
            heads,
            keys_ref,
            values_ref,
            mixed_ref,
            out_weight,
            mlp_gain,
            up_weight,
            down_weight,
        )


def second_query_kernel(picked, rest, gain, weight, picked_query, rest_query):
    for rows, query in ((picked, picked_query), (rest, rest_query)):
        hidden = norm_rows(rows[...].astype(F32), gain[...])
        query[...] = contract(hidden, weight[...], 1, 0).astype(BF16)


def second_kernel(
    target,
    picked,
    rest,
    picked_query,
    rest_query,
    keyval,
    keyval_far,
    out_weight,
    encoded,
    keys_ref,
    values_ref,
    mixed_ref,
    *,
    heads,
    share,
):
    load_keys((keyval, keyval_far), heads, keys_ref, values_ref)
    chunk = target.shape[0]
    rest_share = chunk - share
    back = one_hot(
        lax.broadcasted_iota(jnp.int32, (chunk, chunk), 1)
        == jnp.broadcast_to(target[...], (chunk, chunk))
    )

    @pl.loop(0, encoded.shape[0] // chunk)
    def _(step):
        near = pl.ds(pl.multiple_of(step * share, share), share)
        far = pl.ds(pl.multiple_of(step * rest_share, rest_share), rest_share)
        query = jnp.concatenate([picked_query[near, :], rest_query[far, :]], axis=0)
        attend_rows(query, heads, keys_ref, values_ref, mixed_ref)
        rows = jnp.concatenate([picked[near, :], rest[far, :]], axis=0)
        result = (
            rows.astype(F32) + contract(mixed_ref[...], out_weight[...], 0, 0)
        ).astype(BF16)
        span = pl.ds(pl.multiple_of(step * chunk, chunk), chunk)
        encoded[span, :] = contract(back, result, 1, 0).astype(BF16)


def local_call(kernel, outs, inputs, scratch=(), scalars=0, flops=0, name=None):
    vmem = pl.BlockSpec(memory_space=pltpu.VMEM)
    smem = pl.BlockSpec(memory_space=pltpu.SMEM)
    return pl.pallas_call(
        kernel,
        out_shape=outs,
        in_specs=[smem] * scalars + [vmem] * (len(inputs) - scalars),
        out_specs=[vmem] * len(outs),
        scratch_shapes=scratch,
        compiler_params=pltpu.CompilerParams(vmem_limit_bytes=VMEM_LIMIT),
        cost_estimate=pl.CostEstimate(
            flops=int(flops),
            transcendentals=0,
            bytes_accessed=sum(x.size * x.dtype.itemsize for x in inputs),
        ),
        name=name,
    )(*inputs)


def exchange(keyval, span):
    blocks = [keyval]
    size = lax.axis_size("seq")
    for mask in range(2, span, 2):
        blocks.append(lax.ppermute(keyval, "seq", [(i, i ^ mask) for i in range(size)]))
    near = jnp.concatenate(blocks, axis=1)
    return near, swapped(near, "seq", 0)


def whole_body(
    tokens,
    attn_gain,
    query_first,
    key_first,
    segment_value,
    output_first,
    mlp_gain,
    up_weight,
    down_weight,
    second_gain,
    query_second,
    key_second,
    value_second,
    output_second,
    segment_offset,
    global_offset,
):
    seq_count = lax.axis_size("seq")
    seg_span = min(SEG_MAX, seq_count)
    heads = segment_offset.shape[0]
    count, width = tokens.shape
    head_size = width // heads
    stride = count // (KEYS // seg_span)
    stride_two = count // (KEYS // seq_count)
    groups, groups_two = count // stride, count // stride_two
    chunk = max(ROWS, stride_two)
    share = chunk // stride_two * heads
    picked_count = groups_two * heads
    rest_count = count - picked_count

    def like(*shape):
        return jax.ShapeDtypeStruct(shape, BF16)

    (keyval,) = local_call(
        functools.partial(first_keys_kernel, stride=stride),
        [like(2, groups, width)],
        (segment_offset, tokens, attn_gain, key_first, segment_value),
        scalars=1,
        flops=2 * heads * groups * width * (count + 2 * width),
        name="first_keys",
    )
    near, far = exchange(keyval, seg_span)

    position = jnp.arange(stride_two, dtype=jnp.int32)
    taken = jnp.any(global_offset[:, None] == position[None, :], axis=0)
    order = jnp.where(taken, position, position + stride_two)
    rank = jnp.sum((order[None, :] < order[:, None]).astype(jnp.int32), axis=1)
    slots = jnp.sum(
        jnp.where(global_offset[:, None] == position[None, :], rank[None, :], 0), axis=1
    ).astype(jnp.int32)
    inside = jnp.arange(chunk // stride_two, dtype=jnp.int32)[:, None]
    target = jnp.where(
        rank[None, :] < heads,
        inside * heads + rank[None, :],
        share + inside * (stride_two - heads) + rank[None, :] - heads,
    ).reshape(chunk)

    picked_rows, rest_rows, picked_query, rest_query = local_call(
        functools.partial(query_kernel, share=share),
        [
            like(picked_count, width),
            like(rest_count, width),
            like(picked_count, width),
            like(rest_count, width),
        ],
        (target[None, :], tokens, attn_gain, query_first),
        flops=2 * count * width * (width + chunk),
        name="first_query",
    )
    head_rows = (head_size + 16) // 16 * 16

    def scratch(rows):
        return [
            pltpu.VMEM((heads, KEYS, 256), BF16),
            pltpu.VMEM((heads, head_rows, KEYS), BF16),
            pltpu.VMEM((width, rows), BF16),
        ]

    hidden = up_weight.shape[1]
    row_flops = 2 * width * (2 * hidden + width) + 4 * 256 * KEYS * heads
    picked_second, keyval_two = local_call(
        functools.partial(picked_kernel, heads=heads),
        [like(picked_count, width), like(2, groups_two, width)],
        (
            slots,
            picked_rows,
            picked_query,
            near,
            far,
            output_first,
            mlp_gain,
            up_weight,
            down_weight,
            second_gain,
            key_second,
            value_second,
        ),
        scratch=scratch(picked_count),
        scalars=1,
        flops=row_flops * picked_count,
        name="layer_of_picked",
    )
    near_two, far_two = exchange(keyval_two, seq_count)
    (rest_second,) = local_call(
        functools.partial(rest_kernel, heads=heads),
        [like(rest_count, width)],
        (
            rest_rows,
            rest_query,
            near,
            far,
            output_first,
            mlp_gain,
            up_weight,
            down_weight,
        ),
        scratch=scratch(ROWS),
        flops=row_flops * rest_count,
        name="layer_of_rest",
    )
    picked_query_two, rest_query_two = local_call(
        second_query_kernel,
        [like(picked_count, width), like(rest_count, width)],
        (picked_second, rest_second, second_gain, query_second),
        flops=2 * count * width * width,
        name="second_query",
    )
    (encoded,) = local_call(
        functools.partial(second_kernel, heads=heads, share=share),
        [like(count, width)],
        (
            target[:, None],
            picked_second,
            rest_second,
            picked_query_two,
            rest_query_two,
            near_two,
            far_two,
            output_second,
        ),
        scratch=scratch(chunk),
        flops=count * (2 * width * width + 4 * 256 * KEYS * heads),
        name="second_attention",
    )
    return encoded


def solution(mesh):
    placed = (
        P(("slides", "seq", "mp"), None),
        P(),
        P(None, "mp"),
        P(None, "mp"),
        P(None, "mp"),
        P("mp", None),
        P(),
        P(None, "mp"),
        P("mp", None),
        P(),
        P(None, "mp"),
        P(None, "mp"),
        P(None, "mp"),
        P("mp", None),
        P("mp"),
        P("mp"),
    )
    fits = mesh.shape["mp"] == 1 and 2 <= mesh.shape["seq"] <= SEG_MAX
    return jax.shard_map(
        whole_body if fits else split_body,
        mesh=mesh,
        in_specs=placed,
        out_specs=P(("slides", "seq", "mp"), None),
        check_vma=False,
    )
```

```python
import functools
import math

import jax
import jax.numpy as jnp
from jax import lax
from jax.experimental import pallas as pl
from jax.experimental.pallas import tpu as pltpu
from jax.sharding import PartitionSpec as P

KEYS = 256
SEG_MAX = 16
ROWS = 256
LOG2E = 1.4426950408889634
BF16 = jnp.bfloat16
F32 = jnp.float32
VMEM_LIMIT = 22 * 1024 * 1024


def swapped(x, axis, apart):
    return lax.ppermute(x, axis, [(i, i ^ 1 << apart) for i in range(lax.axis_size(axis))])


def norm_rows(values, gain):
    center = values - jnp.mean(values, axis=-1, keepdims=True)
    spread = jnp.mean(center * center, axis=-1, keepdims=True)
    return (center * lax.rsqrt(spread + 1e-05) * gain).astype(jnp.bfloat16)


def pick_keys(hidden, offsets, stride, key_weight, value_weight):
    token_count, width = hidden.shape
    head_count = offsets.shape[0]
    head_size = key_weight.shape[1] // head_count
    grouped_rows = hidden.reshape(token_count // stride, stride, width)
    dilation_selector = (
        lax.broadcasted_iota(jnp.int32, (stride, head_count), 0) == offsets[None, :]
    ).astype(jnp.bfloat16)
    chosen = jnp.einsum(
        "nof,oj->njf", grouped_rows, dilation_selector, preferred_element_type=jnp.float32
    ).astype(jnp.bfloat16)
    key_heads = jnp.einsum(
        "xkr,rkf->xkf",
        chosen,
        key_weight.reshape(width, head_count, head_size),
        preferred_element_type=jnp.float32,
    ).astype(jnp.bfloat16)
    value_heads = jnp.einsum(
        "xkr,rkf->xkf",
        chosen,
        value_weight.reshape(width, head_count, head_size),
        preferred_element_type=jnp.float32,
    ).astype(jnp.bfloat16)
    picked = token_count // stride
    return jnp.stack(
        [
            key_heads.reshape(picked, head_count * head_size),
            value_heads.reshape(picked, head_count * head_size),
        ]
    )


def attend_local(query, keyval, head_count):
    token_count, width = query.shape
    head_size = width // head_count
    query_heads = query.reshape(token_count, head_count, head_size)
    key_heads = keyval[0].reshape(-1, head_count, head_size)
    value_heads = keyval[1].reshape(-1, head_count, head_size)
    scores = jnp.einsum(
        "thd,khd->htk", query_heads, key_heads, preferred_element_type=jnp.float32
    ) * head_size ** (-0.5)
    highest = jnp.max(scores, axis=-1, keepdims=True)
    weights = jnp.exp(scores - highest)
    weights = (weights / jnp.sum(weights, axis=-1, keepdims=True)).astype(jnp.bfloat16)
    mixed = jnp.einsum(
        "htk,khd->thd", weights, value_heads, preferred_element_type=jnp.float32
    ).astype(jnp.bfloat16)
    return mixed.reshape(token_count, width)


def merge_branch_pair(mine, other, level, token_position):
    lower = token_position >> level & 1 == 0
    return jnp.where(
        lower, jnp.concatenate((mine, other), axis=1), jnp.concatenate((other, mine), axis=1)
    )


def spread_segment(keyval, seg_span, token_position):
    for level in range(seg_span.bit_length() - 1):
        partner = swapped(keyval, "seq", level)
        keyval = merge_branch_pair(keyval, partner, level, token_position)
    return keyval


def spread_global(keyval_two):
    keyval_two = lax.all_gather(keyval_two, "seq", axis=1, tiled=True)
    return keyval_two


def combine(partial_value, residual_full, need_full):
    row_count = residual_full.shape[0] // lax.axis_size("mp")
    row_start = lax.axis_index("mp") * row_count
    share = lax.psum_scatter(partial_value, "mp", scatter_dimension=0, tiled=True)
    own_rows = lax.dynamic_slice_in_dim(residual_full, row_start, row_count, 0)
    own_rows = (own_rows.astype(jnp.float32) + share).astype(jnp.bfloat16)
    full_rows = lax.all_gather(own_rows, "mp", axis=0, tiled=True) if need_full else own_rows
    return (own_rows, full_rows)


def split_body(
    tokens,
    attn_gain,
    query_first,
    key_first,
    segment_value,
    output_first,
    mlp_gain,
    up_weight,
    down_weight,
    second_gain,
    query_second,
    key_second,
    value_second,
    output_second,
    segment_offset,
    global_offset,
):
    seq_count = lax.axis_size("seq")
    token_position = lax.axis_index("seq")
    seg_span = min(SEG_MAX, seq_count)
    head_count = segment_offset.shape[0]
    full_rows = lax.all_gather(tokens, "mp", axis=0, tiled=True)
    token_count = full_rows.shape[0]
    hidden = norm_rows(full_rows.astype(jnp.float32), attn_gain)
    query = jnp.dot(hidden, query_first, preferred_element_type=jnp.float32).astype(jnp.bfloat16)
    seg_stride = token_count // (KEYS // seg_span)
    keyval = pick_keys(hidden, segment_offset, seg_stride, key_first, segment_value)
    keyval = spread_segment(keyval, seg_span, token_position)
    mixed = attend_local(query, keyval, head_count)
    partial_value = jnp.dot(mixed, output_first, preferred_element_type=jnp.float32)
    own_rows, first_rows = combine(partial_value, full_rows, True)
    normed = norm_rows(first_rows.astype(jnp.float32), mlp_gain)
    inner = jax.nn.gelu(
        jnp.dot(normed, up_weight, preferred_element_type=jnp.float32), approximate=True
    ).astype(jnp.bfloat16)
    partial_value = jnp.dot(inner, down_weight, preferred_element_type=jnp.float32)
    own_rows, second_rows = combine(partial_value, first_rows, True)
    hidden_two = norm_rows(second_rows.astype(jnp.float32), second_gain)
    query_two = jnp.dot(hidden_two, query_second, preferred_element_type=jnp.float32).astype(
        jnp.bfloat16
    )
    glob_stride = token_count // (KEYS // seq_count)
    keyval_two = pick_keys(hidden_two, global_offset, glob_stride, key_second, value_second)
    keyval_two = spread_global(keyval_two)
    mixed_two = attend_local(query_two, keyval_two, head_count)
    partial_value = jnp.dot(mixed_two, output_second, preferred_element_type=jnp.float32)
    own_rows, unused_rows = combine(partial_value, second_rows, False)
    return own_rows


def one_hot(condition):
    return jnp.where(condition, 1.0, 0.0).astype(BF16)


def dot(left, right):
    return jnp.dot(left, right, preferred_element_type=F32)


def pieces(count, size):
    size = size if count % size == 0 else count
    return [slice(start, start + size) for start in range(0, count, size)]


def norm_into(out, start, source, gain, count):
    for span in pieces(count, 64):
        out[start + span.start : start + span.stop, :] = norm_rows(
            source[span, :].astype(F32), gain
        )


def bring(source, target, sem):
    copy = pltpu.make_async_copy(source, target, sem)
    copy.start()
    return copy


def pick_matrix(offsets, heads, groups, stride):
    count = groups * stride
    place = lax.broadcasted_iota(jnp.int32, (groups, count), 1)
    place = place - lax.broadcasted_iota(jnp.int32, (groups, count), 0) * stride
    return jnp.concatenate([one_hot(place == offsets[h]) for h in range(heads)], axis=0)


def project_keys(chosen, heads, weights, keyval_ref):
    rows, width = chosen.shape
    groups, head_size = rows // heads, width // heads
    column = lax.broadcasted_iota(jnp.int32, (groups, width), 1)
    for slot, weight in enumerate(weights):
        wide = dot(chosen, weight())
        total = jnp.zeros((groups, width), F32)
        for h in range(heads):
            own = (column >= h * head_size) & (column < (h + 1) * head_size)
            total = jnp.where(own, wide[h * groups : (h + 1) * groups], total)
        total = total.astype(BF16)
        for copy in range(keyval_ref.shape[0]):
            keyval_ref[copy, slot] = total


def ranks(offsets, chunk, stride, share, axis):
    heads = offsets.shape[0]

    def places(way):
        shape = (1, chunk) if way else (chunk, 1)
        place = lax.broadcasted_iota(jnp.int32, shape, way)
        inside = lax.rem(place, stride)
        taken = inside == offsets[0]
        for h in range(1, heads):
            taken = taken | (inside == offsets[h])
        return place, inside, jnp.where(taken, inside, inside + stride)

    place, inside, order = places(axis)
    other_place, _, other_order = places(1 - axis)
    ahead = (other_order < order) & (lax.div(other_place, stride) == lax.div(place, stride))
    rank = jnp.sum(jnp.where(ahead, 1, 0), axis=1 - axis, keepdims=True)
    group = lax.div(place, stride)
    return jnp.where(
        rank < heads, group * heads + rank, share + group * (stride - heads) + rank - heads
    )


def slots_of(offsets, heads):
    values = [offsets[h] for h in range(heads)]
    fresh = []
    for h in range(heads):
        seen = jnp.int32(1)
        for earlier in values[:h]:
            seen = jnp.where(earlier == values[h], 0, seen)
        fresh.append(seen)
    slots = []
    for h in range(heads):
        slot = jnp.int32(0)
        for other in range(heads):
            slot = slot + jnp.where(values[other] < values[h], fresh[other], 0)
        slots.append(slot)
    return slots


def first_keys_kernel(
    offsets, tokens, gain, key_weight, value_weight, keyval, rows, wide, sems, *, stride
):
    copies = [
        bring(tokens, rows, sems.at[0]),
        bring(key_weight, wide.at[0], sems.at[1]),
        bring(value_weight, wide.at[1], sems.at[2]),
    ]
    heads = offsets.shape[0]
    chooser = pick_matrix(offsets, heads, rows.shape[0] // stride, stride)
    copies[0].wait()
    chosen = norm_rows(dot(chooser, rows[...]), gain[...])

    def weight(slot):
        copies[slot + 1].wait()
        return wide[slot]

    project_keys(
        chosen, heads, [functools.partial(weight, slot) for slot in range(2)], keyval
    )


def first_query_kernel(
    offsets, tokens, gain, weight, moved_rows, query, rows, held, normed, sems, *, stride, chunk
):
    copies = [bring(tokens, rows, sems.at[0]), bring(weight, held, sems.at[1])]
    count = tokens.shape[0]
    share = chunk // stride * offsets.shape[0]
    rest = chunk - share
    picked = count // chunk * share
    mover = one_hot(
        lax.broadcasted_iota(jnp.int32, (chunk, chunk), 0)
        == ranks(offsets, chunk, stride, share, 1)
    )
    copies[0].wait()
    for c in range(count // chunk):
        moved = dot(mover, rows[c * chunk : (c + 1) * chunk, :]).astype(BF16)
        moved_rows[c * share : (c + 1) * share, :] = moved[:share]
        moved_rows[picked + c * rest : picked + (c + 1) * rest, :] = moved[share:]
    norm_into(normed, 0, moved_rows, gain[...], count)
    copies[1].wait()
    for span in pieces(count, 512):
        query[span, :] = dot(normed[span, :], held[...]).astype(BF16)


def head_windows(head_size, width):
    period = min(width, math.lcm(head_size, 128))
    windows = []
    for h in range(period // head_size):
        start = h * head_size // 128 * 128
        stop = min(period, -(-(h + 1) * head_size // 128) * 128)
        windows.append((start, stop - start))
    return period, windows


def load_keys(keyvals, heads, keys_ref, values_ref):
    keys = jnp.concatenate([x[i, 0] for x in keyvals for i in range(x.shape[0])], axis=0)
    values = jnp.concatenate([x[i, 1] for x in keyvals for i in range(x.shape[0])], axis=0)
    key_count, width = keys.shape
    head_size = width // heads
    period, windows = head_windows(head_size, width)
    turned = keys.T
    ones = jnp.ones((key_count, 128), BF16)
    for h in range(heads):
        start, size = windows[h % len(windows)]
        start = start + h // len(windows) * period
        low = h * head_size - start
        keys_ref[h, :size, :] = jnp.zeros((size, key_count), BF16)
        keys_ref[h, low : low + head_size, :] = turned[h * head_size : (h + 1) * head_size]
        column = lax.broadcasted_iota(jnp.int32, (key_count, size), 1)
        own = (column >= low) & (column < low + head_size)
        values_ref[h, :, :size] = jnp.where(
            own, values[:, start : start + size], jnp.zeros((), BF16)
        )
        values_ref[h, :, size : size + 128] = ones


def attend_rows(query, first_row, rows, heads, keys_ref, values_ref, mixed_ref, mixed_row, work):
    scores_ref, weights_ref, sum_ref = work
    width = query.shape[1]
    head_size = width // heads
    period, windows = head_windows(head_size, width)
    factor = head_size ** (-0.5) * LOG2E
    span = pl.ds(first_row, rows)
    out_span = pl.ds(mixed_row, rows)

    @pl.loop(0, width // period)
    def _(turn):
        base = pl.multiple_of(turn * period, 128)
        first = turn * len(windows)

        def score(h):
            start, size = windows[h]
            scores_ref[h % 2, :rows] = dot(
                query[span, pl.ds(base + start, size)], keys_ref[first + h, :size, :]
            )

        score(0)
        for h, (start, size) in enumerate(windows):
            if h + 1 < len(windows):
                score(h + 1)
            for part in pieces(rows, 64):
                scores = scores_ref[h % 2, part, :]
                highest = jnp.max(scores, axis=1, keepdims=True)
                weights_ref[h % 2, part, :] = jnp.exp2((scores - highest) * factor).astype(BF16)
            mixed = dot(weights_ref[h % 2, :rows], values_ref[first + h, :, : size + 128])
            share = 1.0 / mixed[:, size:]
            for column in range(0, size, 128):
                own = mixed[:, column : column + 128] * share
                at = start + column
                if h * head_size <= at:
                    sum_ref[:rows, at : at + 128] = own
                else:
                    sum_ref[:rows, at : at + 128] += own
        mixed_ref[out_span, pl.ds(base, period)] = sum_ref[:rows].astype(BF16)


def gelu(x):
    half = 0.5 * x
    return half + half * jnp.tanh(x * (0.7978845608028654 + 0.035677408136300125 * (x * x)))


def feed_forward(rows, normed, up_weight, down_weight, total, work):
    wide_ref, inner_ref = work
    spans = pieces(up_weight.shape[1], wide_ref.shape[2])

    def widen(i):
        wide_ref[i % 2, :rows] = dot(normed[:rows], up_weight[:, spans[i]])

    widen(0)
    for i, span in enumerate(spans):
        if i + 1 < len(spans):
            widen(i + 1)
        for part in pieces(rows, 32):
            inner_ref[i % 2, part, :] = gelu(wide_ref[i % 2, part, :]).astype(BF16)
        total[:rows] += dot(inner_ref[i % 2, :rows], down_weight[span, :])


def finish_rows(
    first_row, rows, tokens, mixed, mixed_row, out_weight, gain, up_weight, down_weight, work
):
    total, normed, wide_ref, inner_ref = work
    total[:rows] = (
        (
            tokens[pl.ds(first_row, rows), :].astype(F32)
            + dot(mixed[pl.ds(mixed_row, rows), :], out_weight[...])
        )
        .astype(BF16)
        .astype(F32)
    )
    norm_into(normed, 0, total, gain[...], rows)
    feed_forward(rows, normed, up_weight, down_weight, total, (wide_ref, inner_ref))


def picked_kernel(
    offsets,
    tokens,
    query,
    keyval,
    keyval_far,
    out_weight,
    mlp_gain,
    up_weight,
    down_weight,
    gain,
    key_weight,
    value_weight,
    second,
    keyval_two,
    keys_ref,
    values_ref,
    held,
    mixed,
    scores,
    weights,
    sums,
    total,
    normed,
    wide,
    inner,
    sems,
    *,
    heads,
):
    sources = (out_weight, key_weight, value_weight)
    copies = [bring(x, held.at[i], sems.at[i]) for i, x in enumerate(sources)]
    rows = second.shape[0]
    load_keys((keyval, keyval_far), heads, keys_ref, values_ref)
    attend_rows(
        query, 0, rows, heads, keys_ref, values_ref, mixed, 0, (scores, weights, sums)
    )
    copies[0].wait()
    finish_rows(
        0,
        rows,
        tokens,
        mixed,
        0,
        held.at[0],
        mlp_gain,
        up_weight,
        down_weight,
        (total, normed, wide, inner),
    )
    second[...] = total[...].astype(BF16)
    norm_into(normed, 0, second, gain[...], rows)
    chooser = pick_matrix(slots_of(offsets, heads), heads, rows // heads, heads)
    chosen = dot(chooser, normed[...]).astype(BF16)

    def weight(slot):
        copies[slot + 1].wait()
        return held[slot + 1]

    project_keys(
        chosen, heads, [functools.partial(weight, slot) for slot in range(2)], keyval_two
    )


def rest_kernel(
    tokens,
    query,
    keys_ref,
    values_ref,
    out_weight,
    mlp_gain,
    up_weight,
    down_weight,
    second,
    held,
    mixed,
    scores,
    weights,
    sums,
    total,
    normed,
    wide,
    inner,
    sems,
    *,
    heads,
):
    copy = bring(out_weight, held.at[0], sems.at[0])
    count = second.shape[0]
    skip = tokens.shape[0] - count
    size, block = scores.shape[1], total.shape[0]

    @pl.loop(0, count // size)
    def _(step):
        row = pl.multiple_of(step * size, size)
        attend_rows(
            query,
            pl.multiple_of(skip + row, size),
            size,
            heads,
            keys_ref,
            values_ref,
            mixed,
            row,
            (scores, weights, sums),
        )

    copy.wait()

    @pl.loop(0, count // block)
    def _(step):
        row = pl.multiple_of(step * block, block)
        finish_rows(
            pl.multiple_of(skip + row, 16),
            block,
            tokens,
            mixed,
            row,
            held.at[0],
            mlp_gain,
            up_weight,
            down_weight,
            (total, normed, wide, inner),
        )
        second[pl.ds(row, block), :] = total[...].astype(BF16)


def second_query_kernel(picked, rest, gain, weight, query, held, normed, sems):
    copy = bring(weight, held.at[0], sems.at[0])
    norm_into(normed, 0, picked, gain[...], picked.shape[0])
    norm_into(normed, picked.shape[0], rest, gain[...], rest.shape[0])
    copy.wait()
    for span in pieces(query.shape[0], 512):
        query[span, :] = dot(normed[span, :], held[0]).astype(BF16)


def second_kernel(
    offsets,
    picked,
    rest,
    query,
    keyval,
    keyval_far,
    out_weight,
    encoded,
    keys_ref,
    values_ref,
    held,
    mixed,
    scores,
    weights,
    sums,
    sems,
    *,
    heads,
    stride,
    chunk,
):
    copy = bring(out_weight, held.at[0], sems.at[0])
    load_keys((keyval, keyval_far), heads, keys_ref, values_ref)
    count, size = query.shape[0], scores.shape[1]

    @pl.loop(0, count // size)
    def _(step):
        row = pl.multiple_of(step * size, size)
        attend_rows(
            query,
            row,
            size,
            heads,
            keys_ref,
            values_ref,
            mixed,
            row,
            (scores, weights, sums),
        )

    share = chunk // stride * heads
    rest_share = chunk - share
    start = picked.shape[0]
    back = one_hot(
        lax.broadcasted_iota(jnp.int32, (chunk, chunk), 1)
        == ranks(offsets, chunk, stride, share, 0)
    )
    copy.wait()

    @pl.loop(0, count // chunk)
    def _(step):
        near = pl.multiple_of(step * share, share)
        far = pl.multiple_of(step * rest_share, rest_share)
        blend = jnp.concatenate(
            [
                mixed[pl.ds(near, share), :],
                mixed[pl.ds(pl.multiple_of(start + far, 16), rest_share), :],
            ],
            axis=0,
        )
        rows = jnp.concatenate(
            [picked[pl.ds(near, share), :], rest[pl.ds(far, rest_share), :]], axis=0
        )
        result = (rows.astype(F32) + dot(blend, held[0])).astype(BF16)
        span = pl.ds(pl.multiple_of(step * chunk, chunk), chunk)
        encoded[span, :] = dot(back, result).astype(BF16)


def local_call(kernel, outs, inputs, scratch, scalars=0, far=(), copies=1, flops=0, name=None):
    specs, placed = [], []
    for i, x in enumerate(inputs):
        if i < scalars:
            specs.append(pl.BlockSpec(memory_space=pltpu.SMEM))
        elif i in far:
            specs.append(pl.BlockSpec(memory_space=pltpu.HBM))
        else:
            specs.append(pl.BlockSpec(memory_space=pltpu.VMEM))
            x = pltpu.with_memory_space_constraint(x, pltpu.VMEM)
        placed.append(x)
    return pl.pallas_call(
        kernel,
        out_shape=outs,
        in_specs=specs,
        out_specs=[pl.BlockSpec(memory_space=pltpu.VMEM)] * len(outs),
        scratch_shapes=list(scratch) + [pltpu.SemaphoreType.DMA((copies,))],
        compiler_params=pltpu.CompilerParams(vmem_limit_bytes=VMEM_LIMIT),
        cost_estimate=pl.CostEstimate(
            flops=int(flops),
            transcendentals=0,
            bytes_accessed=sum(inputs[i].size * inputs[i].dtype.itemsize for i in far),
        ),
        name=name,
    )(*placed)


def exchange(keyval, span):
    size = lax.axis_size("seq")
    teams = [
        [start + parity + 2 * i for i in range(span // 2)]
        for start in range(0, size, span)
        for parity in range(2)
    ]
    near = lax.all_to_all(keyval, "seq", 0, 0, axis_index_groups=teams)
    return near, swapped(near, "seq", 0)


def whole_body(
    tokens,
    attn_gain,
    query_first,
    key_first,
    segment_value,
    output_first,
    mlp_gain,
    up_weight,
    down_weight,
    second_gain,
    query_second,
    key_second,
    value_second,
    output_second,
    segment_offset,
    global_offset,
):
    seq_count = lax.axis_size("seq")
    seg_span = min(SEG_MAX, seq_count)
    heads = segment_offset.shape[0]
    count, width = tokens.shape
    head_size = width // heads
    hidden = up_weight.shape[1]
    stride = count // (KEYS // seg_span)
    stride_two = count // (KEYS // seq_count)
    groups, groups_two = count // stride, count // stride_two
    chunk = max(ROWS, stride_two)
    picked_count = groups_two * heads
    rest_count = count - picked_count
    period, windows = head_windows(head_size, width)
    window = max(size for _, size in windows)
    part = hidden // 4 if hidden % 512 == 0 else hidden
    block = rest_count // 2 if rest_count % 32 == 0 else rest_count

    def near(*shape):
        return pltpu.VMEM(shape, BF16)

    def attention_work(rows):
        return [
            pltpu.VMEM((2, rows, KEYS), F32),
            pltpu.VMEM((2, rows, KEYS), BF16),
            pltpu.VMEM((rows, period), F32),
        ]

    def feed_work(rows):
        return [
            pltpu.VMEM((rows, width), F32),
            pltpu.VMEM((rows, width), BF16),
            pltpu.VMEM((2, rows, part), F32),
            pltpu.VMEM((2, rows, part), BF16),
        ]

    keys_shape, values_shape = near(heads, window, KEYS), near(heads, KEYS, window + 128)

    (keyval,) = local_call(
        functools.partial(first_keys_kernel, stride=stride),
        [near(seg_span // 2, 2, groups, width)],
        (segment_offset, tokens, attn_gain, key_first, segment_value),
        [near(count, width), near(2, width, width)],
        scalars=1,
        far=(1, 3, 4),
        copies=3,
        flops=2 * heads * groups * width * (count + 2 * width),
        name="first_keys",
    )
    keyval, keyval_far = exchange(keyval, seg_span)
    rows, query = local_call(
        functools.partial(first_query_kernel, stride=stride_two, chunk=chunk),
        [near(count, width), near(count, width)],
        (global_offset, tokens, attn_gain, query_first),
        [near(count, width), near(width, width), near(count, width)],
        scalars=1,
        far=(1, 3),
        copies=2,
        flops=2 * count * width * (width + chunk),
        name="first_query",
    )
    row_flops = 2 * width * (2 * hidden + width) + 4 * 256 * KEYS * heads
    picked_second, keyval_two, keys, values = local_call(
        functools.partial(picked_kernel, heads=heads),
        [
            near(picked_count, width),
            near(seq_count // 2, 2, groups_two, width),
            keys_shape,
            values_shape,
        ],
        (
            global_offset,
            rows,
            query,
            keyval,
            keyval_far,
            output_first,
            mlp_gain,
            up_weight,
            down_weight,
            second_gain,
            key_second,
            value_second,
        ),
        [near(3, width, width), near(picked_count, width)]
        + attention_work(picked_count)
        + feed_work(picked_count),
        scalars=1,
        far=(5, 10, 11),
        copies=3,
        flops=row_flops * picked_count,
        name="layer_of_picked",
    )
    keyval_two, keyval_two_far = exchange(keyval_two, seq_count)
    (rest_second,) = local_call(
        functools.partial(rest_kernel, heads=heads),
        [near(rest_count, width)],
        (rows, query, keys, values, output_first, mlp_gain, up_weight, down_weight),
        [near(1, width, width), near(rest_count, width)]
        + attention_work(math.gcd(rest_count, ROWS))
        + feed_work(block),
        far=(4,),
        flops=row_flops * rest_count,
        name="layer_of_rest",
    )
    (query_two,) = local_call(
        second_query_kernel,
        [near(count, width)],
        (picked_second, rest_second, second_gain, query_second),
        [near(1, width, width), near(count, width)],
        far=(3,),
        flops=2 * count * width * width,
        name="second_query",
    )
    (encoded,) = local_call(
        functools.partial(second_kernel, heads=heads, stride=stride_two, chunk=chunk),
        [jax.ShapeDtypeStruct((count, width), BF16)],
        (
            global_offset,
            picked_second,
            rest_second,
            query_two,
            keyval_two,
            keyval_two_far,
            output_second,
        ),
        [keys_shape, values_shape, near(1, width, width), near(count, width)]
        + attention_work(math.gcd(count, ROWS)),
        scalars=1,
        far=(6,),
        flops=count * (2 * width * width + 4 * 256 * KEYS * heads),
        name="second_attention",
    )
    return encoded


def solution(mesh):
    placed = (
        P(("slides", "seq", "mp"), None),
        P(),
        P(None, "mp"),
        P(None, "mp"),
        P(None, "mp"),
        P("mp", None),
        P(),
        P(None, "mp"),
        P("mp", None),
        P(),
        P(None, "mp"),
        P(None, "mp"),
        P(None, "mp"),
        P("mp", None),
        P("mp"),
        P("mp"),
    )
    fits = mesh.shape["mp"] == 1 and 2 <= mesh.shape["seq"] <= SEG_MAX
    return jax.shard_map(
        whole_body if fits else split_body,
        mesh=mesh,
        in_specs=placed,
        out_specs=P(("slides", "seq", "mp"), None),
        check_vma=False,
    )
```

```python
import functools
import math

import jax
import jax.numpy as jnp
from jax import lax
from jax.experimental import pallas as pl
from jax.experimental.pallas import tpu as pltpu
from jax.sharding import PartitionSpec as P

KEYS = 256
SEG_MAX = 16
ROWS = 256
LOG2E = 1.4426950408889634
BF16 = jnp.bfloat16
F32 = jnp.float32
VMEM_LIMIT = 22 * 1024 * 1024


def swapped(x, axis, apart):
    return lax.ppermute(x, axis, [(i, i ^ 1 << apart) for i in range(lax.axis_size(axis))])


def norm_rows(values, gain):
    center = values - jnp.mean(values, axis=-1, keepdims=True)
    spread = jnp.mean(center * center, axis=-1, keepdims=True)
    return (center * lax.rsqrt(spread + 1e-05) * gain).astype(jnp.bfloat16)


def pick_keys(hidden, offsets, stride, key_weight, value_weight):
    token_count, width = hidden.shape
    head_count = offsets.shape[0]
    head_size = key_weight.shape[1] // head_count
    grouped_rows = hidden.reshape(token_count // stride, stride, width)
    dilation_selector = (
        lax.broadcasted_iota(jnp.int32, (stride, head_count), 0) == offsets[None, :]
    ).astype(jnp.bfloat16)
    chosen = jnp.einsum(
        "nof,oj->njf", grouped_rows, dilation_selector, preferred_element_type=jnp.float32
    ).astype(jnp.bfloat16)
    key_heads = jnp.einsum(
        "xkr,rkf->xkf",
        chosen,
        key_weight.reshape(width, head_count, head_size),
        preferred_element_type=jnp.float32,
    ).astype(jnp.bfloat16)
    value_heads = jnp.einsum(
        "xkr,rkf->xkf",
        chosen,
        value_weight.reshape(width, head_count, head_size),
        preferred_element_type=jnp.float32,
    ).astype(jnp.bfloat16)
    picked = token_count // stride
    return jnp.stack(
        [
            key_heads.reshape(picked, head_count * head_size),
            value_heads.reshape(picked, head_count * head_size),
        ]
    )


def attend_local(query, keyval, head_count):
    token_count, width = query.shape
    head_size = width // head_count
    query_heads = query.reshape(token_count, head_count, head_size)
    key_heads = keyval[0].reshape(-1, head_count, head_size)
    value_heads = keyval[1].reshape(-1, head_count, head_size)
    scores = jnp.einsum(
        "thd,khd->htk", query_heads, key_heads, preferred_element_type=jnp.float32
    ) * head_size ** (-0.5)
    highest = jnp.max(scores, axis=-1, keepdims=True)
    weights = jnp.exp(scores - highest)
    weights = (weights / jnp.sum(weights, axis=-1, keepdims=True)).astype(jnp.bfloat16)
    mixed = jnp.einsum(
        "htk,khd->thd", weights, value_heads, preferred_element_type=jnp.float32
    ).astype(jnp.bfloat16)
    return mixed.reshape(token_count, width)


def merge_branch_pair(mine, other, level, token_position):
    lower = token_position >> level & 1 == 0
    return jnp.where(
        lower, jnp.concatenate((mine, other), axis=1), jnp.concatenate((other, mine), axis=1)
    )


def spread_segment(keyval, seg_span, token_position):
    for level in range(seg_span.bit_length() - 1):
        partner = swapped(keyval, "seq", level)
        keyval = merge_branch_pair(keyval, partner, level, token_position)
    return keyval


def spread_global(keyval_two):
    keyval_two = lax.all_gather(keyval_two, "seq", axis=1, tiled=True)
    return keyval_two


def combine(partial_value, residual_full, need_full):
    row_count = residual_full.shape[0] // lax.axis_size("mp")
    row_start = lax.axis_index("mp") * row_count
    share = lax.psum_scatter(partial_value, "mp", scatter_dimension=0, tiled=True)
    own_rows = lax.dynamic_slice_in_dim(residual_full, row_start, row_count, 0)
    own_rows = (own_rows.astype(jnp.float32) + share).astype(jnp.bfloat16)
    full_rows = lax.all_gather(own_rows, "mp", axis=0, tiled=True) if need_full else own_rows
    return (own_rows, full_rows)


def split_body(
    tokens,
    attn_gain,
    query_first,
    key_first,
    segment_value,
    output_first,
    mlp_gain,
    up_weight,
    down_weight,
    second_gain,
    query_second,
    key_second,
    value_second,
    output_second,
    segment_offset,
    global_offset,
):
    seq_count = lax.axis_size("seq")
    token_position = lax.axis_index("seq")
    seg_span = min(SEG_MAX, seq_count)
    head_count = segment_offset.shape[0]
    full_rows = lax.all_gather(tokens, "mp", axis=0, tiled=True)
    token_count = full_rows.shape[0]
    hidden = norm_rows(full_rows.astype(jnp.float32), attn_gain)
    query = jnp.dot(hidden, query_first, preferred_element_type=jnp.float32).astype(jnp.bfloat16)
    seg_stride = token_count // (KEYS // seg_span)
    keyval = pick_keys(hidden, segment_offset, seg_stride, key_first, segment_value)
    keyval = spread_segment(keyval, seg_span, token_position)
    mixed = attend_local(query, keyval, head_count)
    partial_value = jnp.dot(mixed, output_first, preferred_element_type=jnp.float32)
    own_rows, first_rows = combine(partial_value, full_rows, True)
    normed = norm_rows(first_rows.astype(jnp.float32), mlp_gain)
    inner = jax.nn.gelu(
        jnp.dot(normed, up_weight, preferred_element_type=jnp.float32), approximate=True
    ).astype(jnp.bfloat16)
    partial_value = jnp.dot(inner, down_weight, preferred_element_type=jnp.float32)
    own_rows, second_rows = combine(partial_value, first_rows, True)
    hidden_two = norm_rows(second_rows.astype(jnp.float32), second_gain)
    query_two = jnp.dot(hidden_two, query_second, preferred_element_type=jnp.float32).astype(
        jnp.bfloat16
    )
    glob_stride = token_count // (KEYS // seq_count)
    keyval_two = pick_keys(hidden_two, global_offset, glob_stride, key_second, value_second)
    keyval_two = spread_global(keyval_two)
    mixed_two = attend_local(query_two, keyval_two, head_count)
    partial_value = jnp.dot(mixed_two, output_second, preferred_element_type=jnp.float32)
    own_rows, unused_rows = combine(partial_value, second_rows, False)
    return own_rows


def one_hot(condition):
    return jnp.where(condition, 1.0, 0.0).astype(BF16)


def dot(left, right):
    return jnp.dot(left, right, preferred_element_type=F32)


def pieces(count, size):
    size = size if count % size == 0 else count
    return [slice(start, start + size) for start in range(0, count, size)]


def norm_into(out, start, source, gain, count):
    for span in pieces(count, 64):
        out[start + span.start : start + span.stop, :] = norm_rows(
            source[span, :].astype(F32), gain
        )


def bring(source, target, sem):
    copy = pltpu.make_async_copy(source, target, sem)
    copy.start()
    return copy


def pick_matrix(offsets, heads, groups, stride):
    count = groups * stride
    place = lax.broadcasted_iota(jnp.int32, (groups, count), 1)
    place = place - lax.broadcasted_iota(jnp.int32, (groups, count), 0) * stride
    return jnp.concatenate([one_hot(place == offsets[h]) for h in range(heads)], axis=0)


def project_keys(chosen, heads, weights, keyval_ref):
    rows, width = chosen.shape
    groups, head_size = rows // heads, width // heads
    column = lax.broadcasted_iota(jnp.int32, (groups, width), 1)
    for slot, weight in enumerate(weights):
        wide = dot(chosen, weight())
        total = jnp.zeros((groups, width), F32)
        for h in range(heads):
            own = (column >= h * head_size) & (column < (h + 1) * head_size)
            total = jnp.where(own, wide[h * groups : (h + 1) * groups], total)
        total = total.astype(BF16)
        for copy in range(keyval_ref.shape[0]):
            keyval_ref[copy, slot] = total


def ranks(offsets, chunk, stride, share, axis):
    heads = offsets.shape[0]

    def places(way):
        shape = (1, chunk) if way else (chunk, 1)
        place = lax.broadcasted_iota(jnp.int32, shape, way)
        inside = lax.rem(place, stride)
        taken = inside == offsets[0]
        for h in range(1, heads):
            taken = taken | (inside == offsets[h])
        return place, inside, jnp.where(taken, inside, inside + stride)

    place, inside, order = places(axis)
    other_place, _, other_order = places(1 - axis)
    ahead = (other_order < order) & (lax.div(other_place, stride) == lax.div(place, stride))
    rank = jnp.sum(jnp.where(ahead, 1, 0), axis=1 - axis, keepdims=True)
    group = lax.div(place, stride)
    return jnp.where(
        rank < heads, group * heads + rank, share + group * (stride - heads) + rank - heads
    )


def slots_of(offsets, heads):
    values = [offsets[h] for h in range(heads)]
    fresh = []
    for h in range(heads):
        seen = jnp.int32(1)
        for earlier in values[:h]:
            seen = jnp.where(earlier == values[h], 0, seen)
        fresh.append(seen)
    slots = []
    for h in range(heads):
        slot = jnp.int32(0)
        for other in range(heads):
            slot = slot + jnp.where(values[other] < values[h], fresh[other], 0)
        slots.append(slot)
    return slots


def first_keys_kernel(
    offsets, tokens, gain, key_weight, value_weight, keyval, rows, wide, sems, *, stride
):
    copies = [
        bring(tokens, rows, sems.at[0]),
        bring(key_weight, wide.at[0], sems.at[1]),
        bring(value_weight, wide.at[1], sems.at[2]),
    ]
    heads = offsets.shape[0]
    chooser = pick_matrix(offsets, heads, rows.shape[0] // stride, stride)
    copies[0].wait()
    chosen = norm_rows(dot(chooser, rows[...]), gain[...])

    def weight(slot):
        copies[slot + 1].wait()
        return wide[slot]

    project_keys(
        chosen, heads, [functools.partial(weight, slot) for slot in range(2)], keyval
    )


def scaled(query, head_size):
    return (query * (head_size ** (-0.5) * LOG2E)).astype(BF16)


def order_kernel(
    offsets, tokens, gain, moved_rows, normed, rows, sems, *, stride, chunk
):
    copy = bring(tokens, rows, sems.at[0])
    count = tokens.shape[0]
    share = chunk // stride * offsets.shape[0]
    rest = chunk - share
    picked = count // chunk * share
    mover = one_hot(
        lax.broadcasted_iota(jnp.int32, (chunk, chunk), 0)
        == ranks(offsets, chunk, stride, share, 1)
    )
    copy.wait()
    for c in range(count // chunk):
        moved = dot(mover, rows[c * chunk : (c + 1) * chunk, :]).astype(BF16)
        moved_rows[c * share : (c + 1) * share, :] = moved[:share]
        moved_rows[picked + c * rest : picked + (c + 1) * rest, :] = moved[share:]
    norm_into(normed, 0, moved_rows, gain[...], count)


def first_query_kernel(normed, weight, query, held, sems, *, head_size):
    copy = bring(weight, held, sems.at[0])
    copy.wait()
    for span in pieces(normed.shape[0], 512):
        query[span, :] = scaled(dot(normed[span, :], held[...]), head_size)


def head_windows(head_size, width):
    period = min(width, math.lcm(head_size, 128))
    windows = []
    for h in range(period // head_size):
        start = h * head_size // 128 * 128
        stop = min(period, -(-(h + 1) * head_size // 128) * 128)
        windows.append((start, stop - start))
    return period, windows


def load_keys(keyvals, heads, keys_ref, values_ref, peaks_ref):
    keys = jnp.concatenate([x[i, 0] for x in keyvals for i in range(x.shape[0])], axis=0)
    peaks_ref[...] = head_peaks(keys, heads)
    values = jnp.concatenate([x[i, 1] for x in keyvals for i in range(x.shape[0])], axis=0)
    key_count, width = keys.shape
    head_size = width // heads
    period, windows = head_windows(head_size, width)
    turned = keys.T
    ones = jnp.ones((key_count, 128), BF16)
    for h in range(heads):
        start, size = windows[h % len(windows)]
        start = start + h // len(windows) * period
        low = h * head_size - start
        keys_ref[h, :size, :] = jnp.zeros((size, key_count), BF16)
        keys_ref[h, low : low + head_size, :] = turned[h * head_size : (h + 1) * head_size]
        column = lax.broadcasted_iota(jnp.int32, (key_count, size), 1)
        own = (column >= low) & (column < low + head_size)
        values_ref[h, :, :size] = jnp.where(
            own, values[:, start : start + size], jnp.zeros((), BF16)
        )
        values_ref[h, :, size : size + 128] = ones


def head_peaks(rows, heads):
    width = rows.shape[1]
    column = lax.broadcasted_iota(jnp.int32, (width, 128), 0)
    head = lax.broadcasted_iota(jnp.int32, (width, 128), 1)
    low = head * (width // heads)
    sums = one_hot((column >= low) & (column < low + width // heads))
    return jnp.max(dot(rows * rows, sums), axis=0, keepdims=True)


def small_scores(query, first_row, rows, heads, keys):
    bound = head_peaks(query[pl.ds(first_row, rows), :], heads) * keys
    return jnp.max(bound) < 9000.0


def reciprocal(x):
    guess = pl.reciprocal(x, approx=True)
    return guess * (2.0 - x * guess)


def attend_rows(
    query, first_row, rows, heads, keys_ref, values_ref, mixed_ref, mixed_row, work, plain
):
    scores_ref, weights_ref = work
    width = query.shape[1]
    head_size = width // heads
    period, windows = head_windows(head_size, width)
    span = pl.ds(first_row, rows)
    out_span = pl.ds(mixed_row, rows)

    @pl.loop(0, width // period)
    def _(turn):
        base = pl.multiple_of(turn * period, 128)
        first = turn * len(windows)
        sums = {}

        def score(h):
            start, size = windows[h]
            scores_ref[h % 2, :rows] = dot(
                query[span, pl.ds(base + start, size)], keys_ref[first + h, :size, :]
            )

        score(0)
        for h, (start, size) in enumerate(windows):
            if h + 1 < len(windows):
                score(h + 1)
            for part in pieces(rows, 64):
                scores = scores_ref[h % 2, part, :]
                if not plain:
                    scores = scores - jnp.max(scores, axis=1, keepdims=True)
                weights_ref[h % 2, part, :] = jnp.exp2(scores).astype(BF16)
            mixed = dot(weights_ref[h % 2, :rows], values_ref[first + h, :, : size + 128])
            share = reciprocal(mixed[:, size:])
            for column in range(0, size, 128):
                own = mixed[:, column : column + 128] * share
                at = start + column
                sums[at] = own + sums[at] if at in sums else own
                if (h + 1) * head_size >= at + 128:
                    mixed_ref[out_span, pl.ds(base + at, 128)] = sums.pop(at).astype(BF16)


def attend(query, first_row, rows, heads, keys_ref, values_ref, mixed_ref, work, peaks):
    size = work[0].shape[1]
    small = small_scores(query, first_row, rows, heads, peaks)

    def run(plain):
        @pl.loop(0, rows // size)
        def _(step):
            row = pl.multiple_of(step * size, size)
            attend_rows(
                query,
                pl.multiple_of(first_row + row, 16),
                size,
                heads,
                keys_ref,
                values_ref,
                mixed_ref,
                row,
                work,
                plain,
            )

    @pl.when(small)
    def _():
        run(True)

    @pl.when(jnp.logical_not(small))
    def _():
        run(False)


def gelu(x):
    half = 0.5 * x
    return half + half * jnp.tanh(x * (0.7978845608028654 + 0.035677408136300125 * (x * x)))


def feed_forward(rows, normed, up_weight, down_weight, total, work):
    wide_ref, inner_ref = work
    spans = pieces(up_weight.shape[1], wide_ref.shape[2])

    def widen(i):
        wide_ref[i % 2, :rows] = dot(normed[:rows], up_weight[:, spans[i]])

    widen(0)
    for i, span in enumerate(spans):
        if i + 1 < len(spans):
            widen(i + 1)
        for part in pieces(rows, 32):
            inner_ref[i % 2, part, :] = gelu(wide_ref[i % 2, part, :]).astype(BF16)
        total[:rows] += dot(inner_ref[i % 2, :rows], down_weight[span, :])


def finish_rows(
    first_row, rows, tokens, mixed, mixed_row, out_weight, gain, up_weight, down_weight, work
):
    total, normed, wide_ref, inner_ref = work
    total[:rows] = (
        (
            tokens[pl.ds(first_row, rows), :].astype(F32)
            + dot(mixed[pl.ds(mixed_row, rows), :], out_weight[...])
        )
        .astype(BF16)
        .astype(F32)
    )
    norm_into(normed, 0, total, gain[...], rows)
    feed_forward(rows, normed, up_weight, down_weight, total, (wide_ref, inner_ref))


def picked_kernel(
    offsets,
    tokens,
    query,
    keyval,
    keyval_far,
    out_weight,
    mlp_gain,
    up_weight,
    down_weight,
    gain,
    key_weight,
    value_weight,
    second,
    keyval_two,
    keys_ref,
    values_ref,
    peaks,
    held,
    mixed,
    scores,
    weights,
    total,
    normed,
    wide,
    inner,
    sems,
    *,
    heads,
):
    sources = (out_weight, key_weight, value_weight)
    copies = [bring(x, held.at[i], sems.at[i]) for i, x in enumerate(sources)]
    rows = second.shape[0]
    load_keys((keyval, keyval_far), heads, keys_ref, values_ref, peaks)
    attend(query, 0, rows, heads, keys_ref, values_ref, mixed, (scores, weights), peaks[...])
    copies[0].wait()
    finish_rows(
        0,
        rows,
        tokens,
        mixed,
        0,
        held.at[0],
        mlp_gain,
        up_weight,
        down_weight,
        (total, normed, wide, inner),
    )
    second[...] = total[...].astype(BF16)
    norm_into(normed, 0, second, gain[...], rows)
    chooser = pick_matrix(slots_of(offsets, heads), heads, rows // heads, heads)
    chosen = dot(chooser, normed[...]).astype(BF16)

    def weight(slot):
        copies[slot + 1].wait()
        return held[slot + 1]

    project_keys(
        chosen, heads, [functools.partial(weight, slot) for slot in range(2)], keyval_two
    )


def rest_kernel(
    tokens,
    query,
    keys_ref,
    values_ref,
    peaks,
    out_weight,
    mlp_gain,
    up_weight,
    down_weight,
    second,
    held,
    mixed,
    scores,
    weights,
    total,
    normed,
    wide,
    inner,
    sems,
    *,
    heads,
    first_row,
):
    copy = bring(out_weight, held.at[0], sems.at[0])
    rows = second.shape[0]
    attend(
        query, first_row, rows, heads, keys_ref, values_ref, mixed, (scores, weights), peaks[...]
    )
    copy.wait()
    finish_rows(
        first_row,
        rows,
        tokens,
        mixed,
        0,
        held.at[0],
        mlp_gain,
        up_weight,
        down_weight,
        (total, normed, wide, inner),
    )
    second[...] = total[...].astype(BF16)


def second_query_kernel(*refs, head_size):
    *rows, gain, weight, query, held, normed, sems = refs
    copy = bring(weight, held.at[0], sems.at[0])
    start = 0
    for part in rows:
        norm_into(normed, start, part, gain[...], part.shape[0])
        start += part.shape[0]
    copy.wait()
    for span in pieces(query.shape[0], 512):
        query[span, :] = scaled(dot(normed[span, :], held[0]), head_size)


def second_kernel(*refs, heads, stride, chunk, parts):
    offsets, *rows = refs[: 1 + parts]
    query, keyval, keyval_far, out_weight, encoded = refs[1 + parts : 6 + parts]
    keys_ref, values_ref, peaks, held, mixed, second, scores, weights, sems = refs[6 + parts :]
    copy = bring(out_weight, held.at[0], sems.at[0])
    start = 0
    for part in rows:
        second[start : start + part.shape[0], :] = part[...]
        start += part.shape[0]
    load_keys((keyval, keyval_far), heads, keys_ref, values_ref, peaks)
    count = query.shape[0]
    attend(
        query, 0, count, heads, keys_ref, values_ref, mixed, (scores, weights), peaks[...]
    )
    share = chunk // stride * heads
    rest_share = chunk - share
    start = count // chunk * share
    back = one_hot(
        lax.broadcasted_iota(jnp.int32, (chunk, chunk), 1)
        == ranks(offsets, chunk, stride, share, 0)
    )
    copy.wait()

    @pl.loop(0, count // chunk)
    def _(step):
        near = pl.ds(pl.multiple_of(step * share, share), share)
        far = pl.ds(pl.multiple_of(start + step * rest_share, 16), rest_share)
        blend = jnp.concatenate([mixed[near, :], mixed[far, :]], axis=0)
        residual = jnp.concatenate([second[near, :], second[far, :]], axis=0)
        result = (residual.astype(F32) + dot(blend, held[0])).astype(BF16)
        span = pl.ds(pl.multiple_of(step * chunk, chunk), chunk)
        encoded[span, :] = dot(back, result).astype(BF16)


def relaying(kernel, ins, outs, *refs):
    end = ins + 1 + outs
    refs[end][...] = refs[ins][...]
    kernel(*refs[:ins], *refs[ins + 1 : end], *refs[end + 1 :])


def local_call(kernel, outs, inputs, scratch, scalars=0, far=(), relay=None, copies=1, flops=0, name=None):
    outs, inputs = list(outs), list(inputs)
    if relay is not None:
        kernel = functools.partial(relaying, kernel, len(inputs), len(outs))
        inputs.append(relay)
        outs.append(pltpu.VMEM(relay.shape, relay.dtype))
    specs, placed = [], []
    for i, x in enumerate(inputs):
        if i < scalars:
            specs.append(pl.BlockSpec(memory_space=pltpu.SMEM))
        elif i in far:
            specs.append(pl.BlockSpec(memory_space=pltpu.HBM))
            x = pltpu.with_memory_space_constraint(x, pltpu.HBM)
        else:
            specs.append(pl.BlockSpec(memory_space=pltpu.VMEM))
            x = pltpu.with_memory_space_constraint(x, pltpu.VMEM)
        placed.append(x)
    return pl.pallas_call(
        kernel,
        out_shape=outs,
        in_specs=specs,
        out_specs=[pl.BlockSpec(memory_space=pltpu.VMEM)] * len(outs),
        scratch_shapes=list(scratch) + [pltpu.SemaphoreType.DMA((copies,))],
        compiler_params=pltpu.CompilerParams(vmem_limit_bytes=VMEM_LIMIT),
        cost_estimate=pl.CostEstimate(
            flops=int(flops),
            transcendentals=0,
            bytes_accessed=sum(inputs[i].size * inputs[i].dtype.itemsize for i in far),
        ),
        name=name,
    )(*placed)


def exchange(keyval, span, beside):
    levels = span.bit_length() - 1
    for level in reversed(range(levels)):
        partner = swapped(keyval, "seq", level)
        keyval = beside(levels - 1 - level, keyval)
        if level:
            keyval = jnp.concatenate([keyval, partner], axis=0)
    return keyval, partner


def whole_body(
    tokens,
    attn_gain,
    query_first,
    key_first,
    segment_value,
    output_first,
    mlp_gain,
    up_weight,
    down_weight,
    second_gain,
    query_second,
    key_second,
    value_second,
    output_second,
    segment_offset,
    global_offset,
):
    seq_count = lax.axis_size("seq")
    seg_span = min(SEG_MAX, seq_count)
    heads = segment_offset.shape[0]
    count, width = tokens.shape
    head_size = width // heads
    hidden = up_weight.shape[1]
    stride = count // (KEYS // seg_span)
    stride_two = count // (KEYS // seq_count)
    groups, groups_two = count // stride, count // stride_two
    chunk = max(ROWS, stride_two)
    picked_count = groups_two * heads
    rest_count = count - picked_count
    _, windows = head_windows(head_size, width)
    window = max(size for _, size in windows)
    part = hidden // 4 if hidden % 512 == 0 else hidden
    block = ROWS if rest_count % ROWS == 0 else rest_count

    def near(*shape):
        return pltpu.VMEM(shape, BF16)

    def attention_work(rows):
        return [
            pltpu.VMEM((2, rows, KEYS), F32),
            pltpu.VMEM((2, rows, KEYS), BF16),
        ]

    def feed_work(rows):
        return [
            pltpu.VMEM((rows, width), F32),
            pltpu.VMEM((rows, width), BF16),
            pltpu.VMEM((2, rows, part), F32),
            pltpu.VMEM((2, rows, part), BF16),
        ]

    held_shapes = [
        near(heads, window, KEYS),
        near(heads, KEYS, window + 128),
        pltpu.VMEM((1, 128), F32),
    ]

    (keyval,) = local_call(
        functools.partial(first_keys_kernel, stride=stride),
        [near(1, 2, groups, width)],
        (segment_offset, tokens, attn_gain, key_first, segment_value),
        [near(count, width), near(2, width, width)],
        scalars=1,
        far=(1, 3, 4),
        copies=3,
        flops=2 * heads * groups * width * (count + 2 * width),
        name="first_keys",
    )
    made = {}

    def beside_first(level, held):
        if level == 0:
            made["rows"], made["normed"], held = local_call(
                functools.partial(order_kernel, stride=stride_two, chunk=chunk),
                [near(count, width), near(count, width)],
                (global_offset, tokens, attn_gain),
                [near(count, width)],
                scalars=1,
                far=(1,),
                relay=held,
                flops=2 * count * width * chunk,
                name="order",
            )
        if level == min(1, seg_span.bit_length() - 2):
            made["query"], held = local_call(
                functools.partial(first_query_kernel, head_size=head_size),
                [near(count, width)],
                (made["normed"], query_first),
                [near(width, width)],
                far=(1,),
                relay=held,
                flops=2 * count * width * width,
                name="first_query",
            )
        return held

    keyval, keyval_far = exchange(keyval, seg_span, beside_first)
    rows, query = made["rows"], made["query"]
    row_flops = 2 * width * (2 * hidden + width) + 4 * 256 * KEYS * heads
    picked_second, keyval_two, keys, values, peaks = local_call(
        functools.partial(picked_kernel, heads=heads),
        [
            near(picked_count, width),
            near(1, 2, groups_two, width),
        ]
        + held_shapes,
        (
            global_offset,
            rows,
            query,
            keyval,
            keyval_far,
            output_first,
            mlp_gain,
            up_weight,
            down_weight,
            second_gain,
            key_second,
            value_second,
        ),
        [near(3, width, width), near(picked_count, width)]
        + attention_work(picked_count)
        + feed_work(picked_count),
        scalars=1,
        far=(5, 10, 11),
        copies=3,
        flops=row_flops * picked_count,
        name="layer_of_picked",
    )
    seconds = [picked_second]

    def rest_rows(first_row, held):
        result, held = local_call(
            functools.partial(rest_kernel, heads=heads, first_row=first_row),
            [near(block, width)],
            (
                rows,
                query,
                keys,
                values,
                peaks,
                output_first,
                mlp_gain,
                up_weight,
                down_weight,
            ),
            [near(1, width, width), near(block, width)] + attention_work(block) + feed_work(block),
            far=(5,),
            relay=held,
            flops=row_flops * block,
            name="layer_of_rest",
        )
        seconds.append(result)
        return held

    def beside_second(level, held):
        last = level == seq_count.bit_length() - 2
        blocks = rest_count // block
        for i in range(blocks):
            if i == level or (last and i > level):
                held = rest_rows(picked_count + i * block, held)
        if last:
            made["query_two"], held = local_call(
                functools.partial(second_query_kernel, head_size=head_size),
                [near(count, width)],
                (*seconds, second_gain, query_second),
                [near(1, width, width), near(count, width)],
                far=(len(seconds) + 1,),
                relay=held,
                flops=2 * count * width * width,
                name="second_query",
            )
        return held

    keyval_two, keyval_two_far = exchange(keyval_two, seq_count, beside_second)
    (encoded,) = local_call(
        functools.partial(
            second_kernel, heads=heads, stride=stride_two, chunk=chunk, parts=len(seconds)
        ),
        [jax.ShapeDtypeStruct((count, width), BF16)],
        (
            global_offset,
            *seconds,
            made["query_two"],
            keyval_two,
            keyval_two_far,
            output_second,
        ),
        held_shapes
        + [near(1, width, width), near(count, width), near(count, width)]
        + attention_work(math.gcd(count, ROWS)),
        scalars=1,
        far=(len(seconds) + 4,),
        flops=count * (2 * width * width + 4 * 256 * KEYS * heads),
        name="second_attention",
    )
    return encoded


def solution(mesh):
    placed = (
        P(("slides", "seq", "mp"), None),
        P(),
        P(None, "mp"),
        P(None, "mp"),
        P(None, "mp"),
        P("mp", None),
        P(),
        P(None, "mp"),
        P("mp", None),
        P(),
        P(None, "mp"),
        P(None, "mp"),
        P(None, "mp"),
        P("mp", None),
        P("mp"),
        P("mp"),
    )
    fits = mesh.shape["mp"] == 1 and 2 <= mesh.shape["seq"] <= SEG_MAX
    return jax.shard_map(
        whole_body if fits else split_body,
        mesh=mesh,
        in_specs=placed,
        out_specs=P(("slides", "seq", "mp"), None),
        check_vma=False,
    )
```

```python
import functools
import math

import jax
import jax.numpy as jnp
from jax import lax
from jax.experimental import pallas as pl
from jax.experimental.pallas import tpu as pltpu
from jax.sharding import PartitionSpec as P

KEYS = 256
SEG_MAX = 16
ROWS = 256
LOG2E = 1.4426950408889634
BF16 = jnp.bfloat16
F32 = jnp.float32
VMEM_LIMIT = 22 * 1024 * 1024


def swapped(x, axis, apart):
    return lax.ppermute(x, axis, [(i, i ^ 1 << apart) for i in range(lax.axis_size(axis))])


def norm_rows(values, gain):
    center = values - jnp.mean(values, axis=-1, keepdims=True)
    spread = jnp.mean(center * center, axis=-1, keepdims=True)
    return (center * lax.rsqrt(spread + 1e-05) * gain).astype(jnp.bfloat16)


def pick_keys(hidden, offsets, stride, key_weight, value_weight):
    token_count, width = hidden.shape
    head_count = offsets.shape[0]
    head_size = key_weight.shape[1] // head_count
    grouped_rows = hidden.reshape(token_count // stride, stride, width)
    dilation_selector = (
        lax.broadcasted_iota(jnp.int32, (stride, head_count), 0) == offsets[None, :]
    ).astype(jnp.bfloat16)
    chosen = jnp.einsum(
        "nof,oj->njf", grouped_rows, dilation_selector, preferred_element_type=jnp.float32
    ).astype(jnp.bfloat16)
    key_heads = jnp.einsum(
        "xkr,rkf->xkf",
        chosen,
        key_weight.reshape(width, head_count, head_size),
        preferred_element_type=jnp.float32,
    ).astype(jnp.bfloat16)
    value_heads = jnp.einsum(
        "xkr,rkf->xkf",
        chosen,
        value_weight.reshape(width, head_count, head_size),
        preferred_element_type=jnp.float32,
    ).astype(jnp.bfloat16)
    picked = token_count // stride
    return jnp.stack(
        [
            key_heads.reshape(picked, head_count * head_size),
            value_heads.reshape(picked, head_count * head_size),
        ]
    )


def attend_local(query, keyval, head_count):
    token_count, width = query.shape
    head_size = width // head_count
    query_heads = query.reshape(token_count, head_count, head_size)
    key_heads = keyval[0].reshape(-1, head_count, head_size)
    value_heads = keyval[1].reshape(-1, head_count, head_size)
    scores = jnp.einsum(
        "thd,khd->htk", query_heads, key_heads, preferred_element_type=jnp.float32
    ) * head_size ** (-0.5)
    highest = jnp.max(scores, axis=-1, keepdims=True)
    weights = jnp.exp(scores - highest)
    weights = (weights / jnp.sum(weights, axis=-1, keepdims=True)).astype(jnp.bfloat16)
    mixed = jnp.einsum(
        "htk,khd->thd", weights, value_heads, preferred_element_type=jnp.float32
    ).astype(jnp.bfloat16)
    return mixed.reshape(token_count, width)


def merge_branch_pair(mine, other, level, token_position):
    lower = token_position >> level & 1 == 0
    return jnp.where(
        lower, jnp.concatenate((mine, other), axis=1), jnp.concatenate((other, mine), axis=1)
    )


def spread_segment(keyval, seg_span, token_position):
    for level in range(seg_span.bit_length() - 1):
        partner = swapped(keyval, "seq", level)
        keyval = merge_branch_pair(keyval, partner, level, token_position)
    return keyval


def spread_global(keyval_two):
    keyval_two = lax.all_gather(keyval_two, "seq", axis=1, tiled=True)
    return keyval_two


def combine(partial_value, residual_full, need_full):
    row_count = residual_full.shape[0] // lax.axis_size("mp")
    row_start = lax.axis_index("mp") * row_count
    share = lax.psum_scatter(partial_value, "mp", scatter_dimension=0, tiled=True)
    own_rows = lax.dynamic_slice_in_dim(residual_full, row_start, row_count, 0)
    own_rows = (own_rows.astype(jnp.float32) + share).astype(jnp.bfloat16)
    full_rows = lax.all_gather(own_rows, "mp", axis=0, tiled=True) if need_full else own_rows
    return (own_rows, full_rows)


def split_body(
    tokens,
    attn_gain,
    query_first,
    key_first,
    segment_value,
    output_first,
    mlp_gain,
    up_weight,
    down_weight,
    second_gain,
    query_second,
    key_second,
    value_second,
    output_second,
    segment_offset,
    global_offset,
):
    seq_count = lax.axis_size("seq")
    token_position = lax.axis_index("seq")
    seg_span = min(SEG_MAX, seq_count)
    head_count = segment_offset.shape[0]
    full_rows = lax.all_gather(tokens, "mp", axis=0, tiled=True)
    token_count = full_rows.shape[0]
    hidden = norm_rows(full_rows.astype(jnp.float32), attn_gain)
    query = jnp.dot(hidden, query_first, preferred_element_type=jnp.float32).astype(jnp.bfloat16)
    seg_stride = token_count // (KEYS // seg_span)
    keyval = pick_keys(hidden, segment_offset, seg_stride, key_first, segment_value)
    keyval = spread_segment(keyval, seg_span, token_position)
    mixed = attend_local(query, keyval, head_count)
    partial_value = jnp.dot(mixed, output_first, preferred_element_type=jnp.float32)
    own_rows, first_rows = combine(partial_value, full_rows, True)
    normed = norm_rows(first_rows.astype(jnp.float32), mlp_gain)
    inner = jax.nn.gelu(
        jnp.dot(normed, up_weight, preferred_element_type=jnp.float32), approximate=True
    ).astype(jnp.bfloat16)
    partial_value = jnp.dot(inner, down_weight, preferred_element_type=jnp.float32)
    own_rows, second_rows = combine(partial_value, first_rows, True)
    hidden_two = norm_rows(second_rows.astype(jnp.float32), second_gain)
    query_two = jnp.dot(hidden_two, query_second, preferred_element_type=jnp.float32).astype(
        jnp.bfloat16
    )
    glob_stride = token_count // (KEYS // seq_count)
    keyval_two = pick_keys(hidden_two, global_offset, glob_stride, key_second, value_second)
    keyval_two = spread_global(keyval_two)
    mixed_two = attend_local(query_two, keyval_two, head_count)
    partial_value = jnp.dot(mixed_two, output_second, preferred_element_type=jnp.float32)
    own_rows, unused_rows = combine(partial_value, second_rows, False)
    return own_rows


def one_hot(condition):
    return jnp.where(condition, 1.0, 0.0).astype(BF16)


def dot(left, right):
    return jnp.dot(left, right, preferred_element_type=F32)


def pieces(count, size):
    size = size if count % size == 0 else count
    return [slice(start, start + size) for start in range(0, count, size)]


def norm_into(out, start, source, gain, count):
    for span in pieces(count, 64):
        out[start + span.start : start + span.stop, :] = norm_rows(
            source[span, :].astype(F32), gain
        )


def bring(source, target, sem):
    copy = pltpu.make_async_copy(source, target, sem)
    copy.start()
    return copy


def pick_matrix(offsets, heads, groups, stride):
    count = groups * stride
    place = lax.broadcasted_iota(jnp.int32, (groups, count), 1)
    place = place - lax.broadcasted_iota(jnp.int32, (groups, count), 0) * stride
    return jnp.concatenate([one_hot(place == offsets[h]) for h in range(heads)], axis=0)


def project_keys(chosen, heads, weights, keyval_ref):
    rows, width = chosen.shape
    groups, head_size = rows // heads, width // heads
    column = lax.broadcasted_iota(jnp.int32, (groups, width), 1)
    for slot, weight in enumerate(weights):
        wide = dot(chosen, weight())
        total = jnp.zeros((groups, width), F32)
        for h in range(heads):
            own = (column >= h * head_size) & (column < (h + 1) * head_size)
            total = jnp.where(own, wide[h * groups : (h + 1) * groups], total)
        total = total.astype(BF16)
        for copy in range(keyval_ref.shape[0]):
            keyval_ref[copy, slot] = total


def ranks(offsets, chunk, stride, share, axis):
    heads = offsets.shape[0]

    def places(way):
        shape = (1, chunk) if way else (chunk, 1)
        place = lax.broadcasted_iota(jnp.int32, shape, way)
        inside = lax.rem(place, stride)
        taken = inside == offsets[0]
        for h in range(1, heads):
            taken = taken | (inside == offsets[h])
        return place, inside, jnp.where(taken, inside, inside + stride)

    place, inside, order = places(axis)
    other_place, _, other_order = places(1 - axis)
    ahead = (other_order < order) & (lax.div(other_place, stride) == lax.div(place, stride))
    rank = jnp.sum(jnp.where(ahead, 1, 0), axis=1 - axis, keepdims=True)
    group = lax.div(place, stride)
    return jnp.where(
        rank < heads, group * heads + rank, share + group * (stride - heads) + rank - heads
    )


def slots_of(offsets, heads):
    values = [offsets[h] for h in range(heads)]
    fresh = []
    for h in range(heads):
        seen = jnp.int32(1)
        for earlier in values[:h]:
            seen = jnp.where(earlier == values[h], 0, seen)
        fresh.append(seen)
    slots = []
    for h in range(heads):
        slot = jnp.int32(0)
        for other in range(heads):
            slot = slot + jnp.where(values[other] < values[h], fresh[other], 0)
        slots.append(slot)
    return slots


def first_keys_kernel(
    offsets, tokens, gain, key_weight, value_weight, keyval, rows, wide, picks, scale, sems, *, stride
):
    copies = [
        bring(offsets, picks, sems.at[0]),
        bring(tokens, rows, sems.at[1]),
        bring(gain, scale, sems.at[2]),
        bring(key_weight, wide.at[0], sems.at[3]),
        bring(value_weight, wide.at[1], sems.at[4]),
    ]
    heads = offsets.shape[0]
    copies[0].wait()
    chooser = pick_matrix(picks, heads, rows.shape[0] // stride, stride)
    copies[1].wait()
    copies[2].wait()
    chosen = norm_rows(dot(chooser, rows[...]), scale[...])

    def weight(slot):
        copies[slot + 3].wait()
        return wide[slot]

    project_keys(
        chosen, heads, [functools.partial(weight, slot) for slot in range(2)], keyval
    )


def scaled(query, head_size):
    return (query * (head_size ** (-0.5) * LOG2E)).astype(BF16)


def order_kernel(
    offsets, tokens, gain, moved_rows, normed, rows, picks, scale, sems, *, stride, chunk
):
    copies = [
        bring(offsets, picks, sems.at[0]),
        bring(tokens, rows, sems.at[1]),
        bring(gain, scale, sems.at[2]),
    ]
    count = tokens.shape[0]
    share = chunk // stride * offsets.shape[0]
    rest = chunk - share
    picked = count // chunk * share
    copies[0].wait()
    mover = one_hot(
        lax.broadcasted_iota(jnp.int32, (chunk, chunk), 0)
        == ranks(picks, chunk, stride, share, 1)
    )
    copies[1].wait()
    copies[2].wait()
    for c in range(count // chunk):
        moved = dot(mover, rows[c * chunk : (c + 1) * chunk, :]).astype(BF16)
        moved_rows[c * share : (c + 1) * share, :] = moved[:share]
        moved_rows[picked + c * rest : picked + (c + 1) * rest, :] = moved[share:]
    norm_into(normed, 0, moved_rows, scale[...], count)


def first_query_kernel(normed, weight, query, held, sems, *, head_size):
    copy = bring(weight, held, sems.at[0])
    copy.wait()
    for span in pieces(normed.shape[0], 512):
        query[span, :] = scaled(dot(normed[span, :], held[...]), head_size)


def head_windows(head_size, width):
    period = min(width, math.lcm(head_size, 128))
    windows = []
    for h in range(period // head_size):
        start = h * head_size // 128 * 128
        stop = min(period, -(-(h + 1) * head_size // 128) * 128)
        windows.append((start, stop - start))
    return period, windows


def head_peaks(rows, heads):
    count, width = rows.shape
    column = lax.broadcasted_iota(jnp.int32, (width, 128), 0)
    head = lax.broadcasted_iota(jnp.int32, (width, 128), 1)
    low = head * (width // heads)
    sums = one_hot((column >= low) & (column < low + width // heads))
    peak = None
    for span in pieces(count, max(16, count // 16)):
        part = rows[span, :]
        part = part * part
        peak = part if peak is None else jnp.maximum(peak, part)
    return jnp.max(dot(peak, sums), axis=0, keepdims=True)


def load_keys(keyvals, heads, turned, peaks):
    keys = jnp.concatenate([x[i, 0] for x in keyvals for i in range(x.shape[0])], axis=0)
    turned[...] = keys.T
    peaks[...] = head_peaks(keys, heads)


def small_scores(query, first_row, rows, heads, peaks):
    bound = head_peaks(query.at[pl.ds(first_row, rows)], heads) * peaks
    return jnp.max(bound) < 9000.0


def reciprocal(x):
    guess = pl.reciprocal(x, approx=True)
    return guess * (2.0 - x * guess)


def attend_rows(
    query, first_row, rows, heads, turned, keyvals, mixed_ref, mixed_row, work, plain
):
    scores_ref, weights_ref = work
    width = query.shape[1]
    key_count = turned.shape[1]
    head_size = width // heads
    period, windows = head_windows(head_size, width)
    span = pl.ds(first_row, rows)
    out_span = pl.ds(mixed_row, rows)
    lane = lax.broadcasted_iota(jnp.int32, (1, 128), 1)
    ones = jnp.ones((key_count, 128), BF16)

    @pl.loop(0, width // period)
    def _(turn):
        base = pl.multiple_of(turn * period, 128)
        sums = {}

        def score(h):
            start, size = windows[h]
            low = h * head_size - start
            high = low + head_size
            own = turned[pl.ds(pl.multiple_of(base + h * head_size, 16), head_size), :]
            parts = [own]
            if low:
                parts.insert(0, jnp.zeros((low, key_count), BF16))
            if high < size:
                parts.append(jnp.zeros((size - high, key_count), BF16))
            scores_ref[h % 2, :rows] = dot(
                query[span, pl.ds(base + start, size)], jnp.concatenate(parts, axis=0)
            )

        score(0)
        for h, (start, size) in enumerate(windows):
            if h + 1 < len(windows):
                score(h + 1)
            for part in pieces(rows, 64):
                scores = scores_ref[h % 2, part, :]
                if not plain:
                    scores = scores - jnp.max(scores, axis=1, keepdims=True)
                weights_ref[h % 2, part, :] = jnp.exp2(scores).astype(BF16)
            columns = pl.ds(base + start, size)
            values = jnp.concatenate(
                [x[i, 1, :, columns] for x in keyvals for i in range(x.shape[0])], axis=0
            )
            mixed = dot(weights_ref[h % 2, :rows], jnp.concatenate([values, ones], axis=1))
            share = reciprocal(mixed[:, size:])
            for column in range(0, size, 128):
                own = mixed[:, column : column + 128] * share
                at = start + column
                if at in sums:
                    own = jnp.where(lane >= h * head_size - at, own, sums[at])
                sums[at] = own
                if (h + 1) * head_size >= at + 128:
                    mixed_ref[out_span, pl.ds(base + at, 128)] = sums.pop(at).astype(BF16)


def attend(query, first_row, rows, heads, turned, keyvals, mixed_ref, work, peaks):
    small = small_scores(query, first_row, rows, heads, peaks)
    size = math.gcd(rows, ROWS)

    @pl.when(small)
    def _():
        attend_rows(query, first_row, rows, heads, turned, keyvals, mixed_ref, 0, work, True)

    @pl.when(jnp.logical_not(small))
    def _():
        @pl.loop(0, rows // size)
        def _(step):
            row = pl.multiple_of(step * size, size)
            attend_rows(
                query,
                pl.multiple_of(first_row + row, 16),
                size,
                heads,
                turned,
                keyvals,
                mixed_ref,
                row,
                work,
                False,
            )


def gelu(x):
    half = 0.5 * x
    return half + half * jnp.tanh(x * (0.7978845608028654 + 0.035677408136300125 * (x * x)))


def feed_forward(rows, normed, up_weight, down_weight, total, work):
    wide_ref, inner_ref = work
    spans = pieces(up_weight.shape[1], wide_ref.shape[2])

    def widen(i):
        wide_ref[i % 2, :rows] = dot(normed[:rows], up_weight[:, spans[i]])

    widen(0)
    for i, span in enumerate(spans):
        if i + 1 < len(spans):
            widen(i + 1)
        for part in pieces(rows, 32):
            inner_ref[i % 2, part, :] = gelu(wide_ref[i % 2, part, :]).astype(BF16)
        total[:rows] += dot(inner_ref[i % 2, :rows], down_weight[span, :])


def finish_rows(
    first_row, rows, tokens, mixed, mixed_row, out_weight, gain, up_weight, down_weight, work
):
    total, normed, wide_ref, inner_ref = work
    total[:rows] = (
        (
            tokens[pl.ds(first_row, rows), :].astype(F32)
            + dot(mixed[pl.ds(mixed_row, rows), :], out_weight[...])
        )
        .astype(BF16)
        .astype(F32)
    )
    norm_into(normed, 0, total, gain[...], rows)
    feed_forward(rows, normed, up_weight, down_weight, total, (wide_ref, inner_ref))


def picked_kernel(
    offsets,
    tokens,
    query,
    keyval,
    keyval_far,
    out_weight,
    mlp_gain,
    up_weight,
    down_weight,
    gain,
    key_weight,
    value_weight,
    second,
    keyval_two,
    turned,
    peaks,
    held,
    mixed,
    scores,
    weights,
    total,
    normed,
    wide,
    inner,
    sems,
    *,
    heads,
):
    sources = (out_weight, key_weight, value_weight)
    copies = [bring(x, held.at[i], sems.at[i]) for i, x in enumerate(sources)]
    rows = second.shape[0]
    keyvals = (keyval, keyval_far)
    load_keys(keyvals, heads, turned, peaks)
    attend(query, 0, rows, heads, turned, keyvals, mixed, (scores, weights), peaks[...])
    copies[0].wait()
    finish_rows(
        0,
        rows,
        tokens,
        mixed,
        0,
        held.at[0],
        mlp_gain,
        up_weight,
        down_weight,
        (total, normed, wide, inner),
    )
    second[...] = total[...].astype(BF16)
    norm_into(normed, 0, second, gain[...], rows)
    chooser = pick_matrix(slots_of(offsets, heads), heads, rows // heads, heads)
    chosen = dot(chooser, normed[...]).astype(BF16)

    def weight(slot):
        copies[slot + 1].wait()
        return held[slot + 1]

    project_keys(
        chosen, heads, [functools.partial(weight, slot) for slot in range(2)], keyval_two
    )


def rest_attention_kernel(
    query, keyval, keyval_far, turned, peaks, mixed, scores, weights, sems, *, heads
):
    del sems
    rows = mixed.shape[0]
    attend(
        query,
        query.shape[0] - rows,
        rows,
        heads,
        turned,
        (keyval, keyval_far),
        mixed,
        (scores, weights),
        peaks[...],
    )


def rest_feed_kernel(
    tokens,
    mixed,
    out_weight,
    mlp_gain,
    up_weight,
    down_weight,
    second,
    held,
    total,
    normed,
    wide,
    inner,
    sems,
    *,
    first_row,
):
    copy = bring(out_weight, held.at[0], sems.at[0])
    copy.wait()
    finish_rows(
        tokens.shape[0] - mixed.shape[0] + first_row,
        second.shape[0],
        tokens,
        mixed,
        first_row,
        held.at[0],
        mlp_gain,
        up_weight,
        down_weight,
        (total, normed, wide, inner),
    )
    second[...] = total[...].astype(BF16)


def second_query_kernel(*refs, head_size):
    *rows, gain, weight, query, held, normed, sems = refs
    copy = bring(weight, held.at[0], sems.at[0])
    start = 0
    for part in rows:
        norm_into(normed, start, part, gain[...], part.shape[0])
        start += part.shape[0]
    copy.wait()
    for span in pieces(query.shape[0], 512):
        query[span, :] = scaled(dot(normed[span, :], held[0]), head_size)


def second_kernel(*refs, heads, stride, chunk, parts):
    offsets, *rows = refs[: 1 + parts]
    query, keyval, keyval_far, out_weight, encoded = refs[1 + parts : 6 + parts]
    turned, peaks, held, mixed, second, scores, weights, sems = refs[6 + parts :]
    copy = bring(out_weight, held.at[0], sems.at[0])
    start = 0
    for part in rows:
        second[start : start + part.shape[0], :] = part[...]
        start += part.shape[0]
    keyvals = (keyval, keyval_far)
    load_keys(keyvals, heads, turned, peaks)
    count = query.shape[0]
    attend(query, 0, count, heads, turned, keyvals, mixed, (scores, weights), peaks[...])
    share = chunk // stride * heads
    rest_share = chunk - share
    start = count // chunk * share
    back = one_hot(
        lax.broadcasted_iota(jnp.int32, (chunk, chunk), 1)
        == ranks(offsets, chunk, stride, share, 0)
    )
    copy.wait()

    @pl.loop(0, count // chunk)
    def _(step):
        near = pl.ds(pl.multiple_of(step * share, share), share)
        far = pl.ds(pl.multiple_of(start + step * rest_share, 16), rest_share)
        blend = jnp.concatenate([mixed[near, :], mixed[far, :]], axis=0)
        residual = jnp.concatenate([second[near, :], second[far, :]], axis=0)
        result = (residual.astype(F32) + dot(blend, held[0])).astype(BF16)
        span = pl.ds(pl.multiple_of(step * chunk, chunk), chunk)
        encoded[span, :] = dot(back, result).astype(BF16)


def relaying(kernel, ins, outs, *refs):
    end = ins + 1 + outs
    refs[end][...] = refs[ins][...]
    kernel(*refs[:ins], *refs[ins + 1 : end], *refs[end + 1 :])


def local_call(kernel, outs, inputs, scratch, scalars=0, far=(), relay=None, copies=1, flops=0, name=None):
    outs, inputs = list(outs), list(inputs)
    if relay is not None:
        kernel = functools.partial(relaying, kernel, len(inputs), len(outs))
        inputs.append(relay)
        outs.append(pltpu.VMEM(relay.shape, relay.dtype))
    specs, placed = [], []
    for i, x in enumerate(inputs):
        if i < scalars:
            specs.append(pl.BlockSpec(memory_space=pltpu.SMEM))
        elif i in far:
            specs.append(pl.BlockSpec(memory_space=pltpu.HBM))
            x = pltpu.with_memory_space_constraint(x, pltpu.HBM)
        else:
            specs.append(pl.BlockSpec(memory_space=pltpu.VMEM))
            x = pltpu.with_memory_space_constraint(x, pltpu.VMEM)
        placed.append(x)
    return pl.pallas_call(
        kernel,
        out_shape=outs,
        in_specs=specs,
        out_specs=[pl.BlockSpec(memory_space=pltpu.VMEM)] * len(outs),
        scratch_shapes=list(scratch) + [pltpu.SemaphoreType.DMA((copies,))],
        compiler_params=pltpu.CompilerParams(vmem_limit_bytes=VMEM_LIMIT),
        cost_estimate=pl.CostEstimate(
            flops=int(flops),
            transcendentals=0,
            bytes_accessed=sum(inputs[i].size * inputs[i].dtype.itemsize for i in far),
        ),
        name=name,
    )(*placed)


def exchange(keyval, span, beside):
    levels = span.bit_length() - 1
    for level in reversed(range(levels)):
        partner = swapped(keyval, "seq", level)
        keyval = beside(levels - 1 - level, keyval)
        if level:
            keyval = jnp.concatenate([keyval, partner], axis=0)
    return keyval, partner


def whole_body(
    tokens,
    attn_gain,
    query_first,
    key_first,
    segment_value,
    output_first,
    mlp_gain,
    up_weight,
    down_weight,
    second_gain,
    query_second,
    key_second,
    value_second,
    output_second,
    segment_offset,
    global_offset,
):
    seq_count = lax.axis_size("seq")
    seg_span = min(SEG_MAX, seq_count)
    heads = segment_offset.shape[0]
    count, width = tokens.shape
    head_size = width // heads
    hidden = up_weight.shape[1]
    stride = count // (KEYS // seg_span)
    stride_two = count // (KEYS // seq_count)
    groups, groups_two = count // stride, count // stride_two
    chunk = max(ROWS, stride_two)
    picked_count = groups_two * heads
    rest_count = count - picked_count
    part = hidden // 4 if hidden % 512 == 0 else hidden
    block = rest_count // 2 if rest_count % 32 == 0 else rest_count

    def near(*shape):
        return pltpu.VMEM(shape, BF16)

    def attention_work(rows):
        return [
            pltpu.VMEM((2, rows, KEYS), F32),
            pltpu.VMEM((2, rows, KEYS), BF16),
        ]

    def feed_work(rows):
        return [
            pltpu.VMEM((rows, width), F32),
            pltpu.VMEM((rows, width), BF16),
            pltpu.VMEM((2, rows, part), F32),
            pltpu.VMEM((2, rows, part), BF16),
        ]

    held_shapes = [near(width, KEYS), pltpu.VMEM((1, 128), F32)]
    small_work = [pltpu.SMEM((heads,), jnp.int32), pltpu.VMEM((width,), F32)]

    (keyval,) = local_call(
        functools.partial(first_keys_kernel, stride=stride),
        [near(1, 2, groups, width)],
        (segment_offset, tokens, attn_gain, key_first, segment_value),
        [near(count, width), near(2, width, width)] + small_work,
        far=(0, 1, 2, 3, 4),
        copies=5,
        flops=2 * heads * groups * width * (count + 2 * width),
        name="first_keys",
    )
    made = {}

    def beside_first(level, held):
        if level == 0:
            made["rows"], made["normed"], held = local_call(
                functools.partial(order_kernel, stride=stride_two, chunk=chunk),
                [near(count, width), near(count, width)],
                (global_offset, tokens, attn_gain),
                [near(count, width)] + small_work,
                far=(0, 1, 2),
                copies=3,
                relay=held,
                flops=2 * count * width * chunk,
                name="order",
            )
        if level == min(1, seg_span.bit_length() - 2):
            made["query"], held = local_call(
                functools.partial(first_query_kernel, head_size=head_size),
                [near(count, width)],
                (made["normed"], query_first),
                [near(width, width)],
                far=(1,),
                relay=held,
                flops=2 * count * width * width,
                name="first_query",
            )
        return held

    keyval, keyval_far = exchange(keyval, seg_span, beside_first)
    rows, query = made["rows"], made["query"]
    row_flops = 2 * width * (2 * hidden + width) + 4 * 256 * KEYS * heads
    picked_second, keyval_two, turned, peaks = local_call(
        functools.partial(picked_kernel, heads=heads),
        [
            near(picked_count, width),
            near(1, 2, groups_two, width),
        ]
        + held_shapes,
        (
            global_offset,
            rows,
            query,
            keyval,
            keyval_far,
            output_first,
            mlp_gain,
            up_weight,
            down_weight,
            second_gain,
            key_second,
            value_second,
        ),
        [near(3, width, width), near(picked_count, width)]
        + attention_work(picked_count)
        + feed_work(picked_count),
        scalars=1,
        far=(5, 10, 11),
        copies=3,
        flops=row_flops * picked_count,
        name="layer_of_picked",
    )
    seconds = [picked_second]

    def rest_attention(held):
        made["mixed"], held = local_call(
            functools.partial(rest_attention_kernel, heads=heads),
            [near(rest_count, width)],
            (query, keyval, keyval_far, turned, peaks),
            attention_work(rest_count),
            relay=held,
            flops=4 * 256 * KEYS * heads * rest_count,
            name="rest_attention",
        )
        return held

    def rest_feed(first_row, held):
        result, held = local_call(
            functools.partial(rest_feed_kernel, first_row=first_row),
            [near(block, width)],
            (rows, made["mixed"], output_first, mlp_gain, up_weight, down_weight),
            [near(1, width, width)] + feed_work(block),
            far=(2,),
            relay=held,
            flops=2 * width * (2 * hidden + width) * block,
            name="rest_feed",
        )
        seconds.append(result)
        return held

    def second_query(held):
        made["query_two"], held = local_call(
            functools.partial(second_query_kernel, head_size=head_size),
            [near(count, width)],
            (*seconds, second_gain, query_second),
            [near(1, width, width), near(count, width)],
            far=(len(seconds) + 1,),
            relay=held,
            flops=2 * count * width * width,
            name="second_query",
        )
        return held

    tasks = [rest_attention]
    tasks += [functools.partial(rest_feed, row) for row in range(0, rest_count, block)]
    tasks.append(second_query)
    levels = seq_count.bit_length() - 1

    def beside_second(level, held):
        ahead = len(tasks) * level // levels
        for task in tasks[ahead : len(tasks) * (level + 1) // levels]:
            held = task(held)
        return held

    keyval_two, keyval_two_far = exchange(keyval_two, seq_count, beside_second)
    (encoded,) = local_call(
        functools.partial(
            second_kernel, heads=heads, stride=stride_two, chunk=chunk, parts=len(seconds)
        ),
        [jax.ShapeDtypeStruct((count, width), BF16)],
        (
            global_offset,
            *seconds,
            made["query_two"],
            keyval_two,
            keyval_two_far,
            output_second,
        ),
        held_shapes
        + [near(1, width, width), near(count, width), near(count, width)]
        + attention_work(count),
        scalars=1,
        far=(len(seconds) + 4,),
        flops=count * (2 * width * width + 4 * 256 * KEYS * heads),
        name="second_attention",
    )
    return encoded


def solution(mesh):
    placed = (
        P(("slides", "seq", "mp"), None),
        P(),
        P(None, "mp"),
        P(None, "mp"),
        P(None, "mp"),
        P("mp", None),
        P(),
        P(None, "mp"),
        P("mp", None),
        P(),
        P(None, "mp"),
        P(None, "mp"),
        P(None, "mp"),
        P("mp", None),
        P("mp"),
        P("mp"),
    )
    fits = mesh.shape["mp"] == 1 and 2 <= mesh.shape["seq"] <= SEG_MAX
    return jax.shard_map(
        whole_body if fits else split_body,
        mesh=mesh,
        in_specs=placed,
        out_specs=P(("slides", "seq", "mp"), None),
        check_vma=False,
    )
```

```python
import functools
import math

import jax
import jax.numpy as jnp
from jax import lax
from jax.experimental import pallas as pl
from jax.experimental.pallas import tpu as pltpu
from jax.sharding import PartitionSpec as P

KEYS = 256
SEG_MAX = 16
ROWS = 256
LOG2E = 1.4426950408889634
BF16 = jnp.bfloat16
F32 = jnp.float32
VMEM_LIMIT = 22 * 1024 * 1024


def swapped(x, axis, apart):
    return lax.ppermute(x, axis, [(i, i ^ 1 << apart) for i in range(lax.axis_size(axis))])


def norm_rows(values, gain):
    center = values - jnp.mean(values, axis=-1, keepdims=True)
    spread = jnp.mean(center * center, axis=-1, keepdims=True)
    return (center * lax.rsqrt(spread + 1e-05) * gain).astype(jnp.bfloat16)


def pick_keys(hidden, offsets, stride, key_weight, value_weight):
    token_count, width = hidden.shape
    head_count = offsets.shape[0]
    head_size = key_weight.shape[1] // head_count
    grouped_rows = hidden.reshape(token_count // stride, stride, width)
    dilation_selector = (
        lax.broadcasted_iota(jnp.int32, (stride, head_count), 0) == offsets[None, :]
    ).astype(jnp.bfloat16)
    chosen = jnp.einsum(
        "nof,oj->njf", grouped_rows, dilation_selector, preferred_element_type=jnp.float32
    ).astype(jnp.bfloat16)
    key_heads = jnp.einsum(
        "xkr,rkf->xkf",
        chosen,
        key_weight.reshape(width, head_count, head_size),
        preferred_element_type=jnp.float32,
    ).astype(jnp.bfloat16)
    value_heads = jnp.einsum(
        "xkr,rkf->xkf",
        chosen,
        value_weight.reshape(width, head_count, head_size),
        preferred_element_type=jnp.float32,
    ).astype(jnp.bfloat16)
    picked = token_count // stride
    return jnp.stack(
        [
            key_heads.reshape(picked, head_count * head_size),
            value_heads.reshape(picked, head_count * head_size),
        ]
    )


def attend_local(query, keyval, head_count):
    token_count, width = query.shape
    head_size = width // head_count
    query_heads = query.reshape(token_count, head_count, head_size)
    key_heads = keyval[0].reshape(-1, head_count, head_size)
    value_heads = keyval[1].reshape(-1, head_count, head_size)
    scores = jnp.einsum(
        "thd,khd->htk", query_heads, key_heads, preferred_element_type=jnp.float32
    ) * head_size ** (-0.5)
    highest = jnp.max(scores, axis=-1, keepdims=True)
    weights = jnp.exp(scores - highest)
    weights = (weights / jnp.sum(weights, axis=-1, keepdims=True)).astype(jnp.bfloat16)
    mixed = jnp.einsum(
        "htk,khd->thd", weights, value_heads, preferred_element_type=jnp.float32
    ).astype(jnp.bfloat16)
    return mixed.reshape(token_count, width)


def merge_branch_pair(mine, other, level, token_position):
    lower = token_position >> level & 1 == 0
    return jnp.where(
        lower, jnp.concatenate((mine, other), axis=1), jnp.concatenate((other, mine), axis=1)
    )


def spread_segment(keyval, seg_span, token_position):
    for level in range(seg_span.bit_length() - 1):
        partner = swapped(keyval, "seq", level)
        keyval = merge_branch_pair(keyval, partner, level, token_position)
    return keyval


def spread_global(keyval_two):
    keyval_two = lax.all_gather(keyval_two, "seq", axis=1, tiled=True)
    return keyval_two


def combine(partial_value, residual_full, need_full):
    row_count = residual_full.shape[0] // lax.axis_size("mp")
    row_start = lax.axis_index("mp") * row_count
    share = lax.psum_scatter(partial_value, "mp", scatter_dimension=0, tiled=True)
    own_rows = lax.dynamic_slice_in_dim(residual_full, row_start, row_count, 0)
    own_rows = (own_rows.astype(jnp.float32) + share).astype(jnp.bfloat16)
    full_rows = lax.all_gather(own_rows, "mp", axis=0, tiled=True) if need_full else own_rows
    return (own_rows, full_rows)


def split_body(
    tokens,
    attn_gain,
    query_first,
    key_first,
    segment_value,
    output_first,
    mlp_gain,
    up_weight,
    down_weight,
    second_gain,
    query_second,
    key_second,
    value_second,
    output_second,
    segment_offset,
    global_offset,
):
    seq_count = lax.axis_size("seq")
    token_position = lax.axis_index("seq")
    seg_span = min(SEG_MAX, seq_count)
    head_count = segment_offset.shape[0]
    full_rows = lax.all_gather(tokens, "mp", axis=0, tiled=True)
    token_count = full_rows.shape[0]
    hidden = norm_rows(full_rows.astype(jnp.float32), attn_gain)
    query = jnp.dot(hidden, query_first, preferred_element_type=jnp.float32).astype(jnp.bfloat16)
    seg_stride = token_count // (KEYS // seg_span)
    keyval = pick_keys(hidden, segment_offset, seg_stride, key_first, segment_value)
    keyval = spread_segment(keyval, seg_span, token_position)
    mixed = attend_local(query, keyval, head_count)
    partial_value = jnp.dot(mixed, output_first, preferred_element_type=jnp.float32)
    own_rows, first_rows = combine(partial_value, full_rows, True)
    normed = norm_rows(first_rows.astype(jnp.float32), mlp_gain)
    inner = jax.nn.gelu(
        jnp.dot(normed, up_weight, preferred_element_type=jnp.float32), approximate=True
    ).astype(jnp.bfloat16)
    partial_value = jnp.dot(inner, down_weight, preferred_element_type=jnp.float32)
    own_rows, second_rows = combine(partial_value, first_rows, True)
    hidden_two = norm_rows(second_rows.astype(jnp.float32), second_gain)
    query_two = jnp.dot(hidden_two, query_second, preferred_element_type=jnp.float32).astype(
        jnp.bfloat16
    )
    glob_stride = token_count // (KEYS // seq_count)
    keyval_two = pick_keys(hidden_two, global_offset, glob_stride, key_second, value_second)
    keyval_two = spread_global(keyval_two)
    mixed_two = attend_local(query_two, keyval_two, head_count)
    partial_value = jnp.dot(mixed_two, output_second, preferred_element_type=jnp.float32)
    own_rows, unused_rows = combine(partial_value, second_rows, False)
    return own_rows


def one_hot(condition):
    return jnp.where(condition, 1.0, 0.0).astype(BF16)


def dot(left, right):
    return jnp.dot(left, right, preferred_element_type=F32)


def pieces(count, size):
    size = size if count % size == 0 else count
    return [slice(start, start + size) for start in range(0, count, size)]


def norm_into(out, start, source, gain, count):
    for span in pieces(count, 64):
        out[start + span.start : start + span.stop, :] = norm_rows(
            source[span, :].astype(F32), gain
        )


def bring(source, target, sem):
    copy = pltpu.make_async_copy(source, target, sem)
    copy.start()
    return copy


def pick_matrix(offsets, heads, groups, stride):
    count = groups * stride
    place = lax.broadcasted_iota(jnp.int32, (groups, count), 1)
    place = place - lax.broadcasted_iota(jnp.int32, (groups, count), 0) * stride
    return jnp.concatenate([one_hot(place == offsets[h]) for h in range(heads)], axis=0)


def project_keys(chosen, heads, weights, keyval_ref):
    rows, width = chosen.shape
    groups, head_size = rows // heads, width // heads
    column = lax.broadcasted_iota(jnp.int32, (groups, width), 1)
    for slot, weight in enumerate(weights):
        wide = dot(chosen, weight())
        total = jnp.zeros((groups, width), F32)
        for h in range(heads):
            own = (column >= h * head_size) & (column < (h + 1) * head_size)
            total = jnp.where(own, wide[h * groups : (h + 1) * groups], total)
        total = total.astype(BF16)
        for copy in range(keyval_ref.shape[0]):
            keyval_ref[copy, slot] = total


def ranks(offsets, chunk, stride, share, axis):
    heads = offsets.shape[0]

    def places(way):
        shape = (1, chunk) if way else (chunk, 1)
        place = lax.broadcasted_iota(jnp.int32, shape, way)
        inside = lax.rem(place, stride)
        taken = inside == offsets[0]
        for h in range(1, heads):
            taken = taken | (inside == offsets[h])
        return place, inside, jnp.where(taken, inside, inside + stride)

    place, inside, order = places(axis)
    other_place, _, other_order = places(1 - axis)
    ahead = (other_order < order) & (lax.div(other_place, stride) == lax.div(place, stride))
    rank = jnp.sum(jnp.where(ahead, 1, 0), axis=1 - axis, keepdims=True)
    group = lax.div(place, stride)
    return jnp.where(
        rank < heads, group * heads + rank, share + group * (stride - heads) + rank - heads
    )


def slots_of(offsets, heads):
    values = [offsets[h] for h in range(heads)]
    fresh = []
    for h in range(heads):
        seen = jnp.int32(1)
        for earlier in values[:h]:
            seen = jnp.where(earlier == values[h], 0, seen)
        fresh.append(seen)
    slots = []
    for h in range(heads):
        slot = jnp.int32(0)
        for other in range(heads):
            slot = slot + jnp.where(values[other] < values[h], fresh[other], 0)
        slots.append(slot)
    return slots


def first_keys_kernel(
    offsets, tokens, gain, key_weight, value_weight, keyval, rows, wide, picks, scale, sems, *, stride
):
    copies = [
        bring(offsets, picks, sems.at[0]),
        bring(tokens, rows, sems.at[1]),
        bring(gain, scale, sems.at[2]),
        bring(key_weight, wide.at[0], sems.at[3]),
        bring(value_weight, wide.at[1], sems.at[4]),
    ]
    heads = offsets.shape[0]
    copies[0].wait()
    chooser = pick_matrix(picks, heads, rows.shape[0] // stride, stride)
    copies[1].wait()
    copies[2].wait()
    chosen = norm_rows(dot(chooser, rows[...]), scale[...])

    def weight(slot):
        copies[slot + 3].wait()
        return wide[slot]

    project_keys(
        chosen, heads, [functools.partial(weight, slot) for slot in range(2)], keyval
    )


def scaled(query, head_size):
    return (query * (head_size ** (-0.5) * LOG2E)).astype(BF16)


def order_kernel(
    offsets, tokens, gain, moved_rows, normed, rows, picks, scale, sems, *, stride, chunk
):
    copies = [
        bring(offsets, picks, sems.at[0]),
        bring(tokens, rows, sems.at[1]),
        bring(gain, scale, sems.at[2]),
    ]
    count = tokens.shape[0]
    share = chunk // stride * offsets.shape[0]
    rest = chunk - share
    picked = count // chunk * share
    copies[0].wait()
    mover = one_hot(
        lax.broadcasted_iota(jnp.int32, (chunk, chunk), 0)
        == ranks(picks, chunk, stride, share, 1)
    )
    copies[1].wait()
    copies[2].wait()
    for c in range(count // chunk):
        moved = dot(mover, rows[c * chunk : (c + 1) * chunk, :]).astype(BF16)
        moved_rows[c * share : (c + 1) * share, :] = moved[:share]
        moved_rows[picked + c * rest : picked + (c + 1) * rest, :] = moved[share:]
    norm_into(normed, 0, moved_rows, scale[...], count)


def first_query_kernel(normed, weight, query, held, sems, *, head_size):
    copy = bring(weight, held, sems.at[0])
    copy.wait()
    for span in pieces(normed.shape[0], 512):
        query[span, :] = scaled(dot(normed[span, :], held[...]), head_size)


def head_windows(head_size, width):
    period = min(width, math.lcm(head_size, 128))
    windows = []
    for h in range(period // head_size):
        start = h * head_size // 128 * 128
        stop = min(period, -(-(h + 1) * head_size // 128) * 128)
        windows.append((start, stop - start))
    return period, windows


def head_peaks(rows, heads):
    count, width = rows.shape
    column = lax.broadcasted_iota(jnp.int32, (width, 128), 0)
    head = lax.broadcasted_iota(jnp.int32, (width, 128), 1)
    low = head * (width // heads)
    sums = one_hot((column >= low) & (column < low + width // heads))
    peak = None
    for span in pieces(count, max(16, count // 16)):
        part = rows[span, :]
        part = part * part
        peak = part if peak is None else jnp.maximum(peak, part)
    return jnp.max(dot(peak, sums), axis=0, keepdims=True)


def load_keys(keyvals, heads, turned, peaks):
    keys = jnp.concatenate([x[i, 0] for x in keyvals for i in range(x.shape[0])], axis=0)
    turned[...] = keys.T
    peaks[...] = head_peaks(keys, heads)


def small_scores(query, first_row, rows, heads, peaks):
    bound = head_peaks(query.at[pl.ds(first_row, rows)], heads) * peaks
    return jnp.max(bound) < 9000.0


def reciprocal(x):
    guess = pl.reciprocal(x, approx=True)
    return guess * (2.0 - x * guess)


def attend_rows(
    query, first_row, rows, heads, turned, keyvals, mixed_ref, mixed_row, work, plain
):
    scores_ref, weights_ref = work
    width = query.shape[1]
    key_count = turned.shape[1]
    head_size = width // heads
    period, windows = head_windows(head_size, width)
    span = pl.ds(first_row, rows)
    out_span = pl.ds(mixed_row, rows)
    lane = lax.broadcasted_iota(jnp.int32, (1, 128), 1)
    ones = jnp.ones((key_count, 128), BF16)

    @pl.loop(0, width // period)
    def _(turn):
        base = pl.multiple_of(turn * period, 128)
        sums = {}

        def score(h):
            start, size = windows[h]
            low = h * head_size - start
            high = low + head_size
            own = turned[pl.ds(pl.multiple_of(base + h * head_size, 16), head_size), :]
            parts = [own]
            if low:
                parts.insert(0, jnp.zeros((low, key_count), BF16))
            if high < size:
                parts.append(jnp.zeros((size - high, key_count), BF16))
            scores_ref[h % 2, :rows] = dot(
                query[span, pl.ds(base + start, size)], jnp.concatenate(parts, axis=0)
            )

        score(0)
        for h, (start, size) in enumerate(windows):
            if h + 1 < len(windows):
                score(h + 1)
            for part in pieces(rows, 64):
                scores = scores_ref[h % 2, part, :]
                if not plain:
                    scores = scores - jnp.max(scores, axis=1, keepdims=True)
                weights_ref[h % 2, part, :] = jnp.exp2(scores).astype(BF16)
            columns = pl.ds(base + start, size)
            values = jnp.concatenate(
                [x[i, 1, :, columns] for x in keyvals for i in range(x.shape[0])], axis=0
            )
            mixed = dot(weights_ref[h % 2, :rows], jnp.concatenate([values, ones], axis=1))
            share = reciprocal(mixed[:, size:])
            for column in range(0, size, 128):
                own = mixed[:, column : column + 128] * share
                at = start + column
                if at in sums:
                    own = jnp.where(lane >= h * head_size - at, own, sums[at])
                sums[at] = own
                if (h + 1) * head_size >= at + 128:
                    mixed_ref[out_span, pl.ds(base + at, 128)] = sums.pop(at).astype(BF16)


def attend(query, first_row, rows, heads, turned, keyvals, mixed_ref, work, peaks):
    small = small_scores(query, first_row, rows, heads, peaks)
    size = math.gcd(rows, ROWS)

    @pl.when(small)
    def _():
        attend_rows(query, first_row, rows, heads, turned, keyvals, mixed_ref, 0, work, True)

    @pl.when(jnp.logical_not(small))
    def _():
        @pl.loop(0, rows // size)
        def _(step):
            row = pl.multiple_of(step * size, size)
            attend_rows(
                query,
                pl.multiple_of(first_row + row, 16),
                size,
                heads,
                turned,
                keyvals,
                mixed_ref,
                row,
                work,
                False,
            )


def gelu(x):
    half = 0.5 * x
    return half + half * jnp.tanh(x * (0.7978845608028654 + 0.035677408136300125 * (x * x)))


def widen(normed, up_weight, wide_ref, inner):
    rows = normed.shape[0]
    spans = pieces(up_weight.shape[1], wide_ref.shape[2])

    def product(i):
        wide_ref[i % 2] = dot(normed[...], up_weight[:, spans[i]])

    product(0)
    for i, span in enumerate(spans):
        if i + 1 < len(spans):
            product(i + 1)
        for part in pieces(rows, 32):
            inner[part, span] = gelu(wide_ref[i % 2, part, :]).astype(BF16)


def narrow(inner, down_weight, first, second):
    for span in pieces(second.shape[1], 256):
        total = first[:, span].astype(F32) + dot(inner[...], down_weight[:, span])
        second[:, span] = total.astype(BF16)


def add_heads(tokens, first_row, mixed, out_weight, first):
    total = dot(mixed[...], out_weight[...])
    rows = tokens[pl.ds(first_row, mixed.shape[0]), :]
    first[...] = (rows.astype(F32) + total).astype(BF16)


def picked_kernel(
    offsets,
    tokens,
    query,
    keyval,
    keyval_far,
    out_weight,
    mlp_gain,
    up_weight,
    down_weight,
    gain,
    key_weight,
    value_weight,
    second,
    keyval_two,
    turned,
    peaks,
    held,
    mixed,
    scores,
    weights,
    first,
    normed,
    wide,
    inner,
    sems,
    *,
    heads,
):
    copies = [
        bring(x, held.at[i], sems.at[i]) for i, x in enumerate((key_weight, value_weight))
    ]
    rows = second.shape[0]
    keyvals = (keyval, keyval_far)
    load_keys(keyvals, heads, turned, peaks)
    attend(query, 0, rows, heads, turned, keyvals, mixed, (scores, weights), peaks[...])
    add_heads(tokens, 0, mixed, out_weight, first)
    norm_into(normed, 0, first, mlp_gain[...], rows)
    widen(normed, up_weight, wide, inner)
    narrow(inner, down_weight, first, second)
    norm_into(normed, 0, second, gain[...], rows)
    chooser = pick_matrix(slots_of(offsets, heads), heads, rows // heads, heads)
    chosen = dot(chooser, normed[...]).astype(BF16)

    def weight(slot):
        copies[slot].wait()
        return held[slot]

    project_keys(
        chosen, heads, [functools.partial(weight, slot) for slot in range(2)], keyval_two
    )


def rest_attention_kernel(
    query, keyval, keyval_far, turned, peaks, mixed, scores, weights, sems, *, heads
):
    del sems
    rows = mixed.shape[0]
    attend(
        query,
        query.shape[0] - rows,
        rows,
        heads,
        turned,
        (keyval, keyval_far),
        mixed,
        (scores, weights),
        peaks[...],
    )


def rest_up_kernel(
    tokens, mixed, out_weight, gain, up_weight, first, inner, normed, wide, sems
):
    del sems
    rows = mixed.shape[0]
    add_heads(tokens, tokens.shape[0] - rows, mixed, out_weight, first)
    norm_into(normed, 0, first, gain[...], rows)
    widen(normed, up_weight, wide, inner)


def rest_down_kernel(first, inner, down_weight, second, sems):
    del sems
    narrow(inner, down_weight, first, second)


def second_query_kernel(*refs, head_size):
    *rows, gain, weight, query, held, normed, sems = refs
    copy = bring(weight, held.at[0], sems.at[0])
    start = 0
    for part in rows:
        norm_into(normed, start, part, gain[...], part.shape[0])
        start += part.shape[0]
    copy.wait()
    for span in pieces(query.shape[0], 512):
        query[span, :] = scaled(dot(normed[span, :], held[0]), head_size)


def second_kernel(*refs, heads, stride, chunk, parts):
    offsets, *rows = refs[: 1 + parts]
    query, keyval, keyval_far, out_weight, encoded = refs[1 + parts : 6 + parts]
    turned, peaks, held, mixed, result, ready, scores, weights, sems = refs[6 + parts :]
    copy = bring(out_weight, held.at[0], sems.at[0])
    keyvals = (keyval, keyval_far)
    load_keys(keyvals, heads, turned, peaks)
    count = query.shape[0]
    attend(query, 0, count, heads, turned, keyvals, mixed, (scores, weights), peaks[...])
    share = chunk // stride * heads
    rest_share = chunk - share
    back = one_hot(
        lax.broadcasted_iota(jnp.int32, (chunk, chunk), 1)
        == ranks(offsets, chunk, stride, share, 0)
    )
    copy.wait()
    start = 0
    for part in rows:
        span = slice(start, start + part.shape[0])
        total = part[...].astype(F32) + dot(mixed[span, :], held[0])
        result[span, :] = total.astype(BF16)
        start += part.shape[0]
    start = count // chunk * share
    copies = []
    for c in range(count // chunk):
        far = start + c * rest_share
        blend = jnp.concatenate(
            [result[c * share : (c + 1) * share, :], result[far : far + rest_share, :]], axis=0
        )
        span = pl.ds(c * chunk, chunk)
        ready[span, :] = dot(back, blend).astype(BF16)
        copies.append(bring(ready.at[span], encoded.at[span], sems.at[1 + c]))
    for copy in copies:
        copy.wait()


def relaying(kernel, ins, outs, *refs):
    end = ins + 1 + outs
    refs[end][...] = refs[ins][...]
    kernel(*refs[:ins], *refs[ins + 1 : end], *refs[end + 1 :])


def local_call(kernel, outs, inputs, scratch, scalars=0, far=(), relay=None, out_near=True, copies=1, flops=0, name=None):
    outs, inputs = list(outs), list(inputs)
    if relay is not None:
        kernel = functools.partial(relaying, kernel, len(inputs), len(outs))
        inputs.append(relay)
        outs.append(pltpu.VMEM(relay.shape, relay.dtype))
    specs, placed = [], []
    for i, x in enumerate(inputs):
        if i < scalars:
            specs.append(pl.BlockSpec(memory_space=pltpu.SMEM))
        elif i in far:
            specs.append(pl.BlockSpec(memory_space=pltpu.HBM))
            x = pltpu.with_memory_space_constraint(x, pltpu.HBM)
        else:
            specs.append(pl.BlockSpec(memory_space=pltpu.VMEM))
            x = pltpu.with_memory_space_constraint(x, pltpu.VMEM)
        placed.append(x)
    return pl.pallas_call(
        kernel,
        out_shape=outs,
        in_specs=specs,
        out_specs=[
            pl.BlockSpec(memory_space=pltpu.VMEM if out_near else pltpu.HBM)
        ] * len(outs),
        scratch_shapes=list(scratch) + [pltpu.SemaphoreType.DMA((copies,))],
        compiler_params=pltpu.CompilerParams(vmem_limit_bytes=VMEM_LIMIT),
        cost_estimate=pl.CostEstimate(
            flops=int(flops),
            transcendentals=0,
            bytes_accessed=sum(inputs[i].size * inputs[i].dtype.itemsize for i in far),
        ),
        name=name,
    )(*placed)


def exchange(keyval, span, beside, early):
    levels = span.bit_length() - 1
    early = early and levels > 2
    crossed, fresh = [], keyval
    for level in reversed(range(levels)):
        partner = swapped(keyval if level != 1 or not early else fresh, "seq", level)
        if early and level > 1:
            crossed.append(swapped(fresh, "seq", 1))
        keyval = beside(levels - 1 - level, keyval)
        fresh = partner
        if level:
            blocks = [keyval, partner]
            if level == 1:
                blocks = [keyval, *crossed, partner]
            keyval = jnp.concatenate(blocks, axis=0)
    return keyval, partner


def whole_body(
    tokens,
    attn_gain,
    query_first,
    key_first,
    segment_value,
    output_first,
    mlp_gain,
    up_weight,
    down_weight,
    second_gain,
    query_second,
    key_second,
    value_second,
    output_second,
    segment_offset,
    global_offset,
):
    seq_count = lax.axis_size("seq")
    seg_span = min(SEG_MAX, seq_count)
    heads = segment_offset.shape[0]
    count, width = tokens.shape
    head_size = width // heads
    hidden = up_weight.shape[1]
    stride = count // (KEYS // seg_span)
    stride_two = count // (KEYS // seq_count)
    groups, groups_two = count // stride, count // stride_two
    chunk = max(ROWS, stride_two)
    picked_count = groups_two * heads
    rest_count = count - picked_count
    part = hidden // 4 if hidden % 512 == 0 else hidden

    def near(*shape):
        return pltpu.VMEM(shape, BF16)

    def attention_work(rows):
        return [
            pltpu.VMEM((2, rows, KEYS), F32),
            pltpu.VMEM((2, rows, KEYS), BF16),
        ]

    def feed_work(rows):
        return [near(rows, width), pltpu.VMEM((2, rows, part), F32)]

    held_shapes = [near(width, KEYS), pltpu.VMEM((1, 128), F32)]
    small_work = [pltpu.SMEM((heads,), jnp.int32), pltpu.VMEM((width,), F32)]

    (keyval,) = local_call(
        functools.partial(first_keys_kernel, stride=stride),
        [near(1, 2, groups, width)],
        (segment_offset, tokens, attn_gain, key_first, segment_value),
        [near(count, width), near(2, width, width)] + small_work,
        far=(0, 1, 2, 3, 4),
        copies=5,
        flops=2 * heads * groups * width * (count + 2 * width),
        name="first_keys",
    )
    made = {}

    def beside_first(level, held):
        if level == 0:
            made["rows"], made["normed"], held = local_call(
                functools.partial(order_kernel, stride=stride_two, chunk=chunk),
                [near(count, width), near(count, width)],
                (global_offset, tokens, attn_gain),
                [near(count, width)] + small_work,
                far=(0, 1, 2),
                copies=3,
                relay=held,
                flops=2 * count * width * chunk,
                name="order",
            )
        if level == min(1, seg_span.bit_length() - 2):
            made["query"], held = local_call(
                functools.partial(first_query_kernel, head_size=head_size),
                [near(count, width)],
                (made["normed"], query_first),
                [near(width, width)],
                far=(1,),
                relay=held,
                flops=2 * count * width * width,
                name="first_query",
            )
        return held

    keyval, keyval_far = exchange(keyval, seg_span, beside_first, True)
    rows, query = made["rows"], made["query"]
    row_flops = 2 * width * (2 * hidden + width) + 4 * 256 * KEYS * heads
    picked_second, keyval_two, turned, peaks = local_call(
        functools.partial(picked_kernel, heads=heads),
        [
            near(picked_count, width),
            near(1, 2, groups_two, width),
        ]
        + held_shapes,
        (
            global_offset,
            rows,
            query,
            keyval,
            keyval_far,
            output_first,
            mlp_gain,
            up_weight,
            down_weight,
            second_gain,
            key_second,
            value_second,
        ),
        [near(2, width, width), near(picked_count, width)]
        + attention_work(picked_count)
        + [near(picked_count, width)]
        + feed_work(picked_count)
        + [near(picked_count, hidden)],
        scalars=1,
        far=(10, 11),
        copies=2,
        flops=row_flops * picked_count,
        name="layer_of_picked",
    )
    seconds = [picked_second]

    def rest_attention(held):
        made["mixed"], held = local_call(
            functools.partial(rest_attention_kernel, heads=heads),
            [near(rest_count, width)],
            (query, keyval, keyval_far, turned, peaks),
            attention_work(rest_count),
            relay=held,
            flops=4 * 256 * KEYS * heads * rest_count,
            name="rest_attention",
        )
        return held

    def rest_up(held):
        made["first"], made["inner"], held = local_call(
            rest_up_kernel,
            [near(rest_count, width), near(rest_count, hidden)],
            (rows, made["mixed"], output_first, mlp_gain, up_weight),
            feed_work(rest_count),
            relay=held,
            flops=2 * width * (hidden + width) * rest_count,
            name="rest_up",
        )
        return held

    def rest_down(held):
        result, held = local_call(
            rest_down_kernel,
            [near(rest_count, width)],
            (made["first"], made["inner"], down_weight),
            [],
            relay=held,
            flops=2 * width * hidden * rest_count,
            name="rest_down",
        )
        seconds.append(result)
        return held

    def second_query(held):
        made["query_two"], held = local_call(
            functools.partial(second_query_kernel, head_size=head_size),
            [near(count, width)],
            (*seconds, second_gain, query_second),
            [near(1, width, width), near(count, width)],
            far=(len(seconds) + 1,),
            relay=held,
            flops=2 * count * width * width,
            name="second_query",
        )
        return held

    tasks = [rest_attention, rest_up, rest_down, second_query]
    levels = seq_count.bit_length() - 1

    def beside_second(level, held):
        ahead = len(tasks) * level // levels
        for task in tasks[ahead : len(tasks) * (level + 1) // levels]:
            held = task(held)
        return held

    keyval_two, keyval_two_far = exchange(keyval_two, seq_count, beside_second, False)
    (encoded,) = local_call(
        functools.partial(
            second_kernel, heads=heads, stride=stride_two, chunk=chunk, parts=len(seconds)
        ),
        [jax.ShapeDtypeStruct((count, width), BF16)],
        (
            global_offset,
            *seconds,
            made["query_two"],
            keyval_two,
            keyval_two_far,
            output_second,
        ),
        held_shapes
        + [near(1, width, width)]
        + [near(count, width)] * 3
        + attention_work(count),
        scalars=1,
        far=(len(seconds) + 4,),
        out_near=False,
        copies=1 + count // chunk,
        flops=count * (2 * width * width + 4 * 256 * KEYS * heads),
        name="second_attention",
    )
    return encoded


def solution(mesh):
    placed = (
        P(("slides", "seq", "mp"), None),
        P(),
        P(None, "mp"),
        P(None, "mp"),
        P(None, "mp"),
        P("mp", None),
        P(),
        P(None, "mp"),
        P("mp", None),
        P(),
        P(None, "mp"),
        P(None, "mp"),
        P(None, "mp"),
        P("mp", None),
        P("mp"),
        P("mp"),
    )
    fits = mesh.shape["mp"] == 1 and 2 <= mesh.shape["seq"] <= SEG_MAX
    return jax.shard_map(
        whole_body if fits else split_body,
        mesh=mesh,
        in_specs=placed,
        out_specs=P(("slides", "seq", "mp"), None),
        check_vma=False,
    )
```

```python
import functools
import math

import jax
import jax.numpy as jnp
from jax import lax
from jax.experimental import pallas as pl
from jax.experimental.pallas import tpu as pltpu
from jax.sharding import PartitionSpec as P

KEYS = 256
SEG_MAX = 16
ROWS = 256
LOG2E = 1.4426950408889634
BF16 = jnp.bfloat16
F32 = jnp.float32
VMEM_LIMIT = 22 * 1024 * 1024


def swapped(x, axis, apart):
    return lax.ppermute(x, axis, [(i, i ^ 1 << apart) for i in range(lax.axis_size(axis))])


def norm_rows(values, gain):
    center = values - jnp.mean(values, axis=-1, keepdims=True)
    spread = jnp.mean(center * center, axis=-1, keepdims=True)
    return (center * lax.rsqrt(spread + 1e-05) * gain).astype(jnp.bfloat16)


def pick_keys(hidden, offsets, stride, key_weight, value_weight):
    token_count, width = hidden.shape
    head_count = offsets.shape[0]
    head_size = key_weight.shape[1] // head_count
    grouped_rows = hidden.reshape(token_count // stride, stride, width)
    dilation_selector = (
        lax.broadcasted_iota(jnp.int32, (stride, head_count), 0) == offsets[None, :]
    ).astype(jnp.bfloat16)
    chosen = jnp.einsum(
        "nof,oj->njf", grouped_rows, dilation_selector, preferred_element_type=jnp.float32
    ).astype(jnp.bfloat16)
    key_heads = jnp.einsum(
        "xkr,rkf->xkf",
        chosen,
        key_weight.reshape(width, head_count, head_size),
        preferred_element_type=jnp.float32,
    ).astype(jnp.bfloat16)
    value_heads = jnp.einsum(
        "xkr,rkf->xkf",
        chosen,
        value_weight.reshape(width, head_count, head_size),
        preferred_element_type=jnp.float32,
    ).astype(jnp.bfloat16)
    picked = token_count // stride
    return jnp.stack(
        [
            key_heads.reshape(picked, head_count * head_size),
            value_heads.reshape(picked, head_count * head_size),
        ]
    )


def attend_local(query, keyval, head_count):
    token_count, width = query.shape
    head_size = width // head_count
    query_heads = query.reshape(token_count, head_count, head_size)
    key_heads = keyval[0].reshape(-1, head_count, head_size)
    value_heads = keyval[1].reshape(-1, head_count, head_size)
    scores = jnp.einsum(
        "thd,khd->htk", query_heads, key_heads, preferred_element_type=jnp.float32
    ) * head_size ** (-0.5)
    highest = jnp.max(scores, axis=-1, keepdims=True)
    weights = jnp.exp(scores - highest)
    weights = (weights / jnp.sum(weights, axis=-1, keepdims=True)).astype(jnp.bfloat16)
    mixed = jnp.einsum(
        "htk,khd->thd", weights, value_heads, preferred_element_type=jnp.float32
    ).astype(jnp.bfloat16)
    return mixed.reshape(token_count, width)


def merge_branch_pair(mine, other, level, token_position):
    lower = token_position >> level & 1 == 0
    return jnp.where(
        lower, jnp.concatenate((mine, other), axis=1), jnp.concatenate((other, mine), axis=1)
    )


def spread_segment(keyval, seg_span, token_position):
    for level in range(seg_span.bit_length() - 1):
        partner = swapped(keyval, "seq", level)
        keyval = merge_branch_pair(keyval, partner, level, token_position)
    return keyval


def spread_global(keyval_two):
    keyval_two = lax.all_gather(keyval_two, "seq", axis=1, tiled=True)
    return keyval_two


def combine(partial_value, residual_full, need_full):
    row_count = residual_full.shape[0] // lax.axis_size("mp")
    row_start = lax.axis_index("mp") * row_count
    share = lax.psum_scatter(partial_value, "mp", scatter_dimension=0, tiled=True)
    own_rows = lax.dynamic_slice_in_dim(residual_full, row_start, row_count, 0)
    own_rows = (own_rows.astype(jnp.float32) + share).astype(jnp.bfloat16)
    full_rows = lax.all_gather(own_rows, "mp", axis=0, tiled=True) if need_full else own_rows
    return (own_rows, full_rows)


def split_body(
    tokens,
    attn_gain,
    query_first,
    key_first,
    segment_value,
    output_first,
    mlp_gain,
    up_weight,
    down_weight,
    second_gain,
    query_second,
    key_second,
    value_second,
    output_second,
    segment_offset,
    global_offset,
):
    seq_count = lax.axis_size("seq")
    token_position = lax.axis_index("seq")
    seg_span = min(SEG_MAX, seq_count)
    head_count = segment_offset.shape[0]
    full_rows = lax.all_gather(tokens, "mp", axis=0, tiled=True)
    token_count = full_rows.shape[0]
    hidden = norm_rows(full_rows.astype(jnp.float32), attn_gain)
    query = jnp.dot(hidden, query_first, preferred_element_type=jnp.float32).astype(jnp.bfloat16)
    seg_stride = token_count // (KEYS // seg_span)
    keyval = pick_keys(hidden, segment_offset, seg_stride, key_first, segment_value)
    keyval = spread_segment(keyval, seg_span, token_position)
    mixed = attend_local(query, keyval, head_count)
    partial_value = jnp.dot(mixed, output_first, preferred_element_type=jnp.float32)
    own_rows, first_rows = combine(partial_value, full_rows, True)
    normed = norm_rows(first_rows.astype(jnp.float32), mlp_gain)
    inner = jax.nn.gelu(
        jnp.dot(normed, up_weight, preferred_element_type=jnp.float32), approximate=True
    ).astype(jnp.bfloat16)
    partial_value = jnp.dot(inner, down_weight, preferred_element_type=jnp.float32)
    own_rows, second_rows = combine(partial_value, first_rows, True)
    hidden_two = norm_rows(second_rows.astype(jnp.float32), second_gain)
    query_two = jnp.dot(hidden_two, query_second, preferred_element_type=jnp.float32).astype(
        jnp.bfloat16
    )
    glob_stride = token_count // (KEYS // seq_count)
    keyval_two = pick_keys(hidden_two, global_offset, glob_stride, key_second, value_second)
    keyval_two = spread_global(keyval_two)
    mixed_two = attend_local(query_two, keyval_two, head_count)
    partial_value = jnp.dot(mixed_two, output_second, preferred_element_type=jnp.float32)
    own_rows, unused_rows = combine(partial_value, second_rows, False)
    return own_rows


def one_hot(condition):
    return jnp.where(condition, 1.0, 0.0).astype(BF16)


def dot(left, right):
    return jnp.dot(left, right, preferred_element_type=F32)


def pieces(count, size):
    size = size if count % size == 0 else count
    return [slice(start, start + size) for start in range(0, count, size)]


def norm_into(out, start, source, gain, count):
    for span in pieces(count, 64):
        out[start + span.start : start + span.stop, :] = norm_rows(
            source[span, :].astype(F32), gain
        )


def bring(source, target, sem):
    copy = pltpu.make_async_copy(source, target, sem)
    copy.start()
    return copy


def pick_matrix(offsets, heads, groups, stride):
    count = groups * stride
    place = lax.broadcasted_iota(jnp.int32, (groups, count), 1)
    place = place - lax.broadcasted_iota(jnp.int32, (groups, count), 0) * stride
    return jnp.concatenate([one_hot(place == offsets[h]) for h in range(heads)], axis=0)


def project_keys(chosen, heads, weights, keyval_ref):
    rows, width = chosen.shape
    groups, head_size = rows // heads, width // heads
    column = lax.broadcasted_iota(jnp.int32, (groups, width), 1)
    for slot, weight in enumerate(weights):
        wide = dot(chosen, weight())
        total = jnp.zeros((groups, width), F32)
        for h in range(heads):
            own = (column >= h * head_size) & (column < (h + 1) * head_size)
            total = jnp.where(own, wide[h * groups : (h + 1) * groups], total)
        total = total.astype(BF16)
        for copy in range(keyval_ref.shape[0]):
            keyval_ref[copy, slot] = total


def ranks(offsets, chunk, stride, share, axis):
    heads = offsets.shape[0]

    def places(way):
        shape = (1, chunk) if way else (chunk, 1)
        place = lax.broadcasted_iota(jnp.int32, shape, way)
        inside = lax.rem(place, stride)
        taken = inside == offsets[0]
        for h in range(1, heads):
            taken = taken | (inside == offsets[h])
        return place, inside, jnp.where(taken, inside, inside + stride)

    place, inside, order = places(axis)
    other_place, _, other_order = places(1 - axis)
    ahead = (other_order < order) & (lax.div(other_place, stride) == lax.div(place, stride))
    rank = jnp.sum(jnp.where(ahead, 1, 0), axis=1 - axis, keepdims=True)
    group = lax.div(place, stride)
    return jnp.where(
        rank < heads, group * heads + rank, share + group * (stride - heads) + rank - heads
    )


def slots_of(offsets, heads):
    values = [offsets[h] for h in range(heads)]
    fresh = []
    for h in range(heads):
        seen = jnp.int32(1)
        for earlier in values[:h]:
            seen = jnp.where(earlier == values[h], 0, seen)
        fresh.append(seen)
    slots = []
    for h in range(heads):
        slot = jnp.int32(0)
        for other in range(heads):
            slot = slot + jnp.where(values[other] < values[h], fresh[other], 0)
        slots.append(slot)
    return slots


def first_keys_kernel(
    offsets, tokens, gain, key_weight, value_weight, keyval, rows, wide, picks, scale, sems, *, stride
):
    copies = [
        bring(offsets, picks, sems.at[0]),
        bring(tokens, rows, sems.at[1]),
        bring(gain, scale, sems.at[2]),
        bring(key_weight, wide.at[0], sems.at[3]),
        bring(value_weight, wide.at[1], sems.at[4]),
    ]
    heads = offsets.shape[0]
    copies[0].wait()
    chooser = pick_matrix(picks, heads, rows.shape[0] // stride, stride)
    copies[1].wait()
    copies[2].wait()
    chosen = norm_rows(dot(chooser, rows[...]), scale[...])

    def weight(slot):
        copies[slot + 3].wait()
        return wide[slot]

    project_keys(
        chosen, heads, [functools.partial(weight, slot) for slot in range(2)], keyval
    )


def scaled(query, head_size):
    return (query * (head_size ** (-0.5) * LOG2E)).astype(BF16)


def order_kernel(
    offsets, tokens, gain, moved_rows, normed, rows, picks, scale, sems, *, stride, chunk
):
    copies = [
        bring(offsets, picks, sems.at[0]),
        bring(tokens, rows, sems.at[1]),
        bring(gain, scale, sems.at[2]),
    ]
    count = tokens.shape[0]
    share = chunk // stride * offsets.shape[0]
    rest = chunk - share
    picked = count // chunk * share
    copies[0].wait()
    mover = one_hot(
        lax.broadcasted_iota(jnp.int32, (chunk, chunk), 0)
        == ranks(picks, chunk, stride, share, 1)
    )
    copies[1].wait()
    copies[2].wait()
    for c in range(count // chunk):
        moved = dot(mover, rows[c * chunk : (c + 1) * chunk, :]).astype(BF16)
        moved_rows[c * share : (c + 1) * share, :] = moved[:share]
        moved_rows[picked + c * rest : picked + (c + 1) * rest, :] = moved[share:]
    norm_into(normed, 0, moved_rows, scale[...], count)


def first_query_kernel(normed, weight, query, held, sems, *, head_size):
    copy = bring(weight, held, sems.at[0])
    copy.wait()
    for span in pieces(normed.shape[0], 512):
        query[span, :] = scaled(dot(normed[span, :], held[...]), head_size)


def head_windows(head_size, width):
    period = min(width, math.lcm(head_size, 128))
    windows = []
    for h in range(period // head_size):
        start = h * head_size // 128 * 128
        stop = min(period, -(-(h + 1) * head_size // 128) * 128)
        windows.append((start, stop - start))
    return period, windows


def head_peaks(rows, heads):
    count, width = rows.shape
    column = lax.broadcasted_iota(jnp.int32, (width, 128), 0)
    head = lax.broadcasted_iota(jnp.int32, (width, 128), 1)
    low = head * (width // heads)
    sums = one_hot((column >= low) & (column < low + width // heads))
    peak = None
    for span in pieces(count, max(16, count // 16)):
        part = rows[span, :]
        part = part * part
        peak = part if peak is None else jnp.maximum(peak, part)
    return jnp.max(dot(peak, sums), axis=0, keepdims=True)


def load_keys(keyvals, heads, turned, peaks):
    keys = jnp.concatenate([x[i, 0] for x in keyvals for i in range(x.shape[0])], axis=0)
    turned[...] = keys.T
    peaks[...] = head_peaks(keys, heads)


def small_scores(query, first_row, rows, heads, peaks):
    bound = head_peaks(query.at[pl.ds(first_row, rows)], heads) * peaks
    return jnp.max(bound) < 9000.0


def reciprocal(x):
    guess = pl.reciprocal(x, approx=True)
    return guess * (2.0 - x * guess)


def attend_rows(
    query, first_row, rows, heads, turned, keyvals, mixed_ref, mixed_row, work, plain
):
    scores_ref, weights_ref = work
    width = query.shape[1]
    key_count = turned.shape[1]
    head_size = width // heads
    period, windows = head_windows(head_size, width)
    span = pl.ds(first_row, rows)
    out_span = pl.ds(mixed_row, rows)
    lane = lax.broadcasted_iota(jnp.int32, (1, 128), 1)
    ones = jnp.ones((key_count, 128), BF16)

    @pl.loop(0, width // period)
    def _(turn):
        base = pl.multiple_of(turn * period, 128)
        sums = {}

        def product(h):
            start, size = windows[h]
            low = h * head_size - start
            high = low + head_size
            own = turned[pl.ds(pl.multiple_of(base + h * head_size, 16), head_size), :]
            parts = [own]
            if low:
                parts.insert(0, jnp.zeros((low, key_count), BF16))
            if high < size:
                parts.append(jnp.zeros((size - high, key_count), BF16))
            return dot(query[span, pl.ds(base + start, size)], jnp.concatenate(parts, axis=0))

        for h, (start, size) in enumerate(windows):
            if plain:
                weights = jnp.exp2(product(h)).astype(BF16)
            else:
                scores_ref[...] = product(h)
                for part in pieces(rows, 64):
                    scores = scores_ref[part, :]
                    scores = scores - jnp.max(scores, axis=1, keepdims=True)
                    weights_ref[part, :] = jnp.exp2(scores).astype(BF16)
                weights = weights_ref[...]
            columns = pl.ds(base + start, size)
            values = jnp.concatenate(
                [x[i, 1, :, columns] for x in keyvals for i in range(x.shape[0])], axis=0
            )
            mixed = dot(weights, jnp.concatenate([values, ones], axis=1))
            share = reciprocal(mixed[:, size:])
            for column in range(0, size, 128):
                own = mixed[:, column : column + 128] * share
                at = start + column
                if at in sums:
                    own = jnp.where(lane >= h * head_size - at, own, sums[at])
                sums[at] = own
                if (h + 1) * head_size >= at + 128:
                    mixed_ref[out_span, pl.ds(base + at, 128)] = sums.pop(at).astype(BF16)


def attend(query, first_row, rows, heads, turned, keyvals, mixed_ref, work, peaks):
    small = small_scores(query, first_row, rows, heads, peaks)
    size = math.gcd(rows, ROWS)

    @pl.when(small)
    def _():
        attend_rows(query, first_row, rows, heads, turned, keyvals, mixed_ref, 0, work, True)

    @pl.when(jnp.logical_not(small))
    def _():
        @pl.loop(0, rows // size)
        def _(step):
            row = pl.multiple_of(step * size, size)
            attend_rows(
                query,
                pl.multiple_of(first_row + row, 16),
                size,
                heads,
                turned,
                keyvals,
                mixed_ref,
                row,
                work,
                False,
            )


def gelu(x):
    half = 0.5 * x
    return half + half * jnp.tanh(x * (0.7978845608028654 + 0.035677408136300125 * (x * x)))


def widen(normed, up_weight, low, wide_ref, inner):
    rows = normed.shape[0]
    spans = pieces(inner.shape[1], wide_ref.shape[2])

    def product(i):
        columns = slice(low + spans[i].start, low + spans[i].stop)
        wide_ref[i % 2] = dot(normed[...], up_weight[:, columns])

    product(0)
    for i, span in enumerate(spans):
        if i + 1 < len(spans):
            product(i + 1)
        for part in pieces(rows, 32):
            inner[part, span] = gelu(wide_ref[i % 2, part, :]).astype(BF16)


def narrow(inners, down_weight, first, second, size):
    for span in pieces(second.shape[1], size):
        total = first[:, span].astype(F32)
        low = 0
        for inner in inners:
            high = low + inner.shape[1]
            total = total + dot(inner[...], down_weight[low:high, span])
            low = high
        second[:, span] = total.astype(BF16)


def add_heads(tokens, first_row, mixed, out_weight, gain, first, normed):
    before = None
    for span in pieces(mixed.shape[0], 256):
        total = dot(mixed[span, :], out_weight[...])
        rows = tokens[first_row + span.start : first_row + span.stop, :]
        first[span, :] = (rows.astype(F32) + total).astype(BF16)
        if before is not None:
            norm_into(normed, before.start, first.at[before], gain, before.stop - before.start)
        before = span
    norm_into(normed, before.start, first.at[before], gain, before.stop - before.start)


def picked_kernel(
    offsets,
    tokens,
    query,
    keyval,
    keyval_far,
    out_weight,
    mlp_gain,
    up_weight,
    down_weight,
    gain,
    key_weight,
    value_weight,
    second,
    keyval_two,
    turned,
    peaks,
    held,
    mixed,
    scores,
    weights,
    first,
    normed,
    wide,
    inner,
    sems,
    *,
    heads,
):
    copies = [
        bring(x, held.at[i], sems.at[i]) for i, x in enumerate((key_weight, value_weight))
    ]
    rows = second.shape[0]
    keyvals = (keyval, keyval_far)
    load_keys(keyvals, heads, turned, peaks)
    attend(query, 0, rows, heads, turned, keyvals, mixed, (scores, weights), peaks[...])
    add_heads(tokens, 0, mixed, out_weight, mlp_gain[...], first, normed)
    widen(normed, up_weight, 0, wide, inner)
    narrow([inner], down_weight, first, second, second.shape[1])
    norm_into(normed, 0, second, gain[...], rows)
    chooser = pick_matrix(slots_of(offsets, heads), heads, rows // heads, heads)
    chosen = dot(chooser, normed[...]).astype(BF16)

    def weight(slot):
        copies[slot].wait()
        return held[slot]

    project_keys(
        chosen, heads, [functools.partial(weight, slot) for slot in range(2)], keyval_two
    )


def rest_attention_kernel(
    query, keyval, keyval_far, turned, peaks, mixed, scores, weights, sems, *, heads
):
    del sems
    rows = mixed.shape[0]
    attend(
        query,
        query.shape[0] - rows,
        rows,
        heads,
        turned,
        (keyval, keyval_far),
        mixed,
        (scores, weights),
        peaks[...],
    )


def rest_up_kernel(
    tokens, mixed, out_weight, gain, up_weight, first, normed, inner, wide, sems
):
    del sems
    add_heads(
        tokens, tokens.shape[0] - mixed.shape[0], mixed, out_weight, gain[...], first, normed
    )
    widen(normed, up_weight, 0, wide, inner)


def rest_down_kernel(
    first, normed, inner, up_weight, down_weight, second, wide, inner_more, sems
):
    del sems
    widen(normed, up_weight, inner.shape[1], wide, inner_more)
    narrow([inner, inner_more], down_weight, first, second, 256)


def second_query_kernel(*refs, head_size):
    *rows, gain, weight, query, held, normed, sems = refs
    copy = bring(weight, held.at[0], sems.at[0])
    steps, start = [], 0
    for part in rows:
        for span in pieces(part.shape[0], 256):
            steps.append((part.at[span], slice(start + span.start, start + span.stop)))
        start += part.shape[0]

    def norm_step(i):
        part, span = steps[i]
        norm_into(normed, span.start, part, gain[...], part.shape[0])

    norm_step(0)
    copy.wait()
    for i, (_, span) in enumerate(steps):
        query[span, :] = scaled(dot(normed[span, :], held[0]), head_size)
        if i + 1 < len(steps):
            norm_step(i + 1)


def second_kernel(*refs, heads, stride, chunk, parts):
    offsets, *rows = refs[: 1 + parts]
    query, keyval, keyval_far, out_weight, encoded = refs[1 + parts : 6 + parts]
    turned, peaks, held, mixed, result, ready, scores, weights, sems = refs[6 + parts :]
    copy = bring(out_weight, held.at[0], sems.at[0])
    keyvals = (keyval, keyval_far)
    load_keys(keyvals, heads, turned, peaks)
    count = query.shape[0]
    attend(query, 0, count, heads, turned, keyvals, mixed, (scores, weights), peaks[...])
    share = chunk // stride * heads
    rest_share = chunk - share
    back = one_hot(
        lax.broadcasted_iota(jnp.int32, (chunk, chunk), 1)
        == ranks(offsets, chunk, stride, share, 0)
    )
    copy.wait()
    start = 0
    for part in rows:
        span = slice(start, start + part.shape[0])
        total = part[...].astype(F32) + dot(mixed[span, :], held[0])
        result[span, :] = total.astype(BF16)
        start += part.shape[0]
    start = count // chunk * share
    copies = []
    for c in range(count // chunk):
        far = start + c * rest_share
        blend = jnp.concatenate(
            [result[c * share : (c + 1) * share, :], result[far : far + rest_share, :]], axis=0
        )
        span = pl.ds(c * chunk, chunk)
        ready[span, :] = dot(back, blend).astype(BF16)
        copies.append(bring(ready.at[span], encoded.at[span], sems.at[1 + c]))
    for copy in copies:
        copy.wait()


def relaying(kernel, ins, outs, *refs):
    end = ins + 1 + outs
    refs[end][...] = refs[ins][...]
    kernel(*refs[:ins], *refs[ins + 1 : end], *refs[end + 1 :])


def local_call(kernel, outs, inputs, scratch, scalars=0, far=(), relay=None, out_near=True, copies=1, flops=0, name=None):
    outs, inputs = list(outs), list(inputs)
    if relay is not None:
        kernel = functools.partial(relaying, kernel, len(inputs), len(outs))
        inputs.append(relay)
        outs.append(pltpu.VMEM(relay.shape, relay.dtype))
    specs, placed = [], []
    for i, x in enumerate(inputs):
        if i < scalars:
            specs.append(pl.BlockSpec(memory_space=pltpu.SMEM))
        elif i in far:
            specs.append(pl.BlockSpec(memory_space=pltpu.HBM))
            x = pltpu.with_memory_space_constraint(x, pltpu.HBM)
        else:
            specs.append(pl.BlockSpec(memory_space=pltpu.VMEM))
            x = pltpu.with_memory_space_constraint(x, pltpu.VMEM)
        placed.append(x)
    return pl.pallas_call(
        kernel,
        out_shape=outs,
        in_specs=specs,
        out_specs=[
            pl.BlockSpec(memory_space=pltpu.VMEM if out_near else pltpu.HBM)
        ] * len(outs),
        scratch_shapes=list(scratch) + [pltpu.SemaphoreType.DMA((copies,))],
        compiler_params=pltpu.CompilerParams(vmem_limit_bytes=VMEM_LIMIT),
        cost_estimate=pl.CostEstimate(
            flops=int(flops),
            transcendentals=0,
            bytes_accessed=sum(inputs[i].size * inputs[i].dtype.itemsize for i in far),
        ),
        name=name,
    )(*placed)


def exchange(keyval, span, beside, early):
    levels = span.bit_length() - 1
    early = early and levels > 2
    crossed, fresh = [], keyval
    for level in reversed(range(levels)):
        partner = swapped(keyval if level != 1 or not early else fresh, "seq", level)
        if early and level > 1:
            crossed.append(swapped(fresh, "seq", 1))
        keyval = beside(levels - 1 - level, keyval)
        fresh = partner
        if level:
            blocks = [keyval, partner]
            if level == 1:
                blocks = [keyval, *crossed, partner]
            keyval = jnp.concatenate(blocks, axis=0)
    return keyval, partner


def whole_body(
    tokens,
    attn_gain,
    query_first,
    key_first,
    segment_value,
    output_first,
    mlp_gain,
    up_weight,
    down_weight,
    second_gain,
    query_second,
    key_second,
    value_second,
    output_second,
    segment_offset,
    global_offset,
):
    seq_count = lax.axis_size("seq")
    seg_span = min(SEG_MAX, seq_count)
    heads = segment_offset.shape[0]
    count, width = tokens.shape
    head_size = width // heads
    hidden = up_weight.shape[1]
    stride = count // (KEYS // seg_span)
    stride_two = count // (KEYS // seq_count)
    groups, groups_two = count // stride, count // stride_two
    chunk = max(ROWS, stride_two)
    picked_count = groups_two * heads
    rest_count = count - picked_count
    part = hidden // 4

    def near(*shape):
        return pltpu.VMEM(shape, BF16)

    def attention_work(rows):
        rows = math.gcd(rows, ROWS)
        return [pltpu.VMEM((rows, KEYS), F32), near(rows, KEYS)]

    def feed_work(rows):
        return [near(rows, width), pltpu.VMEM((2, rows, part), F32)]

    held_shapes = [near(width, KEYS), pltpu.VMEM((1, 128), F32)]
    small_work = [pltpu.SMEM((heads,), jnp.int32), pltpu.VMEM((width,), F32)]

    (keyval,) = local_call(
        functools.partial(first_keys_kernel, stride=stride),
        [near(1, 2, groups, width)],
        (segment_offset, tokens, attn_gain, key_first, segment_value),
        [near(count, width), near(2, width, width)] + small_work,
        far=(0, 1, 2, 3, 4),
        copies=5,
        flops=2 * heads * groups * width * (count + 2 * width),
        name="first_keys",
    )
    made = {}

    def beside_first(level, held):
        if level == 0:
            made["rows"], made["normed"], held = local_call(
                functools.partial(order_kernel, stride=stride_two, chunk=chunk),
                [near(count, width), near(count, width)],
                (global_offset, tokens, attn_gain),
                [near(count, width)] + small_work,
                far=(0, 1, 2),
                copies=3,
                relay=held,
                flops=2 * count * width * chunk,
                name="order",
            )
        if level == min(1, seg_span.bit_length() - 2):
            made["query"], held = local_call(
                functools.partial(first_query_kernel, head_size=head_size),
                [near(count, width)],
                (made["normed"], query_first),
                [near(width, width)],
                far=(1,),
                relay=held,
                flops=2 * count * width * width,
                name="first_query",
            )
        return held

    keyval, keyval_far = exchange(keyval, seg_span, beside_first, True)
    rows, query = made["rows"], made["query"]
    row_flops = 2 * width * (2 * hidden + width) + 4 * 256 * KEYS * heads
    picked_second, keyval_two, turned, peaks = local_call(
        functools.partial(picked_kernel, heads=heads),
        [
            near(picked_count, width),
            near(1, 2, groups_two, width),
        ]
        + held_shapes,
        (
            global_offset,
            rows,
            query,
            keyval,
            keyval_far,
            output_first,
            mlp_gain,
            up_weight,
            down_weight,
            second_gain,
            key_second,
            value_second,
        ),
        [near(2, width, width), near(picked_count, width)]
        + attention_work(picked_count)
        + [near(picked_count, width)]
        + feed_work(picked_count)
        + [near(picked_count, hidden)],
        scalars=1,
        far=(10, 11),
        copies=2,
        flops=row_flops * picked_count,
        name="layer_of_picked",
    )
    seconds = [picked_second]

    def rest_attention(held):
        made["mixed"], held = local_call(
            functools.partial(rest_attention_kernel, heads=heads),
            [near(rest_count, width)],
            (query, keyval, keyval_far, turned, peaks),
            attention_work(rest_count),
            relay=held,
            flops=4 * 256 * KEYS * heads * rest_count,
            name="rest_attention",
        )
        return held

    half = hidden // 2

    def rest_up(held):
        made["first"], made["normed"], made["inner"], held = local_call(
            rest_up_kernel,
            [near(rest_count, width), near(rest_count, width), near(rest_count, half)],
            (rows, made["mixed"], output_first, mlp_gain, up_weight),
            [pltpu.VMEM((2, rest_count, part), F32)],
            relay=held,
            flops=2 * width * (half + width) * rest_count,
            name="rest_up",
        )
        return held

    def rest_down(held):
        result, held = local_call(
            rest_down_kernel,
            [near(rest_count, width)],
            (made["first"], made["normed"], made["inner"], up_weight, down_weight),
            [pltpu.VMEM((2, rest_count, part), F32), near(rest_count, hidden - half)],
            relay=held,
            flops=2 * width * (2 * hidden - half) * rest_count,
            name="rest_down",
        )
        seconds.append(result)
        return held

    def second_query(held):
        made["query_two"], held = local_call(
            functools.partial(second_query_kernel, head_size=head_size),
            [near(count, width)],
            (*seconds, second_gain, query_second),
            [near(1, width, width), near(count, width)],
            far=(len(seconds) + 1,),
            relay=held,
            flops=2 * count * width * width,
            name="second_query",
        )
        return held

    tasks = [rest_attention, rest_up, rest_down, second_query]
    levels = seq_count.bit_length() - 1

    def beside_second(level, held):
        ahead = len(tasks) * level // levels
        for task in tasks[ahead : len(tasks) * (level + 1) // levels]:
            held = task(held)
        return held

    keyval_two, keyval_two_far = exchange(keyval_two, seq_count, beside_second, False)
    (encoded,) = local_call(
        functools.partial(
            second_kernel, heads=heads, stride=stride_two, chunk=chunk, parts=len(seconds)
        ),
        [jax.ShapeDtypeStruct((count, width), BF16)],
        (
            global_offset,
            *seconds,
            made["query_two"],
            keyval_two,
            keyval_two_far,
            output_second,
        ),
        held_shapes
        + [near(1, width, width)]
        + [near(count, width)] * 3
        + attention_work(count),
        scalars=1,
        far=(len(seconds) + 4,),
        out_near=False,
        copies=1 + count // chunk,
        flops=count * (2 * width * width + 4 * 256 * KEYS * heads),
        name="second_attention",
    )
    return encoded


def solution(mesh):
    placed = (
        P(("slides", "seq", "mp"), None),
        P(),
        P(None, "mp"),
        P(None, "mp"),
        P(None, "mp"),
        P("mp", None),
        P(),
        P(None, "mp"),
        P("mp", None),
        P(),
        P(None, "mp"),
        P(None, "mp"),
        P(None, "mp"),
        P("mp", None),
        P("mp"),
        P("mp"),
    )
    fits = mesh.shape["mp"] == 1 and 2 <= mesh.shape["seq"] <= SEG_MAX
    return jax.shard_map(
        whole_body if fits else split_body,
        mesh=mesh,
        in_specs=placed,
        out_specs=P(("slides", "seq", "mp"), None),
        check_vma=False,
    )
```

```python
import functools
import math

import jax
import jax.numpy as jnp
from jax import lax
from jax.experimental import pallas as pl
from jax.experimental.pallas import tpu as pltpu
from jax.sharding import PartitionSpec as P

KEYS = 256
SEG_MAX = 16
ROWS = 256
LOG2E = 1.4426950408889634
BF16 = jnp.bfloat16
F32 = jnp.float32
VMEM_LIMIT = 22 * 1024 * 1024


def swapped(x, axis, apart):
    return lax.ppermute(x, axis, [(i, i ^ 1 << apart) for i in range(lax.axis_size(axis))])


def norm_rows(values, gain):
    center = values - jnp.mean(values, axis=-1, keepdims=True)
    spread = jnp.mean(center * center, axis=-1, keepdims=True)
    return (center * lax.rsqrt(spread + 1e-05) * gain).astype(jnp.bfloat16)


def pick_keys(hidden, offsets, stride, key_weight, value_weight):
    token_count, width = hidden.shape
    head_count = offsets.shape[0]
    head_size = key_weight.shape[1] // head_count
    grouped_rows = hidden.reshape(token_count // stride, stride, width)
    dilation_selector = (
        lax.broadcasted_iota(jnp.int32, (stride, head_count), 0) == offsets[None, :]
    ).astype(jnp.bfloat16)
    chosen = jnp.einsum(
        "nof,oj->njf", grouped_rows, dilation_selector, preferred_element_type=jnp.float32
    ).astype(jnp.bfloat16)
    key_heads = jnp.einsum(
        "xkr,rkf->xkf",
        chosen,
        key_weight.reshape(width, head_count, head_size),
        preferred_element_type=jnp.float32,
    ).astype(jnp.bfloat16)
    value_heads = jnp.einsum(
        "xkr,rkf->xkf",
        chosen,
        value_weight.reshape(width, head_count, head_size),
        preferred_element_type=jnp.float32,
    ).astype(jnp.bfloat16)
    picked = token_count // stride
    return jnp.stack(
        [
            key_heads.reshape(picked, head_count * head_size),
            value_heads.reshape(picked, head_count * head_size),
        ]
    )


def attend_local(query, keyval, head_count):
    token_count, width = query.shape
    head_size = width // head_count
    query_heads = query.reshape(token_count, head_count, head_size)
    key_heads = keyval[0].reshape(-1, head_count, head_size)
    value_heads = keyval[1].reshape(-1, head_count, head_size)
    scores = jnp.einsum(
        "thd,khd->htk", query_heads, key_heads, preferred_element_type=jnp.float32
    ) * head_size ** (-0.5)
    highest = jnp.max(scores, axis=-1, keepdims=True)
    weights = jnp.exp(scores - highest)
    weights = (weights / jnp.sum(weights, axis=-1, keepdims=True)).astype(jnp.bfloat16)
    mixed = jnp.einsum(
        "htk,khd->thd", weights, value_heads, preferred_element_type=jnp.float32
    ).astype(jnp.bfloat16)
    return mixed.reshape(token_count, width)


def merge_branch_pair(mine, other, level, token_position):
    lower = token_position >> level & 1 == 0
    return jnp.where(
        lower, jnp.concatenate((mine, other), axis=1), jnp.concatenate((other, mine), axis=1)
    )


def spread_segment(keyval, seg_span, token_position):
    for level in range(seg_span.bit_length() - 1):
        partner = swapped(keyval, "seq", level)
        keyval = merge_branch_pair(keyval, partner, level, token_position)
    return keyval


def spread_global(keyval_two):
    keyval_two = lax.all_gather(keyval_two, "seq", axis=1, tiled=True)
    return keyval_two


def combine(partial_value, residual_full, need_full):
    row_count = residual_full.shape[0] // lax.axis_size("mp")
    row_start = lax.axis_index("mp") * row_count
    share = lax.psum_scatter(partial_value, "mp", scatter_dimension=0, tiled=True)
    own_rows = lax.dynamic_slice_in_dim(residual_full, row_start, row_count, 0)
    own_rows = (own_rows.astype(jnp.float32) + share).astype(jnp.bfloat16)
    full_rows = lax.all_gather(own_rows, "mp", axis=0, tiled=True) if need_full else own_rows
    return (own_rows, full_rows)


def split_body(
    tokens,
    attn_gain,
    query_first,
    key_first,
    segment_value,
    output_first,
    mlp_gain,
    up_weight,
    down_weight,
    second_gain,
    query_second,
    key_second,
    value_second,
    output_second,
    segment_offset,
    global_offset,
):
    seq_count = lax.axis_size("seq")
    token_position = lax.axis_index("seq")
    seg_span = min(SEG_MAX, seq_count)
    head_count = segment_offset.shape[0]
    full_rows = lax.all_gather(tokens, "mp", axis=0, tiled=True)
    token_count = full_rows.shape[0]
    hidden = norm_rows(full_rows.astype(jnp.float32), attn_gain)
    query = jnp.dot(hidden, query_first, preferred_element_type=jnp.float32).astype(jnp.bfloat16)
    seg_stride = token_count // (KEYS // seg_span)
    keyval = pick_keys(hidden, segment_offset, seg_stride, key_first, segment_value)
    keyval = spread_segment(keyval, seg_span, token_position)
    mixed = attend_local(query, keyval, head_count)
    partial_value = jnp.dot(mixed, output_first, preferred_element_type=jnp.float32)
    own_rows, first_rows = combine(partial_value, full_rows, True)
    normed = norm_rows(first_rows.astype(jnp.float32), mlp_gain)
    inner = jax.nn.gelu(
        jnp.dot(normed, up_weight, preferred_element_type=jnp.float32), approximate=True
    ).astype(jnp.bfloat16)
    partial_value = jnp.dot(inner, down_weight, preferred_element_type=jnp.float32)
    own_rows, second_rows = combine(partial_value, first_rows, True)
    hidden_two = norm_rows(second_rows.astype(jnp.float32), second_gain)
    query_two = jnp.dot(hidden_two, query_second, preferred_element_type=jnp.float32).astype(
        jnp.bfloat16
    )
    glob_stride = token_count // (KEYS // seq_count)
    keyval_two = pick_keys(hidden_two, global_offset, glob_stride, key_second, value_second)
    keyval_two = spread_global(keyval_two)
    mixed_two = attend_local(query_two, keyval_two, head_count)
    partial_value = jnp.dot(mixed_two, output_second, preferred_element_type=jnp.float32)
    own_rows, unused_rows = combine(partial_value, second_rows, False)
    return own_rows


def one_hot(condition):
    return jnp.where(condition, 1.0, 0.0).astype(BF16)


def dot(left, right):
    return jnp.dot(left, right, preferred_element_type=F32)


def pieces(count, size):
    size = size if count % size == 0 else count
    return [slice(start, start + size) for start in range(0, count, size)]


def norm_into(out, start, source, gain, count):
    for span in pieces(count, 64):
        out[start + span.start : start + span.stop, :] = norm_rows(
            source[span, :].astype(F32), gain
        )


def bring(source, target, sem):
    copy = pltpu.make_async_copy(source, target, sem)
    copy.start()
    return copy


def pick_matrix(offsets, heads, groups, stride):
    count = groups * stride
    place = lax.broadcasted_iota(jnp.int32, (groups, count), 1)
    place = place - lax.broadcasted_iota(jnp.int32, (groups, count), 0) * stride
    return jnp.concatenate([one_hot(place == offsets[h]) for h in range(heads)], axis=0)


def project_keys(chosen, heads, weights, keyval_ref):
    rows, width = chosen.shape
    groups, head_size = rows // heads, width // heads
    column = lax.broadcasted_iota(jnp.int32, (groups, width), 1)
    for slot, weight in enumerate(weights):
        wide = dot(chosen, weight())
        total = jnp.zeros((groups, width), F32)
        for h in range(heads):
            own = (column >= h * head_size) & (column < (h + 1) * head_size)
            total = jnp.where(own, wide[h * groups : (h + 1) * groups], total)
        total = total.astype(BF16)
        for copy in range(keyval_ref.shape[0]):
            keyval_ref[copy, slot] = total


def ranks(offsets, chunk, stride, share, axis):
    heads = offsets.shape[0]

    def places(way):
        shape = (1, chunk) if way else (chunk, 1)
        place = lax.broadcasted_iota(jnp.int32, shape, way)
        inside = lax.rem(place, stride)
        taken = inside == offsets[0]
        for h in range(1, heads):
            taken = taken | (inside == offsets[h])
        return place, inside, jnp.where(taken, inside, inside + stride)

    place, inside, order = places(axis)
    other_place, _, other_order = places(1 - axis)
    ahead = (other_order < order) & (lax.div(other_place, stride) == lax.div(place, stride))
    rank = jnp.sum(jnp.where(ahead, 1, 0), axis=1 - axis, keepdims=True)
    group = lax.div(place, stride)
    return jnp.where(
        rank < heads, group * heads + rank, share + group * (stride - heads) + rank - heads
    )


def slots_of(offsets, heads):
    values = [offsets[h] for h in range(heads)]
    fresh = []
    for h in range(heads):
        seen = jnp.int32(1)
        for earlier in values[:h]:
            seen = jnp.where(earlier == values[h], 0, seen)
        fresh.append(seen)
    slots = []
    for h in range(heads):
        slot = jnp.int32(0)
        for other in range(heads):
            slot = slot + jnp.where(values[other] < values[h], fresh[other], 0)
        slots.append(slot)
    return slots


def first_keys_kernel(
    offsets, tokens, gain, key_weight, value_weight, keyval, rows, wide, picks, scale, sems, *, stride
):
    copies = [
        bring(offsets, picks, sems.at[0]),
        bring(tokens, rows, sems.at[1]),
        bring(gain, scale, sems.at[2]),
        bring(key_weight, wide.at[0], sems.at[3]),
        bring(value_weight, wide.at[1], sems.at[4]),
    ]
    heads = offsets.shape[0]
    copies[0].wait()
    chooser = pick_matrix(picks, heads, rows.shape[0] // stride, stride)
    copies[1].wait()
    copies[2].wait()
    chosen = norm_rows(dot(chooser, rows[...]), scale[...])

    def weight(slot):
        copies[slot + 3].wait()
        return wide[slot]

    project_keys(
        chosen, heads, [functools.partial(weight, slot) for slot in range(2)], keyval
    )


def scaled(query, head_size):
    return (query * (head_size ** (-0.5) * LOG2E)).astype(BF16)


def order_kernel(
    offsets, tokens, gain, moved_rows, normed, rows, picks, scale, sems, *, stride, chunk
):
    copies = [
        bring(offsets, picks, sems.at[0]),
        bring(tokens, rows, sems.at[1]),
        bring(gain, scale, sems.at[2]),
    ]
    count = tokens.shape[0]
    share = chunk // stride * offsets.shape[0]
    rest = chunk - share
    picked = count // chunk * share
    copies[0].wait()
    mover = one_hot(
        lax.broadcasted_iota(jnp.int32, (chunk, chunk), 0)
        == ranks(picks, chunk, stride, share, 1)
    )
    copies[1].wait()
    copies[2].wait()
    for c in range(count // chunk):
        moved = dot(mover, rows[c * chunk : (c + 1) * chunk, :]).astype(BF16)
        moved_rows[c * share : (c + 1) * share, :] = moved[:share]
        moved_rows[picked + c * rest : picked + (c + 1) * rest, :] = moved[share:]
    norm_into(normed, 0, moved_rows, scale[...], count)


def first_query_kernel(normed, weight, query, peaks, sems, *, first_row, heads):
    del sems
    rows, width = query.shape
    part = normed.at[pl.ds(first_row, rows)]
    query[...] = scaled(dot(part[...], weight[...]), width // heads)
    peaks[...] = head_peaks(query, heads)


def head_windows(head_size, width):
    period = min(width, math.lcm(head_size, 128))
    windows = []
    for h in range(period // head_size):
        start = h * head_size // 128 * 128
        stop = min(period, -(-(h + 1) * head_size // 128) * 128)
        windows.append((start, stop - start))
    return period, windows


def head_peaks(rows, heads):
    count, width = rows.shape
    column = lax.broadcasted_iota(jnp.int32, (width, 128), 0)
    head = lax.broadcasted_iota(jnp.int32, (width, 128), 1)
    low = head * (width // heads)
    sums = one_hot((column >= low) & (column < low + width // heads))
    peak = None
    for span in pieces(count, max(16, count // 16)):
        part = rows[span, :]
        part = part * part
        peak = part if peak is None else jnp.maximum(peak, part)
    return jnp.max(dot(peak, sums), axis=0, keepdims=True)


def load_keys(keyvals, heads, turned, peaks):
    keys = jnp.concatenate([x[i, 0] for x in keyvals for i in range(x.shape[0])], axis=0)
    turned[...] = keys.T
    peaks[...] = head_peaks(keys, heads)


def small_scores(query_peaks, key_peaks):
    query = query_peaks[0][...]
    for other in query_peaks[1:]:
        query = jnp.maximum(query, other[...])
    return jnp.max(query * key_peaks[...]) < 9000.0


def reciprocal(x):
    guess = pl.reciprocal(x, approx=True)
    return guess * (2.0 - x * guess)


def attend_rows(
    query, first_row, rows, heads, turned, keyvals, mixed_ref, mixed_row, work, plain
):
    scores_ref, weights_ref = work
    width = query.shape[1]
    key_count = turned.shape[1]
    head_size = width // heads
    period, windows = head_windows(head_size, width)
    span = pl.ds(first_row, rows)
    out_span = pl.ds(mixed_row, rows)
    lane = lax.broadcasted_iota(jnp.int32, (1, 128), 1)

    @pl.loop(0, width // period)
    def _(turn):
        base = pl.multiple_of(turn * period, 128)
        sums = {}

        def score(h):
            start, size = windows[h]
            low = h * head_size - start
            high = low + head_size
            own = turned[pl.ds(pl.multiple_of(base + h * head_size, 16), head_size), :]
            parts = [own]
            if low:
                parts.insert(0, jnp.zeros((low, key_count), BF16))
            if high < size:
                parts.append(jnp.zeros((size - high, key_count), BF16))
            scores_ref[h % 2, :rows] = dot(
                query[span, pl.ds(base + start, size)], jnp.concatenate(parts, axis=0)
            )

        def weigh(h):
            for part in pieces(rows, 64):
                scores = scores_ref[h % 2, part, :]
                if not plain:
                    scores = scores - jnp.max(scores, axis=1, keepdims=True)
                weights_ref[h % 2, part, :] = jnp.exp2(scores).astype(BF16)

        def mix(h):
            start, size = windows[h]
            low = h * head_size - start
            values = jnp.concatenate(
                [
                    x[i, 1, :, pl.ds(base + start, size)]
                    for x in keyvals
                    for i in range(x.shape[0])
                ],
                axis=0,
            )
            column = lax.broadcasted_iota(jnp.int32, (key_count, size), 1)
            own = (column >= low) & (column < low + head_size)
            values = jnp.where(own, values, jnp.ones((), BF16))
            mixed = dot(weights_ref[h % 2, :rows], values)
            for offset in range(0, size, 128):
                own = mixed[:, offset : offset + 128]
                own = own * reciprocal(pltpu.roll(own, 64, 1))
                at = start + offset
                if at in sums:
                    own = jnp.where(lane >= h * head_size - at, own, sums[at])
                sums[at] = own
                if (h + 1) * head_size >= at + 128:
                    mixed_ref[out_span, pl.ds(base + at, 128)] = sums.pop(at).astype(BF16)

        score(0)
        for h in range(len(windows)):
            if h:
                mix(h - 1)
            if h + 1 < len(windows):
                score(h + 1)
            weigh(h)
        mix(len(windows) - 1)


def attend(query, first_row, rows, heads, turned, keyvals, mixed_ref, work, small):
    size = math.gcd(rows, ROWS)

    @pl.when(small)
    def _():
        attend_rows(query, first_row, rows, heads, turned, keyvals, mixed_ref, 0, work, True)

    @pl.when(jnp.logical_not(small))
    def _():
        @pl.loop(0, rows // size)
        def _(step):
            row = pl.multiple_of(step * size, size)
            attend_rows(
                query,
                pl.multiple_of(first_row + row, 16),
                size,
                heads,
                turned,
                keyvals,
                mixed_ref,
                row,
                work,
                False,
            )


def gelu(x):
    half = 0.5 * x
    return half + half * jnp.tanh(x * (0.7978845608028654 + 0.035677408136300125 * (x * x)))


def widen(normed, up_weight, low, wide_ref, inner):
    rows = normed.shape[0]
    spans = pieces(inner.shape[1], wide_ref.shape[2])

    def product(i):
        columns = slice(low + spans[i].start, low + spans[i].stop)
        wide_ref[i % 2] = dot(normed[...], up_weight[:, columns])

    product(0)
    for i, span in enumerate(spans):
        if i + 1 < len(spans):
            product(i + 1)
        for part in pieces(rows, 32):
            inner[part, span] = gelu(wide_ref[i % 2, part, :]).astype(BF16)


def feed_forward(normed, up_weight, down_weight, total, wide_ref, inner):
    rows = normed.shape[0]
    spans = pieces(up_weight.shape[1], wide_ref.shape[2])

    def product(i):
        wide_ref[i % 2] = dot(normed[...], up_weight[:, spans[i]])

    product(0)
    for i, span in enumerate(spans):
        if i + 1 < len(spans):
            product(i + 1)
        for part in pieces(rows, 32):
            inner[i % 2, part, :] = gelu(wide_ref[i % 2, part, :]).astype(BF16)
        total[...] += dot(inner[i % 2], down_weight[span, :])


def narrow(inners, down_weight, first, second, size):
    for span in pieces(second.shape[1], size):
        total = first[:, span].astype(F32)
        low = 0
        for inner in inners:
            high = low + inner.shape[1]
            total = total + dot(inner[...], down_weight[low:high, span])
            low = high
        second[:, span] = total.astype(BF16)


def add_heads(tokens, first_row, mixed, out_weight, gain, first, normed):
    before = None
    for span in pieces(mixed.shape[0], 256):
        total = dot(mixed[span, :], out_weight[...])
        rows = tokens[first_row + span.start : first_row + span.stop, :]
        first[span, :] = (rows.astype(F32) + total).astype(BF16)
        if before is not None:
            norm_into(normed, before.start, first.at[before], gain, before.stop - before.start)
        before = span
    norm_into(normed, before.start, first.at[before], gain, before.stop - before.start)


def picked_kernel(
    offsets,
    tokens,
    query,
    query_peaks,
    query_peaks_more,
    keyval,
    keyval_far,
    out_weight,
    mlp_gain,
    up_weight,
    down_weight,
    gain,
    key_weight,
    value_weight,
    second,
    keyval_two,
    turned,
    peaks,
    held,
    mixed,
    scores,
    weights,
    first,
    normed,
    wide,
    inner,
    total,
    sems,
    *,
    heads,
):
    copies = [
        bring(x, held.at[i], sems.at[i]) for i, x in enumerate((key_weight, value_weight))
    ]
    rows = second.shape[0]
    keyvals = (keyval, keyval_far)
    load_keys(keyvals, heads, turned, peaks)
    small = small_scores((query_peaks, query_peaks_more), peaks)
    attend(query, 0, rows, heads, turned, keyvals, mixed, (scores, weights), small)
    add_heads(tokens, 0, mixed, out_weight, mlp_gain[...], first, normed)
    total[...] = first[...].astype(F32)
    feed_forward(normed, up_weight, down_weight, total, wide, inner)
    second[...] = total[...].astype(BF16)
    norm_into(normed, 0, second, gain[...], rows)
    chooser = pick_matrix(slots_of(offsets, heads), heads, rows // heads, heads)
    chosen = dot(chooser, normed[...]).astype(BF16)

    def weight(slot):
        copies[slot].wait()
        return held[slot]

    project_keys(
        chosen, heads, [functools.partial(weight, slot) for slot in range(2)], keyval_two
    )


def rest_attention_kernel(
    query,
    query_peaks,
    query_peaks_more,
    keyval,
    keyval_far,
    turned,
    peaks,
    mixed,
    scores,
    weights,
    sems,
    *,
    heads,
):
    del sems
    rows = mixed.shape[0]
    attend(
        query,
        0,
        rows,
        heads,
        turned,
        (keyval, keyval_far),
        mixed,
        (scores, weights),
        small_scores((query_peaks, query_peaks_more), peaks),
    )


def rest_up_kernel(
    tokens, mixed, out_weight, gain, up_weight, first, normed, inner, wide, sems
):
    del sems
    add_heads(
        tokens, tokens.shape[0] - mixed.shape[0], mixed, out_weight, gain[...], first, normed
    )
    widen(normed, up_weight, 0, wide, inner)


def rest_down_kernel(
    first, normed, inner, up_weight, down_weight, second, wide, inner_more, sems
):
    del sems
    widen(normed, up_weight, inner.shape[1], wide, inner_more)
    narrow([inner, inner_more], down_weight, first, second, 256)


def second_query_kernel(*refs, heads):
    *rows, gain, weight, query, peaks, held, normed, sems = refs
    copy = bring(weight, held.at[0], sems.at[0])
    start = 0
    for part in rows:
        norm_into(normed, start, part, gain[...], part.shape[0])
        start += part.shape[0]
    copy.wait()
    for span in pieces(query.shape[0], 512):
        query[span, :] = scaled(dot(normed[span, :], held[0]), query.shape[1] // heads)
    peaks[...] = head_peaks(query, heads)


def second_kernel(*refs, heads, stride, chunk, parts):
    offsets, *rows = refs[: 1 + parts]
    query, query_peaks, keyval, keyval_far, out_weight, encoded = refs[1 + parts : 7 + parts]
    turned, peaks, held, mixed, result, ready, scores, weights, sems = refs[7 + parts :]
    copy = bring(out_weight, held.at[0], sems.at[0])
    keyvals = (keyval, keyval_far)
    load_keys(keyvals, heads, turned, peaks)
    count = query.shape[0]
    small = small_scores((query_peaks,), peaks)
    attend(query, 0, count, heads, turned, keyvals, mixed, (scores, weights), small)
    share = chunk // stride * heads
    rest_share = chunk - share
    back = one_hot(
        lax.broadcasted_iota(jnp.int32, (chunk, chunk), 1)
        == ranks(offsets, chunk, stride, share, 0)
    )
    copy.wait()
    start = 0
    for part in rows:
        span = slice(start, start + part.shape[0])
        total = part[...].astype(F32) + dot(mixed[span, :], held[0])
        result[span, :] = total.astype(BF16)
        start += part.shape[0]
    start = count // chunk * share
    copies = []
    for c in range(count // chunk):
        far = start + c * rest_share
        blend = jnp.concatenate(
            [result[c * share : (c + 1) * share, :], result[far : far + rest_share, :]], axis=0
        )
        span = pl.ds(c * chunk, chunk)
        ready[span, :] = dot(back, blend).astype(BF16)
        copies.append(bring(ready.at[span], encoded.at[span], sems.at[1 + c]))
    for copy in copies:
        copy.wait()


def relaying(kernel, ins, outs, *refs):
    end = ins + 1 + outs
    refs[end][...] = refs[ins][...]
    kernel(*refs[:ins], *refs[ins + 1 : end], *refs[end + 1 :])


def local_call(kernel, outs, inputs, scratch, scalars=0, far=(), relay=None, out_near=True, copies=1, flops=0, name=None):
    outs, inputs = list(outs), list(inputs)
    if relay is not None:
        kernel = functools.partial(relaying, kernel, len(inputs), len(outs))
        inputs.append(relay)
        outs.append(pltpu.VMEM(relay.shape, relay.dtype))
    specs, placed = [], []
    for i, x in enumerate(inputs):
        if i < scalars:
            specs.append(pl.BlockSpec(memory_space=pltpu.SMEM))
        elif i in far:
            specs.append(pl.BlockSpec(memory_space=pltpu.HBM))
            x = pltpu.with_memory_space_constraint(x, pltpu.HBM)
        else:
            specs.append(pl.BlockSpec(memory_space=pltpu.VMEM))
            x = pltpu.with_memory_space_constraint(x, pltpu.VMEM)
        placed.append(x)
    return pl.pallas_call(
        kernel,
        out_shape=outs,
        in_specs=specs,
        out_specs=[
            pl.BlockSpec(memory_space=pltpu.VMEM if out_near else pltpu.HBM)
        ] * len(outs),
        scratch_shapes=list(scratch) + [pltpu.SemaphoreType.DMA((copies,))],
        compiler_params=pltpu.CompilerParams(vmem_limit_bytes=VMEM_LIMIT),
        cost_estimate=pl.CostEstimate(
            flops=int(flops),
            transcendentals=0,
            bytes_accessed=sum(inputs[i].size * inputs[i].dtype.itemsize for i in far),
        ),
        name=name,
    )(*placed)


def exchange(keyval, span, beside, early):
    levels = span.bit_length() - 1
    early = early and levels > 2
    crossed, fresh = [], keyval
    for level in reversed(range(levels)):
        partner = swapped(keyval if level != 1 or not early else fresh, "seq", level)
        if early and level > 1:
            crossed.append(swapped(fresh, "seq", 1))
        keyval = beside(levels - 1 - level, keyval)
        fresh = partner
        if level:
            blocks = [keyval, partner]
            if level == 1:
                blocks = [keyval, *crossed, partner]
            keyval = jnp.concatenate(blocks, axis=0)
    return keyval, partner


def whole_body(
    tokens,
    attn_gain,
    query_first,
    key_first,
    segment_value,
    output_first,
    mlp_gain,
    up_weight,
    down_weight,
    second_gain,
    query_second,
    key_second,
    value_second,
    output_second,
    segment_offset,
    global_offset,
):
    seq_count = lax.axis_size("seq")
    seg_span = min(SEG_MAX, seq_count)
    heads = segment_offset.shape[0]
    count, width = tokens.shape
    head_size = width // heads
    hidden = up_weight.shape[1]
    stride = count // (KEYS // seg_span)
    stride_two = count // (KEYS // seq_count)
    groups, groups_two = count // stride, count // stride_two
    chunk = max(ROWS, stride_two)
    picked_count = groups_two * heads
    rest_count = count - picked_count
    part = hidden // 4

    def near(*shape):
        return pltpu.VMEM(shape, BF16)

    def attention_work(rows):
        return [pltpu.VMEM((2, rows, KEYS), F32), near(2, rows, KEYS)]

    def feed_work(rows):
        return [near(rows, width), pltpu.VMEM((2, rows, part), F32)]

    held_shapes = [near(width, KEYS), pltpu.VMEM((1, 128), F32)]
    small_work = [pltpu.SMEM((heads,), jnp.int32), pltpu.VMEM((width,), F32)]

    (keyval,) = local_call(
        functools.partial(first_keys_kernel, stride=stride),
        [near(1, 2, groups, width)],
        (segment_offset, tokens, attn_gain, key_first, segment_value),
        [near(count, width), near(2, width, width)] + small_work,
        far=(0, 1, 2, 3, 4),
        copies=5,
        flops=2 * heads * groups * width * (count + 2 * width),
        name="first_keys",
    )
    made = {}

    def beside_first(level, held):
        if level == 0:
            made["rows"], made["normed"], held = local_call(
                functools.partial(order_kernel, stride=stride_two, chunk=chunk),
                [near(count, width), near(count, width)],
                (global_offset, tokens, attn_gain),
                [near(count, width)] + small_work,
                far=(0, 1, 2),
                copies=3,
                relay=held,
                flops=2 * count * width * chunk,
                name="order",
            )
        tasks = {"rest": (0, picked_count, rest_count), "picked": (1, 0, picked_count)}
        for name, (step, row, size) in tasks.items():
            if level == min(step, seg_span.bit_length() - 2):
                made[name], made[name + "_peaks"], held = local_call(
                    functools.partial(first_query_kernel, first_row=row, heads=heads),
                    [near(size, width), pltpu.VMEM((1, 128), F32)],
                    (made["normed"], query_first),
                    [],
                    relay=held,
                    flops=2 * size * width * width,
                    name="first_query",
                )
        return held

    keyval, keyval_far = exchange(keyval, seg_span, beside_first, True)
    rows = made["rows"]
    query_peaks = (made["rest_peaks"], made["picked_peaks"])
    row_flops = 2 * width * (2 * hidden + width) + 4 * 256 * KEYS * heads
    picked_second, keyval_two, turned, peaks = local_call(
        functools.partial(picked_kernel, heads=heads),
        [
            near(picked_count, width),
            near(1, 2, groups_two, width),
        ]
        + held_shapes,
        (
            global_offset,
            rows,
            made["picked"],
            *query_peaks,
            keyval,
            keyval_far,
            output_first,
            mlp_gain,
            up_weight,
            down_weight,
            second_gain,
            key_second,
            value_second,
        ),
        [near(2, width, width), near(picked_count, width)]
        + attention_work(picked_count)
        + [near(picked_count, width)]
        + feed_work(picked_count)
        + [near(2, picked_count, part), pltpu.VMEM((picked_count, width), F32)],
        scalars=1,
        far=(12, 13),
        copies=2,
        flops=row_flops * picked_count,
        name="layer_of_picked",
    )
    seconds = [picked_second]

    def rest_attention(held):
        made["mixed"], held = local_call(
            functools.partial(rest_attention_kernel, heads=heads),
            [near(rest_count, width)],
            (made["rest"], *query_peaks, keyval, keyval_far, turned, peaks),
            attention_work(rest_count),
            relay=held,
            flops=4 * 256 * KEYS * heads * rest_count,
            name="rest_attention",
        )
        return held

    half = hidden // 2

    def rest_up(held):
        made["first"], made["normed"], made["inner"], held = local_call(
            rest_up_kernel,
            [near(rest_count, width), near(rest_count, width), near(rest_count, half)],
            (rows, made["mixed"], output_first, mlp_gain, up_weight),
            [pltpu.VMEM((2, rest_count, part), F32)],
            relay=held,
            flops=2 * width * (half + width) * rest_count,
            name="rest_up",
        )
        return held

    def rest_down(held):
        result, held = local_call(
            rest_down_kernel,
            [near(rest_count, width)],
            (made["first"], made["normed"], made["inner"], up_weight, down_weight),
            [pltpu.VMEM((2, rest_count, part), F32), near(rest_count, hidden - half)],
            relay=held,
            flops=2 * width * (2 * hidden - half) * rest_count,
            name="rest_down",
        )
        seconds.append(result)
        return held

    def second_query(held):
        made["query_two"], made["peaks_two"], held = local_call(
            functools.partial(second_query_kernel, heads=heads),
            [near(count, width), pltpu.VMEM((1, 128), F32)],
            (*seconds, second_gain, query_second),
            [near(1, width, width), near(count, width)],
            far=(len(seconds) + 1,),
            relay=held,
            flops=2 * count * width * width,
            name="second_query",
        )
        return held

    tasks = [rest_attention, rest_up, rest_down, second_query]
    levels = seq_count.bit_length() - 1

    def beside_second(level, held):
        ahead = len(tasks) * level // levels
        for task in tasks[ahead : len(tasks) * (level + 1) // levels]:
            held = task(held)
        return held

    keyval_two, keyval_two_far = exchange(keyval_two, seq_count, beside_second, False)
    (encoded,) = local_call(
        functools.partial(
            second_kernel, heads=heads, stride=stride_two, chunk=chunk, parts=len(seconds)
        ),
        [jax.ShapeDtypeStruct((count, width), BF16)],
        (
            global_offset,
            *seconds,
            made["query_two"],
            made["peaks_two"],
            keyval_two,
            keyval_two_far,
            output_second,
        ),
        held_shapes
        + [near(1, width, width)]
        + [near(count, width)] * 3
        + attention_work(count),
        scalars=1,
        far=(len(seconds) + 5,),
        out_near=False,
        copies=1 + count // chunk,
        flops=count * (2 * width * width + 4 * 256 * KEYS * heads),
        name="second_attention",
    )
    return encoded


def solution(mesh):
    placed = (
        P(("slides", "seq", "mp"), None),
        P(),
        P(None, "mp"),
        P(None, "mp"),
        P(None, "mp"),
        P("mp", None),
        P(),
        P(None, "mp"),
        P("mp", None),
        P(),
        P(None, "mp"),
        P(None, "mp"),
        P(None, "mp"),
        P("mp", None),
        P("mp"),
        P("mp"),
    )
    fits = mesh.shape["mp"] == 1 and 2 <= mesh.shape["seq"] <= SEG_MAX
    return jax.shard_map(
        whole_body if fits else split_body,
        mesh=mesh,
        in_specs=placed,
        out_specs=P(("slides", "seq", "mp"), None),
        check_vma=False,
    )
```

```python
import functools
import math

import jax
import jax.numpy as jnp
from jax import lax
from jax.experimental import pallas as pl
from jax.experimental.pallas import tpu as pltpu
from jax.sharding import PartitionSpec as P

KEYS = 256
SEG_MAX = 16
ROWS = 256
LOG2E = 1.4426950408889634
BF16 = jnp.bfloat16
F32 = jnp.float32
VMEM_LIMIT = 22 * 1024 * 1024


def swapped(x, axis, apart):
    return lax.ppermute(x, axis, [(i, i ^ 1 << apart) for i in range(lax.axis_size(axis))])


def norm_rows(values, gain):
    center = values - jnp.mean(values, axis=-1, keepdims=True)
    spread = jnp.mean(center * center, axis=-1, keepdims=True)
    return (center * lax.rsqrt(spread + 1e-05) * gain).astype(jnp.bfloat16)


def pick_keys(hidden, offsets, stride, key_weight, value_weight):
    token_count, width = hidden.shape
    head_count = offsets.shape[0]
    head_size = key_weight.shape[1] // head_count
    grouped_rows = hidden.reshape(token_count // stride, stride, width)
    dilation_selector = (
        lax.broadcasted_iota(jnp.int32, (stride, head_count), 0) == offsets[None, :]
    ).astype(jnp.bfloat16)
    chosen = jnp.einsum(
        "nof,oj->njf", grouped_rows, dilation_selector, preferred_element_type=jnp.float32
    ).astype(jnp.bfloat16)
    key_heads = jnp.einsum(
        "xkr,rkf->xkf",
        chosen,
        key_weight.reshape(width, head_count, head_size),
        preferred_element_type=jnp.float32,
    ).astype(jnp.bfloat16)
    value_heads = jnp.einsum(
        "xkr,rkf->xkf",
        chosen,
        value_weight.reshape(width, head_count, head_size),
        preferred_element_type=jnp.float32,
    ).astype(jnp.bfloat16)
    picked = token_count // stride
    return jnp.stack(
        [
            key_heads.reshape(picked, head_count * head_size),
            value_heads.reshape(picked, head_count * head_size),
        ]
    )


def attend_local(query, keyval, head_count):
    token_count, width = query.shape
    head_size = width // head_count
    query_heads = query.reshape(token_count, head_count, head_size)
    key_heads = keyval[0].reshape(-1, head_count, head_size)
    value_heads = keyval[1].reshape(-1, head_count, head_size)
    scores = jnp.einsum(
        "thd,khd->htk", query_heads, key_heads, preferred_element_type=jnp.float32
    ) * head_size ** (-0.5)
    highest = jnp.max(scores, axis=-1, keepdims=True)
    weights = jnp.exp(scores - highest)
    weights = (weights / jnp.sum(weights, axis=-1, keepdims=True)).astype(jnp.bfloat16)
    mixed = jnp.einsum(
        "htk,khd->thd", weights, value_heads, preferred_element_type=jnp.float32
    ).astype(jnp.bfloat16)
    return mixed.reshape(token_count, width)


def merge_branch_pair(mine, other, level, token_position):
    lower = token_position >> level & 1 == 0
    return jnp.where(
        lower, jnp.concatenate((mine, other), axis=1), jnp.concatenate((other, mine), axis=1)
    )


def spread_segment(keyval, seg_span, token_position):
    for level in range(seg_span.bit_length() - 1):
        partner = swapped(keyval, "seq", level)
        keyval = merge_branch_pair(keyval, partner, level, token_position)
    return keyval


def spread_global(keyval_two):
    keyval_two = lax.all_gather(keyval_two, "seq", axis=1, tiled=True)
    return keyval_two


def combine(partial_value, residual_full, need_full):
    row_count = residual_full.shape[0] // lax.axis_size("mp")
    row_start = lax.axis_index("mp") * row_count
    share = lax.psum_scatter(partial_value, "mp", scatter_dimension=0, tiled=True)
    own_rows = lax.dynamic_slice_in_dim(residual_full, row_start, row_count, 0)
    own_rows = (own_rows.astype(jnp.float32) + share).astype(jnp.bfloat16)
    full_rows = lax.all_gather(own_rows, "mp", axis=0, tiled=True) if need_full else own_rows
    return (own_rows, full_rows)


def split_body(
    tokens,
    attn_gain,
    query_first,
    key_first,
    segment_value,
    output_first,
    mlp_gain,
    up_weight,
    down_weight,
    second_gain,
    query_second,
    key_second,
    value_second,
    output_second,
    segment_offset,
    global_offset,
):
    seq_count = lax.axis_size("seq")
    token_position = lax.axis_index("seq")
    seg_span = min(SEG_MAX, seq_count)
    head_count = segment_offset.shape[0]
    full_rows = lax.all_gather(tokens, "mp", axis=0, tiled=True)
    token_count = full_rows.shape[0]
    hidden = norm_rows(full_rows.astype(jnp.float32), attn_gain)
    query = jnp.dot(hidden, query_first, preferred_element_type=jnp.float32).astype(jnp.bfloat16)
    seg_stride = token_count // (KEYS // seg_span)
    keyval = pick_keys(hidden, segment_offset, seg_stride, key_first, segment_value)
    keyval = spread_segment(keyval, seg_span, token_position)
    mixed = attend_local(query, keyval, head_count)
    partial_value = jnp.dot(mixed, output_first, preferred_element_type=jnp.float32)
    own_rows, first_rows = combine(partial_value, full_rows, True)
    normed = norm_rows(first_rows.astype(jnp.float32), mlp_gain)
    inner = jax.nn.gelu(
        jnp.dot(normed, up_weight, preferred_element_type=jnp.float32), approximate=True
    ).astype(jnp.bfloat16)
    partial_value = jnp.dot(inner, down_weight, preferred_element_type=jnp.float32)
    own_rows, second_rows = combine(partial_value, first_rows, True)
    hidden_two = norm_rows(second_rows.astype(jnp.float32), second_gain)
    query_two = jnp.dot(hidden_two, query_second, preferred_element_type=jnp.float32).astype(
        jnp.bfloat16
    )
    glob_stride = token_count // (KEYS // seq_count)
    keyval_two = pick_keys(hidden_two, global_offset, glob_stride, key_second, value_second)
    keyval_two = spread_global(keyval_two)
    mixed_two = attend_local(query_two, keyval_two, head_count)
    partial_value = jnp.dot(mixed_two, output_second, preferred_element_type=jnp.float32)
    own_rows, unused_rows = combine(partial_value, second_rows, False)
    return own_rows


def one_hot(condition):
    return jnp.where(condition, 1.0, 0.0).astype(BF16)


def dot(left, right):
    return jnp.dot(left, right, preferred_element_type=F32)


def pieces(count, size):
    size = size if count % size == 0 else count
    return [slice(start, start + size) for start in range(0, count, size)]


def norm_into(out, start, source, gain, count):
    for span in pieces(count, 64):
        out[start + span.start : start + span.stop, :] = norm_rows(
            source[span, :].astype(F32), gain
        )


def bring(source, target, sem):
    copy = pltpu.make_async_copy(source, target, sem)
    copy.start()
    return copy


def pick_matrix(offsets, heads, groups, stride):
    count = groups * stride
    place = lax.broadcasted_iota(jnp.int32, (groups, count), 1)
    place = place - lax.broadcasted_iota(jnp.int32, (groups, count), 0) * stride
    return jnp.concatenate([one_hot(place == offsets[h]) for h in range(heads)], axis=0)


def project_keys(chosen, heads, weights, keyval_ref):
    rows, width = chosen.shape
    groups, head_size = rows // heads, width // heads
    for slot, weight in enumerate(weights):
        held = weight()
        for span in pieces(width, 256):
            first, last = span.start // head_size, (span.stop - 1) // head_size + 1
            wide = dot(chosen[first * groups : last * groups], held[:, span])
            column = lax.broadcasted_iota(jnp.int32, (groups, span.stop - span.start), 1)
            total = wide[:groups]
            for h in range(first + 1, last):
                row = (h - first) * groups
                own = column >= h * head_size - span.start
                total = jnp.where(own, wide[row : row + groups], total)
            total = total.astype(BF16)
            for copy in range(keyval_ref.shape[0]):
                keyval_ref[copy, slot, :, span] = total


def ranks(offsets, chunk, stride, share, axis):
    heads = offsets.shape[0]

    def places(way):
        shape = (1, chunk) if way else (chunk, 1)
        place = lax.broadcasted_iota(jnp.int32, shape, way)
        inside = lax.rem(place, stride)
        taken = inside == offsets[0]
        for h in range(1, heads):
            taken = taken | (inside == offsets[h])
        return place, inside, jnp.where(taken, inside, inside + stride)

    place, inside, order = places(axis)
    other_place, _, other_order = places(1 - axis)
    ahead = (other_order < order) & (lax.div(other_place, stride) == lax.div(place, stride))
    rank = jnp.sum(jnp.where(ahead, 1, 0), axis=1 - axis, keepdims=True)
    group = lax.div(place, stride)
    return jnp.where(
        rank < heads, group * heads + rank, share + group * (stride - heads) + rank - heads
    )


def slots_of(offsets, heads):
    values = [offsets[h] for h in range(heads)]
    fresh = []
    for h in range(heads):
        seen = jnp.int32(1)
        for earlier in values[:h]:
            seen = jnp.where(earlier == values[h], 0, seen)
        fresh.append(seen)
    slots = []
    for h in range(heads):
        slot = jnp.int32(0)
        for other in range(heads):
            slot = slot + jnp.where(values[other] < values[h], fresh[other], 0)
        slots.append(slot)
    return slots


def first_keys_kernel(
    offsets, tokens, gain, key_weight, value_weight, keyval, rows, wide, picks, scale, sems, *, stride
):
    copies = [
        bring(offsets, picks, sems.at[0]),
        bring(tokens, rows, sems.at[1]),
        bring(gain, scale, sems.at[2]),
        bring(key_weight, wide.at[0], sems.at[3]),
        bring(value_weight, wide.at[1], sems.at[4]),
    ]
    heads = offsets.shape[0]
    copies[0].wait()
    chooser = pick_matrix(picks, heads, rows.shape[0] // stride, stride)
    copies[1].wait()
    copies[2].wait()
    chosen = norm_rows(dot(chooser, rows[...]), scale[...])

    def weight(slot):
        copies[slot + 3].wait()
        return wide[slot]

    project_keys(
        chosen, heads, [functools.partial(weight, slot) for slot in range(2)], keyval
    )


def order_kernel(
    offsets, tokens, gain, moved_rows, normed, rows, picks, scale, sems, *, stride, chunk
):
    copies = [
        bring(offsets, picks, sems.at[0]),
        bring(tokens, rows, sems.at[1]),
        bring(gain, scale, sems.at[2]),
    ]
    count = tokens.shape[0]
    share = chunk // stride * offsets.shape[0]
    rest = chunk - share
    picked = count // chunk * share
    copies[0].wait()
    mover = one_hot(
        lax.broadcasted_iota(jnp.int32, (chunk, chunk), 0)
        == ranks(picks, chunk, stride, share, 1)
    )
    copies[1].wait()
    copies[2].wait()
    for c in range(count // chunk):
        moved = dot(mover, rows[c * chunk : (c + 1) * chunk, :]).astype(BF16)
        moved_rows[c * share : (c + 1) * share, :] = moved[:share]
        moved_rows[picked + c * rest : picked + (c + 1) * rest, :] = moved[share:]
    norm_into(normed, 0, moved_rows, scale[...], count)


def scaled_query(normed, weight, outs, heads, peaks):
    width = normed.shape[1]
    factor = (width // heads) ** (-0.5) * LOG2E
    peak = None
    for out, row in outs:
        for span in pieces(out.shape[0], 512 if out.shape[0] % 512 == 0 else 256):
            query = dot(normed[row + span.start : row + span.stop, :], weight[...]) * factor
            out[span, :] = query.astype(BF16)
            for part in pieces(query.shape[0], 64):
                square = query[part] * query[part]
                peak = square if peak is None else jnp.maximum(peak, square)
    peaks[...] = summed_peaks(peak.astype(BF16), heads)


def first_query_kernel(normed, weight, picked, rest, peaks, sems, *, heads):
    del sems
    scaled_query(normed, weight, [(picked, 0), (rest, picked.shape[0])], heads, peaks)


def head_windows(head_size, width):
    period = min(width, math.lcm(head_size, 128))
    windows = []
    for h in range(period // head_size):
        start = h * head_size // 128 * 128
        stop = min(period, -(-(h + 1) * head_size // 128) * 128)
        windows.append((start, stop - start))
    return period, windows


def summed_peaks(peak, heads):
    width = peak.shape[1]
    column = lax.broadcasted_iota(jnp.int32, (width, 128), 0)
    head = lax.broadcasted_iota(jnp.int32, (width, 128), 1)
    low = head * (width // heads)
    sums = one_hot((column >= low) & (column < low + width // heads))
    return jnp.max(dot(peak, sums), axis=0, keepdims=True)


def load_keys(keyval, heads, turned, peaks):
    keys = jnp.concatenate([keyval[i, 0] for i in range(keyval.shape[0])], axis=0)
    turned[...] = keys.T
    peaks[...] = summed_peaks(keys * keys, heads)


def small_scores(query_peaks, key_peaks):
    keys = jnp.maximum(key_peaks[0][...], key_peaks[1][...])
    return jnp.max(query_peaks[...] * keys) < 9000.0


def reciprocal(x):
    guess = pl.reciprocal(x, approx=True)
    return guess * (2.0 - x * guess)


def padded_keys(turned, base, head, head_size, start, size):
    rows = pl.ds(pl.multiple_of(base + head * head_size, 16), head_size)
    own = jnp.concatenate([part[rows, :] for part in turned], axis=1)
    low = head * head_size - start
    parts = [own]
    if low:
        parts.insert(0, jnp.zeros((low, own.shape[1]), BF16))
    if low + head_size < size:
        parts.append(jnp.zeros((size - low - head_size, own.shape[1]), BF16))
    return jnp.concatenate(parts, axis=0)


def score_pair(query, span, base, head, head_size, windows, turned):
    start = windows[head][0]
    size = windows[head + 1][0] + windows[head + 1][1] - start
    keys = [padded_keys([turned], base, head + i, head_size, start, size) for i in range(2)]
    return dot(query[span, pl.ds(base + start, size)], jnp.concatenate(keys, axis=1))


def near_weights_kernel(
    picked, rest, keyval, picked_early, rest_early, turned, peaks, scores_ref, sems, *, heads
):
    del sems
    load_keys(keyval, heads, turned, peaks)
    width = picked.shape[1]
    head_size = width // heads
    key_count = turned.shape[1]
    period, windows = head_windows(head_size, width)
    jobs = [
        (query, early, head)
        for query, early in ((picked, picked_early), (rest, rest_early))
        for head in range(0, len(windows), 2)
    ]

    @pl.loop(0, width // period)
    def _(turn):
        base = pl.multiple_of(turn * period, 128)

        def score(i):
            query, _, head = jobs[i]
            rows = query.shape[0]
            scores_ref[i % 2, :rows] = score_pair(
                query, slice(0, rows), base, head, head_size, windows, turned
            )

        score(0)
        for i, (query, early, head) in enumerate(jobs):
            if i + 1 < len(jobs):
                score(i + 1)
            for part in pieces(query.shape[0], 64):
                weights = jnp.exp2(scores_ref[i % 2, part, :]).astype(BF16)
                for j in range(2):
                    early[turn * len(windows) + head + j, part, :] = weights[
                        :, j * key_count : (j + 1) * key_count
                    ]


def attend_rows(
    query, first_row, rows, heads, turned, keyvals, mixed_ref, mixed_row, work, plain, early=None
):
    scores_ref, weights_ref = work
    width = query.shape[1]
    key_count = sum(part.shape[1] for part in turned)
    head_size = width // heads
    period, windows = head_windows(head_size, width)
    span = pl.ds(first_row, rows)
    out_span = pl.ds(mixed_row, rows)
    lane = lax.broadcasted_iota(jnp.int32, (1, 128), 1)
    step = 2 if early is not None else 1

    @pl.loop(0, width // period)
    def _(turn):
        base = pl.multiple_of(turn * period, 128)
        sums = {}

        def score(i):
            if early is not None:
                scores = score_pair(query, span, base, 2 * i, head_size, windows, turned[1])
            else:
                start, size = windows[i]
                scores = dot(
                    query[span, pl.ds(base + start, size)],
                    padded_keys(turned, base, i, head_size, start, size),
                )
            scores_ref[i % 2, :rows] = scores

        def weigh(h):
            for part in pieces(rows, 64):
                scores = scores_ref[h % 2, part, :]
                if not plain:
                    scores = scores - jnp.max(scores, axis=1, keepdims=True)
                weights_ref[h % 2, part, :] = jnp.exp2(scores).astype(BF16)

        def mix(h):
            start, size = windows[h]
            low = h * head_size - start
            values = jnp.concatenate(
                [
                    x[i, 1, :, pl.ds(base + start, size)]
                    for x in keyvals
                    for i in range(x.shape[0])
                ],
                axis=0,
            )
            column = lax.broadcasted_iota(jnp.int32, (key_count, size), 1)
            own = (column >= low) & (column < low + head_size)
            values = jnp.where(own, values, jnp.ones((), BF16))
            if early is not None:
                half = key_count // 2
                far = weights_ref[h // 2 % 2, :rows, h % 2 * half : (h % 2 + 1) * half]
                near = early[turn * len(windows) + h, span, :]
                weights = jnp.concatenate([near, far], axis=1)
            else:
                weights = weights_ref[h % 2, :rows]
            mixed = dot(weights, values)
            for offset in range(0, size, 128):
                own = mixed[:, offset : offset + 128]
                own = own * reciprocal(pltpu.roll(own, 64, 1))
                at = start + offset
                if at in sums:
                    own = jnp.where(lane >= h * head_size - at, own, sums[at])
                sums[at] = own
                if (h + 1) * head_size >= at + 128:
                    mixed_ref[out_span, pl.ds(base + at, 128)] = sums.pop(at).astype(BF16)

        count = len(windows) // step
        score(0)
        for i in range(count):
            if i:
                for h in range((i - 1) * step, i * step):
                    mix(h)
            if i + 1 < count:
                score(i + 1)
            weigh(i)
        for h in range((count - 1) * step, count * step):
            mix(h)


def attend(query, rows, heads, turned, keyvals, mixed_ref, work, small, early=None):
    size = math.gcd(rows, ROWS)

    @pl.when(small)
    def _():
        attend_rows(query, 0, rows, heads, turned, keyvals, mixed_ref, 0, work, True, early)

    @pl.when(jnp.logical_not(small))
    def _():
        @pl.loop(0, rows // size)
        def _(step):
            row = pl.multiple_of(step * size, size)
            attend_rows(
                query,
                row,
                size,
                heads,
                turned,
                keyvals,
                mixed_ref,
                row,
                work,
                False,
            )


def gelu(x):
    half = 0.5 * x
    return half + half * jnp.tanh(x * (0.7978845608028654 + 0.035677408136300125 * (x * x)))


def widen(normed, up_weight, low, wide_ref, inner):
    rows = normed.shape[0]
    spans = pieces(inner.shape[1], wide_ref.shape[2])

    def product(i):
        columns = slice(low + spans[i].start, low + spans[i].stop)
        wide_ref[i % 2] = dot(normed[...], up_weight[:, columns])

    product(0)
    for i, span in enumerate(spans):
        if i + 1 < len(spans):
            product(i + 1)
        for part in pieces(rows, 32):
            inner[part, span] = gelu(wide_ref[i % 2, part, :]).astype(BF16)


def feed_forward(normed, up_weight, down_weight, total, wide_ref, inner):
    rows = normed.shape[0]
    spans = pieces(up_weight.shape[1], wide_ref.shape[2])

    def product(i):
        wide_ref[i % 2] = dot(normed[...], up_weight[:, spans[i]])

    product(0)
    for i, span in enumerate(spans):
        if i + 1 < len(spans):
            product(i + 1)
        for part in pieces(rows, 32):
            inner[i % 2, part, :] = gelu(wide_ref[i % 2, part, :]).astype(BF16)
        total[...] += dot(inner[i % 2], down_weight[span, :])


def narrow(inners, down_weight, first, second, size):
    for span in pieces(second.shape[1], size):
        total = first[:, span].astype(F32)
        low = 0
        for inner in inners:
            high = low + inner.shape[1]
            total = total + dot(inner[...], down_weight[low:high, span])
            low = high
        second[:, span] = total.astype(BF16)


def add_heads(tokens, first_row, mixed, out_weight, gain, first, normed):
    before = None
    for span in pieces(mixed.shape[0], 256):
        total = dot(mixed[span, :], out_weight[...])
        rows = tokens[first_row + span.start : first_row + span.stop, :]
        first[span, :] = (rows.astype(F32) + total).astype(BF16)
        if before is not None:
            norm_into(normed, before.start, first.at[before], gain, before.stop - before.start)
        before = span
    norm_into(normed, before.start, first.at[before], gain, before.stop - before.start)


def picked_kernel(
    offsets,
    tokens,
    query,
    query_peaks,
    early,
    keyval,
    keyval_far,
    turned_near,
    peaks_near,
    out_weight,
    mlp_gain,
    up_weight,
    down_weight,
    gain,
    key_weight,
    value_weight,
    second,
    keyval_two,
    turned,
    peaks,
    held,
    mixed,
    scores,
    weights,
    first,
    normed,
    wide,
    inner,
    total,
    sems,
    *,
    heads,
):
    copies = [
        bring(x, held.at[i], sems.at[i]) for i, x in enumerate((key_weight, value_weight))
    ]
    rows = second.shape[0]
    keyvals = (keyval, keyval_far)
    load_keys(keyval_far, heads, turned, peaks)
    small = small_scores(query_peaks, (peaks_near, peaks))
    attend(
        query,
        rows,
        heads,
        (turned_near, turned),
        keyvals,
        mixed,
        (scores, weights),
        small,
        early,
    )
    add_heads(tokens, 0, mixed, out_weight, mlp_gain[...], first, normed)
    total[...] = first[...].astype(F32)
    feed_forward(normed, up_weight, down_weight, total, wide, inner)
    second[...] = total[...].astype(BF16)
    norm_into(normed, 0, second, gain[...], rows)
    chooser = pick_matrix(slots_of(offsets, heads), heads, rows // heads, heads)
    chosen = dot(chooser, normed[...]).astype(BF16)

    def weight(slot):
        copies[slot].wait()
        return held[slot]

    project_keys(
        chosen, heads, [functools.partial(weight, slot) for slot in range(2)], keyval_two
    )


def rest_attention_kernel(
    query,
    query_peaks,
    early,
    keyval,
    keyval_far,
    turned_near,
    peaks_near,
    turned,
    peaks,
    mixed,
    scores,
    weights,
    sems,
    *,
    heads,
):
    del sems
    attend(
        query,
        mixed.shape[0],
        heads,
        (turned_near, turned),
        (keyval, keyval_far),
        mixed,
        (scores, weights),
        small_scores(query_peaks, (peaks_near, peaks)),
        early,
    )


def rest_up_kernel(
    tokens, mixed, out_weight, gain, up_weight, first, normed, inner, wide, sems
):
    del sems
    add_heads(
        tokens, tokens.shape[0] - mixed.shape[0], mixed, out_weight, gain[...], first, normed
    )
    widen(normed, up_weight, 0, wide, inner)


def rest_down_kernel(
    first, normed, inner, up_weight, down_weight, second, wide, inner_more, sems
):
    del sems
    widen(normed, up_weight, inner.shape[1], wide, inner_more)
    narrow([inner, inner_more], down_weight, first, second, 256)


def second_query_kernel(*refs, heads):
    *rows, gain, weight, query, peaks, held, normed, sems = refs
    copy = bring(weight, held.at[0], sems.at[0])
    start = 0
    for part in rows:
        norm_into(normed, start, part, gain[...], part.shape[0])
        start += part.shape[0]
    copy.wait()
    scaled_query(normed, held.at[0], [(query, 0)], heads, peaks)


def second_kernel(*refs, heads, stride, chunk, parts):
    offsets, *rows = refs[: 1 + parts]
    query, query_peaks, keyval, keyval_far, out_weight, encoded = refs[1 + parts : 7 + parts]
    turned_near, peaks_near, turned, peaks, held, mixed = refs[7 + parts : 13 + parts]
    result, ready, scores, weights, sems = refs[13 + parts :]
    copy = bring(out_weight, held.at[0], sems.at[0])
    keyvals = (keyval, keyval_far)
    load_keys(keyval, heads, turned_near, peaks_near)
    load_keys(keyval_far, heads, turned, peaks)
    count = query.shape[0]
    small = small_scores(query_peaks, (peaks_near, peaks))
    attend(
        query, count, heads, (turned_near, turned), keyvals, mixed, (scores, weights), small
    )
    share = chunk // stride * heads
    rest_share = chunk - share
    back = one_hot(
        lax.broadcasted_iota(jnp.int32, (chunk, chunk), 1)
        == ranks(offsets, chunk, stride, share, 0)
    )
    copy.wait()
    start = 0
    for part in rows:
        span = slice(start, start + part.shape[0])
        total = part[...].astype(F32) + dot(mixed[span, :], held[0])
        result[span, :] = total.astype(BF16)
        start += part.shape[0]
    start = count // chunk * share
    copies = []
    for c in range(count // chunk):
        far = start + c * rest_share
        blend = jnp.concatenate(
            [result[c * share : (c + 1) * share, :], result[far : far + rest_share, :]], axis=0
        )
        span = pl.ds(c * chunk, chunk)
        ready[span, :] = dot(back, blend).astype(BF16)
        copies.append(bring(ready.at[span], encoded.at[span], sems.at[1 + c]))
    for copy in copies:
        copy.wait()


def relaying(kernel, ins, outs, *refs):
    end = ins + 1 + outs
    refs[end][...] = refs[ins][...]
    kernel(*refs[:ins], *refs[ins + 1 : end], *refs[end + 1 :])


def local_call(kernel, outs, inputs, scratch, scalars=0, far=(), relay=None, out_near=True, copies=1, flops=0, name=None):
    outs, inputs = list(outs), list(inputs)
    if relay is not None:
        kernel = functools.partial(relaying, kernel, len(inputs), len(outs))
        inputs.append(relay)
        outs.append(pltpu.VMEM(relay.shape, relay.dtype))
    specs, placed = [], []
    for i, x in enumerate(inputs):
        if i < scalars:
            specs.append(pl.BlockSpec(memory_space=pltpu.SMEM))
        elif i in far:
            specs.append(pl.BlockSpec(memory_space=pltpu.HBM))
            x = pltpu.with_memory_space_constraint(x, pltpu.HBM)
        else:
            specs.append(pl.BlockSpec(memory_space=pltpu.VMEM))
            x = pltpu.with_memory_space_constraint(x, pltpu.VMEM)
        placed.append(x)
    return pl.pallas_call(
        kernel,
        out_shape=outs,
        in_specs=specs,
        out_specs=[
            pl.BlockSpec(memory_space=pltpu.VMEM if out_near else pltpu.HBM)
        ] * len(outs),
        scratch_shapes=list(scratch) + [pltpu.SemaphoreType.DMA((copies,))],
        compiler_params=pltpu.CompilerParams(vmem_limit_bytes=VMEM_LIMIT),
        cost_estimate=pl.CostEstimate(
            flops=int(flops),
            transcendentals=0,
            bytes_accessed=sum(inputs[i].size * inputs[i].dtype.itemsize for i in far),
        ),
        name=name,
    )(*placed)


def exchange(keyval, span, beside, early):
    levels = span.bit_length() - 1
    early = early and levels > 2
    crossed, fresh = [], keyval
    for level in reversed(range(levels)):
        partner = swapped(keyval if level != 1 or not early else fresh, "seq", level)
        if early and level > 1:
            crossed.append(swapped(fresh, "seq", 1))
        keyval = beside(levels - 1 - level, keyval)
        fresh = partner
        if level:
            blocks = [keyval, partner]
            if level == 1:
                blocks = [keyval, *crossed, partner]
            keyval = jnp.concatenate(blocks, axis=0)
    return keyval, partner


def whole_body(
    tokens,
    attn_gain,
    query_first,
    key_first,
    segment_value,
    output_first,
    mlp_gain,
    up_weight,
    down_weight,
    second_gain,
    query_second,
    key_second,
    value_second,
    output_second,
    segment_offset,
    global_offset,
):
    seq_count = lax.axis_size("seq")
    seg_span = min(SEG_MAX, seq_count)
    heads = segment_offset.shape[0]
    count, width = tokens.shape
    head_size = width // heads
    hidden = up_weight.shape[1]
    stride = count // (KEYS // seg_span)
    stride_two = count // (KEYS // seq_count)
    groups, groups_two = count // stride, count // stride_two
    chunk = max(ROWS, stride_two)
    picked_count = groups_two * heads
    rest_count = count - picked_count
    part = hidden // 4

    def near(*shape):
        return pltpu.VMEM(shape, BF16)

    def attention_work(rows):
        return [pltpu.VMEM((2, rows, KEYS), F32), near(2, rows, KEYS)]

    def feed_work(rows):
        return [near(rows, width), pltpu.VMEM((2, rows, part), F32)]

    held_shapes = [near(width, KEYS // 2), pltpu.VMEM((1, 128), F32)]
    small_work = [pltpu.SMEM((heads,), jnp.int32), pltpu.VMEM((width,), F32)]

    (keyval,) = local_call(
        functools.partial(first_keys_kernel, stride=stride),
        [near(1, 2, groups, width)],
        (segment_offset, tokens, attn_gain, key_first, segment_value),
        [near(count, width), near(2, width, width)] + small_work,
        far=(0, 1, 2, 3, 4),
        copies=5,
        flops=2 * heads * groups * width * (count + 2 * width),
        name="first_keys",
    )
    made = {}

    def beside_first(level, held):
        if level == 0:
            made["rows"], made["normed"], held = local_call(
                functools.partial(order_kernel, stride=stride_two, chunk=chunk),
                [near(count, width), near(count, width)],
                (global_offset, tokens, attn_gain),
                [near(count, width)] + small_work,
                far=(0, 1, 2),
                copies=3,
                relay=held,
                flops=2 * count * width * chunk,
                name="order",
            )
        if level == min(1, seg_span.bit_length() - 2):
            made["picked"], made["rest"], made["peaks"], held = local_call(
                functools.partial(first_query_kernel, heads=heads),
                [near(picked_count, width), near(rest_count, width), pltpu.VMEM((1, 128), F32)],
                (made["normed"], query_first),
                [],
                relay=held,
                flops=2 * count * width * width,
                name="first_query",
            )
        if level == seg_span.bit_length() - 2:
            made["picked_early"], made["rest_early"], made["turned"], made["key_peaks"] = local_call(
                functools.partial(near_weights_kernel, heads=heads),
                [near(heads, picked_count, KEYS // 2), near(heads, rest_count, KEYS // 2)]
                + held_shapes,
                (made["picked"], made["rest"], held),
                [pltpu.VMEM((2, rest_count, KEYS), F32)],
                flops=2 * 256 * KEYS // 2 * heads * count,
                name="near_weights",
            )
        return held

    keyval, keyval_far = exchange(keyval, seg_span, beside_first, True)
    rows = made["rows"]
    query_peaks, near_held = made["peaks"], (made["turned"], made["key_peaks"])
    row_flops = 2 * width * (2 * hidden + width) + 4 * 256 * KEYS * heads
    picked_second, keyval_two, turned, peaks = local_call(
        functools.partial(picked_kernel, heads=heads),
        [
            near(picked_count, width),
            near(1, 2, groups_two, width),
        ]
        + held_shapes,
        (
            global_offset,
            rows,
            made["picked"],
            query_peaks,
            made["picked_early"],
            keyval,
            keyval_far,
            *near_held,
            output_first,
            mlp_gain,
            up_weight,
            down_weight,
            second_gain,
            key_second,
            value_second,
        ),
        [near(2, width, width), near(picked_count, width)]
        + attention_work(picked_count)
        + [near(picked_count, width)]
        + feed_work(picked_count)
        + [near(2, picked_count, part), pltpu.VMEM((picked_count, width), F32)],
        scalars=1,
        far=(14, 15),
        copies=2,
        flops=row_flops * picked_count,
        name="layer_of_picked",
    )
    seconds = [picked_second]

    def rest_attention(held):
        made["mixed"], held = local_call(
            functools.partial(rest_attention_kernel, heads=heads),
            [near(rest_count, width)],
            (
                made["rest"],
                query_peaks,
                made["rest_early"],
                keyval,
                keyval_far,
                *near_held,
                turned,
                peaks,
            ),
            attention_work(rest_count),
            relay=held,
            flops=4 * 256 * KEYS * heads * rest_count,
            name="rest_attention",
        )
        return held

    half = hidden // 2

    def rest_up(held):
        made["first"], made["normed"], made["inner"], held = local_call(
            rest_up_kernel,
            [near(rest_count, width), near(rest_count, width), near(rest_count, half)],
            (rows, made["mixed"], output_first, mlp_gain, up_weight),
            [pltpu.VMEM((2, rest_count, part), F32)],
            relay=held,
            flops=2 * width * (half + width) * rest_count,
            name="rest_up",
        )
        return held

    def rest_down(held):
        result, held = local_call(
            rest_down_kernel,
            [near(rest_count, width)],
            (made["first"], made["normed"], made["inner"], up_weight, down_weight),
            [pltpu.VMEM((2, rest_count, part), F32), near(rest_count, hidden - half)],
            relay=held,
            flops=2 * width * (2 * hidden - half) * rest_count,
            name="rest_down",
        )
        seconds.append(result)
        return held

    def second_query(held):
        made["query_two"], made["peaks_two"], held = local_call(
            functools.partial(second_query_kernel, heads=heads),
            [near(count, width), pltpu.VMEM((1, 128), F32)],
            (*seconds, second_gain, query_second),
            [near(1, width, width), near(count, width)],
            far=(len(seconds) + 1,),
            relay=held,
            flops=2 * count * width * width,
            name="second_query",
        )
        return held

    tasks = [rest_attention, rest_up, rest_down, second_query]
    levels = seq_count.bit_length() - 1

    def beside_second(level, held):
        ahead = len(tasks) * level // levels
        for task in tasks[ahead : len(tasks) * (level + 1) // levels]:
            held = task(held)
        return held

    keyval_two, keyval_two_far = exchange(keyval_two, seq_count, beside_second, False)
    (encoded,) = local_call(
        functools.partial(
            second_kernel, heads=heads, stride=stride_two, chunk=chunk, parts=len(seconds)
        ),
        [jax.ShapeDtypeStruct((count, width), BF16)],
        (
            global_offset,
            *seconds,
            made["query_two"],
            made["peaks_two"],
            keyval_two,
            keyval_two_far,
            output_second,
        ),
        held_shapes * 2
        + [near(1, width, width)]
        + [near(count, width)] * 3
        + attention_work(count),
        scalars=1,
        far=(len(seconds) + 5,),
        out_near=False,
        copies=1 + count // chunk,
        flops=count * (2 * width * width + 4 * 256 * KEYS * heads),
        name="second_attention",
    )
    return encoded


def solution(mesh):
    placed = (
        P(("slides", "seq", "mp"), None),
        P(),
        P(None, "mp"),
        P(None, "mp"),
        P(None, "mp"),
        P("mp", None),
        P(),
        P(None, "mp"),
        P("mp", None),
        P(),
        P(None, "mp"),
        P(None, "mp"),
        P(None, "mp"),
        P("mp", None),
        P("mp"),
        P("mp"),
    )
    fits = mesh.shape["mp"] == 1 and 2 <= mesh.shape["seq"] <= SEG_MAX
    return jax.shard_map(
        whole_body if fits else split_body,
        mesh=mesh,
        in_specs=placed,
        out_specs=P(("slides", "seq", "mp"), None),
        check_vma=False,
    )
```

```python
import functools
import math

import jax
import jax.numpy as jnp
from jax import lax
from jax.experimental import pallas as pl
from jax.experimental.pallas import tpu as pltpu
from jax.sharding import PartitionSpec as P

KEYS = 256
SEG_MAX = 16
ROWS = 256
LOG2E = 1.4426950408889634
BF16 = jnp.bfloat16
F32 = jnp.float32
VMEM_LIMIT = 22 * 1024 * 1024


def swapped(x, axis, apart):
    return lax.ppermute(x, axis, [(i, i ^ 1 << apart) for i in range(lax.axis_size(axis))])


def norm_rows(values, gain):
    center = values - jnp.mean(values, axis=-1, keepdims=True)
    spread = jnp.mean(center * center, axis=-1, keepdims=True)
    return (center * lax.rsqrt(spread + 1e-05) * gain).astype(jnp.bfloat16)


def pick_keys(hidden, offsets, stride, key_weight, value_weight):
    token_count, width = hidden.shape
    head_count = offsets.shape[0]
    head_size = key_weight.shape[1] // head_count
    grouped_rows = hidden.reshape(token_count // stride, stride, width)
    dilation_selector = (
        lax.broadcasted_iota(jnp.int32, (stride, head_count), 0) == offsets[None, :]
    ).astype(jnp.bfloat16)
    chosen = jnp.einsum(
        "nof,oj->njf", grouped_rows, dilation_selector, preferred_element_type=jnp.float32
    ).astype(jnp.bfloat16)
    key_heads = jnp.einsum(
        "xkr,rkf->xkf",
        chosen,
        key_weight.reshape(width, head_count, head_size),
        preferred_element_type=jnp.float32,
    ).astype(jnp.bfloat16)
    value_heads = jnp.einsum(
        "xkr,rkf->xkf",
        chosen,
        value_weight.reshape(width, head_count, head_size),
        preferred_element_type=jnp.float32,
    ).astype(jnp.bfloat16)
    picked = token_count // stride
    return jnp.stack(
        [
            key_heads.reshape(picked, head_count * head_size),
            value_heads.reshape(picked, head_count * head_size),
        ]
    )


def attend_local(query, keyval, head_count):
    token_count, width = query.shape
    head_size = width // head_count
    query_heads = query.reshape(token_count, head_count, head_size)
    key_heads = keyval[0].reshape(-1, head_count, head_size)
    value_heads = keyval[1].reshape(-1, head_count, head_size)
    scores = jnp.einsum(
        "thd,khd->htk", query_heads, key_heads, preferred_element_type=jnp.float32
    ) * head_size ** (-0.5)
    highest = jnp.max(scores, axis=-1, keepdims=True)
    weights = jnp.exp(scores - highest)
    weights = (weights / jnp.sum(weights, axis=-1, keepdims=True)).astype(jnp.bfloat16)
    mixed = jnp.einsum(
        "htk,khd->thd", weights, value_heads, preferred_element_type=jnp.float32
    ).astype(jnp.bfloat16)
    return mixed.reshape(token_count, width)


def merge_branch_pair(mine, other, level, token_position):
    lower = token_position >> level & 1 == 0
    return jnp.where(
        lower, jnp.concatenate((mine, other), axis=1), jnp.concatenate((other, mine), axis=1)
    )


def spread_segment(keyval, seg_span, token_position):
    for level in range(seg_span.bit_length() - 1):
        partner = swapped(keyval, "seq", level)
        keyval = merge_branch_pair(keyval, partner, level, token_position)
    return keyval


def spread_global(keyval_two):
    keyval_two = lax.all_gather(keyval_two, "seq", axis=1, tiled=True)
    return keyval_two


def combine(partial_value, residual_full, need_full):
    row_count = residual_full.shape[0] // lax.axis_size("mp")
    row_start = lax.axis_index("mp") * row_count
    share = lax.psum_scatter(partial_value, "mp", scatter_dimension=0, tiled=True)
    own_rows = lax.dynamic_slice_in_dim(residual_full, row_start, row_count, 0)
    own_rows = (own_rows.astype(jnp.float32) + share).astype(jnp.bfloat16)
    full_rows = lax.all_gather(own_rows, "mp", axis=0, tiled=True) if need_full else own_rows
    return (own_rows, full_rows)


def split_body(
    tokens,
    attn_gain,
    query_first,
    key_first,
    segment_value,
    output_first,
    mlp_gain,
    up_weight,
    down_weight,
    second_gain,
    query_second,
    key_second,
    value_second,
    output_second,
    segment_offset,
    global_offset,
):
    seq_count = lax.axis_size("seq")
    token_position = lax.axis_index("seq")
    seg_span = min(SEG_MAX, seq_count)
    head_count = segment_offset.shape[0]
    full_rows = lax.all_gather(tokens, "mp", axis=0, tiled=True)
    token_count = full_rows.shape[0]
    hidden = norm_rows(full_rows.astype(jnp.float32), attn_gain)
    query = jnp.dot(hidden, query_first, preferred_element_type=jnp.float32).astype(jnp.bfloat16)
    seg_stride = token_count // (KEYS // seg_span)
    keyval = pick_keys(hidden, segment_offset, seg_stride, key_first, segment_value)
    keyval = spread_segment(keyval, seg_span, token_position)
    mixed = attend_local(query, keyval, head_count)
    partial_value = jnp.dot(mixed, output_first, preferred_element_type=jnp.float32)
    own_rows, first_rows = combine(partial_value, full_rows, True)
    normed = norm_rows(first_rows.astype(jnp.float32), mlp_gain)
    inner = jax.nn.gelu(
        jnp.dot(normed, up_weight, preferred_element_type=jnp.float32), approximate=True
    ).astype(jnp.bfloat16)
    partial_value = jnp.dot(inner, down_weight, preferred_element_type=jnp.float32)
    own_rows, second_rows = combine(partial_value, first_rows, True)
    hidden_two = norm_rows(second_rows.astype(jnp.float32), second_gain)
    query_two = jnp.dot(hidden_two, query_second, preferred_element_type=jnp.float32).astype(
        jnp.bfloat16
    )
    glob_stride = token_count // (KEYS // seq_count)
    keyval_two = pick_keys(hidden_two, global_offset, glob_stride, key_second, value_second)
    keyval_two = spread_global(keyval_two)
    mixed_two = attend_local(query_two, keyval_two, head_count)
    partial_value = jnp.dot(mixed_two, output_second, preferred_element_type=jnp.float32)
    own_rows, unused_rows = combine(partial_value, second_rows, False)
    return own_rows


def one_hot(condition):
    return jnp.where(condition, 1.0, 0.0).astype(BF16)


def dot(left, right):
    return jnp.dot(left, right, preferred_element_type=F32)


def pieces(count, size):
    size = size if count % size == 0 else count
    return [slice(start, start + size) for start in range(0, count, size)]


def norm_into(out, start, source, gain, count):
    for span in pieces(count, 64):
        out[start + span.start : start + span.stop, :] = norm_rows(
            source[span, :].astype(F32), gain
        )


def bring(source, target, sem):
    copy = pltpu.make_async_copy(source, target, sem)
    copy.start()
    return copy


def pick_matrix(offsets, heads, groups, stride):
    count = groups * stride
    place = lax.broadcasted_iota(jnp.int32, (groups, count), 1)
    place = place - lax.broadcasted_iota(jnp.int32, (groups, count), 0) * stride
    return jnp.concatenate([one_hot(place == offsets[h]) for h in range(heads)], axis=0)


def project_keys(chosen, heads, weights, keyval_ref):
    rows, width = chosen.shape
    groups, head_size = rows // heads, width // heads
    for slot, weight in enumerate(weights):
        held = weight()
        for span in pieces(width, 256):
            first, last = span.start // head_size, (span.stop - 1) // head_size + 1
            wide = dot(chosen[first * groups : last * groups], held[:, span])
            column = lax.broadcasted_iota(jnp.int32, (groups, span.stop - span.start), 1)
            total = wide[:groups]
            for h in range(first + 1, last):
                row = (h - first) * groups
                own = column >= h * head_size - span.start
                total = jnp.where(own, wide[row : row + groups], total)
            total = total.astype(BF16)
            for copy in range(keyval_ref.shape[0]):
                keyval_ref[copy, slot, :, span] = total


def ranks(offsets, chunk, stride, share, axis):
    heads = offsets.shape[0]

    def places(way):
        shape = (1, chunk) if way else (chunk, 1)
        place = lax.broadcasted_iota(jnp.int32, shape, way)
        inside = lax.rem(place, stride)
        taken = inside == offsets[0]
        for h in range(1, heads):
            taken = taken | (inside == offsets[h])
        return place, inside, jnp.where(taken, inside, inside + stride)

    place, inside, order = places(axis)
    other_place, _, other_order = places(1 - axis)
    ahead = (other_order < order) & (lax.div(other_place, stride) == lax.div(place, stride))
    rank = jnp.sum(jnp.where(ahead, 1, 0), axis=1 - axis, keepdims=True)
    group = lax.div(place, stride)
    return jnp.where(
        rank < heads, group * heads + rank, share + group * (stride - heads) + rank - heads
    )


def slots_of(offsets, heads):
    values = [offsets[h] for h in range(heads)]
    fresh = []
    for h in range(heads):
        seen = jnp.int32(1)
        for earlier in values[:h]:
            seen = jnp.where(earlier == values[h], 0, seen)
        fresh.append(seen)
    slots = []
    for h in range(heads):
        slot = jnp.int32(0)
        for other in range(heads):
            slot = slot + jnp.where(values[other] < values[h], fresh[other], 0)
        slots.append(slot)
    return slots


def first_keys_kernel(
    offsets, tokens, gain, key_weight, value_weight, keyval, rows, wide, picks, scale, sems, *, stride
):
    copies = [
        bring(offsets, picks, sems.at[0]),
        bring(tokens, rows, sems.at[1]),
        bring(gain, scale, sems.at[2]),
        bring(key_weight, wide.at[0], sems.at[3]),
        bring(value_weight, wide.at[1], sems.at[4]),
    ]
    heads = offsets.shape[0]
    copies[0].wait()
    chooser = pick_matrix(picks, heads, rows.shape[0] // stride, stride)
    copies[1].wait()
    copies[2].wait()
    chosen = norm_rows(dot(chooser, rows[...]), scale[...])

    def weight(slot):
        copies[slot + 3].wait()
        return wide[slot]

    project_keys(
        chosen, heads, [functools.partial(weight, slot) for slot in range(2)], keyval
    )


def order_kernel(
    offsets, tokens, gain, moved_rows, normed, rows, picks, scale, sems, *, stride, chunk
):
    copies = [
        bring(offsets, picks, sems.at[0]),
        bring(tokens, rows, sems.at[1]),
        bring(gain, scale, sems.at[2]),
    ]
    count = tokens.shape[0]
    share = chunk // stride * offsets.shape[0]
    rest = chunk - share
    picked = count // chunk * share
    copies[0].wait()
    mover = one_hot(
        lax.broadcasted_iota(jnp.int32, (chunk, chunk), 0)
        == ranks(picks, chunk, stride, share, 1)
    )
    copies[1].wait()
    copies[2].wait()
    for c in range(count // chunk):
        moved = dot(mover, rows[c * chunk : (c + 1) * chunk, :]).astype(BF16)
        moved_rows[c * share : (c + 1) * share, :] = moved[:share]
        moved_rows[picked + c * rest : picked + (c + 1) * rest, :] = moved[share:]
    norm_into(normed, 0, moved_rows, scale[...], count)


def scaled_query(normed, weight, outs, heads, peaks):
    width = normed.shape[1]
    factor = (width // heads) ** (-0.5) * LOG2E
    peak = None
    for out, row in outs:
        for span in pieces(out.shape[0], 512 if out.shape[0] % 512 == 0 else 256):
            query = dot(normed[row + span.start : row + span.stop, :], weight[...]) * factor
            out[span, :] = query.astype(BF16)
            for part in pieces(query.shape[0], 64):
                square = query[part] * query[part]
                peak = square if peak is None else jnp.maximum(peak, square)
    peaks[...] = summed_peaks(peak.astype(BF16), heads)


def first_query_kernel(normed, weight, picked, rest, peaks, sems, *, heads):
    del sems
    scaled_query(normed, weight, [(picked, 0), (rest, picked.shape[0])], heads, peaks)


def head_windows(head_size, width):
    period = min(width, math.lcm(head_size, 128))
    windows = []
    for h in range(period // head_size):
        start = h * head_size // 128 * 128
        stop = min(period, -(-(h + 1) * head_size // 128) * 128)
        windows.append((start, stop - start))
    return period, windows


def summed_peaks(peak, heads):
    width = peak.shape[1]
    column = lax.broadcasted_iota(jnp.int32, (width, 128), 0)
    head = lax.broadcasted_iota(jnp.int32, (width, 128), 1)
    low = head * (width // heads)
    sums = one_hot((column >= low) & (column < low + width // heads))
    return jnp.max(dot(peak, sums), axis=0, keepdims=True)


def load_keys(keyval, heads, turned, peaks):
    keys = jnp.concatenate([keyval[i, 0] for i in range(keyval.shape[0])], axis=0)
    turned[...] = keys.T
    peaks[...] = summed_peaks(keys * keys, heads)


def small_scores(query_peaks, key_peaks):
    keys = jnp.maximum(key_peaks[0][...], key_peaks[1][...])
    return jnp.max(query_peaks[...] * keys) < 9000.0


def reciprocal(x):
    guess = pl.reciprocal(x, approx=True)
    return guess * (2.0 - x * guess)


def padded_keys(turned, base, head, head_size, start, size):
    rows = pl.ds(pl.multiple_of(base + head * head_size, 16), head_size)
    own = jnp.concatenate([part[rows, :] for part in turned], axis=1)
    low = head * head_size - start
    parts = [own]
    if low:
        parts.insert(0, jnp.zeros((low, own.shape[1]), BF16))
    if low + head_size < size:
        parts.append(jnp.zeros((size - low - head_size, own.shape[1]), BF16))
    return jnp.concatenate(parts, axis=0)


def score_pair(query, span, base, head, head_size, windows, turned):
    start = windows[head][0]
    size = windows[head + 1][0] + windows[head + 1][1] - start
    keys = [padded_keys([turned], base, head + i, head_size, start, size) for i in range(2)]
    return dot(query[span, pl.ds(base + start, size)], jnp.concatenate(keys, axis=1))


def near_weights_kernel(
    picked, rest, keyval, picked_early, rest_early, turned, peaks, scores_ref, sems, *, heads
):
    del sems
    load_keys(keyval, heads, turned, peaks)
    width = picked.shape[1]
    head_size = width // heads
    key_count = turned.shape[1]
    period, windows = head_windows(head_size, width)
    jobs = [
        (query, early, head)
        for query, early in ((picked, picked_early), (rest, rest_early))
        for head in range(0, len(windows), 2)
    ]

    @pl.loop(0, width // period)
    def _(turn):
        base = pl.multiple_of(turn * period, 128)

        def score(i):
            query, _, head = jobs[i]
            rows = query.shape[0]
            scores_ref[i % 2, :rows] = score_pair(
                query, slice(0, rows), base, head, head_size, windows, turned
            )

        score(0)
        for i, (query, early, head) in enumerate(jobs):
            if i + 1 < len(jobs):
                score(i + 1)
            for part in pieces(query.shape[0], 64):
                weights = jnp.exp2(scores_ref[i % 2, part, :]).astype(BF16)
                for j in range(2):
                    early[turn * len(windows) + head + j, part, :] = weights[
                        :, j * key_count : (j + 1) * key_count
                    ]


def attend_rows(
    query, first_row, rows, heads, turned, keyvals, mixed_ref, mixed_row, work, plain, early=None
):
    scores_ref, weights_ref = work
    width = query.shape[1]
    key_count = sum(part.shape[1] for part in turned)
    head_size = width // heads
    period, windows = head_windows(head_size, width)
    span = pl.ds(first_row, rows)
    out_span = pl.ds(mixed_row, rows)
    lane = lax.broadcasted_iota(jnp.int32, (1, 128), 1)
    step = 2 if early is not None else 1

    @pl.loop(0, width // period)
    def _(turn):
        base = pl.multiple_of(turn * period, 128)
        sums = {}

        def score(i):
            if early is not None:
                scores = score_pair(query, span, base, 2 * i, head_size, windows, turned[1])
            else:
                start, size = windows[i]
                scores = dot(
                    query[span, pl.ds(base + start, size)],
                    padded_keys(turned, base, i, head_size, start, size),
                )
            scores_ref[i % 2, :rows] = scores

        def weigh(h):
            for part in pieces(rows, 64):
                scores = scores_ref[h % 2, part, :]
                if not plain:
                    scores = scores - jnp.max(scores, axis=1, keepdims=True)
                weights_ref[h % 2, part, :] = jnp.exp2(scores).astype(BF16)

        def mix(h):
            start, size = windows[h]
            low = h * head_size - start
            values = jnp.concatenate(
                [
                    x[i, 1, :, pl.ds(base + start, size)]
                    for x in keyvals
                    for i in range(x.shape[0])
                ],
                axis=0,
            )
            column = lax.broadcasted_iota(jnp.int32, (key_count, size), 1)
            own = (column >= low) & (column < low + head_size)
            values = jnp.where(own, values, jnp.ones((), BF16))
            if early is not None:
                half = key_count // 2
                far = weights_ref[h // 2 % 2, :rows, h % 2 * half : (h % 2 + 1) * half]
                near = early[turn * len(windows) + h, span, :]
                weights = jnp.concatenate([near, far], axis=1)
            else:
                weights = weights_ref[h % 2, :rows]
            mixed = dot(weights, values)
            for offset in range(0, size, 128):
                own = mixed[:, offset : offset + 128]
                own = own * reciprocal(pltpu.roll(own, 64, 1))
                at = start + offset
                if at in sums:
                    own = jnp.where(lane >= h * head_size - at, own, sums[at])
                sums[at] = own
                if (h + 1) * head_size >= at + 128:
                    mixed_ref[out_span, pl.ds(base + at, 128)] = sums.pop(at).astype(BF16)

        count = len(windows) // step
        score(0)
        for i in range(count):
            if i:
                for h in range((i - 1) * step, i * step):
                    mix(h)
            if i + 1 < count:
                score(i + 1)
            weigh(i)
        for h in range((count - 1) * step, count * step):
            mix(h)


def attend(query, rows, heads, turned, keyvals, mixed_ref, work, small, early=None):
    size = math.gcd(rows, ROWS)

    @pl.when(small)
    def _():
        attend_rows(query, 0, rows, heads, turned, keyvals, mixed_ref, 0, work, True, early)

    @pl.when(jnp.logical_not(small))
    def _():
        @pl.loop(0, rows // size)
        def _(step):
            row = pl.multiple_of(step * size, size)
            attend_rows(
                query,
                row,
                size,
                heads,
                turned,
                keyvals,
                mixed_ref,
                row,
                work,
                False,
            )


def gelu(x):
    half = 0.5 * x
    return half + half * jnp.tanh(x * (0.7978845608028654 + 0.035677408136300125 * (x * x)))


def widen(normed, up_weight, low, wide_ref, inner):
    rows = normed.shape[0]
    spans = pieces(inner.shape[1], wide_ref.shape[2])

    def product(i):
        columns = slice(low + spans[i].start, low + spans[i].stop)
        wide_ref[i % 2] = dot(normed[...], up_weight[:, columns])

    product(0)
    for i, span in enumerate(spans):
        if i + 1 < len(spans):
            product(i + 1)
        for part in pieces(rows, 32):
            inner[part, span] = gelu(wide_ref[i % 2, part, :]).astype(BF16)


def feed_forward(normed, up_weight, down_weight, total, wide_ref, inner):
    rows = normed.shape[0]
    spans = pieces(up_weight.shape[1], wide_ref.shape[2])

    def product(i):
        wide_ref[i % 2] = dot(normed[...], up_weight[:, spans[i]])

    product(0)
    for i, span in enumerate(spans):
        if i + 1 < len(spans):
            product(i + 1)
        for part in pieces(rows, 32):
            inner[i % 2, part, :] = gelu(wide_ref[i % 2, part, :]).astype(BF16)
        total[...] += dot(inner[i % 2], down_weight[span, :])


def narrow(inners, down_weight, first, second, size):
    for span in pieces(second.shape[1], size):
        total = first[:, span].astype(F32)
        low = 0
        for inner in inners:
            high = low + inner.shape[1]
            total = total + dot(inner[...], down_weight[low:high, span])
            low = high
        second[:, span] = total.astype(BF16)


def add_heads(tokens, first_row, mixed, out_weight, gain, first, normed):
    before = None
    for span in pieces(mixed.shape[0], 256):
        total = dot(mixed[span, :], out_weight[...])
        rows = tokens[first_row + span.start : first_row + span.stop, :]
        first[span, :] = (rows.astype(F32) + total).astype(BF16)
        if before is not None:
            norm_into(normed, before.start, first.at[before], gain, before.stop - before.start)
        before = span
    norm_into(normed, before.start, first.at[before], gain, before.stop - before.start)


def picked_kernel(
    offsets,
    tokens,
    query,
    query_peaks,
    early,
    keyval,
    keyval_far,
    turned_near,
    peaks_near,
    out_weight,
    mlp_gain,
    up_weight,
    down_weight,
    gain,
    key_weight,
    value_weight,
    second,
    normed,
    keyval_two,
    turned,
    peaks,
    held,
    mixed,
    scores,
    weights,
    first,
    wide,
    inner,
    total,
    sems,
    *,
    heads,
):
    copies = [
        bring(x, held.at[i], sems.at[i]) for i, x in enumerate((key_weight, value_weight))
    ]
    rows = second.shape[0]
    keyvals = (keyval, keyval_far)
    load_keys(keyval_far, heads, turned, peaks)
    small = small_scores(query_peaks, (peaks_near, peaks))
    attend(
        query,
        rows,
        heads,
        (turned_near, turned),
        keyvals,
        mixed,
        (scores, weights),
        small,
        early,
    )
    add_heads(tokens, 0, mixed, out_weight, mlp_gain[...], first, normed)
    total[...] = first[...].astype(F32)
    feed_forward(normed, up_weight, down_weight, total, wide, inner)
    second[...] = total[...].astype(BF16)
    norm_into(normed, 0, second, gain[...], rows)
    chooser = pick_matrix(slots_of(offsets, heads), heads, rows // heads, heads)
    chosen = dot(chooser, normed[...]).astype(BF16)

    def weight(slot):
        copies[slot].wait()
        return held[slot]

    project_keys(
        chosen, heads, [functools.partial(weight, slot) for slot in range(2)], keyval_two
    )


def rest_attention_kernel(
    query,
    query_peaks,
    early,
    keyval,
    keyval_far,
    turned_near,
    peaks_near,
    turned,
    peaks,
    mixed,
    scores,
    weights,
    sems,
    *,
    heads,
):
    del sems
    attend(
        query,
        mixed.shape[0],
        heads,
        (turned_near, turned),
        (keyval, keyval_far),
        mixed,
        (scores, weights),
        small_scores(query_peaks, (peaks_near, peaks)),
        early,
    )


def rest_up_kernel(
    tokens, mixed, out_weight, gain, up_weight, first, normed, inner, wide, sems
):
    del sems
    add_heads(
        tokens, tokens.shape[0] - mixed.shape[0], mixed, out_weight, gain[...], first, normed
    )
    widen(normed, up_weight, 0, wide, inner)


def rest_down_kernel(
    first, normed, inner, up_weight, down_weight, second, wide, inner_more, sems
):
    del sems
    widen(normed, up_weight, inner.shape[1], wide, inner_more)
    narrow([inner, inner_more], down_weight, first, second, 256)


def picked_query_kernel(normed, weight, query, peaks, sems, *, heads):
    del sems
    scaled_query(normed, weight, [(query, 0)], heads, peaks)


def rest_query_kernel(
    picked, picked_peaks, rows, gain, weight, query, peaks, normed, sems, *, heads
):
    del sems
    start = picked.shape[0]
    query[:start, :] = picked[...]
    norm_into(normed, 0, rows, gain[...], rows.shape[0])
    out = query.at[pl.ds(start, rows.shape[0])]
    scaled_query(normed, weight, [(out, 0)], heads, peaks)
    peaks[...] = jnp.maximum(peaks[...], picked_peaks[...])


def second_kernel(*refs, heads, stride, chunk, parts):
    offsets, *rows = refs[: 1 + parts]
    query, query_peaks, keyval, keyval_far, out_weight, encoded = refs[1 + parts : 7 + parts]
    turned_near, peaks_near, turned, peaks, held, mixed = refs[7 + parts : 13 + parts]
    result, ready, scores, weights, sems = refs[13 + parts :]
    copy = bring(out_weight, held.at[0], sems.at[0])
    keyvals = (keyval, keyval_far)
    load_keys(keyval, heads, turned_near, peaks_near)
    load_keys(keyval_far, heads, turned, peaks)
    count = query.shape[0]
    small = small_scores(query_peaks, (peaks_near, peaks))
    attend(
        query, count, heads, (turned_near, turned), keyvals, mixed, (scores, weights), small
    )
    share = chunk // stride * heads
    rest_share = chunk - share
    back = one_hot(
        lax.broadcasted_iota(jnp.int32, (chunk, chunk), 1)
        == ranks(offsets, chunk, stride, share, 0)
    )
    copy.wait()
    start = 0
    for part in rows:
        span = slice(start, start + part.shape[0])
        total = part[...].astype(F32) + dot(mixed[span, :], held[0])
        result[span, :] = total.astype(BF16)
        start += part.shape[0]
    start = count // chunk * share
    copies = []
    for c in range(count // chunk):
        far = start + c * rest_share
        blend = jnp.concatenate(
            [result[c * share : (c + 1) * share, :], result[far : far + rest_share, :]], axis=0
        )
        span = pl.ds(c * chunk, chunk)
        ready[span, :] = dot(back, blend).astype(BF16)
        copies.append(bring(ready.at[span], encoded.at[span], sems.at[1 + c]))
    for copy in copies:
        copy.wait()


def relaying(kernel, ins, outs, *refs):
    end = ins + 1 + outs
    refs[end][...] = refs[ins][...]
    kernel(*refs[:ins], *refs[ins + 1 : end], *refs[end + 1 :])


def local_call(kernel, outs, inputs, scratch, scalars=0, far=(), relay=None, out_near=True, copies=1, flops=0, name=None):
    outs, inputs = list(outs), list(inputs)
    if relay is not None:
        kernel = functools.partial(relaying, kernel, len(inputs), len(outs))
        inputs.append(relay)
        outs.append(pltpu.VMEM(relay.shape, relay.dtype))
    specs, placed = [], []
    for i, x in enumerate(inputs):
        if i < scalars:
            specs.append(pl.BlockSpec(memory_space=pltpu.SMEM))
        elif i in far:
            specs.append(pl.BlockSpec(memory_space=pltpu.HBM))
            x = pltpu.with_memory_space_constraint(x, pltpu.HBM)
        else:
            specs.append(pl.BlockSpec(memory_space=pltpu.VMEM))
            x = pltpu.with_memory_space_constraint(x, pltpu.VMEM)
        placed.append(x)
    return pl.pallas_call(
        kernel,
        out_shape=outs,
        in_specs=specs,
        out_specs=[
            pl.BlockSpec(memory_space=pltpu.VMEM if out_near else pltpu.HBM)
        ] * len(outs),
        scratch_shapes=list(scratch) + [pltpu.SemaphoreType.DMA((copies,))],
        compiler_params=pltpu.CompilerParams(vmem_limit_bytes=VMEM_LIMIT),
        cost_estimate=pl.CostEstimate(
            flops=int(flops),
            transcendentals=0,
            bytes_accessed=sum(inputs[i].size * inputs[i].dtype.itemsize for i in far),
        ),
        name=name,
    )(*placed)


def exchange(keyval, span, beside):
    size = lax.axis_size("seq")
    levels = span.bit_length() - 1
    even = list(range(levels - 1, 0, -1))
    orders = (even, even[-1:] + even[:-1])
    for step in range(levels - 1):
        pairs = [(i, i ^ 1 << orders[i % 2][step]) for i in range(size)]
        partner = lax.ppermute(keyval, "seq", pairs)
        keyval = jnp.concatenate([beside(step, keyval), partner], axis=0)
    far = swapped(keyval, "seq", 0)
    return beside(levels - 1, keyval), far


def whole_body(
    tokens,
    attn_gain,
    query_first,
    key_first,
    segment_value,
    output_first,
    mlp_gain,
    up_weight,
    down_weight,
    second_gain,
    query_second,
    key_second,
    value_second,
    output_second,
    segment_offset,
    global_offset,
):
    seq_count = lax.axis_size("seq")
    seg_span = min(SEG_MAX, seq_count)
    heads = segment_offset.shape[0]
    count, width = tokens.shape
    head_size = width // heads
    hidden = up_weight.shape[1]
    stride = count // (KEYS // seg_span)
    stride_two = count // (KEYS // seq_count)
    groups, groups_two = count // stride, count // stride_two
    chunk = max(ROWS, stride_two)
    picked_count = groups_two * heads
    rest_count = count - picked_count
    part = hidden // 4

    def near(*shape):
        return pltpu.VMEM(shape, BF16)

    def attention_work(rows):
        return [pltpu.VMEM((2, rows, KEYS), F32), near(2, rows, KEYS)]

    held_shapes = [near(width, KEYS // 2), pltpu.VMEM((1, 128), F32)]
    small_work = [pltpu.SMEM((heads,), jnp.int32), pltpu.VMEM((width,), F32)]

    (keyval,) = local_call(
        functools.partial(first_keys_kernel, stride=stride),
        [near(1, 2, groups, width)],
        (segment_offset, tokens, attn_gain, key_first, segment_value),
        [near(count, width), near(2, width, width)] + small_work,
        far=(0, 1, 2, 3, 4),
        copies=5,
        flops=2 * heads * groups * width * (count + 2 * width),
        name="first_keys",
    )
    made = {}

    def beside_first(level, held):
        if level == 0:
            made["rows"], made["normed"], held = local_call(
                functools.partial(order_kernel, stride=stride_two, chunk=chunk),
                [near(count, width), near(count, width)],
                (global_offset, tokens, attn_gain),
                [near(count, width)] + small_work,
                far=(0, 1, 2),
                copies=3,
                relay=held,
                flops=2 * count * width * chunk,
                name="order",
            )
        if level == min(1, seg_span.bit_length() - 2):
            made["picked"], made["rest"], made["peaks"], held = local_call(
                functools.partial(first_query_kernel, heads=heads),
                [near(picked_count, width), near(rest_count, width), pltpu.VMEM((1, 128), F32)],
                (made["normed"], query_first),
                [],
                relay=held,
                flops=2 * count * width * width,
                name="first_query",
            )
        if level == seg_span.bit_length() - 2:
            made["picked_early"], made["rest_early"], made["turned"], made["key_peaks"] = local_call(
                functools.partial(near_weights_kernel, heads=heads),
                [near(heads, picked_count, KEYS // 2), near(heads, rest_count, KEYS // 2)]
                + held_shapes,
                (made["picked"], made["rest"], held),
                [pltpu.VMEM((2, rest_count, KEYS), F32)],
                flops=2 * 256 * KEYS // 2 * heads * count,
                name="near_weights",
            )
        return held

    keyval, keyval_far = exchange(keyval, seg_span, beside_first)
    rows = made["rows"]
    query_peaks, near_held = made["peaks"], (made["turned"], made["key_peaks"])
    row_flops = 2 * width * (2 * hidden + width) + 4 * 256 * KEYS * heads
    picked_second, picked_normed, keyval_two, turned, peaks = local_call(
        functools.partial(picked_kernel, heads=heads),
        [
            near(picked_count, width),
            near(picked_count, width),
            near(1, 2, groups_two, width),
        ]
        + held_shapes,
        (
            global_offset,
            rows,
            made["picked"],
            query_peaks,
            made["picked_early"],
            keyval,
            keyval_far,
            *near_held,
            output_first,
            mlp_gain,
            up_weight,
            down_weight,
            second_gain,
            key_second,
            value_second,
        ),
        [near(2, width, width), near(picked_count, width)]
        + attention_work(picked_count)
        + [near(picked_count, width), pltpu.VMEM((2, picked_count, part), F32)]
        + [near(2, picked_count, part), pltpu.VMEM((picked_count, width), F32)],
        scalars=1,
        far=(14, 15),
        copies=2,
        flops=row_flops * picked_count,
        name="layer_of_picked",
    )
    seconds = [picked_second]

    def rest_attention(held):
        made["mixed"], held = local_call(
            functools.partial(rest_attention_kernel, heads=heads),
            [near(rest_count, width)],
            (
                made["rest"],
                query_peaks,
                made["rest_early"],
                keyval,
                keyval_far,
                *near_held,
                turned,
                peaks,
            ),
            attention_work(rest_count),
            relay=held,
            flops=4 * 256 * KEYS * heads * rest_count,
            name="rest_attention",
        )
        return held

    half = hidden // 2

    def rest_up(held):
        made["first"], made["normed"], made["inner"], held = local_call(
            rest_up_kernel,
            [near(rest_count, width), near(rest_count, width), near(rest_count, half)],
            (rows, made["mixed"], output_first, mlp_gain, up_weight),
            [pltpu.VMEM((2, rest_count, part), F32)],
            relay=held,
            flops=2 * width * (half + width) * rest_count,
            name="rest_up",
        )
        return held

    def rest_down(held):
        result, held = local_call(
            rest_down_kernel,
            [near(rest_count, width)],
            (made["first"], made["normed"], made["inner"], up_weight, down_weight),
            [pltpu.VMEM((2, rest_count, part), F32), near(rest_count, hidden - half)],
            relay=held,
            flops=2 * width * (2 * hidden - half) * rest_count,
            name="rest_down",
        )
        seconds.append(result)
        return held

    def picked_query(held):
        made["picked_two"], made["picked_peaks"], held = local_call(
            functools.partial(picked_query_kernel, heads=heads),
            [near(picked_count, width), pltpu.VMEM((1, 128), F32)],
            (picked_normed, query_second),
            [],
            relay=held,
            flops=2 * picked_count * width * width,
            name="picked_query",
        )
        return held

    def rest_query(held):
        made["query_two"], made["peaks_two"], held = local_call(
            functools.partial(rest_query_kernel, heads=heads),
            [near(count, width), pltpu.VMEM((1, 128), F32)],
            (made["picked_two"], made["picked_peaks"], seconds[1], second_gain, query_second),
            [near(rest_count, width)],
            relay=held,
            flops=2 * rest_count * width * width,
            name="rest_query",
        )
        return held

    tasks = [[rest_attention], [rest_up, picked_query], [rest_down], [rest_query]]
    levels = seq_count.bit_length() - 1

    def beside_second(level, held):
        for work in tasks[len(tasks) * level // levels : len(tasks) * (level + 1) // levels]:
            for task in work:
                held = task(held)
        return held

    keyval_two, keyval_two_far = exchange(keyval_two, seq_count, beside_second)
    (encoded,) = local_call(
        functools.partial(
            second_kernel, heads=heads, stride=stride_two, chunk=chunk, parts=len(seconds)
        ),
        [jax.ShapeDtypeStruct((count, width), BF16)],
        (
            global_offset,
            *seconds,
            made["query_two"],
            made["peaks_two"],
            keyval_two,
            keyval_two_far,
            output_second,
        ),
        held_shapes * 2
        + [near(1, width, width)]
        + [near(count, width)] * 3
        + attention_work(count),
        scalars=1,
        far=(len(seconds) + 5,),
        out_near=False,
        copies=1 + count // chunk,
        flops=count * (2 * width * width + 4 * 256 * KEYS * heads),
        name="second_attention",
    )
    return encoded


def solution(mesh):
    placed = (
        P(("slides", "seq", "mp"), None),
        P(),
        P(None, "mp"),
        P(None, "mp"),
        P(None, "mp"),
        P("mp", None),
        P(),
        P(None, "mp"),
        P("mp", None),
        P(),
        P(None, "mp"),
        P(None, "mp"),
        P(None, "mp"),
        P("mp", None),
        P("mp"),
        P("mp"),
    )
    fits = mesh.shape["mp"] == 1 and mesh.shape["seq"] in (2, 4, 8, 16)
    return jax.shard_map(
        whole_body if fits else split_body,
        mesh=mesh,
        in_specs=placed,
        out_specs=P(("slides", "seq", "mp"), None),
        check_vma=False,
    )
```

```python
import functools
import math

import jax
import jax.numpy as jnp
from jax import lax
from jax.experimental import pallas as pl
from jax.experimental.pallas import tpu as pltpu
from jax.sharding import PartitionSpec as P

KEYS = 256
SEG_MAX = 16
ROWS = 256
LOG2E = 1.4426950408889634
BF16 = jnp.bfloat16
F32 = jnp.float32
VMEM_LIMIT = 22 * 1024 * 1024


def swapped(x, axis, apart):
    return lax.ppermute(x, axis, [(i, i ^ 1 << apart) for i in range(lax.axis_size(axis))])


def norm_rows(values, gain):
    center = values - jnp.mean(values, axis=-1, keepdims=True)
    spread = jnp.mean(center * center, axis=-1, keepdims=True)
    return (center * lax.rsqrt(spread + 1e-05) * gain).astype(jnp.bfloat16)


def pick_keys(hidden, offsets, stride, key_weight, value_weight):
    token_count, width = hidden.shape
    head_count = offsets.shape[0]
    head_size = key_weight.shape[1] // head_count
    grouped_rows = hidden.reshape(token_count // stride, stride, width)
    dilation_selector = (
        lax.broadcasted_iota(jnp.int32, (stride, head_count), 0) == offsets[None, :]
    ).astype(jnp.bfloat16)
    chosen = jnp.einsum(
        "nof,oj->njf", grouped_rows, dilation_selector, preferred_element_type=jnp.float32
    ).astype(jnp.bfloat16)
    key_heads = jnp.einsum(
        "xkr,rkf->xkf",
        chosen,
        key_weight.reshape(width, head_count, head_size),
        preferred_element_type=jnp.float32,
    ).astype(jnp.bfloat16)
    value_heads = jnp.einsum(
        "xkr,rkf->xkf",
        chosen,
        value_weight.reshape(width, head_count, head_size),
        preferred_element_type=jnp.float32,
    ).astype(jnp.bfloat16)
    picked = token_count // stride
    return jnp.stack(
        [
            key_heads.reshape(picked, head_count * head_size),
            value_heads.reshape(picked, head_count * head_size),
        ]
    )


def attend_local(query, keyval, head_count):
    token_count, width = query.shape
    head_size = width // head_count
    query_heads = query.reshape(token_count, head_count, head_size)
    key_heads = keyval[0].reshape(-1, head_count, head_size)
    value_heads = keyval[1].reshape(-1, head_count, head_size)
    scores = jnp.einsum(
        "thd,khd->htk", query_heads, key_heads, preferred_element_type=jnp.float32
    ) * head_size ** (-0.5)
    highest = jnp.max(scores, axis=-1, keepdims=True)
    weights = jnp.exp(scores - highest)
    weights = (weights / jnp.sum(weights, axis=-1, keepdims=True)).astype(jnp.bfloat16)
    mixed = jnp.einsum(
        "htk,khd->thd", weights, value_heads, preferred_element_type=jnp.float32
    ).astype(jnp.bfloat16)
    return mixed.reshape(token_count, width)


def merge_branch_pair(mine, other, level, token_position):
    lower = token_position >> level & 1 == 0
    return jnp.where(
        lower, jnp.concatenate((mine, other), axis=1), jnp.concatenate((other, mine), axis=1)
    )


def spread_segment(keyval, seg_span, token_position):
    for level in range(seg_span.bit_length() - 1):
        partner = swapped(keyval, "seq", level)
        keyval = merge_branch_pair(keyval, partner, level, token_position)
    return keyval


def spread_global(keyval_two):
    keyval_two = lax.all_gather(keyval_two, "seq", axis=1, tiled=True)
    return keyval_two


def combine(partial_value, residual_full, need_full):
    row_count = residual_full.shape[0] // lax.axis_size("mp")
    row_start = lax.axis_index("mp") * row_count
    share = lax.psum_scatter(partial_value, "mp", scatter_dimension=0, tiled=True)
    own_rows = lax.dynamic_slice_in_dim(residual_full, row_start, row_count, 0)
    own_rows = (own_rows.astype(jnp.float32) + share).astype(jnp.bfloat16)
    full_rows = lax.all_gather(own_rows, "mp", axis=0, tiled=True) if need_full else own_rows
    return (own_rows, full_rows)


def split_body(
    tokens,
    attn_gain,
    query_first,
    key_first,
    segment_value,
    output_first,
    mlp_gain,
    up_weight,
    down_weight,
    second_gain,
    query_second,
    key_second,
    value_second,
    output_second,
    segment_offset,
    global_offset,
):
    seq_count = lax.axis_size("seq")
    token_position = lax.axis_index("seq")
    seg_span = min(SEG_MAX, seq_count)
    head_count = segment_offset.shape[0]
    full_rows = lax.all_gather(tokens, "mp", axis=0, tiled=True)
    token_count = full_rows.shape[0]
    hidden = norm_rows(full_rows.astype(jnp.float32), attn_gain)
    query = jnp.dot(hidden, query_first, preferred_element_type=jnp.float32).astype(jnp.bfloat16)
    seg_stride = token_count // (KEYS // seg_span)
    keyval = pick_keys(hidden, segment_offset, seg_stride, key_first, segment_value)
    keyval = spread_segment(keyval, seg_span, token_position)
    mixed = attend_local(query, keyval, head_count)
    partial_value = jnp.dot(mixed, output_first, preferred_element_type=jnp.float32)
    own_rows, first_rows = combine(partial_value, full_rows, True)
    normed = norm_rows(first_rows.astype(jnp.float32), mlp_gain)
    inner = jax.nn.gelu(
        jnp.dot(normed, up_weight, preferred_element_type=jnp.float32), approximate=True
    ).astype(jnp.bfloat16)
    partial_value = jnp.dot(inner, down_weight, preferred_element_type=jnp.float32)
    own_rows, second_rows = combine(partial_value, first_rows, True)
    hidden_two = norm_rows(second_rows.astype(jnp.float32), second_gain)
    query_two = jnp.dot(hidden_two, query_second, preferred_element_type=jnp.float32).astype(
        jnp.bfloat16
    )
    glob_stride = token_count // (KEYS // seq_count)
    keyval_two = pick_keys(hidden_two, global_offset, glob_stride, key_second, value_second)
    keyval_two = spread_global(keyval_two)
    mixed_two = attend_local(query_two, keyval_two, head_count)
    partial_value = jnp.dot(mixed_two, output_second, preferred_element_type=jnp.float32)
    own_rows, unused_rows = combine(partial_value, second_rows, False)
    return own_rows


def one_hot(condition):
    return jnp.where(condition, 1.0, 0.0).astype(BF16)


def dot(left, right):
    return jnp.dot(left, right, preferred_element_type=F32)


def pieces(count, size):
    size = size if count % size == 0 else count
    return [slice(start, start + size) for start in range(0, count, size)]


def norm_into(out, start, source, gain, count):
    for span in pieces(count, 64):
        out[start + span.start : start + span.stop, :] = norm_rows(
            source[span, :].astype(F32), gain
        )


def bring(source, target, sem):
    copy = pltpu.make_async_copy(source, target, sem)
    copy.start()
    return copy


def pick_matrix(offsets, heads, groups, stride):
    count = groups * stride
    place = lax.broadcasted_iota(jnp.int32, (groups, count), 1)
    place = place - lax.broadcasted_iota(jnp.int32, (groups, count), 0) * stride
    return jnp.concatenate([one_hot(place == offsets[h]) for h in range(heads)], axis=0)


def project_keys(chosen, heads, weights, keyval_ref):
    rows, width = chosen.shape
    groups, head_size = rows // heads, width // heads
    for slot, weight in enumerate(weights):
        held = weight()
        for span in pieces(width, 256):
            first, last = span.start // head_size, (span.stop - 1) // head_size + 1
            wide = dot(chosen[first * groups : last * groups], held[:, span])
            column = lax.broadcasted_iota(jnp.int32, (groups, span.stop - span.start), 1)
            total = wide[:groups]
            for h in range(first + 1, last):
                row = (h - first) * groups
                own = column >= h * head_size - span.start
                total = jnp.where(own, wide[row : row + groups], total)
            total = total.astype(BF16)
            for copy in range(keyval_ref.shape[0]):
                keyval_ref[copy, slot, :, span] = total


def ranks(offsets, chunk, stride, share, axis):
    heads = offsets.shape[0]

    def places(way):
        shape = (1, chunk) if way else (chunk, 1)
        place = lax.broadcasted_iota(jnp.int32, shape, way)
        inside = lax.rem(place, stride)
        taken = inside == offsets[0]
        for h in range(1, heads):
            taken = taken | (inside == offsets[h])
        return place, inside, jnp.where(taken, inside, inside + stride)

    place, inside, order = places(axis)
    other_place, _, other_order = places(1 - axis)
    ahead = (other_order < order) & (lax.div(other_place, stride) == lax.div(place, stride))
    rank = jnp.sum(jnp.where(ahead, 1, 0), axis=1 - axis, keepdims=True)
    group = lax.div(place, stride)
    return jnp.where(
        rank < heads, group * heads + rank, share + group * (stride - heads) + rank - heads
    )


def slots_of(offsets, heads):
    values = [offsets[h] for h in range(heads)]
    fresh = []
    for h in range(heads):
        seen = jnp.int32(1)
        for earlier in values[:h]:
            seen = jnp.where(earlier == values[h], 0, seen)
        fresh.append(seen)
    slots = []
    for h in range(heads):
        slot = jnp.int32(0)
        for other in range(heads):
            slot = slot + jnp.where(values[other] < values[h], fresh[other], 0)
        slots.append(slot)
    return slots


def first_keys_kernel(
    offsets, tokens, gain, key_weight, value_weight, keyval, rows, wide, picks, scale, sems, *, stride
):
    copies = [
        bring(offsets, picks, sems.at[0]),
        bring(tokens, rows, sems.at[1]),
        bring(gain, scale, sems.at[2]),
        bring(key_weight, wide.at[0], sems.at[3]),
        bring(value_weight, wide.at[1], sems.at[4]),
    ]
    heads = offsets.shape[0]
    copies[0].wait()
    chooser = pick_matrix(picks, heads, rows.shape[0] // stride, stride)
    copies[1].wait()
    copies[2].wait()
    chosen = norm_rows(dot(chooser, rows[...]), scale[...])

    def weight(slot):
        copies[slot + 3].wait()
        return wide[slot]

    project_keys(
        chosen, heads, [functools.partial(weight, slot) for slot in range(2)], keyval
    )


def order_kernel(
    offsets,
    tokens,
    gain,
    moved_rows,
    normed,
    chooser,
    back,
    rows,
    picks,
    scale,
    sems,
    *,
    stride,
    chunk,
):
    copies = [
        bring(offsets, picks, sems.at[0]),
        bring(tokens, rows, sems.at[1]),
        bring(gain, scale, sems.at[2]),
    ]
    count = tokens.shape[0]
    share = chunk // stride * offsets.shape[0]
    rest = chunk - share
    picked = count // chunk * share
    copies[0].wait()
    mover = one_hot(
        lax.broadcasted_iota(jnp.int32, (chunk, chunk), 0)
        == ranks(picks, chunk, stride, share, 1)
    )
    heads = offsets.shape[0]
    chooser[...] = pick_matrix(slots_of(picks, heads), heads, picked // heads, heads)
    back[...] = one_hot(
        lax.broadcasted_iota(jnp.int32, (chunk, chunk), 1)
        == ranks(picks, chunk, stride, share, 0)
    )
    copies[1].wait()
    copies[2].wait()
    for c in range(count // chunk):
        moved = dot(mover, rows[c * chunk : (c + 1) * chunk, :]).astype(BF16)
        moved_rows[c * share : (c + 1) * share, :] = moved[:share]
        moved_rows[picked + c * rest : picked + (c + 1) * rest, :] = moved[share:]
    norm_into(normed, 0, moved_rows, scale[...], count)


def scaled_query(normed, weight, outs, heads, peaks):
    width = normed.shape[1]
    factor = (width // heads) ** (-0.5) * LOG2E
    peak = None
    for out, row in outs:
        for span in pieces(out.shape[0], 512 if out.shape[0] % 512 == 0 else 256):
            query = dot(normed[row + span.start : row + span.stop, :], weight[...]) * factor
            out[span, :] = query.astype(BF16)
            for part in pieces(query.shape[0], 64):
                square = query[part] * query[part]
                peak = square if peak is None else jnp.maximum(peak, square)
    peaks[...] = summed_peaks(peak.astype(BF16), heads)


def first_query_kernel(normed, weight, picked, rest, peaks, sems, *, heads):
    del sems
    scaled_query(normed, weight, [(picked, 0), (rest, picked.shape[0])], heads, peaks)


def head_windows(head_size, width):
    period = min(width, math.lcm(head_size, 128))
    windows = []
    for h in range(period // head_size):
        start = h * head_size // 128 * 128
        stop = min(period, -(-(h + 1) * head_size // 128) * 128)
        windows.append((start, stop - start))
    return period, windows


def summed_peaks(peak, heads):
    width = peak.shape[1]
    column = lax.broadcasted_iota(jnp.int32, (width, 128), 0)
    head = lax.broadcasted_iota(jnp.int32, (width, 128), 1)
    low = head * (width // heads)
    sums = one_hot((column >= low) & (column < low + width // heads))
    return jnp.max(dot(peak, sums), axis=0, keepdims=True)


def load_keys(keyval, turned):
    keys = jnp.concatenate([keyval[i, 0] for i in range(keyval.shape[0])], axis=0)
    turned[...] = keys.T
    return keys * keys


def small_scores(query_peaks, key_peaks):
    return jnp.max(query_peaks[...] * key_peaks[...]) < 9000.0


def reciprocal(x):
    guess = pl.reciprocal(x, approx=True)
    return guess * (2.0 - x * guess)


def padded_keys(turned, base, head, head_size, start, size):
    low = base + head * head_size
    rows = pl.ds(low if isinstance(low, int) else pl.multiple_of(low, 16), head_size)
    own = jnp.concatenate([part[rows, :] for part in turned], axis=1)
    low = head * head_size - start
    parts = [own]
    if low:
        parts.insert(0, jnp.zeros((low, own.shape[1]), BF16))
    if low + head_size < size:
        parts.append(jnp.zeros((size - low - head_size, own.shape[1]), BF16))
    return jnp.concatenate(parts, axis=0)


def score_pair(query, span, base, head, head_size, windows, turned):
    start = windows[head][0]
    size = windows[head + 1][0] + windows[head + 1][1] - start
    keys = [padded_keys([turned], base, head + i, head_size, start, size) for i in range(2)]
    return dot(query[span, pl.ds(base + start, size)], jnp.concatenate(keys, axis=1))


def near_weights_kernel(
    picked, rest, keyval, picked_early, rest_early, turned, peaks, scores_ref, sems, *, heads
):
    del sems
    peaks[...] = summed_peaks(load_keys(keyval, turned), heads)
    width = picked.shape[1]
    head_size = width // heads
    key_count = turned.shape[1]
    period, windows = head_windows(head_size, width)
    jobs = [
        (query, early, head)
        for query, early in ((picked, picked_early), (rest, rest_early))
        for head in range(0, len(windows), 2)
    ]

    @pl.loop(0, width // period)
    def _(turn):
        base = pl.multiple_of(turn * period, 128)

        def score(i):
            query, _, head = jobs[i]
            rows = query.shape[0]
            scores_ref[i % 2, :rows] = score_pair(
                query, slice(0, rows), base, head, head_size, windows, turned
            )

        score(0)
        for i, (query, early, head) in enumerate(jobs):
            if i + 1 < len(jobs):
                score(i + 1)
            for part in pieces(query.shape[0], 64):
                weights = jnp.exp2(scores_ref[i % 2, part, :]).astype(BF16)
                for j in range(2):
                    early[turn * len(windows) + head + j, part, :] = weights[
                        :, j * key_count : (j + 1) * key_count
                    ]


def attend_rows(
    query, first_row, rows, heads, turned, keyvals, mixed_ref, mixed_row, work, plain, early=None
):
    scores_ref, weights_ref = work
    width = query.shape[1]
    key_count = sum(part.shape[1] for part in turned)
    head_size = width // heads
    period, windows = head_windows(head_size, width)
    span = pl.ds(first_row, rows)
    out_span = pl.ds(mixed_row, rows)
    lane = lax.broadcasted_iota(jnp.int32, (1, 128), 1)
    step = 2 if early is not None else 1

    def take_turn(turn):
        base = turn * period if plain else pl.multiple_of(turn * period, 128)
        sums = {}

        def score(i):
            if early is not None:
                scores = score_pair(query, span, base, 2 * i, head_size, windows, turned[1])
            else:
                start, size = windows[i]
                scores = dot(
                    query[span, pl.ds(base + start, size)],
                    padded_keys(turned, base, i, head_size, start, size),
                )
            scores_ref[i % 2, :rows] = scores

        def weigh(h):
            for part in pieces(rows, 64):
                scores = scores_ref[h % 2, part, :]
                if not plain:
                    scores = scores - jnp.max(scores, axis=1, keepdims=True)
                weights_ref[h % 2, part, :] = jnp.exp2(scores).astype(BF16)

        def mix(h):
            start, size = windows[h]
            low = h * head_size - start
            values = jnp.concatenate(
                [
                    x[i, 1, :, pl.ds(base + start, size)]
                    for x in keyvals
                    for i in range(x.shape[0])
                ],
                axis=0,
            )
            column = lax.broadcasted_iota(jnp.int32, (key_count, size), 1)
            own = (column >= low) & (column < low + head_size)
            values = jnp.where(own, values, jnp.ones((), BF16))
            if early is not None:
                half = key_count // 2
                far = weights_ref[h // 2 % 2, :rows, h % 2 * half : (h % 2 + 1) * half]
                near = early[turn * len(windows) + h, span, :]
                weights = jnp.concatenate([near, far], axis=1)
            else:
                weights = weights_ref[h % 2, :rows]
            mixed = dot(weights, values)
            for offset in range(0, size, 128):
                own = mixed[:, offset : offset + 128]
                own = own * reciprocal(pltpu.roll(own, 64, 1))
                at = start + offset
                if at in sums:
                    own = jnp.where(lane >= h * head_size - at, own, sums[at])
                sums[at] = own
                if (h + 1) * head_size >= at + 128:
                    mixed_ref[out_span, pl.ds(base + at, 128)] = sums.pop(at).astype(BF16)

        count = len(windows) // step
        score(0)
        for i in range(count):
            if i:
                for h in range((i - 1) * step, i * step):
                    mix(h)
            if i + 1 < count:
                score(i + 1)
            weigh(i)
        for h in range((count - 1) * step, count * step):
            mix(h)

    if plain:
        for turn in range(width // period):
            take_turn(turn)
    else:
        pl.loop(0, width // period)(take_turn)


def attend(query, rows, heads, turned, keyvals, mixed_ref, work, small, early=None):
    size = math.gcd(rows, ROWS)

    @pl.when(small)
    def _():
        attend_rows(query, 0, rows, heads, turned, keyvals, mixed_ref, 0, work, True, early)

    @pl.when(jnp.logical_not(small))
    def _():
        @pl.loop(0, rows // size)
        def _(step):
            row = pl.multiple_of(step * size, size)
            attend_rows(
                query,
                row,
                size,
                heads,
                turned,
                keyvals,
                mixed_ref,
                row,
                work,
                False,
            )


def gelu(x):
    half = 0.5 * x
    return half + half * jnp.tanh(x * (0.7978845608028654 + 0.035677408136300125 * (x * x)))


def widen(normed, up_weight, low, wide_ref, inner):
    rows = normed.shape[0]
    spans = pieces(inner.shape[1], wide_ref.shape[2])

    def product(i):
        columns = slice(low + spans[i].start, low + spans[i].stop)
        wide_ref[i % 2] = dot(normed[...], up_weight[:, columns])

    product(0)
    for i, span in enumerate(spans):
        if i + 1 < len(spans):
            product(i + 1)
        for part in pieces(rows, 32):
            inner[part, span] = gelu(wide_ref[i % 2, part, :]).astype(BF16)


def feed_forward(normed, up_weight, down_weight, total, wide_ref, inner):
    rows = normed.shape[0]
    spans = pieces(up_weight.shape[1], wide_ref.shape[2])

    def product(i):
        wide_ref[i % 2] = dot(normed[...], up_weight[:, spans[i]])

    product(0)
    for i, span in enumerate(spans):
        if i + 1 < len(spans):
            product(i + 1)
        for part in pieces(rows, 32):
            inner[i % 2, part, :] = gelu(wide_ref[i % 2, part, :]).astype(BF16)
        total[...] += dot(inner[i % 2], down_weight[span, :])


def narrow(inners, down_weight, first, second, size):
    for span in pieces(second.shape[1], size):
        total = first[:, span].astype(F32)
        low = 0
        for inner in inners:
            high = low + inner.shape[1]
            total = total + dot(inner[...], down_weight[low:high, span])
            low = high
        second[:, span] = total.astype(BF16)


def add_heads(tokens, first_row, mixed, out_weight, gain, first, normed):
    before = None
    for span in pieces(mixed.shape[0], 256):
        total = dot(mixed[span, :], out_weight[...])
        rows = tokens[first_row + span.start : first_row + span.stop, :]
        first[span, :] = (rows.astype(F32) + total).astype(BF16)
        if before is not None:
            norm_into(normed, before.start, first.at[before], gain, before.stop - before.start)
        before = span
    norm_into(normed, before.start, first.at[before], gain, before.stop - before.start)


def picked_kernel(
    chooser,
    tokens,
    query,
    query_peaks,
    early,
    keyval,
    keyval_far,
    turned_near,
    peaks_near,
    out_weight,
    mlp_gain,
    up_weight,
    down_weight,
    gain,
    key_weight,
    value_weight,
    second,
    normed,
    keyval_two,
    turned,
    peaks,
    held,
    mixed,
    scores,
    weights,
    first,
    wide,
    inner,
    total,
    sems,
    *,
    heads,
):
    copies = [
        bring(x, held.at[i], sems.at[i]) for i, x in enumerate((key_weight, value_weight))
    ]
    rows = second.shape[0]
    keyvals = (keyval, keyval_far)
    squares = load_keys(keyval_far, turned)
    peaks[...] = jnp.maximum(peaks_near[...], summed_peaks(squares, heads))
    small = small_scores(query_peaks, peaks)
    attend(
        query,
        rows,
        heads,
        (turned_near, turned),
        keyvals,
        mixed,
        (scores, weights),
        small,
        early,
    )
    add_heads(tokens, 0, mixed, out_weight, mlp_gain[...], first, normed)
    total[...] = first[...].astype(F32)
    feed_forward(normed, up_weight, down_weight, total, wide, inner)
    second[...] = total[...].astype(BF16)
    norm_into(normed, 0, second, gain[...], rows)
    chosen = dot(chooser[...], normed[...]).astype(BF16)

    def weight(slot):
        copies[slot].wait()
        return held[slot]

    project_keys(
        chosen, heads, [functools.partial(weight, slot) for slot in range(2)], keyval_two
    )


def rest_attention_kernel(
    query,
    query_peaks,
    early,
    keyval,
    keyval_far,
    turned_near,
    turned,
    peaks,
    mixed,
    scores,
    weights,
    sems,
    *,
    heads,
):
    del sems
    attend(
        query,
        mixed.shape[0],
        heads,
        (turned_near, turned),
        (keyval, keyval_far),
        mixed,
        (scores, weights),
        small_scores(query_peaks, peaks),
        early,
    )


def rest_up_kernel(
    tokens, mixed, out_weight, gain, up_weight, first, normed, inner, wide, sems
):
    del sems
    add_heads(
        tokens, tokens.shape[0] - mixed.shape[0], mixed, out_weight, gain[...], first, normed
    )
    widen(normed, up_weight, 0, wide, inner)


def rest_down_kernel(
    first, normed, inner, up_weight, down_weight, second, wide, inner_more, sems
):
    del sems
    widen(normed, up_weight, inner.shape[1], wide, inner_more)
    narrow([inner, inner_more], down_weight, first, second, 256)


def picked_query_kernel(normed, weight, query, peaks, sems, *, heads):
    del sems
    scaled_query(normed, weight, [(query, 0)], heads, peaks)


def rest_query_kernel(
    picked, picked_peaks, rows, gain, weight, query, peaks, normed, sems, *, heads
):
    del sems
    start = picked.shape[0]
    query[:start, :] = picked[...]
    norm_into(normed, 0, rows, gain[...], rows.shape[0])
    out = query.at[pl.ds(start, rows.shape[0])]
    scaled_query(normed, weight, [(out, 0)], heads, peaks)
    peaks[...] = jnp.maximum(peaks[...], picked_peaks[...])


def second_kernel(*refs, heads, parts):
    back, *rows = refs[: 1 + parts]
    query, query_peaks, keyval, keyval_far, out_weight, encoded = refs[1 + parts : 7 + parts]
    turned_near, turned, held, mixed = refs[7 + parts : 11 + parts]
    result, ready, scores, weights, sems = refs[11 + parts :]
    copy = bring(out_weight, held.at[0], sems.at[0])
    keyvals = (keyval, keyval_far)
    squares = jnp.maximum(load_keys(keyval, turned_near), load_keys(keyval_far, turned))
    count = query.shape[0]
    small = small_scores(query_peaks, summed_peaks(squares, heads))
    attend(
        query, count, heads, (turned_near, turned), keyvals, mixed, (scores, weights), small
    )
    chunk = back.shape[0]
    share = rows[0].shape[0] * chunk // count
    rest_share = chunk - share
    copy.wait()
    start = 0
    for part in rows:
        span = slice(start, start + part.shape[0])
        total = part[...].astype(F32) + dot(mixed[span, :], held[0])
        result[span, :] = total.astype(BF16)
        start += part.shape[0]
    start = count // chunk * share
    copies = []
    for c in range(count // chunk):
        far = start + c * rest_share
        blend = jnp.concatenate(
            [result[c * share : (c + 1) * share, :], result[far : far + rest_share, :]], axis=0
        )
        span = pl.ds(c * chunk, chunk)
        ready[span, :] = dot(back[...], blend).astype(BF16)
        copies.append(bring(ready.at[span], encoded.at[span], sems.at[1 + c]))
    for copy in copies:
        copy.wait()


def relaying(kernel, ins, outs, *refs):
    end = ins + 1 + outs
    refs[end][...] = refs[ins][...]
    kernel(*refs[:ins], *refs[ins + 1 : end], *refs[end + 1 :])


def local_call(kernel, outs, inputs, scratch, scalars=0, far=(), relay=None, out_near=True, copies=1, flops=0, name=None):
    outs, inputs = list(outs), list(inputs)
    if relay is not None:
        kernel = functools.partial(relaying, kernel, len(inputs), len(outs))
        inputs.append(relay)
        outs.append(pltpu.VMEM(relay.shape, relay.dtype))
    specs, placed = [], []
    for i, x in enumerate(inputs):
        if i < scalars:
            specs.append(pl.BlockSpec(memory_space=pltpu.SMEM))
        elif i in far:
            specs.append(pl.BlockSpec(memory_space=pltpu.HBM))
            x = pltpu.with_memory_space_constraint(x, pltpu.HBM)
        else:
            specs.append(pl.BlockSpec(memory_space=pltpu.VMEM))
            x = pltpu.with_memory_space_constraint(x, pltpu.VMEM)
        placed.append(x)
    return pl.pallas_call(
        kernel,
        out_shape=outs,
        in_specs=specs,
        out_specs=[
            pl.BlockSpec(memory_space=pltpu.VMEM if out_near else pltpu.HBM)
        ] * len(outs),
        scratch_shapes=list(scratch) + [pltpu.SemaphoreType.DMA((copies,))],
        compiler_params=pltpu.CompilerParams(vmem_limit_bytes=VMEM_LIMIT),
        cost_estimate=pl.CostEstimate(
            flops=int(flops),
            transcendentals=0,
            bytes_accessed=sum(inputs[i].size * inputs[i].dtype.itemsize for i in far),
        ),
        name=name,
    )(*placed)


def exchange(keyval, span, beside):
    size = lax.axis_size("seq")
    levels = span.bit_length() - 1
    even = list(range(levels - 1, 0, -1))
    orders = (even, even[-1:] + even[:-1])
    for step in range(levels - 1):
        pairs = [(i, i ^ 1 << orders[i % 2][step]) for i in range(size)]
        partner = lax.ppermute(keyval, "seq", pairs)
        keyval = jnp.concatenate([beside(step, keyval), partner], axis=0)
    far = swapped(keyval, "seq", 0)
    return beside(levels - 1, keyval), far


def whole_body(
    tokens,
    attn_gain,
    query_first,
    key_first,
    segment_value,
    output_first,
    mlp_gain,
    up_weight,
    down_weight,
    second_gain,
    query_second,
    key_second,
    value_second,
    output_second,
    segment_offset,
    global_offset,
):
    seq_count = lax.axis_size("seq")
    seg_span = min(SEG_MAX, seq_count)
    heads = segment_offset.shape[0]
    count, width = tokens.shape
    head_size = width // heads
    hidden = up_weight.shape[1]
    stride = count // (KEYS // seg_span)
    stride_two = count // (KEYS // seq_count)
    groups, groups_two = count // stride, count // stride_two
    chunk = max(ROWS, stride_two)
    picked_count = groups_two * heads
    rest_count = count - picked_count
    part = hidden // 4

    def near(*shape):
        return pltpu.VMEM(shape, BF16)

    def attention_work(rows):
        return [pltpu.VMEM((2, rows, KEYS), F32), near(2, rows, KEYS)]

    held_shapes = [near(width, KEYS // 2), pltpu.VMEM((1, 128), F32)]
    small_work = [pltpu.SMEM((heads,), jnp.int32), pltpu.VMEM((width,), F32)]

    (keyval,) = local_call(
        functools.partial(first_keys_kernel, stride=stride),
        [near(1, 2, groups, width)],
        (segment_offset, tokens, attn_gain, key_first, segment_value),
        [near(count, width), near(2, width, width)] + small_work,
        far=(0, 1, 2, 3, 4),
        copies=5,
        flops=2 * heads * groups * width * (count + 2 * width),
        name="first_keys",
    )
    made = {}

    def beside_first(level, held):
        if level == 0:
            made["rows"], made["normed"], made["chooser"], made["back"], held = local_call(
                functools.partial(order_kernel, stride=stride_two, chunk=chunk),
                [
                    near(count, width),
                    near(count, width),
                    near(picked_count, picked_count),
                    near(chunk, chunk),
                ],
                (global_offset, tokens, attn_gain),
                [near(count, width)] + small_work,
                far=(0, 1, 2),
                copies=3,
                relay=held,
                flops=2 * count * width * chunk,
                name="order",
            )
        if level == min(1, seg_span.bit_length() - 2):
            made["picked"], made["rest"], made["peaks"], held = local_call(
                functools.partial(first_query_kernel, heads=heads),
                [near(picked_count, width), near(rest_count, width), pltpu.VMEM((1, 128), F32)],
                (made["normed"], query_first),
                [],
                relay=held,
                flops=2 * count * width * width,
                name="first_query",
            )
        if level == seg_span.bit_length() - 2:
            made["picked_early"], made["rest_early"], made["turned"], made["key_peaks"] = local_call(
                functools.partial(near_weights_kernel, heads=heads),
                [near(heads, picked_count, KEYS // 2), near(heads, rest_count, KEYS // 2)]
                + held_shapes,
                (made["picked"], made["rest"], held),
                [pltpu.VMEM((2, rest_count, KEYS), F32)],
                flops=2 * 256 * KEYS // 2 * heads * count,
                name="near_weights",
            )
        return held

    keyval, keyval_far = exchange(keyval, seg_span, beside_first)
    rows = made["rows"]
    query_peaks, near_held = made["peaks"], (made["turned"], made["key_peaks"])
    row_flops = 2 * width * (2 * hidden + width) + 4 * 256 * KEYS * heads
    picked_second, picked_normed, keyval_two, turned, peaks = local_call(
        functools.partial(picked_kernel, heads=heads),
        [
            near(picked_count, width),
            near(picked_count, width),
            near(1, 2, groups_two, width),
        ]
        + held_shapes,
        (
            made["chooser"],
            rows,
            made["picked"],
            query_peaks,
            made["picked_early"],
            keyval,
            keyval_far,
            *near_held,
            output_first,
            mlp_gain,
            up_weight,
            down_weight,
            second_gain,
            key_second,
            value_second,
        ),
        [near(2, width, width), near(picked_count, width)]
        + attention_work(picked_count)
        + [near(picked_count, width), pltpu.VMEM((2, picked_count, part), F32)]
        + [near(2, picked_count, part), pltpu.VMEM((picked_count, width), F32)],
        far=(14, 15),
        copies=2,
        flops=row_flops * picked_count,
        name="layer_of_picked",
    )
    seconds = [picked_second]

    def rest_attention(held):
        made["mixed"], held = local_call(
            functools.partial(rest_attention_kernel, heads=heads),
            [near(rest_count, width)],
            (
                made["rest"],
                query_peaks,
                made["rest_early"],
                keyval,
                keyval_far,
                made["turned"],
                turned,
                peaks,
            ),
            attention_work(rest_count),
            relay=held,
            flops=4 * 256 * KEYS * heads * rest_count,
            name="rest_attention",
        )
        return held

    half = hidden // 4 * 3

    def rest_up(held):
        made["first"], made["normed"], made["inner"], held = local_call(
            rest_up_kernel,
            [near(rest_count, width), near(rest_count, width), near(rest_count, half)],
            (rows, made["mixed"], output_first, mlp_gain, up_weight),
            [pltpu.VMEM((2, rest_count, part), F32)],
            relay=held,
            flops=2 * width * (half + width) * rest_count,
            name="rest_up",
        )
        return held

    def rest_down(held):
        result, held = local_call(
            rest_down_kernel,
            [near(rest_count, width)],
            (made["first"], made["normed"], made["inner"], up_weight, down_weight),
            [pltpu.VMEM((1, rest_count, part), F32), near(rest_count, hidden - half)],
            relay=held,
            flops=2 * width * (2 * hidden - half) * rest_count,
            name="rest_down",
        )
        seconds.append(result)
        return held

    def picked_query(held):
        made["picked_two"], made["picked_peaks"], held = local_call(
            functools.partial(picked_query_kernel, heads=heads),
            [near(picked_count, width), pltpu.VMEM((1, 128), F32)],
            (picked_normed, query_second),
            [],
            relay=held,
            flops=2 * picked_count * width * width,
            name="picked_query",
        )
        return held

    def rest_query(held):
        made["query_two"], made["peaks_two"], held = local_call(
            functools.partial(rest_query_kernel, heads=heads),
            [near(count, width), pltpu.VMEM((1, 128), F32)],
            (made["picked_two"], made["picked_peaks"], seconds[1], second_gain, query_second),
            [near(rest_count, width)],
            relay=held,
            flops=2 * rest_count * width * width,
            name="rest_query",
        )
        return held

    tasks = [[rest_attention], [rest_up, picked_query], [rest_down], [rest_query]]
    levels = seq_count.bit_length() - 1

    def beside_second(level, held):
        for work in tasks[len(tasks) * level // levels : len(tasks) * (level + 1) // levels]:
            for task in work:
                held = task(held)
        return held

    keyval_two, keyval_two_far = exchange(keyval_two, seq_count, beside_second)
    (encoded,) = local_call(
        functools.partial(second_kernel, heads=heads, parts=len(seconds)),
        [jax.ShapeDtypeStruct((count, width), BF16)],
        (
            made["back"],
            *seconds,
            made["query_two"],
            made["peaks_two"],
            keyval_two,
            keyval_two_far,
            output_second,
        ),
        held_shapes[:1] * 2
        + [near(1, width, width)]
        + [near(count, width)] * 3
        + attention_work(count),
        far=(len(seconds) + 5,),
        out_near=False,
        copies=1 + count // chunk,
        flops=count * (2 * width * width + 4 * 256 * KEYS * heads),
        name="second_attention",
    )
    return encoded


def solution(mesh):
    placed = (
        P(("slides", "seq", "mp"), None),
        P(),
        P(None, "mp"),
        P(None, "mp"),
        P(None, "mp"),
        P("mp", None),
        P(),
        P(None, "mp"),
        P("mp", None),
        P(),
        P(None, "mp"),
        P(None, "mp"),
        P(None, "mp"),
        P("mp", None),
        P("mp"),
        P("mp"),
    )
    fits = mesh.shape["mp"] == 1 and mesh.shape["seq"] in (2, 4, 8, 16)
    return jax.shard_map(
        whole_body if fits else split_body,
        mesh=mesh,
        in_specs=placed,
        out_specs=P(("slides", "seq", "mp"), None),
        check_vma=False,
    )
```

```python
import functools
import math

import jax
import jax.numpy as jnp
from jax import lax
from jax.experimental import pallas as pl
from jax.experimental.pallas import tpu as pltpu
from jax.sharding import PartitionSpec as P

KEYS = 256
SEG_MAX = 16
ROWS = 256
LOG2E = 1.4426950408889634
BF16 = jnp.bfloat16
F32 = jnp.float32
VMEM_LIMIT = 22 * 1024 * 1024


def swapped(x, axis, apart):
    return lax.ppermute(x, axis, [(i, i ^ 1 << apart) for i in range(lax.axis_size(axis))])


def norm_rows(values, gain):
    center = values - jnp.mean(values, axis=-1, keepdims=True)
    spread = jnp.mean(center * center, axis=-1, keepdims=True)
    return (center * lax.rsqrt(spread + 1e-05) * gain).astype(jnp.bfloat16)


def pick_keys(hidden, offsets, stride, key_weight, value_weight):
    token_count, width = hidden.shape
    head_count = offsets.shape[0]
    head_size = key_weight.shape[1] // head_count
    grouped_rows = hidden.reshape(token_count // stride, stride, width)
    dilation_selector = (
        lax.broadcasted_iota(jnp.int32, (stride, head_count), 0) == offsets[None, :]
    ).astype(jnp.bfloat16)
    chosen = jnp.einsum(
        "nof,oj->njf", grouped_rows, dilation_selector, preferred_element_type=jnp.float32
    ).astype(jnp.bfloat16)
    key_heads = jnp.einsum(
        "xkr,rkf->xkf",
        chosen,
        key_weight.reshape(width, head_count, head_size),
        preferred_element_type=jnp.float32,
    ).astype(jnp.bfloat16)
    value_heads = jnp.einsum(
        "xkr,rkf->xkf",
        chosen,
        value_weight.reshape(width, head_count, head_size),
        preferred_element_type=jnp.float32,
    ).astype(jnp.bfloat16)
    picked = token_count // stride
    return jnp.stack(
        [
            key_heads.reshape(picked, head_count * head_size),
            value_heads.reshape(picked, head_count * head_size),
        ]
    )


def attend_local(query, keyval, head_count):
    token_count, width = query.shape
    head_size = width // head_count
    query_heads = query.reshape(token_count, head_count, head_size)
    key_heads = keyval[0].reshape(-1, head_count, head_size)
    value_heads = keyval[1].reshape(-1, head_count, head_size)
    scores = jnp.einsum(
        "thd,khd->htk", query_heads, key_heads, preferred_element_type=jnp.float32
    ) * head_size ** (-0.5)
    highest = jnp.max(scores, axis=-1, keepdims=True)
    weights = jnp.exp(scores - highest)
    weights = (weights / jnp.sum(weights, axis=-1, keepdims=True)).astype(jnp.bfloat16)
    mixed = jnp.einsum(
        "htk,khd->thd", weights, value_heads, preferred_element_type=jnp.float32
    ).astype(jnp.bfloat16)
    return mixed.reshape(token_count, width)


def merge_branch_pair(mine, other, level, token_position):
    lower = token_position >> level & 1 == 0
    return jnp.where(
        lower, jnp.concatenate((mine, other), axis=1), jnp.concatenate((other, mine), axis=1)
    )


def spread_segment(keyval, seg_span, token_position):
    for level in range(seg_span.bit_length() - 1):
        partner = swapped(keyval, "seq", level)
        keyval = merge_branch_pair(keyval, partner, level, token_position)
    return keyval


def spread_global(keyval_two):
    keyval_two = lax.all_gather(keyval_two, "seq", axis=1, tiled=True)
    return keyval_two


def combine(partial_value, residual_full, need_full):
    row_count = residual_full.shape[0] // lax.axis_size("mp")
    row_start = lax.axis_index("mp") * row_count
    share = lax.psum_scatter(partial_value, "mp", scatter_dimension=0, tiled=True)
    own_rows = lax.dynamic_slice_in_dim(residual_full, row_start, row_count, 0)
    own_rows = (own_rows.astype(jnp.float32) + share).astype(jnp.bfloat16)
    full_rows = lax.all_gather(own_rows, "mp", axis=0, tiled=True) if need_full else own_rows
    return (own_rows, full_rows)


def split_body(
    tokens,
    attn_gain,
    query_first,
    key_first,
    segment_value,
    output_first,
    mlp_gain,
    up_weight,
    down_weight,
    second_gain,
    query_second,
    key_second,
    value_second,
    output_second,
    segment_offset,
    global_offset,
):
    seq_count = lax.axis_size("seq")
    token_position = lax.axis_index("seq")
    seg_span = min(SEG_MAX, seq_count)
    head_count = segment_offset.shape[0]
    full_rows = lax.all_gather(tokens, "mp", axis=0, tiled=True)
    token_count = full_rows.shape[0]
    hidden = norm_rows(full_rows.astype(jnp.float32), attn_gain)
    query = jnp.dot(hidden, query_first, preferred_element_type=jnp.float32).astype(jnp.bfloat16)
    seg_stride = token_count // (KEYS // seg_span)
    keyval = pick_keys(hidden, segment_offset, seg_stride, key_first, segment_value)
    keyval = spread_segment(keyval, seg_span, token_position)
    mixed = attend_local(query, keyval, head_count)
    partial_value = jnp.dot(mixed, output_first, preferred_element_type=jnp.float32)
    own_rows, first_rows = combine(partial_value, full_rows, True)
    normed = norm_rows(first_rows.astype(jnp.float32), mlp_gain)
    inner = jax.nn.gelu(
        jnp.dot(normed, up_weight, preferred_element_type=jnp.float32), approximate=True
    ).astype(jnp.bfloat16)
    partial_value = jnp.dot(inner, down_weight, preferred_element_type=jnp.float32)
    own_rows, second_rows = combine(partial_value, first_rows, True)
    hidden_two = norm_rows(second_rows.astype(jnp.float32), second_gain)
    query_two = jnp.dot(hidden_two, query_second, preferred_element_type=jnp.float32).astype(
        jnp.bfloat16
    )
    glob_stride = token_count // (KEYS // seq_count)
    keyval_two = pick_keys(hidden_two, global_offset, glob_stride, key_second, value_second)
    keyval_two = spread_global(keyval_two)
    mixed_two = attend_local(query_two, keyval_two, head_count)
    partial_value = jnp.dot(mixed_two, output_second, preferred_element_type=jnp.float32)
    own_rows, unused_rows = combine(partial_value, second_rows, False)
    return own_rows


def one_hot(condition):
    return jnp.where(condition, 1.0, 0.0).astype(BF16)


def dot(left, right):
    return jnp.dot(left, right, preferred_element_type=F32)


def pieces(count, size):
    size = size if count % size == 0 else count
    return [slice(start, start + size) for start in range(0, count, size)]


def norm_into(out, start, source, gain, count):
    for span in pieces(count, 64):
        out[start + span.start : start + span.stop, :] = norm_rows(
            source[span, :].astype(F32), gain
        )


def bring(source, target, sem):
    copy = pltpu.make_async_copy(source, target, sem)
    copy.start()
    return copy


def pick_matrix(offsets, heads, groups, stride):
    count = groups * stride
    place = lax.broadcasted_iota(jnp.int32, (groups, count), 1)
    place = place - lax.broadcasted_iota(jnp.int32, (groups, count), 0) * stride
    return jnp.concatenate([one_hot(place == offsets[h]) for h in range(heads)], axis=0)


def project_keys(chosen, heads, weights, keyval_ref):
    rows, width = chosen.shape
    groups, head_size = rows // heads, width // heads
    for slot, weight in enumerate(weights):
        held = weight()
        for span in pieces(width, 256):
            first, last = span.start // head_size, (span.stop - 1) // head_size + 1
            wide = dot(chosen[first * groups : last * groups], held[:, span])
            column = lax.broadcasted_iota(jnp.int32, (groups, span.stop - span.start), 1)
            total = wide[:groups]
            for h in range(first + 1, last):
                row = (h - first) * groups
                own = column >= h * head_size - span.start
                total = jnp.where(own, wide[row : row + groups], total)
            total = total.astype(BF16)
            for copy in range(keyval_ref.shape[0]):
                keyval_ref[copy, slot, :, span] = total


def ranks(offsets, chunk, stride, share, axis):
    heads = offsets.shape[0]

    def places(way):
        shape = (1, chunk) if way else (chunk, 1)
        place = lax.broadcasted_iota(jnp.int32, shape, way)
        inside = lax.rem(place, stride)
        taken = inside == offsets[0]
        for h in range(1, heads):
            taken = taken | (inside == offsets[h])
        return place, inside, jnp.where(taken, inside, inside + stride)

    place, inside, order = places(axis)
    other_place, _, other_order = places(1 - axis)
    ahead = (other_order < order) & (lax.div(other_place, stride) == lax.div(place, stride))
    rank = jnp.sum(jnp.where(ahead, 1, 0), axis=1 - axis, keepdims=True)
    group = lax.div(place, stride)
    return jnp.where(
        rank < heads, group * heads + rank, share + group * (stride - heads) + rank - heads
    )


def slots_of(offsets, heads):
    values = [offsets[h] for h in range(heads)]
    fresh = []
    for h in range(heads):
        seen = jnp.int32(1)
        for earlier in values[:h]:
            seen = jnp.where(earlier == values[h], 0, seen)
        fresh.append(seen)
    slots = []
    for h in range(heads):
        slot = jnp.int32(0)
        for other in range(heads):
            slot = slot + jnp.where(values[other] < values[h], fresh[other], 0)
        slots.append(slot)
    return slots


def first_keys_kernel(
    offsets, tokens, gain, key_weight, value_weight, keyval, rows, wide, picks, scale, sems, *, stride
):
    copies = [
        bring(offsets, picks, sems.at[0]),
        bring(tokens, rows, sems.at[1]),
        bring(gain, scale, sems.at[2]),
        bring(key_weight, wide.at[0], sems.at[3]),
        bring(value_weight, wide.at[1], sems.at[4]),
    ]
    heads = offsets.shape[0]
    copies[0].wait()
    chooser = pick_matrix(picks, heads, rows.shape[0] // stride, stride)
    copies[1].wait()
    copies[2].wait()
    chosen = norm_rows(dot(chooser, rows[...]), scale[...])

    def weight(slot):
        copies[slot + 3].wait()
        return wide[slot]

    project_keys(
        chosen, heads, [functools.partial(weight, slot) for slot in range(2)], keyval
    )


def order_kernel(
    offsets,
    tokens,
    gain,
    moved_rows,
    normed,
    chooser,
    back,
    rows,
    picks,
    scale,
    sems,
    *,
    stride,
    chunk,
):
    copies = [
        bring(offsets, picks, sems.at[0]),
        bring(tokens, rows, sems.at[1]),
        bring(gain, scale, sems.at[2]),
    ]
    count = tokens.shape[0]
    share = chunk // stride * offsets.shape[0]
    rest = chunk - share
    picked = count // chunk * share
    copies[0].wait()
    mover = one_hot(
        lax.broadcasted_iota(jnp.int32, (chunk, chunk), 0)
        == ranks(picks, chunk, stride, share, 1)
    )
    heads = offsets.shape[0]
    chooser[...] = pick_matrix(slots_of(picks, heads), heads, picked // heads, heads)
    back[...] = one_hot(
        lax.broadcasted_iota(jnp.int32, (chunk, chunk), 1)
        == ranks(picks, chunk, stride, share, 0)
    )
    copies[1].wait()
    copies[2].wait()
    for c in range(count // chunk):
        moved = dot(mover, rows[c * chunk : (c + 1) * chunk, :]).astype(BF16)
        moved_rows[c * share : (c + 1) * share, :] = moved[:share]
        moved_rows[picked + c * rest : picked + (c + 1) * rest, :] = moved[share:]
    norm_into(normed, 0, moved_rows, scale[...], count)


def scaled_query(normed, weight, outs, heads, peaks):
    width = normed.shape[1]
    factor = (width // heads) ** (-0.5) * LOG2E
    peak = None
    for out, row in outs:
        for span in pieces(out.shape[0], 512 if out.shape[0] % 512 == 0 else 256):
            query = dot(normed[row + span.start : row + span.stop, :], weight[...]) * factor
            out[span, :] = query.astype(BF16)
            for part in pieces(query.shape[0], 64):
                square = query[part] * query[part]
                peak = square if peak is None else jnp.maximum(peak, square)
    peaks[...] = summed_peaks(peak.astype(BF16), heads)


def first_query_kernel(normed, weight, picked, rest, peaks, sems, *, heads):
    del sems
    scaled_query(normed, weight, [(picked, 0), (rest, picked.shape[0])], heads, peaks)


def head_windows(head_size, width):
    period = min(width, math.lcm(head_size, 128))
    windows = []
    for h in range(period // head_size):
        start = h * head_size // 128 * 128
        stop = min(period, -(-(h + 1) * head_size // 128) * 128)
        windows.append((start, stop - start))
    return period, windows


def summed_peaks(peak, heads):
    width = peak.shape[1]
    column = lax.broadcasted_iota(jnp.int32, (width, 128), 0)
    head = lax.broadcasted_iota(jnp.int32, (width, 128), 1)
    low = head * (width // heads)
    sums = one_hot((column >= low) & (column < low + width // heads))
    return jnp.max(dot(peak, sums), axis=0, keepdims=True)


def load_keys(keyval, turned):
    keys = jnp.concatenate([keyval[i, 0] for i in range(keyval.shape[0])], axis=0)
    turned[...] = keys.T
    return keys * keys


def small_scores(query_peaks, key_peaks):
    return jnp.max(query_peaks[...] * key_peaks[...]) < 9000.0


def reciprocal(x):
    guess = pl.reciprocal(x, approx=True)
    return guess * (2.0 - x * guess)


def padded_keys(turned, base, head, head_size, start, size):
    low = base + head * head_size
    rows = pl.ds(low if isinstance(low, int) else pl.multiple_of(low, 16), head_size)
    own = jnp.concatenate([part[rows, :] for part in turned], axis=1)
    low = head * head_size - start
    parts = [own]
    if low:
        parts.insert(0, jnp.zeros((low, own.shape[1]), BF16))
    if low + head_size < size:
        parts.append(jnp.zeros((size - low - head_size, own.shape[1]), BF16))
    return jnp.concatenate(parts, axis=0)


def score_pair(query, span, base, head, head_size, windows, turned):
    start = windows[head][0]
    size = windows[head + 1][0] + windows[head + 1][1] - start
    keys = [padded_keys([turned], base, head + i, head_size, start, size) for i in range(2)]
    return dot(query[span, pl.ds(base + start, size)], jnp.concatenate(keys, axis=1))


def near_weights_kernel(
    picked, rest, keyval, picked_early, rest_early, turned, peaks, scores_ref, sems, *, heads
):
    del sems
    peaks[...] = summed_peaks(load_keys(keyval, turned), heads)
    width = picked.shape[1]
    head_size = width // heads
    key_count = turned.shape[1]
    period, windows = head_windows(head_size, width)
    jobs = [
        (query, early, head)
        for query, early in ((picked, picked_early), (rest, rest_early))
        for head in range(0, len(windows), 2)
    ]

    @pl.loop(0, width // period)
    def _(turn):
        base = pl.multiple_of(turn * period, 128)

        def score(i):
            query, _, head = jobs[i]
            rows = query.shape[0]
            scores_ref[i % 2, :rows] = score_pair(
                query, slice(0, rows), base, head, head_size, windows, turned
            )

        score(0)
        for i, (query, early, head) in enumerate(jobs):
            if i + 1 < len(jobs):
                score(i + 1)
            for part in pieces(query.shape[0], 64):
                weights = jnp.exp2(scores_ref[i % 2, part, :]).astype(BF16)
                for j in range(2):
                    early[turn * len(windows) + head + j, part, :] = weights[
                        :, j * key_count : (j + 1) * key_count
                    ]


def attend_rows(
    query, first_row, rows, heads, turned, keyvals, mixed_ref, mixed_row, work, plain, early=None
):
    scores_ref, weights_ref = work
    width = query.shape[1]
    key_count = sum(part.shape[1] for part in turned)
    head_size = width // heads
    period, windows = head_windows(head_size, width)
    span = pl.ds(first_row, rows)
    out_span = pl.ds(mixed_row, rows)
    lane = lax.broadcasted_iota(jnp.int32, (1, 128), 1)
    step = 2 if early is not None else 1

    def take_turn(turn):
        base = turn * period if plain else pl.multiple_of(turn * period, 128)
        sums = {}

        def score(i):
            if early is not None:
                scores = score_pair(query, span, base, 2 * i, head_size, windows, turned[1])
            else:
                start, size = windows[i]
                scores = dot(
                    query[span, pl.ds(base + start, size)],
                    padded_keys(turned, base, i, head_size, start, size),
                )
            scores_ref[i % 2, :rows] = scores

        def weigh(h):
            for part in pieces(rows, 64):
                scores = scores_ref[h % 2, part, :]
                if not plain:
                    scores = scores - jnp.max(scores, axis=1, keepdims=True)
                weights_ref[h % 2, part, :] = jnp.exp2(scores).astype(BF16)

        def mix(h):
            start, size = windows[h]
            low = h * head_size - start
            values = jnp.concatenate(
                [
                    x[i, 1, :, pl.ds(base + start, size)]
                    for x in keyvals
                    for i in range(x.shape[0])
                ],
                axis=0,
            )
            column = lax.broadcasted_iota(jnp.int32, (key_count, size), 1)
            own = (column >= low) & (column < low + head_size)
            values = jnp.where(own, values, jnp.ones((), BF16))
            if early is not None:
                half = key_count // 2
                far = weights_ref[h // 2 % 2, :rows, h % 2 * half : (h % 2 + 1) * half]
                near = early[turn * len(windows) + h, span, :]
                weights = jnp.concatenate([near, far], axis=1)
            else:
                weights = weights_ref[h % 2, :rows]
            mixed = dot(weights, values)
            for offset in range(0, size, 128):
                own = mixed[:, offset : offset + 128]
                total = pltpu.roll(own, 64, 1)
                at = start + offset
                if at in sums:
                    mine = lane >= h * head_size - at
                    own = jnp.where(mine, own, sums[at][0])
                    total = jnp.where(mine, total, sums[at][1])
                sums[at] = own, total
                if (h + 1) * head_size >= at + 128:
                    own, total = sums.pop(at)
                    mixed_ref[out_span, pl.ds(base + at, 128)] = (
                        own * reciprocal(total)
                    ).astype(BF16)

        count = len(windows) // step
        score(0)
        for i in range(count):
            if i:
                for h in range((i - 1) * step, i * step):
                    mix(h)
            if i + 1 < count:
                score(i + 1)
            weigh(i)
        for h in range((count - 1) * step, count * step):
            mix(h)

    if plain:
        for turn in range(width // period):
            take_turn(turn)
    else:
        pl.loop(0, width // period)(take_turn)


def attend(query, rows, heads, turned, keyvals, mixed_ref, work, small, early=None):
    size = math.gcd(rows, ROWS)

    @pl.when(small)
    def _():
        attend_rows(query, 0, rows, heads, turned, keyvals, mixed_ref, 0, work, True, early)

    @pl.when(jnp.logical_not(small))
    def _():
        @pl.loop(0, rows // size)
        def _(step):
            row = pl.multiple_of(step * size, size)
            attend_rows(
                query,
                row,
                size,
                heads,
                turned,
                keyvals,
                mixed_ref,
                row,
                work,
                False,
            )


def gelu(x):
    half = 0.5 * x
    return half + half * jnp.tanh(x * (0.7978845608028654 + 0.035677408136300125 * (x * x)))


def widen(normed, up_weight, low, wide_ref, inner):
    rows = normed.shape[0]
    spans = pieces(inner.shape[1], wide_ref.shape[2])

    def product(i):
        columns = slice(low + spans[i].start, low + spans[i].stop)
        wide_ref[i % 2] = dot(normed[...], up_weight[:, columns])

    product(0)
    for i, span in enumerate(spans):
        if i + 1 < len(spans):
            product(i + 1)
        for part in pieces(rows, 32):
            inner[part, span] = gelu(wide_ref[i % 2, part, :]).astype(BF16)


def feed_forward(normed, up_weight, down_weight, total, wide_ref, inner):
    rows = normed.shape[0]
    spans = pieces(up_weight.shape[1], wide_ref.shape[2])

    def product(i):
        wide_ref[i % 2] = dot(normed[...], up_weight[:, spans[i]])

    product(0)
    for i, span in enumerate(spans):
        if i + 1 < len(spans):
            product(i + 1)
        for part in pieces(rows, 32):
            inner[i % 2, part, :] = gelu(wide_ref[i % 2, part, :]).astype(BF16)
        total[...] += dot(inner[i % 2], down_weight[span, :])


def narrow(inners, down_weight, first, second, size):
    for span in pieces(second.shape[1], size):
        total = first[:, span].astype(F32)
        low = 0
        for inner in inners:
            high = low + inner.shape[1]
            total = total + dot(inner[...], down_weight[low:high, span])
            low = high
        second[:, span] = total.astype(BF16)


def add_heads(tokens, first_row, mixed, out_weight, gain, first, normed):
    before = None
    for span in pieces(mixed.shape[0], 256):
        total = dot(mixed[span, :], out_weight[...])
        rows = tokens[first_row + span.start : first_row + span.stop, :]
        first[span, :] = (rows.astype(F32) + total).astype(BF16)
        if before is not None:
            norm_into(normed, before.start, first.at[before], gain, before.stop - before.start)
        before = span
    norm_into(normed, before.start, first.at[before], gain, before.stop - before.start)


def picked_kernel(
    chooser,
    tokens,
    query,
    query_peaks,
    early,
    keyval,
    keyval_far,
    turned_near,
    peaks_near,
    out_weight,
    mlp_gain,
    up_weight,
    down_weight,
    gain,
    key_weight,
    value_weight,
    second,
    normed,
    keyval_two,
    turned,
    peaks,
    held,
    mixed,
    scores,
    weights,
    first,
    wide,
    inner,
    total,
    sems,
    *,
    heads,
):
    copies = [
        bring(x, held.at[i], sems.at[i]) for i, x in enumerate((key_weight, value_weight))
    ]
    rows = second.shape[0]
    keyvals = (keyval, keyval_far)
    squares = load_keys(keyval_far, turned)
    peaks[...] = jnp.maximum(peaks_near[...], summed_peaks(squares, heads))
    small = small_scores(query_peaks, peaks)
    attend(
        query,
        rows,
        heads,
        (turned_near, turned),
        keyvals,
        mixed,
        (scores, weights),
        small,
        early,
    )
    add_heads(tokens, 0, mixed, out_weight, mlp_gain[...], first, normed)
    total[...] = first[...].astype(F32)
    feed_forward(normed, up_weight, down_weight, total, wide, inner)
    second[...] = total[...].astype(BF16)
    norm_into(normed, 0, second, gain[...], rows)
    chosen = dot(chooser[...], normed[...]).astype(BF16)

    def weight(slot):
        copies[slot].wait()
        return held[slot]

    project_keys(
        chosen, heads, [functools.partial(weight, slot) for slot in range(2)], keyval_two
    )


def rest_attention_kernel(
    query,
    query_peaks,
    early,
    keyval,
    keyval_far,
    turned_near,
    turned,
    peaks,
    mixed,
    scores,
    weights,
    sems,
    *,
    heads,
):
    del sems
    attend(
        query,
        mixed.shape[0],
        heads,
        (turned_near, turned),
        (keyval, keyval_far),
        mixed,
        (scores, weights),
        small_scores(query_peaks, peaks),
        early,
    )


def rest_up_kernel(
    tokens, mixed, out_weight, gain, up_weight, first, normed, inner, wide, sems
):
    del sems
    add_heads(
        tokens, tokens.shape[0] - mixed.shape[0], mixed, out_weight, gain[...], first, normed
    )
    widen(normed, up_weight, 0, wide, inner)


def rest_down_kernel(
    first, normed, inner, up_weight, down_weight, second, wide, inner_more, sems
):
    del sems
    widen(normed, up_weight, inner.shape[1], wide, inner_more)
    narrow([inner, inner_more], down_weight, first, second, 256)


def picked_query_kernel(normed, weight, query, peaks, sems, *, heads):
    del sems
    scaled_query(normed, weight, [(query, 0)], heads, peaks)


def rest_query_kernel(
    picked, picked_peaks, rows, gain, weight, query, peaks, normed, sems, *, heads
):
    del sems
    start = picked.shape[0]
    query[:start, :] = picked[...]
    norm_into(normed, 0, rows, gain[...], rows.shape[0])
    out = query.at[pl.ds(start, rows.shape[0])]
    scaled_query(normed, weight, [(out, 0)], heads, peaks)
    peaks[...] = jnp.maximum(peaks[...], picked_peaks[...])


def second_kernel(*refs, heads, parts):
    back, *rows = refs[: 1 + parts]
    query, query_peaks, keyval, keyval_far, out_weight, encoded = refs[1 + parts : 7 + parts]
    turned_near, turned, held, mixed = refs[7 + parts : 11 + parts]
    result, ready, scores, weights, sems = refs[11 + parts :]
    copy = bring(out_weight, held.at[0], sems.at[0])
    keyvals = (keyval, keyval_far)
    squares = jnp.maximum(load_keys(keyval, turned_near), load_keys(keyval_far, turned))
    count = query.shape[0]
    small = small_scores(query_peaks, summed_peaks(squares, heads))
    attend(
        query, count, heads, (turned_near, turned), keyvals, mixed, (scores, weights), small
    )
    chunk = back.shape[0]
    share = rows[0].shape[0] * chunk // count
    rest_share = chunk - share
    copy.wait()
    start = 0
    for part in rows:
        span = slice(start, start + part.shape[0])
        total = part[...].astype(F32) + dot(mixed[span, :], held[0])
        result[span, :] = total.astype(BF16)
        start += part.shape[0]
    start = count // chunk * share
    copies = []
    for c in range(count // chunk):
        far = start + c * rest_share
        blend = jnp.concatenate(
            [result[c * share : (c + 1) * share, :], result[far : far + rest_share, :]], axis=0
        )
        span = pl.ds(c * chunk, chunk)
        ready[span, :] = dot(back[...], blend).astype(BF16)
        copies.append(bring(ready.at[span], encoded.at[span], sems.at[1 + c]))
    for copy in copies:
        copy.wait()


def relaying(kernel, ins, outs, *refs):
    end = ins + 1 + outs
    refs[end][...] = refs[ins][...]
    kernel(*refs[:ins], *refs[ins + 1 : end], *refs[end + 1 :])


def local_call(kernel, outs, inputs, scratch, scalars=0, far=(), relay=None, out_near=True, copies=1, flops=0, name=None):
    outs, inputs = list(outs), list(inputs)
    if relay is not None:
        kernel = functools.partial(relaying, kernel, len(inputs), len(outs))
        inputs.append(relay)
        outs.append(pltpu.VMEM(relay.shape, relay.dtype))
    specs, placed = [], []
    for i, x in enumerate(inputs):
        if i < scalars:
            specs.append(pl.BlockSpec(memory_space=pltpu.SMEM))
        elif i in far:
            specs.append(pl.BlockSpec(memory_space=pltpu.HBM))
            x = pltpu.with_memory_space_constraint(x, pltpu.HBM)
        else:
            specs.append(pl.BlockSpec(memory_space=pltpu.VMEM))
            x = pltpu.with_memory_space_constraint(x, pltpu.VMEM)
        placed.append(x)
    return pl.pallas_call(
        kernel,
        out_shape=outs,
        in_specs=specs,
        out_specs=[
            pl.BlockSpec(memory_space=pltpu.VMEM if out_near else pltpu.HBM)
        ] * len(outs),
        scratch_shapes=list(scratch) + [pltpu.SemaphoreType.DMA((copies,))],
        compiler_params=pltpu.CompilerParams(vmem_limit_bytes=VMEM_LIMIT),
        cost_estimate=pl.CostEstimate(
            flops=int(flops),
            transcendentals=0,
            bytes_accessed=sum(inputs[i].size * inputs[i].dtype.itemsize for i in far),
        ),
        name=name,
    )(*placed)


def exchange(keyval, span, beside):
    size = lax.axis_size("seq")
    levels = span.bit_length() - 1
    even = list(range(levels - 1, 0, -1))
    orders = (even, even[-1:] + even[:-1])
    for step in range(levels - 1):
        pairs = [(i, i ^ 1 << orders[i % 2][step]) for i in range(size)]
        partner = lax.ppermute(keyval, "seq", pairs)
        keyval = jnp.concatenate([beside(step, keyval), partner], axis=0)
    far = swapped(keyval, "seq", 0)
    return beside(levels - 1, keyval), far


def early_exchange(keyval, span, beside):
    levels = span.bit_length() - 1
    crossed, fresh = [], keyval
    for level in range(levels - 1, 1, -1):
        crossed.append(swapped(fresh, "seq", 1))
        partner = swapped(keyval, "seq", level)
        keyval = jnp.concatenate([beside(levels - 1 - level, keyval), partner], axis=0)
        fresh = partner
    if levels > 1:
        crossed.append(swapped(fresh, "seq", 1))
        keyval = jnp.concatenate([beside(levels - 2, keyval), *crossed], axis=0)
    far = swapped(keyval, "seq", 0)
    return beside(levels - 1, keyval), far


def whole_body(
    tokens,
    attn_gain,
    query_first,
    key_first,
    segment_value,
    output_first,
    mlp_gain,
    up_weight,
    down_weight,
    second_gain,
    query_second,
    key_second,
    value_second,
    output_second,
    segment_offset,
    global_offset,
):
    seq_count = lax.axis_size("seq")
    seg_span = min(SEG_MAX, seq_count)
    heads = segment_offset.shape[0]
    count, width = tokens.shape
    head_size = width // heads
    hidden = up_weight.shape[1]
    stride = count // (KEYS // seg_span)
    stride_two = count // (KEYS // seq_count)
    groups, groups_two = count // stride, count // stride_two
    chunk = max(ROWS, stride_two)
    picked_count = groups_two * heads
    rest_count = count - picked_count
    part = hidden // 4

    def near(*shape):
        return pltpu.VMEM(shape, BF16)

    def attention_work(rows):
        return [pltpu.VMEM((2, rows, KEYS), F32), near(2, rows, KEYS)]

    held_shapes = [near(width, KEYS // 2), pltpu.VMEM((1, 128), F32)]
    small_work = [pltpu.SMEM((heads,), jnp.int32), pltpu.VMEM((width,), F32)]

    (keyval,) = local_call(
        functools.partial(first_keys_kernel, stride=stride),
        [near(1, 2, groups, width)],
        (segment_offset, tokens, attn_gain, key_first, segment_value),
        [near(count, width), near(2, width, width)] + small_work,
        far=(0, 1, 2, 3, 4),
        copies=5,
        flops=2 * heads * groups * width * (count + 2 * width),
        name="first_keys",
    )
    made = {}

    def beside_first(level, held):
        if level == 0:
            made["rows"], made["normed"], made["chooser"], made["back"], held = local_call(
                functools.partial(order_kernel, stride=stride_two, chunk=chunk),
                [
                    near(count, width),
                    near(count, width),
                    near(picked_count, picked_count),
                    near(chunk, chunk),
                ],
                (global_offset, tokens, attn_gain),
                [near(count, width)] + small_work,
                far=(0, 1, 2),
                copies=3,
                relay=held,
                flops=2 * count * width * chunk,
                name="order",
            )
        if level == min(1, seg_span.bit_length() - 2):
            made["picked"], made["rest"], made["peaks"], held = local_call(
                functools.partial(first_query_kernel, heads=heads),
                [near(picked_count, width), near(rest_count, width), pltpu.VMEM((1, 128), F32)],
                (made["normed"], query_first),
                [],
                relay=held,
                flops=2 * count * width * width,
                name="first_query",
            )
        if level == seg_span.bit_length() - 2:
            made["picked_early"], made["rest_early"], made["turned"], made["key_peaks"] = local_call(
                functools.partial(near_weights_kernel, heads=heads),
                [near(heads, picked_count, KEYS // 2), near(heads, rest_count, KEYS // 2)]
                + held_shapes,
                (made["picked"], made["rest"], held),
                [pltpu.VMEM((2, rest_count, KEYS), F32)],
                flops=2 * 256 * KEYS // 2 * heads * count,
                name="near_weights",
            )
        return held

    keyval, keyval_far = early_exchange(keyval, seg_span, beside_first)
    rows = made["rows"]
    query_peaks, near_held = made["peaks"], (made["turned"], made["key_peaks"])
    row_flops = 2 * width * (2 * hidden + width) + 4 * 256 * KEYS * heads
    picked_second, picked_normed, keyval_two, turned, peaks = local_call(
        functools.partial(picked_kernel, heads=heads),
        [
            near(picked_count, width),
            near(picked_count, width),
            near(1, 2, groups_two, width),
        ]
        + held_shapes,
        (
            made["chooser"],
            rows,
            made["picked"],
            query_peaks,
            made["picked_early"],
            keyval,
            keyval_far,
            *near_held,
            output_first,
            mlp_gain,
            up_weight,
            down_weight,
            second_gain,
            key_second,
            value_second,
        ),
        [near(2, width, width), near(picked_count, width)]
        + attention_work(picked_count)
        + [near(picked_count, width), pltpu.VMEM((2, picked_count, part), F32)]
        + [near(2, picked_count, part), pltpu.VMEM((picked_count, width), F32)],
        far=(14, 15),
        copies=2,
        flops=row_flops * picked_count,
        name="layer_of_picked",
    )
    seconds = [picked_second]

    def rest_attention(held):
        made["mixed"], held = local_call(
            functools.partial(rest_attention_kernel, heads=heads),
            [near(rest_count, width)],
            (
                made["rest"],
                query_peaks,
                made["rest_early"],
                keyval,
                keyval_far,
                made["turned"],
                turned,
                peaks,
            ),
            attention_work(rest_count),
            relay=held,
            flops=4 * 256 * KEYS * heads * rest_count,
            name="rest_attention",
        )
        return held

    half = hidden // 4 * 3

    def rest_up(held):
        made["first"], made["normed"], made["inner"], held = local_call(
            rest_up_kernel,
            [near(rest_count, width), near(rest_count, width), near(rest_count, half)],
            (rows, made["mixed"], output_first, mlp_gain, up_weight),
            [pltpu.VMEM((2, rest_count, part), F32)],
            relay=held,
            flops=2 * width * (half + width) * rest_count,
            name="rest_up",
        )
        return held

    def rest_down(held):
        result, held = local_call(
            rest_down_kernel,
            [near(rest_count, width)],
            (made["first"], made["normed"], made["inner"], up_weight, down_weight),
            [pltpu.VMEM((1, rest_count, part), F32), near(rest_count, hidden - half)],
            relay=held,
            flops=2 * width * (2 * hidden - half) * rest_count,
            name="rest_down",
        )
        seconds.append(result)
        return held

    def picked_query(held):
        made["picked_two"], made["picked_peaks"], held = local_call(
            functools.partial(picked_query_kernel, heads=heads),
            [near(picked_count, width), pltpu.VMEM((1, 128), F32)],
            (picked_normed, query_second),
            [],
            relay=held,
            flops=2 * picked_count * width * width,
            name="picked_query",
        )
        return held

    def rest_query(held):
        made["query_two"], made["peaks_two"], held = local_call(
            functools.partial(rest_query_kernel, heads=heads),
            [near(count, width), pltpu.VMEM((1, 128), F32)],
            (made["picked_two"], made["picked_peaks"], seconds[1], second_gain, query_second),
            [near(rest_count, width)],
            relay=held,
            flops=2 * rest_count * width * width,
            name="rest_query",
        )
        return held

    tasks = [[rest_attention], [rest_up, picked_query], [rest_down], [rest_query]]
    levels = seq_count.bit_length() - 1

    def beside_second(level, held):
        for work in tasks[len(tasks) * level // levels : len(tasks) * (level + 1) // levels]:
            for task in work:
                held = task(held)
        return held

    keyval_two, keyval_two_far = exchange(keyval_two, seq_count, beside_second)
    (encoded,) = local_call(
        functools.partial(second_kernel, heads=heads, parts=len(seconds)),
        [jax.ShapeDtypeStruct((count, width), BF16)],
        (
            made["back"],
            *seconds,
            made["query_two"],
            made["peaks_two"],
            keyval_two,
            keyval_two_far,
            output_second,
        ),
        held_shapes[:1] * 2
        + [near(1, width, width)]
        + [near(count, width)] * 3
        + attention_work(count),
        far=(len(seconds) + 5,),
        out_near=False,
        copies=1 + count // chunk,
        flops=count * (2 * width * width + 4 * 256 * KEYS * heads),
        name="second_attention",
    )
    return encoded


def solution(mesh):
    placed = (
        P(("slides", "seq", "mp"), None),
        P(),
        P(None, "mp"),
        P(None, "mp"),
        P(None, "mp"),
        P("mp", None),
        P(),
        P(None, "mp"),
        P("mp", None),
        P(),
        P(None, "mp"),
        P(None, "mp"),
        P(None, "mp"),
        P("mp", None),
        P("mp"),
        P("mp"),
    )
    fits = mesh.shape["mp"] == 1 and mesh.shape["seq"] in (2, 4, 8, 16)
    return jax.shard_map(
        whole_body if fits else split_body,
        mesh=mesh,
        in_specs=placed,
        out_specs=P(("slides", "seq", "mp"), None),
        check_vma=False,
    )
```

```python
import functools
import math

import jax
import jax.numpy as jnp
from jax import lax
from jax.experimental import pallas as pl
from jax.experimental.pallas import tpu as pltpu
from jax.sharding import PartitionSpec as P

KEYS = 256
SEG_MAX = 16
ROWS = 256
LOG2E = 1.4426950408889634
BF16 = jnp.bfloat16
F32 = jnp.float32
VMEM_LIMIT = 22 * 1024 * 1024


def swapped(x, axis, apart):
    return lax.ppermute(x, axis, [(i, i ^ 1 << apart) for i in range(lax.axis_size(axis))])


def norm_rows(values, gain):
    center = values - jnp.mean(values, axis=-1, keepdims=True)
    spread = jnp.mean(center * center, axis=-1, keepdims=True)
    return (center * lax.rsqrt(spread + 1e-05) * gain).astype(jnp.bfloat16)


def pick_keys(hidden, offsets, stride, key_weight, value_weight):
    token_count, width = hidden.shape
    head_count = offsets.shape[0]
    head_size = key_weight.shape[1] // head_count
    grouped_rows = hidden.reshape(token_count // stride, stride, width)
    dilation_selector = (
        lax.broadcasted_iota(jnp.int32, (stride, head_count), 0) == offsets[None, :]
    ).astype(jnp.bfloat16)
    chosen = jnp.einsum(
        "nof,oj->njf", grouped_rows, dilation_selector, preferred_element_type=jnp.float32
    ).astype(jnp.bfloat16)
    key_heads = jnp.einsum(
        "xkr,rkf->xkf",
        chosen,
        key_weight.reshape(width, head_count, head_size),
        preferred_element_type=jnp.float32,
    ).astype(jnp.bfloat16)
    value_heads = jnp.einsum(
        "xkr,rkf->xkf",
        chosen,
        value_weight.reshape(width, head_count, head_size),
        preferred_element_type=jnp.float32,
    ).astype(jnp.bfloat16)
    picked = token_count // stride
    return jnp.stack(
        [
            key_heads.reshape(picked, head_count * head_size),
            value_heads.reshape(picked, head_count * head_size),
        ]
    )


def attend_local(query, keyval, head_count):
    token_count, width = query.shape
    head_size = width // head_count
    query_heads = query.reshape(token_count, head_count, head_size)
    key_heads = keyval[0].reshape(-1, head_count, head_size)
    value_heads = keyval[1].reshape(-1, head_count, head_size)
    scores = jnp.einsum(
        "thd,khd->htk", query_heads, key_heads, preferred_element_type=jnp.float32
    ) * head_size ** (-0.5)
    highest = jnp.max(scores, axis=-1, keepdims=True)
    weights = jnp.exp(scores - highest)
    weights = (weights / jnp.sum(weights, axis=-1, keepdims=True)).astype(jnp.bfloat16)
    mixed = jnp.einsum(
        "htk,khd->thd", weights, value_heads, preferred_element_type=jnp.float32
    ).astype(jnp.bfloat16)
    return mixed.reshape(token_count, width)


def merge_branch_pair(mine, other, level, token_position):
    lower = token_position >> level & 1 == 0
    return jnp.where(
        lower, jnp.concatenate((mine, other), axis=1), jnp.concatenate((other, mine), axis=1)
    )


def spread_segment(keyval, seg_span, token_position):
    for level in range(seg_span.bit_length() - 1):
        partner = swapped(keyval, "seq", level)
        keyval = merge_branch_pair(keyval, partner, level, token_position)
    return keyval


def spread_global(keyval_two):
    keyval_two = lax.all_gather(keyval_two, "seq", axis=1, tiled=True)
    return keyval_two


def combine(partial_value, residual_full, need_full):
    row_count = residual_full.shape[0] // lax.axis_size("mp")
    row_start = lax.axis_index("mp") * row_count
    share = lax.psum_scatter(partial_value, "mp", scatter_dimension=0, tiled=True)
    own_rows = lax.dynamic_slice_in_dim(residual_full, row_start, row_count, 0)
    own_rows = (own_rows.astype(jnp.float32) + share).astype(jnp.bfloat16)
    full_rows = lax.all_gather(own_rows, "mp", axis=0, tiled=True) if need_full else own_rows
    return (own_rows, full_rows)


def split_body(
    tokens,
    attn_gain,
    query_first,
    key_first,
    segment_value,
    output_first,
    mlp_gain,
    up_weight,
    down_weight,
    second_gain,
    query_second,
    key_second,
    value_second,
    output_second,
    segment_offset,
    global_offset,
):
    seq_count = lax.axis_size("seq")
    token_position = lax.axis_index("seq")
    seg_span = min(SEG_MAX, seq_count)
    head_count = segment_offset.shape[0]
    full_rows = lax.all_gather(tokens, "mp", axis=0, tiled=True)
    token_count = full_rows.shape[0]
    hidden = norm_rows(full_rows.astype(jnp.float32), attn_gain)
    query = jnp.dot(hidden, query_first, preferred_element_type=jnp.float32).astype(jnp.bfloat16)
    seg_stride = token_count // (KEYS // seg_span)
    keyval = pick_keys(hidden, segment_offset, seg_stride, key_first, segment_value)
    keyval = spread_segment(keyval, seg_span, token_position)
    mixed = attend_local(query, keyval, head_count)
    partial_value = jnp.dot(mixed, output_first, preferred_element_type=jnp.float32)
    own_rows, first_rows = combine(partial_value, full_rows, True)
    normed = norm_rows(first_rows.astype(jnp.float32), mlp_gain)
    inner = jax.nn.gelu(
        jnp.dot(normed, up_weight, preferred_element_type=jnp.float32), approximate=True
    ).astype(jnp.bfloat16)
    partial_value = jnp.dot(inner, down_weight, preferred_element_type=jnp.float32)
    own_rows, second_rows = combine(partial_value, first_rows, True)
    hidden_two = norm_rows(second_rows.astype(jnp.float32), second_gain)
    query_two = jnp.dot(hidden_two, query_second, preferred_element_type=jnp.float32).astype(
        jnp.bfloat16
    )
    glob_stride = token_count // (KEYS // seq_count)
    keyval_two = pick_keys(hidden_two, global_offset, glob_stride, key_second, value_second)
    keyval_two = spread_global(keyval_two)
    mixed_two = attend_local(query_two, keyval_two, head_count)
    partial_value = jnp.dot(mixed_two, output_second, preferred_element_type=jnp.float32)
    own_rows, unused_rows = combine(partial_value, second_rows, False)
    return own_rows


def one_hot(condition):
    return jnp.where(condition, 1.0, 0.0).astype(BF16)


def dot(left, right):
    return jnp.dot(left, right, preferred_element_type=F32)


def pieces(count, size):
    size = size if count % size == 0 else count
    return [slice(start, start + size) for start in range(0, count, size)]


def norm_into(out, start, source, gain, count):
    for span in pieces(count, 64):
        out[start + span.start : start + span.stop, :] = norm_rows(
            source[span, :].astype(F32), gain
        )


def bring(source, target, sem):
    copy = pltpu.make_async_copy(source, target, sem)
    copy.start()
    return copy


def pick_matrix(offsets, heads, groups, stride):
    count = groups * stride
    place = lax.broadcasted_iota(jnp.int32, (groups, count), 1)
    place = place - lax.broadcasted_iota(jnp.int32, (groups, count), 0) * stride
    return jnp.concatenate([one_hot(place == offsets[h]) for h in range(heads)], axis=0)


def project_keys(chosen, heads, weights, keyval_ref):
    rows, width = chosen.shape
    groups, head_size = rows // heads, width // heads
    for slot, weight in enumerate(weights):
        held = weight()
        for span in pieces(width, 256):
            first, last = span.start // head_size, (span.stop - 1) // head_size + 1
            wide = dot(chosen[first * groups : last * groups], held[:, span])
            column = lax.broadcasted_iota(jnp.int32, (groups, span.stop - span.start), 1)
            total = wide[:groups]
            for h in range(first + 1, last):
                row = (h - first) * groups
                own = column >= h * head_size - span.start
                total = jnp.where(own, wide[row : row + groups], total)
            total = total.astype(BF16)
            for copy in range(keyval_ref.shape[0]):
                keyval_ref[copy, slot, :, span] = total


def ranks(offsets, chunk, stride, share, axis):
    heads = offsets.shape[0]

    def places(way):
        shape = (1, chunk) if way else (chunk, 1)
        place = lax.broadcasted_iota(jnp.int32, shape, way)
        inside = lax.rem(place, stride)
        taken = inside == offsets[0]
        for h in range(1, heads):
            taken = taken | (inside == offsets[h])
        return place, inside, jnp.where(taken, inside, inside + stride)

    place, inside, order = places(axis)
    other_place, _, other_order = places(1 - axis)
    ahead = (other_order < order) & (lax.div(other_place, stride) == lax.div(place, stride))
    rank = jnp.sum(jnp.where(ahead, 1, 0), axis=1 - axis, keepdims=True)
    group = lax.div(place, stride)
    return jnp.where(
        rank < heads, group * heads + rank, share + group * (stride - heads) + rank - heads
    )


def slots_of(offsets, heads):
    values = [offsets[h] for h in range(heads)]
    fresh = []
    for h in range(heads):
        seen = jnp.int32(1)
        for earlier in values[:h]:
            seen = jnp.where(earlier == values[h], 0, seen)
        fresh.append(seen)
    slots = []
    for h in range(heads):
        slot = jnp.int32(0)
        for other in range(heads):
            slot = slot + jnp.where(values[other] < values[h], fresh[other], 0)
        slots.append(slot)
    return slots


def first_keys_kernel(
    offsets, tokens, gain, key_weight, value_weight, keyval, rows, wide, picks, scale, sems, *, stride
):
    copies = [
        bring(offsets, picks, sems.at[0]),
        bring(tokens, rows, sems.at[1]),
        bring(gain, scale, sems.at[2]),
        bring(key_weight, wide.at[0], sems.at[3]),
        bring(value_weight, wide.at[1], sems.at[4]),
    ]
    heads = offsets.shape[0]
    copies[0].wait()
    chooser = pick_matrix(picks, heads, rows.shape[0] // stride, stride)
    copies[1].wait()
    copies[2].wait()
    chosen = norm_rows(dot(chooser, rows[...]), scale[...])

    def weight(slot):
        copies[slot + 3].wait()
        return wide[slot]

    project_keys(
        chosen, heads, [functools.partial(weight, slot) for slot in range(2)], keyval
    )


def order_kernel(
    offsets,
    tokens,
    gain,
    moved_rows,
    normed,
    chooser,
    back,
    rows,
    picks,
    scale,
    sems,
    *,
    stride,
    chunk,
):
    copies = [
        bring(offsets, picks, sems.at[0]),
        bring(tokens, rows, sems.at[1]),
        bring(gain, scale, sems.at[2]),
    ]
    count = tokens.shape[0]
    share = chunk // stride * offsets.shape[0]
    rest = chunk - share
    picked = count // chunk * share
    copies[0].wait()
    mover = one_hot(
        lax.broadcasted_iota(jnp.int32, (chunk, chunk), 0)
        == ranks(picks, chunk, stride, share, 1)
    )
    heads = offsets.shape[0]
    chooser[...] = pick_matrix(slots_of(picks, heads), heads, picked // heads, heads)
    back[...] = one_hot(
        lax.broadcasted_iota(jnp.int32, (chunk, chunk), 1)
        == ranks(picks, chunk, stride, share, 0)
    )
    copies[1].wait()
    copies[2].wait()
    for c in range(count // chunk):
        moved = dot(mover, rows[c * chunk : (c + 1) * chunk, :]).astype(BF16)
        moved_rows[c * share : (c + 1) * share, :] = moved[:share]
        moved_rows[picked + c * rest : picked + (c + 1) * rest, :] = moved[share:]
    norm_into(normed, 0, moved_rows, scale[...], count)


def score_scale(head_size):
    return head_size ** (-0.5) * LOG2E


def project_query(normed, weight, outs, heads, peaks):
    peak = None
    for out, row in outs:
        for span in pieces(out.shape[0], 512 if out.shape[0] % 512 == 0 else 256):
            query = dot(normed[row + span.start : row + span.stop, :], weight[...])
            out[span, :] = query.astype(BF16)
            for part in pieces(query.shape[0], 64):
                square = query[part] * query[part]
                peak = square if peak is None else jnp.maximum(peak, square)
    peaks[...] = summed_peaks(peak.astype(BF16), heads)


def first_query_kernel(normed, weight, picked, rest, peaks, sems, *, heads):
    del sems
    project_query(normed, weight, [(picked, 0), (rest, picked.shape[0])], heads, peaks)


def head_windows(head_size, width):
    period = min(width, math.lcm(head_size, 128))
    windows = []
    for h in range(period // head_size):
        start = h * head_size // 128 * 128
        stop = min(period, -(-(h + 1) * head_size // 128) * 128)
        windows.append((start, stop - start))
    return period, windows


def summed_peaks(peak, heads):
    width = peak.shape[1]
    column = lax.broadcasted_iota(jnp.int32, (width, 128), 0)
    head = lax.broadcasted_iota(jnp.int32, (width, 128), 1)
    low = head * (width // heads)
    sums = one_hot((column >= low) & (column < low + width // heads))
    return jnp.max(dot(peak, sums), axis=0, keepdims=True)


def load_keys(keyval, turned):
    keys = jnp.concatenate([keyval[i, 0] for i in range(keyval.shape[0])], axis=0)
    turned[...] = keys.T
    return keys * keys


def small_scores(query_peaks, key_peaks, head_size):
    scale = score_scale(head_size)
    return jnp.max(query_peaks[...] * key_peaks[...]) < 9000.0 / (scale * scale)


def reciprocal(x):
    guess = pl.reciprocal(x, approx=True)
    return guess * (2.0 - x * guess)


def padded_keys(turned, base, head, head_size, start, size):
    low = base + head * head_size
    rows = pl.ds(low if isinstance(low, int) else pl.multiple_of(low, 16), head_size)
    own = jnp.concatenate([part[rows, :] for part in turned], axis=1)
    low = head * head_size - start
    parts = [own]
    if low:
        parts.insert(0, jnp.zeros((low, own.shape[1]), BF16))
    if low + head_size < size:
        parts.append(jnp.zeros((size - low - head_size, own.shape[1]), BF16))
    return jnp.concatenate(parts, axis=0)


def score_pair(query, span, base, head, head_size, windows, turned):
    start = windows[head][0]
    size = windows[head + 1][0] + windows[head + 1][1] - start
    keys = [padded_keys([turned], base, head + i, head_size, start, size) for i in range(2)]
    return dot(query[span, pl.ds(base + start, size)], jnp.concatenate(keys, axis=1))


def near_weights_kernel(
    picked, rest, keyval, picked_early, rest_early, turned, peaks, scores_ref, sems, *, heads
):
    del sems
    peaks[...] = summed_peaks(load_keys(keyval, turned), heads)
    width = picked.shape[1]
    head_size = width // heads
    scale = score_scale(head_size)
    key_count = turned.shape[1]
    period, windows = head_windows(head_size, width)
    jobs = [
        (query, early, head)
        for query, early in ((picked, picked_early), (rest, rest_early))
        for head in range(0, len(windows), 2)
    ]

    @pl.loop(0, width // period)
    def _(turn):
        base = pl.multiple_of(turn * period, 128)

        def score(i):
            query, _, head = jobs[i]
            rows = query.shape[0]
            scores_ref[i % 2, :rows] = score_pair(
                query, slice(0, rows), base, head, head_size, windows, turned
            )

        score(0)
        for i, (query, early, head) in enumerate(jobs):
            if i + 1 < len(jobs):
                score(i + 1)
            for part in pieces(query.shape[0], 64):
                weights = jnp.exp2(scores_ref[i % 2, part, :] * scale).astype(BF16)
                for j in range(2):
                    early[turn * len(windows) + head + j, part, :] = weights[
                        :, j * key_count : (j + 1) * key_count
                    ]


def attend_rows(
    query, first_row, rows, heads, turned, keyvals, mixed_ref, mixed_row, work, plain, early=None
):
    scores_ref, weights_ref = work
    width = query.shape[1]
    key_count = sum(part.shape[1] for part in turned)
    head_size = width // heads
    period, windows = head_windows(head_size, width)
    span = pl.ds(first_row, rows)
    out_span = pl.ds(mixed_row, rows)
    scale = score_scale(head_size)
    lane = lax.broadcasted_iota(jnp.int32, (1, 128), 1)
    step = 2 if early is not None else 1

    def take_turn(turn):
        base = turn * period if plain else pl.multiple_of(turn * period, 128)
        sums = {}

        def score(i):
            if early is not None:
                scores = score_pair(query, span, base, 2 * i, head_size, windows, turned[1])
            else:
                start, size = windows[i]
                scores = dot(
                    query[span, pl.ds(base + start, size)],
                    padded_keys(turned, base, i, head_size, start, size),
                )
            scores_ref[i % 2, :rows] = scores

        def weigh(h):
            for part in pieces(rows, 64):
                scores = scores_ref[h % 2, part, :]
                if not plain:
                    scores = scores - jnp.max(scores, axis=1, keepdims=True)
                weights_ref[h % 2, part, :] = jnp.exp2(scores * scale).astype(BF16)

        def mix(h):
            start, size = windows[h]
            low = h * head_size - start
            values = jnp.concatenate(
                [
                    x[i, 1, :, pl.ds(base + start, size)]
                    for x in keyvals
                    for i in range(x.shape[0])
                ],
                axis=0,
            )
            column = lax.broadcasted_iota(jnp.int32, (key_count, size), 1)
            own = (column >= low) & (column < low + head_size)
            values = jnp.where(own, values, jnp.ones((), BF16))
            if early is not None:
                half = key_count // 2
                far = weights_ref[h // 2 % 2, :rows, h % 2 * half : (h % 2 + 1) * half]
                near = early[turn * len(windows) + h, span, :]
                weights = jnp.concatenate([near, far], axis=1)
            else:
                weights = weights_ref[h % 2, :rows]
            mixed = dot(weights, values)
            for offset in range(0, size, 128):
                own = mixed[:, offset : offset + 128]
                total = pltpu.roll(own, 64, 1)
                at = start + offset
                if at in sums:
                    mine = lane >= h * head_size - at
                    own = jnp.where(mine, own, sums[at][0])
                    total = jnp.where(mine, total, sums[at][1])
                sums[at] = own, total
                if (h + 1) * head_size >= at + 128:
                    own, total = sums.pop(at)
                    mixed_ref[out_span, pl.ds(base + at, 128)] = (
                        own * reciprocal(total)
                    ).astype(BF16)

        count = len(windows) // step
        score(0)
        for i in range(count):
            if i:
                for h in range((i - 1) * step, i * step):
                    mix(h)
            if i + 1 < count:
                score(i + 1)
            weigh(i)
        for h in range((count - 1) * step, count * step):
            mix(h)

    if plain:
        for turn in range(width // period):
            take_turn(turn)
    else:
        pl.loop(0, width // period)(take_turn)


def attend(query, rows, heads, turned, keyvals, mixed_ref, work, small, early=None):
    size = math.gcd(rows, ROWS)

    @pl.when(small)
    def _():
        attend_rows(query, 0, rows, heads, turned, keyvals, mixed_ref, 0, work, True, early)

    @pl.when(jnp.logical_not(small))
    def _():
        @pl.loop(0, rows // size)
        def _(step):
            row = pl.multiple_of(step * size, size)
            attend_rows(
                query,
                row,
                size,
                heads,
                turned,
                keyvals,
                mixed_ref,
                row,
                work,
                False,
            )


def gelu(x):
    half = 0.5 * x
    return half + half * jnp.tanh(x * (0.7978845608028654 + 0.035677408136300125 * (x * x)))


def widen(normed, up_weight, low, wide_ref, inner):
    rows = normed.shape[0]
    spans = pieces(inner.shape[1], wide_ref.shape[2])

    def product(i):
        columns = slice(low + spans[i].start, low + spans[i].stop)
        wide_ref[i % 2] = dot(normed[...], up_weight[:, columns])

    product(0)
    for i, span in enumerate(spans):
        if i + 1 < len(spans):
            product(i + 1)
        for part in pieces(rows, 32):
            inner[part, span] = gelu(wide_ref[i % 2, part, :]).astype(BF16)


def feed_forward(normed, up_weight, down_weight, total, wide_ref, inner):
    rows = normed.shape[0]
    spans = pieces(up_weight.shape[1], wide_ref.shape[2])

    def product(i):
        wide_ref[i % 2] = dot(normed[...], up_weight[:, spans[i]])

    product(0)
    for i, span in enumerate(spans):
        if i + 1 < len(spans):
            product(i + 1)
        for part in pieces(rows, 32):
            inner[i % 2, part, :] = gelu(wide_ref[i % 2, part, :]).astype(BF16)
        total[...] += dot(inner[i % 2], down_weight[span, :])


def narrow(inners, down_weight, first, second, size):
    for span in pieces(second.shape[1], size):
        total = first[:, span].astype(F32)
        low = 0
        for inner in inners:
            high = low + inner.shape[1]
            total = total + dot(inner[...], down_weight[low:high, span])
            low = high
        second[:, span] = total.astype(BF16)


def add_heads(tokens, first_row, mixed, out_weight, gain, first, normed):
    before = None
    for span in pieces(mixed.shape[0], 256):
        total = dot(mixed[span, :], out_weight[...])
        rows = tokens[first_row + span.start : first_row + span.stop, :]
        first[span, :] = (rows.astype(F32) + total).astype(BF16)
        if before is not None:
            norm_into(normed, before.start, first.at[before], gain, before.stop - before.start)
        before = span
    norm_into(normed, before.start, first.at[before], gain, before.stop - before.start)


def picked_kernel(
    chooser,
    tokens,
    query,
    query_peaks,
    early,
    keyval,
    keyval_far,
    turned_near,
    peaks_near,
    out_weight,
    mlp_gain,
    up_weight,
    down_weight,
    gain,
    key_weight,
    value_weight,
    second,
    normed,
    keyval_two,
    turned,
    peaks,
    held,
    mixed,
    scores,
    weights,
    first,
    wide,
    inner,
    total,
    sems,
    *,
    heads,
):
    copies = [
        bring(x, held.at[i], sems.at[i]) for i, x in enumerate((key_weight, value_weight))
    ]
    rows = second.shape[0]
    keyvals = (keyval, keyval_far)
    squares = load_keys(keyval_far, turned)
    peaks[...] = jnp.maximum(peaks_near[...], summed_peaks(squares, heads))
    small = small_scores(query_peaks, peaks, query.shape[1] // heads)
    attend(
        query,
        rows,
        heads,
        (turned_near, turned),
        keyvals,
        mixed,
        (scores, weights),
        small,
        early,
    )
    add_heads(tokens, 0, mixed, out_weight, mlp_gain[...], first, normed)
    total[...] = first[...].astype(F32)
    feed_forward(normed, up_weight, down_weight, total, wide, inner)
    second[...] = total[...].astype(BF16)
    norm_into(normed, 0, second, gain[...], rows)
    chosen = dot(chooser[...], normed[...]).astype(BF16)

    def weight(slot):
        copies[slot].wait()
        return held[slot]

    project_keys(
        chosen, heads, [functools.partial(weight, slot) for slot in range(2)], keyval_two
    )


def rest_attention_kernel(
    query,
    query_peaks,
    early,
    keyval,
    keyval_far,
    turned_near,
    turned,
    peaks,
    mixed,
    scores,
    weights,
    sems,
    *,
    heads,
):
    del sems
    attend(
        query,
        mixed.shape[0],
        heads,
        (turned_near, turned),
        (keyval, keyval_far),
        mixed,
        (scores, weights),
        small_scores(query_peaks, peaks, query.shape[1] // heads),
        early,
    )


def rest_up_kernel(
    tokens, mixed, out_weight, gain, up_weight, first, normed, inner, wide, sems
):
    del sems
    add_heads(
        tokens, tokens.shape[0] - mixed.shape[0], mixed, out_weight, gain[...], first, normed
    )
    widen(normed, up_weight, 0, wide, inner)


def rest_down_kernel(
    first, normed, inner, up_weight, down_weight, second, wide, inner_more, sems
):
    del sems
    widen(normed, up_weight, inner.shape[1], wide, inner_more)
    narrow([inner, inner_more], down_weight, first, second, 256)


def picked_query_kernel(normed, weight, query, peaks, sems, *, heads):
    del sems
    project_query(normed, weight, [(query, 0)], heads, peaks)


def rest_query_kernel(
    picked, picked_peaks, rows, gain, weight, query, peaks, normed, sems, *, heads
):
    del sems
    start = picked.shape[0]
    query[:start, :] = picked[...]
    norm_into(normed, 0, rows, gain[...], rows.shape[0])
    out = query.at[pl.ds(start, rows.shape[0])]
    project_query(normed, weight, [(out, 0)], heads, peaks)
    peaks[...] = jnp.maximum(peaks[...], picked_peaks[...])


def second_kernel(*refs, heads, parts):
    back, *rows = refs[: 1 + parts]
    query, query_peaks, keyval, keyval_far, out_weight, encoded = refs[1 + parts : 7 + parts]
    turned_near, turned, held, mixed = refs[7 + parts : 11 + parts]
    result, ready, scores, weights, sems = refs[11 + parts :]
    copy = bring(out_weight, held.at[0], sems.at[0])
    keyvals = (keyval, keyval_far)
    squares = jnp.maximum(load_keys(keyval, turned_near), load_keys(keyval_far, turned))
    count = query.shape[0]
    small = small_scores(query_peaks, summed_peaks(squares, heads), query.shape[1] // heads)
    attend(
        query, count, heads, (turned_near, turned), keyvals, mixed, (scores, weights), small
    )
    chunk = back.shape[0]
    share = rows[0].shape[0] * chunk // count
    rest_share = chunk - share
    copy.wait()
    start = 0
    for part in rows:
        span = slice(start, start + part.shape[0])
        total = part[...].astype(F32) + dot(mixed[span, :], held[0])
        result[span, :] = total.astype(BF16)
        start += part.shape[0]
    start = count // chunk * share
    copies = []
    for c in range(count // chunk):
        far = start + c * rest_share
        blend = jnp.concatenate(
            [result[c * share : (c + 1) * share, :], result[far : far + rest_share, :]], axis=0
        )
        span = pl.ds(c * chunk, chunk)
        ready[span, :] = dot(back[...], blend).astype(BF16)
        copies.append(bring(ready.at[span], encoded.at[span], sems.at[1 + c]))
    for copy in copies:
        copy.wait()


def relaying(kernel, ins, outs, *refs):
    end = ins + 1 + outs
    refs[end][...] = refs[ins][...]
    kernel(*refs[:ins], *refs[ins + 1 : end], *refs[end + 1 :])


def local_call(kernel, outs, inputs, scratch, scalars=0, far=(), relay=None, out_near=True, copies=1, flops=0, name=None):
    outs, inputs = list(outs), list(inputs)
    if relay is not None:
        kernel = functools.partial(relaying, kernel, len(inputs), len(outs))
        inputs.append(relay)
        outs.append(pltpu.VMEM(relay.shape, relay.dtype))
    specs, placed = [], []
    for i, x in enumerate(inputs):
        if i < scalars:
            specs.append(pl.BlockSpec(memory_space=pltpu.SMEM))
        elif i in far:
            specs.append(pl.BlockSpec(memory_space=pltpu.HBM))
            x = pltpu.with_memory_space_constraint(x, pltpu.HBM)
        else:
            specs.append(pl.BlockSpec(memory_space=pltpu.VMEM))
            x = pltpu.with_memory_space_constraint(x, pltpu.VMEM)
        placed.append(x)
    return pl.pallas_call(
        kernel,
        out_shape=outs,
        in_specs=specs,
        out_specs=[
            pl.BlockSpec(memory_space=pltpu.VMEM if out_near else pltpu.HBM)
        ] * len(outs),
        scratch_shapes=list(scratch) + [pltpu.SemaphoreType.DMA((copies,))],
        compiler_params=pltpu.CompilerParams(vmem_limit_bytes=VMEM_LIMIT),
        cost_estimate=pl.CostEstimate(
            flops=int(flops),
            transcendentals=0,
            bytes_accessed=sum(inputs[i].size * inputs[i].dtype.itemsize for i in far),
        ),
        name=name,
    )(*placed)


def exchange(keyval, span, beside):
    size = lax.axis_size("seq")
    levels = span.bit_length() - 1
    even = list(range(levels - 1, 0, -1))
    orders = (even, even[-1:] + even[:-1])
    for step in range(levels - 1):
        pairs = [(i, i ^ 1 << orders[i % 2][step]) for i in range(size)]
        partner = lax.ppermute(keyval, "seq", pairs)
        keyval = jnp.concatenate([beside(step, keyval), partner], axis=0)
    far = swapped(keyval, "seq", 0)
    return beside(levels - 1, keyval), far


def early_exchange(keyval, span, beside):
    levels = span.bit_length() - 1
    crossed, fresh = [], keyval
    for level in range(levels - 1, 1, -1):
        crossed.append(swapped(fresh, "seq", 1))
        partner = swapped(keyval, "seq", level)
        keyval = jnp.concatenate([beside(levels - 1 - level, keyval), partner], axis=0)
        fresh = partner
    if levels > 1:
        crossed.append(swapped(fresh, "seq", 1))
        keyval = jnp.concatenate([beside(levels - 2, keyval), *crossed], axis=0)
    far = swapped(keyval, "seq", 0)
    return beside(levels - 1, keyval), far


def whole_body(
    tokens,
    attn_gain,
    query_first,
    key_first,
    segment_value,
    output_first,
    mlp_gain,
    up_weight,
    down_weight,
    second_gain,
    query_second,
    key_second,
    value_second,
    output_second,
    segment_offset,
    global_offset,
):
    seq_count = lax.axis_size("seq")
    seg_span = min(SEG_MAX, seq_count)
    heads = segment_offset.shape[0]
    count, width = tokens.shape
    head_size = width // heads
    hidden = up_weight.shape[1]
    stride = count // (KEYS // seg_span)
    stride_two = count // (KEYS // seq_count)
    groups, groups_two = count // stride, count // stride_two
    chunk = max(ROWS, stride_two)
    picked_count = groups_two * heads
    rest_count = count - picked_count
    part = hidden // 4

    def near(*shape):
        return pltpu.VMEM(shape, BF16)

    def attention_work(rows):
        return [pltpu.VMEM((2, rows, KEYS), F32), near(2, rows, KEYS)]

    held_shapes = [near(width, KEYS // 2), pltpu.VMEM((1, 128), F32)]
    small_work = [pltpu.SMEM((heads,), jnp.int32), pltpu.VMEM((width,), F32)]

    (keyval,) = local_call(
        functools.partial(first_keys_kernel, stride=stride),
        [near(1, 2, groups, width)],
        (segment_offset, tokens, attn_gain, key_first, segment_value),
        [near(count, width), near(2, width, width)] + small_work,
        far=(0, 1, 2, 3, 4),
        copies=5,
        flops=2 * heads * groups * width * (count + 2 * width),
        name="first_keys",
    )
    made = {}

    def beside_first(level, held):
        if level == 0:
            made["rows"], made["normed"], made["chooser"], made["back"], held = local_call(
                functools.partial(order_kernel, stride=stride_two, chunk=chunk),
                [
                    near(count, width),
                    near(count, width),
                    near(picked_count, picked_count),
                    near(chunk, chunk),
                ],
                (global_offset, tokens, attn_gain),
                [near(count, width)] + small_work,
                far=(0, 1, 2),
                copies=3,
                relay=held,
                flops=2 * count * width * chunk,
                name="order",
            )
        if level == min(1, seg_span.bit_length() - 2):
            made["picked"], made["rest"], made["peaks"], held = local_call(
                functools.partial(first_query_kernel, heads=heads),
                [near(picked_count, width), near(rest_count, width), pltpu.VMEM((1, 128), F32)],
                (made["normed"], query_first),
                [],
                relay=held,
                flops=2 * count * width * width,
                name="first_query",
            )
        if level == seg_span.bit_length() - 2:
            made["picked_early"], made["rest_early"], made["turned"], made["key_peaks"] = local_call(
                functools.partial(near_weights_kernel, heads=heads),
                [near(heads, picked_count, KEYS // 2), near(heads, rest_count, KEYS // 2)]
                + held_shapes,
                (made["picked"], made["rest"], held),
                [pltpu.VMEM((2, rest_count, KEYS), F32)],
                flops=2 * 256 * KEYS // 2 * heads * count,
                name="near_weights",
            )
        return held

    keyval, keyval_far = early_exchange(keyval, seg_span, beside_first)
    rows = made["rows"]
    query_peaks, near_held = made["peaks"], (made["turned"], made["key_peaks"])
    row_flops = 2 * width * (2 * hidden + width) + 4 * 256 * KEYS * heads
    picked_second, picked_normed, keyval_two, turned, peaks = local_call(
        functools.partial(picked_kernel, heads=heads),
        [
            near(picked_count, width),
            near(picked_count, width),
            near(1, 2, groups_two, width),
        ]
        + held_shapes,
        (
            made["chooser"],
            rows,
            made["picked"],
            query_peaks,
            made["picked_early"],
            keyval,
            keyval_far,
            *near_held,
            output_first,
            mlp_gain,
            up_weight,
            down_weight,
            second_gain,
            key_second,
            value_second,
        ),
        [near(2, width, width), near(picked_count, width)]
        + attention_work(picked_count)
        + [near(picked_count, width), pltpu.VMEM((2, picked_count, part), F32)]
        + [near(2, picked_count, part), pltpu.VMEM((picked_count, width), F32)],
        far=(14, 15),
        copies=2,
        flops=row_flops * picked_count,
        name="layer_of_picked",
    )
    seconds = [picked_second]

    def rest_attention(held):
        made["mixed"], held = local_call(
            functools.partial(rest_attention_kernel, heads=heads),
            [near(rest_count, width)],
            (
                made["rest"],
                query_peaks,
                made["rest_early"],
                keyval,
                keyval_far,
                made["turned"],
                turned,
                peaks,
            ),
            attention_work(rest_count),
            relay=held,
            flops=4 * 256 * KEYS * heads * rest_count,
            name="rest_attention",
        )
        return held

    half = hidden // 4 * 3

    def rest_up(held):
        made["first"], made["normed"], made["inner"], held = local_call(
            rest_up_kernel,
            [near(rest_count, width), near(rest_count, width), near(rest_count, half)],
            (rows, made["mixed"], output_first, mlp_gain, up_weight),
            [pltpu.VMEM((2, rest_count, part), F32)],
            relay=held,
            flops=2 * width * (half + width) * rest_count,
            name="rest_up",
        )
        return held

    def rest_down(held):
        result, held = local_call(
            rest_down_kernel,
            [near(rest_count, width)],
            (made["first"], made["normed"], made["inner"], up_weight, down_weight),
            [pltpu.VMEM((1, rest_count, part), F32), near(rest_count, hidden - half)],
            relay=held,
            flops=2 * width * (2 * hidden - half) * rest_count,
            name="rest_down",
        )
        seconds.append(result)
        return held

    def picked_query(held):
        made["picked_two"], made["picked_peaks"], held = local_call(
            functools.partial(picked_query_kernel, heads=heads),
            [near(picked_count, width), pltpu.VMEM((1, 128), F32)],
            (picked_normed, query_second),
            [],
            relay=held,
            flops=2 * picked_count * width * width,
            name="picked_query",
        )
        return held

    def rest_query(held):
        made["query_two"], made["peaks_two"], held = local_call(
            functools.partial(rest_query_kernel, heads=heads),
            [near(count, width), pltpu.VMEM((1, 128), F32)],
            (made["picked_two"], made["picked_peaks"], seconds[1], second_gain, query_second),
            [near(rest_count, width)],
            relay=held,
            flops=2 * rest_count * width * width,
            name="rest_query",
        )
        return held

    tasks = [[rest_attention, picked_query], [rest_up], [rest_down], [rest_query]]
    levels = seq_count.bit_length() - 1

    def beside_second(level, held):
        for work in tasks[len(tasks) * level // levels : len(tasks) * (level + 1) // levels]:
            for task in work:
                held = task(held)
        return held

    keyval_two, keyval_two_far = exchange(keyval_two, seq_count, beside_second)
    (encoded,) = local_call(
        functools.partial(second_kernel, heads=heads, parts=len(seconds)),
        [jax.ShapeDtypeStruct((count, width), BF16)],
        (
            made["back"],
            *seconds,
            made["query_two"],
            made["peaks_two"],
            keyval_two,
            keyval_two_far,
            output_second,
        ),
        held_shapes[:1] * 2
        + [near(1, width, width)]
        + [near(count, width)] * 3
        + attention_work(count),
        far=(len(seconds) + 5,),
        out_near=False,
        copies=1 + count // chunk,
        flops=count * (2 * width * width + 4 * 256 * KEYS * heads),
        name="second_attention",
    )
    return encoded


def solution(mesh):
    placed = (
        P(("slides", "seq", "mp"), None),
        P(),
        P(None, "mp"),
        P(None, "mp"),
        P(None, "mp"),
        P("mp", None),
        P(),
        P(None, "mp"),
        P("mp", None),
        P(),
        P(None, "mp"),
        P(None, "mp"),
        P(None, "mp"),
        P("mp", None),
        P("mp"),
        P("mp"),
    )
    fits = mesh.shape["mp"] == 1 and mesh.shape["seq"] in (2, 4, 8, 16)
    return jax.shard_map(
        whole_body if fits else split_body,
        mesh=mesh,
        in_specs=placed,
        out_specs=P(("slides", "seq", "mp"), None),
        check_vma=False,
    )
```

```python
import functools
import math

import jax
import jax.numpy as jnp
from jax import lax
from jax.experimental import pallas as pl
from jax.experimental.pallas import tpu as pltpu
from jax.sharding import PartitionSpec as P

KEYS = 256
SEG_MAX = 16
ROWS = 256
LOG2E = 1.4426950408889634
BF16 = jnp.bfloat16
F32 = jnp.float32
VMEM_LIMIT = 22 * 1024 * 1024


def swapped(x, axis, apart):
    return lax.ppermute(x, axis, [(i, i ^ 1 << apart) for i in range(lax.axis_size(axis))])


def norm_rows(values, gain):
    center = values - jnp.mean(values, axis=-1, keepdims=True)
    spread = jnp.mean(center * center, axis=-1, keepdims=True)
    return (center * lax.rsqrt(spread + 1e-05) * gain).astype(jnp.bfloat16)


def pick_keys(hidden, offsets, stride, key_weight, value_weight):
    token_count, width = hidden.shape
    head_count = offsets.shape[0]
    head_size = key_weight.shape[1] // head_count
    grouped_rows = hidden.reshape(token_count // stride, stride, width)
    dilation_selector = (
        lax.broadcasted_iota(jnp.int32, (stride, head_count), 0) == offsets[None, :]
    ).astype(jnp.bfloat16)
    chosen = jnp.einsum(
        "nof,oj->njf", grouped_rows, dilation_selector, preferred_element_type=jnp.float32
    ).astype(jnp.bfloat16)
    key_heads = jnp.einsum(
        "xkr,rkf->xkf",
        chosen,
        key_weight.reshape(width, head_count, head_size),
        preferred_element_type=jnp.float32,
    ).astype(jnp.bfloat16)
    value_heads = jnp.einsum(
        "xkr,rkf->xkf",
        chosen,
        value_weight.reshape(width, head_count, head_size),
        preferred_element_type=jnp.float32,
    ).astype(jnp.bfloat16)
    picked = token_count // stride
    return jnp.stack(
        [
            key_heads.reshape(picked, head_count * head_size),
            value_heads.reshape(picked, head_count * head_size),
        ]
    )


def attend_local(query, keyval, head_count):
    token_count, width = query.shape
    head_size = width // head_count
    query_heads = query.reshape(token_count, head_count, head_size)
    key_heads = keyval[0].reshape(-1, head_count, head_size)
    value_heads = keyval[1].reshape(-1, head_count, head_size)
    scores = jnp.einsum(
        "thd,khd->htk", query_heads, key_heads, preferred_element_type=jnp.float32
    ) * head_size ** (-0.5)
    highest = jnp.max(scores, axis=-1, keepdims=True)
    weights = jnp.exp(scores - highest)
    weights = (weights / jnp.sum(weights, axis=-1, keepdims=True)).astype(jnp.bfloat16)
    mixed = jnp.einsum(
        "htk,khd->thd", weights, value_heads, preferred_element_type=jnp.float32
    ).astype(jnp.bfloat16)
    return mixed.reshape(token_count, width)


def merge_branch_pair(mine, other, level, token_position):
    lower = token_position >> level & 1 == 0
    return jnp.where(
        lower, jnp.concatenate((mine, other), axis=1), jnp.concatenate((other, mine), axis=1)
    )


def spread_segment(keyval, seg_span, token_position):
    for level in range(seg_span.bit_length() - 1):
        partner = swapped(keyval, "seq", level)
        keyval = merge_branch_pair(keyval, partner, level, token_position)
    return keyval


def spread_global(keyval_two):
    keyval_two = lax.all_gather(keyval_two, "seq", axis=1, tiled=True)
    return keyval_two


def combine(partial_value, residual_full, need_full):
    row_count = residual_full.shape[0] // lax.axis_size("mp")
    row_start = lax.axis_index("mp") * row_count
    share = lax.psum_scatter(partial_value, "mp", scatter_dimension=0, tiled=True)
    own_rows = lax.dynamic_slice_in_dim(residual_full, row_start, row_count, 0)
    own_rows = (own_rows.astype(jnp.float32) + share).astype(jnp.bfloat16)
    full_rows = lax.all_gather(own_rows, "mp", axis=0, tiled=True) if need_full else own_rows
    return (own_rows, full_rows)


def split_body(
    tokens,
    attn_gain,
    query_first,
    key_first,
    segment_value,
    output_first,
    mlp_gain,
    up_weight,
    down_weight,
    second_gain,
    query_second,
    key_second,
    value_second,
    output_second,
    segment_offset,
    global_offset,
):
    seq_count = lax.axis_size("seq")
    token_position = lax.axis_index("seq")
    seg_span = min(SEG_MAX, seq_count)
    head_count = segment_offset.shape[0]
    full_rows = lax.all_gather(tokens, "mp", axis=0, tiled=True)
    token_count = full_rows.shape[0]
    hidden = norm_rows(full_rows.astype(jnp.float32), attn_gain)
    query = jnp.dot(hidden, query_first, preferred_element_type=jnp.float32).astype(jnp.bfloat16)
    seg_stride = token_count // (KEYS // seg_span)
    keyval = pick_keys(hidden, segment_offset, seg_stride, key_first, segment_value)
    keyval = spread_segment(keyval, seg_span, token_position)
    mixed = attend_local(query, keyval, head_count)
    partial_value = jnp.dot(mixed, output_first, preferred_element_type=jnp.float32)
    own_rows, first_rows = combine(partial_value, full_rows, True)
    normed = norm_rows(first_rows.astype(jnp.float32), mlp_gain)
    inner = jax.nn.gelu(
        jnp.dot(normed, up_weight, preferred_element_type=jnp.float32), approximate=True
    ).astype(jnp.bfloat16)
    partial_value = jnp.dot(inner, down_weight, preferred_element_type=jnp.float32)
    own_rows, second_rows = combine(partial_value, first_rows, True)
    hidden_two = norm_rows(second_rows.astype(jnp.float32), second_gain)
    query_two = jnp.dot(hidden_two, query_second, preferred_element_type=jnp.float32).astype(
        jnp.bfloat16
    )
    glob_stride = token_count // (KEYS // seq_count)
    keyval_two = pick_keys(hidden_two, global_offset, glob_stride, key_second, value_second)
    keyval_two = spread_global(keyval_two)
    mixed_two = attend_local(query_two, keyval_two, head_count)
    partial_value = jnp.dot(mixed_two, output_second, preferred_element_type=jnp.float32)
    own_rows, unused_rows = combine(partial_value, second_rows, False)
    return own_rows


def one_hot(condition):
    return jnp.where(condition, 1.0, 0.0).astype(BF16)


def dot(left, right):
    return jnp.dot(left, right, preferred_element_type=F32)


def pieces(count, size):
    size = size if count % size == 0 else count
    return [slice(start, start + size) for start in range(0, count, size)]


def norm_into(out, start, source, gain, count):
    for span in pieces(count, 64):
        out[start + span.start : start + span.stop, :] = norm_rows(
            source[span, :].astype(F32), gain
        )


def bring(source, target, sem):
    copy = pltpu.make_async_copy(source, target, sem)
    copy.start()
    return copy


def pick_matrix(offsets, heads, groups, stride):
    count = groups * stride
    place = lax.broadcasted_iota(jnp.int32, (groups, count), 1)
    place = place - lax.broadcasted_iota(jnp.int32, (groups, count), 0) * stride
    return jnp.concatenate([one_hot(place == offsets[h]) for h in range(heads)], axis=0)


def project_keys(chosen, heads, weights, keyval_ref):
    rows, width = chosen.shape
    groups, head_size = rows // heads, width // heads
    for slot, weight in enumerate(weights):
        held = weight()
        for span in pieces(width, 256):
            first, last = span.start // head_size, (span.stop - 1) // head_size + 1
            wide = dot(chosen[first * groups : last * groups], held[:, span])
            column = lax.broadcasted_iota(jnp.int32, (groups, span.stop - span.start), 1)
            total = wide[:groups]
            for h in range(first + 1, last):
                row = (h - first) * groups
                own = column >= h * head_size - span.start
                total = jnp.where(own, wide[row : row + groups], total)
            total = total.astype(BF16)
            for copy in range(keyval_ref.shape[0]):
                keyval_ref[copy, slot, :, span] = total


def ranks(offsets, chunk, stride, share, axis):
    heads = offsets.shape[0]

    def places(way):
        shape = (1, chunk) if way else (chunk, 1)
        place = lax.broadcasted_iota(jnp.int32, shape, way)
        inside = lax.rem(place, stride)
        taken = inside == offsets[0]
        for h in range(1, heads):
            taken = taken | (inside == offsets[h])
        return place, inside, jnp.where(taken, inside, inside + stride)

    place, inside, order = places(axis)
    other_place, _, other_order = places(1 - axis)
    ahead = (other_order < order) & (lax.div(other_place, stride) == lax.div(place, stride))
    rank = jnp.sum(jnp.where(ahead, 1, 0), axis=1 - axis, keepdims=True)
    group = lax.div(place, stride)
    return jnp.where(
        rank < heads, group * heads + rank, share + group * (stride - heads) + rank - heads
    )


def slots_of(offsets, heads):
    values = [offsets[h] for h in range(heads)]
    fresh = []
    for h in range(heads):
        seen = jnp.int32(1)
        for earlier in values[:h]:
            seen = jnp.where(earlier == values[h], 0, seen)
        fresh.append(seen)
    slots = []
    for h in range(heads):
        slot = jnp.int32(0)
        for other in range(heads):
            slot = slot + jnp.where(values[other] < values[h], fresh[other], 0)
        slots.append(slot)
    return slots


def first_keys_kernel(
    offsets, tokens, gain, key_weight, value_weight, keyval, rows, wide, picks, scale, sems, *, stride
):
    spans = pieces(tokens.shape[0], tokens.shape[0] // 4)
    copies = [
        bring(offsets, picks, sems.at[0]),
        bring(gain, scale, sems.at[1]),
        *[bring(tokens.at[x], rows.at[x], sems.at[4 + i]) for i, x in enumerate(spans)],
        bring(key_weight, wide.at[0], sems.at[2]),
        bring(value_weight, wide.at[1], sems.at[3]),
    ]
    heads = offsets.shape[0]
    copies[0].wait()
    chooser = pick_matrix(picks, heads, rows.shape[0] // stride, stride)
    copies[1].wait()
    chosen = None
    for copy, span in zip(copies[2:-2], spans):
        copy.wait()
        part = dot(chooser[:, span], rows[span, :])
        chosen = part if chosen is None else chosen + part
    chosen = norm_rows(chosen, scale[...])

    def weight(slot):
        copies[slot - 2].wait()
        return wide[slot]

    project_keys(
        chosen, heads, [functools.partial(weight, slot) for slot in range(2)], keyval
    )


def order_kernel(
    offsets,
    tokens,
    gain,
    moved_rows,
    normed,
    chooser,
    back,
    rows,
    picks,
    scale,
    sems,
    *,
    stride,
    chunk,
):
    copies = [
        bring(offsets, picks, sems.at[0]),
        bring(tokens, rows, sems.at[1]),
        bring(gain, scale, sems.at[2]),
    ]
    count = tokens.shape[0]
    share = chunk // stride * offsets.shape[0]
    rest = chunk - share
    picked = count // chunk * share
    copies[0].wait()
    mover = one_hot(
        lax.broadcasted_iota(jnp.int32, (chunk, chunk), 0)
        == ranks(picks, chunk, stride, share, 1)
    )
    heads = offsets.shape[0]
    chooser[...] = pick_matrix(slots_of(picks, heads), heads, picked // heads, heads)
    back[...] = one_hot(
        lax.broadcasted_iota(jnp.int32, (chunk, chunk), 1)
        == ranks(picks, chunk, stride, share, 0)
    )
    copies[1].wait()
    copies[2].wait()
    for c in range(count // chunk):
        moved = dot(mover, rows[c * chunk : (c + 1) * chunk, :]).astype(BF16)
        moved_rows[c * share : (c + 1) * share, :] = moved[:share]
        moved_rows[picked + c * rest : picked + (c + 1) * rest, :] = moved[share:]
    norm_into(normed, 0, moved_rows, scale[...], count)


def score_scale(head_size):
    return head_size ** (-0.5) * LOG2E


def project_rows(normed, span, weight, out, peak):
    query = dot(normed[span, :], weight[...])
    out[...] = query.astype(BF16)
    for part in pieces(query.shape[0], 64):
        square = query[part] * query[part]
        peak = square if peak is None else jnp.maximum(peak, square)
    return peak


def project_query(normed, weight, outs, heads, peaks):
    peak = None
    for out, row in outs:
        for span in pieces(out.shape[0], 512 if out.shape[0] % 512 == 0 else 256):
            place = slice(row + span.start, row + span.stop)
            peak = project_rows(normed, place, weight, out.at[span], peak)
    peaks[...] = summed_peaks(peak.astype(BF16), heads)


def first_query_kernel(normed, weight, picked, rest, peaks, sems, *, heads):
    del sems
    project_query(normed, weight, [(picked, 0), (rest, picked.shape[0])], heads, peaks)


def head_windows(head_size, width):
    period = min(width, math.lcm(head_size, 128))
    windows = []
    for h in range(period // head_size):
        start = h * head_size // 128 * 128
        stop = min(period, -(-(h + 1) * head_size // 128) * 128)
        windows.append((start, stop - start))
    return period, windows


def summed_peaks(peak, heads):
    width = peak.shape[1]
    column = lax.broadcasted_iota(jnp.int32, (width, 128), 0)
    head = lax.broadcasted_iota(jnp.int32, (width, 128), 1)
    low = head * (width // heads)
    sums = one_hot((column >= low) & (column < low + width // heads))
    return jnp.max(dot(peak, sums), axis=0, keepdims=True)


def load_keys(keyval, turned):
    keys = jnp.concatenate([keyval[i, 0] for i in range(keyval.shape[0])], axis=0)
    turned[...] = keys.T
    return keys * keys


def small_scores(query_peaks, key_peaks, head_size):
    scale = score_scale(head_size)
    return jnp.max(query_peaks[...] * key_peaks[...]) < 9000.0 / (scale * scale)


def reciprocal(x):
    guess = pl.reciprocal(x, approx=True)
    return guess * (2.0 - x * guess)


def padded_keys(turned, base, head, head_size, start, size):
    low = base + head * head_size
    rows = pl.ds(low if isinstance(low, int) else pl.multiple_of(low, 16), head_size)
    own = jnp.concatenate([part[rows, :] for part in turned], axis=1)
    low = head * head_size - start
    parts = [own]
    if low:
        parts.insert(0, jnp.zeros((low, own.shape[1]), BF16))
    if low + head_size < size:
        parts.append(jnp.zeros((size - low - head_size, own.shape[1]), BF16))
    return jnp.concatenate(parts, axis=0)


def score_pair(query, span, base, head, head_size, windows, turned):
    start = windows[head][0]
    size = windows[head + 1][0] + windows[head + 1][1] - start
    keys = [padded_keys([turned], base, head + i, head_size, start, size) for i in range(2)]
    return dot(query[span, pl.ds(base + start, size)], jnp.concatenate(keys, axis=1))


def near_weights_kernel(
    picked, rest, keyval, picked_early, rest_early, turned, peaks, scores_ref, sems, *, heads
):
    del sems
    peaks[...] = summed_peaks(load_keys(keyval, turned), heads)
    width = picked.shape[1]
    head_size = width // heads
    scale = score_scale(head_size)
    key_count = turned.shape[1]
    period, windows = head_windows(head_size, width)
    jobs = [
        (query, early, head)
        for query, early in ((picked, picked_early), (rest, rest_early))
        for head in range(0, len(windows), 2)
    ]

    @pl.loop(0, width // period)
    def _(turn):
        base = pl.multiple_of(turn * period, 128)

        def score(i):
            query, _, head = jobs[i]
            rows = query.shape[0]
            scores_ref[i % 2, :rows] = score_pair(
                query, slice(0, rows), base, head, head_size, windows, turned
            )

        score(0)
        for i, (query, early, head) in enumerate(jobs):
            if i + 1 < len(jobs):
                score(i + 1)
            for part in pieces(query.shape[0], 64):
                weights = jnp.exp2(scores_ref[i % 2, part, :] * scale).astype(BF16)
                for j in range(2):
                    early[turn * len(windows) + head + j, part, :] = weights[
                        :, j * key_count : (j + 1) * key_count
                    ]


def attend_rows(
    query, first_row, rows, heads, turned, keyvals, mixed_ref, mixed_row, work, plain, early=None
):
    scores_ref, weights_ref = work
    width = query.shape[1]
    key_count = sum(part.shape[1] for part in turned)
    head_size = width // heads
    period, windows = head_windows(head_size, width)
    span = pl.ds(first_row, rows)
    out_span = pl.ds(mixed_row, rows)
    scale = score_scale(head_size)
    lane = lax.broadcasted_iota(jnp.int32, (1, 128), 1)
    step = 2 if early is not None else 1

    def take_turn(turn):
        base = turn * period if plain else pl.multiple_of(turn * period, 128)
        sums = {}

        def score(i):
            if early is not None:
                scores = score_pair(query, span, base, 2 * i, head_size, windows, turned[1])
            else:
                start, size = windows[i]
                scores = dot(
                    query[span, pl.ds(base + start, size)],
                    padded_keys(turned, base, i, head_size, start, size),
                )
            scores_ref[i % 2, :rows] = scores

        def weigh(h):
            for part in pieces(rows, 64):
                scores = scores_ref[h % 2, part, :]
                if not plain:
                    scores = scores - jnp.max(scores, axis=1, keepdims=True)
                weights_ref[h % 2, part, :] = jnp.exp2(scores * scale).astype(BF16)

        def mix(h):
            start, size = windows[h]
            low = h * head_size - start
            values = jnp.concatenate(
                [
                    x[i, 1, :, pl.ds(base + start, size)]
                    for x in keyvals
                    for i in range(x.shape[0])
                ],
                axis=0,
            )
            column = lax.broadcasted_iota(jnp.int32, (key_count, size), 1)
            own = (column >= low) & (column < low + head_size)
            values = jnp.where(own, values, jnp.ones((), BF16))
            if early is not None:
                half = key_count // 2
                far = weights_ref[h // 2 % 2, :rows, h % 2 * half : (h % 2 + 1) * half]
                near = early[turn * len(windows) + h, span, :]
                weights = jnp.concatenate([near, far], axis=1)
            else:
                weights = weights_ref[h % 2, :rows]
            mixed = dot(weights, values)
            for offset in range(0, size, 128):
                own = mixed[:, offset : offset + 128]
                total = pltpu.roll(own, 64, 1)
                at = start + offset
                if at in sums:
                    mine = lane >= h * head_size - at
                    own = jnp.where(mine, own, sums[at][0])
                    total = jnp.where(mine, total, sums[at][1])
                sums[at] = own, total
                if (h + 1) * head_size >= at + 128:
                    own, total = sums.pop(at)
                    mixed_ref[out_span, pl.ds(base + at, 128)] = (
                        own * reciprocal(total)
                    ).astype(BF16)

        count = len(windows) // step
        score(0)
        for i in range(count):
            if i:
                for h in range((i - 1) * step, i * step):
                    mix(h)
            if i + 1 < count:
                score(i + 1)
            weigh(i)
        for h in range((count - 1) * step, count * step):
            mix(h)

    if plain:
        for turn in range(width // period):
            take_turn(turn)
    else:
        pl.loop(0, width // period)(take_turn)


def attend(query, rows, heads, turned, keyvals, mixed_ref, work, small, early=None):
    size = math.gcd(rows, ROWS)

    @pl.when(small)
    def _():
        attend_rows(query, 0, rows, heads, turned, keyvals, mixed_ref, 0, work, True, early)

    @pl.when(jnp.logical_not(small))
    def _():
        @pl.loop(0, rows // size)
        def _(step):
            row = pl.multiple_of(step * size, size)
            attend_rows(
                query,
                row,
                size,
                heads,
                turned,
                keyvals,
                mixed_ref,
                row,
                work,
                False,
            )


def gelu(x):
    half = 0.5 * x
    return half + half * jnp.tanh(x * (0.7978845608028654 + 0.035677408136300125 * (x * x)))


def widen(normed, up_weight, low, wide_ref, inner):
    rows = normed.shape[0]
    spans = pieces(inner.shape[1], wide_ref.shape[2])

    def product(i):
        columns = slice(low + spans[i].start, low + spans[i].stop)
        wide_ref[i % 2] = dot(normed[...], up_weight[:, columns])

    product(0)
    for i, span in enumerate(spans):
        if i + 1 < len(spans):
            product(i + 1)
        for part in pieces(rows, 32):
            inner[part, span] = gelu(wide_ref[i % 2, part, :]).astype(BF16)


def feed_forward(normed, up_weight, down_weight, total, wide_ref, inner):
    rows = normed.shape[0]
    spans = pieces(up_weight.shape[1], wide_ref.shape[2])

    def product(i):
        wide_ref[i % 2] = dot(normed[...], up_weight[:, spans[i]])

    product(0)
    for i, span in enumerate(spans):
        if i + 1 < len(spans):
            product(i + 1)
        for part in pieces(rows, 32):
            inner[i % 2, part, :] = gelu(wide_ref[i % 2, part, :]).astype(BF16)
        total[...] += dot(inner[i % 2], down_weight[span, :])


def narrow(inners, down_weight, first, second, size):
    for span in pieces(second.shape[1], size):
        total = first[:, span].astype(F32)
        low = 0
        for inner in inners:
            high = low + inner.shape[1]
            total = total + dot(inner[...], down_weight[low:high, span])
            low = high
        second[:, span] = total.astype(BF16)


def add_heads(tokens, first_row, mixed, out_weight, gain, first, normed):
    before = None
    for span in pieces(mixed.shape[0], 384):
        total = dot(mixed[span, :], out_weight[...])
        rows = tokens[first_row + span.start : first_row + span.stop, :]
        first[span, :] = (rows.astype(F32) + total).astype(BF16)
        if before is not None:
            norm_into(normed, before.start, first.at[before], gain, before.stop - before.start)
        before = span
    norm_into(normed, before.start, first.at[before], gain, before.stop - before.start)


def picked_kernel(
    chooser,
    tokens,
    query,
    query_peaks,
    early,
    keyval,
    keyval_far,
    turned_near,
    peaks_near,
    out_weight,
    mlp_gain,
    up_weight,
    down_weight,
    gain,
    key_weight,
    value_weight,
    second,
    normed,
    keyval_two,
    turned,
    peaks,
    held,
    mixed,
    scores,
    weights,
    first,
    wide,
    inner,
    total,
    sems,
    *,
    heads,
):
    copies = [
        bring(x, held.at[i], sems.at[i]) for i, x in enumerate((key_weight, value_weight))
    ]
    rows = second.shape[0]
    keyvals = (keyval, keyval_far)
    squares = load_keys(keyval_far, turned)
    peaks[...] = jnp.maximum(peaks_near[...], summed_peaks(squares, heads))
    small = small_scores(query_peaks, peaks, query.shape[1] // heads)
    attend(
        query,
        rows,
        heads,
        (turned_near, turned),
        keyvals,
        mixed,
        (scores, weights),
        small,
        early,
    )
    add_heads(tokens, 0, mixed, out_weight, mlp_gain[...], first, normed)
    total[...] = first[...].astype(F32)
    feed_forward(normed, up_weight, down_weight, total, wide, inner)
    second[...] = total[...].astype(BF16)
    norm_into(normed, 0, second, gain[...], rows)
    chosen = dot(chooser[...], normed[...]).astype(BF16)

    def weight(slot):
        copies[slot].wait()
        return held[slot]

    project_keys(
        chosen, heads, [functools.partial(weight, slot) for slot in range(2)], keyval_two
    )


def rest_attention_kernel(
    query,
    query_peaks,
    early,
    keyval,
    keyval_far,
    turned_near,
    turned,
    peaks,
    mixed,
    scores,
    weights,
    sems,
    *,
    heads,
):
    del sems
    attend(
        query,
        mixed.shape[0],
        heads,
        (turned_near, turned),
        (keyval, keyval_far),
        mixed,
        (scores, weights),
        small_scores(query_peaks, peaks, query.shape[1] // heads),
        early,
    )


def rest_up_kernel(
    tokens, mixed, out_weight, gain, up_weight, first, normed, inner, wide, sems
):
    del sems
    add_heads(
        tokens, tokens.shape[0] - mixed.shape[0], mixed, out_weight, gain[...], first, normed
    )
    widen(normed, up_weight, 0, wide, inner)


def rest_down_kernel(
    first, normed, inner, up_weight, down_weight, second, wide, inner_more, sems
):
    del sems
    widen(normed, up_weight, inner.shape[1], wide, inner_more)
    narrow([inner, inner_more], down_weight, first, second, 256)


def picked_query_kernel(normed, weight, query, peaks, sems, *, heads):
    del sems
    project_query(normed, weight, [(query, 0)], heads, peaks)


def rest_query_kernel(
    picked, picked_peaks, rows, gain, weight, query, peaks, normed, sems, *, heads
):
    del sems
    start = picked.shape[0]
    query[:start, :] = picked[...]
    spans = pieces(rows.shape[0], rows.shape[0] // 2)

    def norm_part(i):
        span = spans[i]
        norm_into(normed, span.start, rows.at[span], gain[...], span.stop - span.start)

    norm_part(0)
    peak = None
    for i, span in enumerate(spans):
        out = query.at[pl.ds(start + span.start, span.stop - span.start)]
        peak = project_rows(normed, span, weight, out, peak)
        if i + 1 < len(spans):
            norm_part(i + 1)
    peaks[...] = jnp.maximum(summed_peaks(peak.astype(BF16), heads), picked_peaks[...])


def second_kernel(*refs, heads, parts):
    back, *rows = refs[: 1 + parts]
    query, query_peaks, keyval, keyval_far, out_weight, encoded = refs[1 + parts : 7 + parts]
    turned_near, turned, held, mixed = refs[7 + parts : 11 + parts]
    result, ready, scores, weights, sems = refs[11 + parts :]
    copy = bring(out_weight, held.at[0], sems.at[0])
    keyvals = (keyval, keyval_far)
    squares = jnp.maximum(load_keys(keyval, turned_near), load_keys(keyval_far, turned))
    count = query.shape[0]
    small = small_scores(query_peaks, summed_peaks(squares, heads), query.shape[1] // heads)
    attend(
        query, count, heads, (turned_near, turned), keyvals, mixed, (scores, weights), small
    )
    chunk = back.shape[0]
    share = rows[0].shape[0] * chunk // count
    rest_share = chunk - share
    copy.wait()
    start = 0
    for part in rows:
        span = slice(start, start + part.shape[0])
        total = part[...].astype(F32) + dot(mixed[span, :], held[0])
        result[span, :] = total.astype(BF16)
        start += part.shape[0]
    start = count // chunk * share
    copies = []
    for c in range(count // chunk):
        far = start + c * rest_share
        blend = jnp.concatenate(
            [result[c * share : (c + 1) * share, :], result[far : far + rest_share, :]], axis=0
        )
        span = pl.ds(c * chunk, chunk)
        ready[span, :] = dot(back[...], blend).astype(BF16)
        copies.append(bring(ready.at[span], encoded.at[span], sems.at[1 + c]))
    for copy in copies:
        copy.wait()


def relaying(kernel, ins, outs, *refs):
    end = ins + 1 + outs
    refs[end][...] = refs[ins][...]
    kernel(*refs[:ins], *refs[ins + 1 : end], *refs[end + 1 :])


def local_call(kernel, outs, inputs, scratch, scalars=0, far=(), relay=None, out_near=True, copies=1, flops=0, name=None):
    outs, inputs = list(outs), list(inputs)
    if relay is not None:
        kernel = functools.partial(relaying, kernel, len(inputs), len(outs))
        inputs.append(relay)
        outs.append(pltpu.VMEM(relay.shape, relay.dtype))
    specs, placed = [], []
    for i, x in enumerate(inputs):
        if i < scalars:
            specs.append(pl.BlockSpec(memory_space=pltpu.SMEM))
        elif i in far:
            specs.append(pl.BlockSpec(memory_space=pltpu.HBM))
            x = pltpu.with_memory_space_constraint(x, pltpu.HBM)
        else:
            specs.append(pl.BlockSpec(memory_space=pltpu.VMEM))
            x = pltpu.with_memory_space_constraint(x, pltpu.VMEM)
        placed.append(x)
    return pl.pallas_call(
        kernel,
        out_shape=outs,
        in_specs=specs,
        out_specs=[
            pl.BlockSpec(memory_space=pltpu.VMEM if out_near else pltpu.HBM)
        ] * len(outs),
        scratch_shapes=list(scratch) + [pltpu.SemaphoreType.DMA((copies,))],
        compiler_params=pltpu.CompilerParams(vmem_limit_bytes=VMEM_LIMIT),
        cost_estimate=pl.CostEstimate(
            flops=int(flops),
            transcendentals=0,
            bytes_accessed=sum(inputs[i].size * inputs[i].dtype.itemsize for i in far),
        ),
        name=name,
    )(*placed)


def exchange(keyval, span, beside):
    size = lax.axis_size("seq")
    levels = span.bit_length() - 1
    even = list(range(levels - 1, 0, -1))
    orders = (even, even[-1:] + even[:-1])
    for step in range(levels - 1):
        pairs = [(i, i ^ 1 << orders[i % 2][step]) for i in range(size)]
        partner = lax.ppermute(keyval, "seq", pairs)
        keyval = jnp.concatenate([beside(step, keyval), partner], axis=0)
    far = swapped(keyval, "seq", 0)
    return beside(levels - 1, keyval), far


def early_exchange(keyval, span, beside):
    levels = span.bit_length() - 1
    crossed, fresh = [], keyval
    for level in range(levels - 1, 1, -1):
        crossed.append(swapped(fresh, "seq", 1))
        partner = swapped(keyval, "seq", level)
        keyval = jnp.concatenate([beside(levels - 1 - level, keyval), partner], axis=0)
        fresh = partner
    if levels > 1:
        crossed.append(swapped(fresh, "seq", 1))
        keyval = jnp.concatenate([beside(levels - 2, keyval), *crossed], axis=0)
    far = swapped(keyval, "seq", 0)
    return beside(levels - 1, keyval), far


def whole_body(
    tokens,
    attn_gain,
    query_first,
    key_first,
    segment_value,
    output_first,
    mlp_gain,
    up_weight,
    down_weight,
    second_gain,
    query_second,
    key_second,
    value_second,
    output_second,
    segment_offset,
    global_offset,
):
    seq_count = lax.axis_size("seq")
    seg_span = min(SEG_MAX, seq_count)
    heads = segment_offset.shape[0]
    count, width = tokens.shape
    head_size = width // heads
    hidden = up_weight.shape[1]
    stride = count // (KEYS // seg_span)
    stride_two = count // (KEYS // seq_count)
    groups, groups_two = count // stride, count // stride_two
    chunk = max(ROWS, stride_two)
    picked_count = groups_two * heads
    rest_count = count - picked_count
    part = hidden // 4

    def near(*shape):
        return pltpu.VMEM(shape, BF16)

    def attention_work(rows):
        return [pltpu.VMEM((2, rows, KEYS), F32), near(2, rows, KEYS)]

    held_shapes = [near(width, KEYS // 2), pltpu.VMEM((1, 128), F32)]
    small_work = [pltpu.SMEM((heads,), jnp.int32), pltpu.VMEM((width,), F32)]

    (keyval,) = local_call(
        functools.partial(first_keys_kernel, stride=stride),
        [near(1, 2, groups, width)],
        (segment_offset, tokens, attn_gain, key_first, segment_value),
        [near(count, width), near(2, width, width)] + small_work,
        far=(0, 1, 2, 3, 4),
        copies=8,
        flops=2 * heads * groups * width * (count + 2 * width),
        name="first_keys",
    )
    made = {}

    def beside_first(level, held):
        if level == 0:
            made["rows"], made["normed"], made["chooser"], made["back"], held = local_call(
                functools.partial(order_kernel, stride=stride_two, chunk=chunk),
                [
                    near(count, width),
                    near(count, width),
                    near(picked_count, picked_count),
                    near(chunk, chunk),
                ],
                (global_offset, tokens, attn_gain),
                [near(count, width)] + small_work,
                far=(0, 1, 2),
                copies=3,
                relay=held,
                flops=2 * count * width * chunk,
                name="order",
            )
        if level == min(1, seg_span.bit_length() - 2):
            made["picked"], made["rest"], made["peaks"], held = local_call(
                functools.partial(first_query_kernel, heads=heads),
                [near(picked_count, width), near(rest_count, width), pltpu.VMEM((1, 128), F32)],
                (made["normed"], query_first),
                [],
                relay=held,
                flops=2 * count * width * width,
                name="first_query",
            )
        if level == seg_span.bit_length() - 2:
            made["picked_early"], made["rest_early"], made["turned"], made["key_peaks"] = local_call(
                functools.partial(near_weights_kernel, heads=heads),
                [near(heads, picked_count, KEYS // 2), near(heads, rest_count, KEYS // 2)]
                + held_shapes,
                (made["picked"], made["rest"], held),
                [pltpu.VMEM((2, rest_count, KEYS), F32)],
                flops=2 * 256 * KEYS // 2 * heads * count,
                name="near_weights",
            )
        return held

    keyval, keyval_far = early_exchange(keyval, seg_span, beside_first)
    rows = made["rows"]
    query_peaks, near_held = made["peaks"], (made["turned"], made["key_peaks"])
    row_flops = 2 * width * (2 * hidden + width) + 4 * 256 * KEYS * heads
    picked_second, picked_normed, keyval_two, turned, peaks = local_call(
        functools.partial(picked_kernel, heads=heads),
        [
            near(picked_count, width),
            near(picked_count, width),
            near(1, 2, groups_two, width),
        ]
        + held_shapes,
        (
            made["chooser"],
            rows,
            made["picked"],
            query_peaks,
            made["picked_early"],
            keyval,
            keyval_far,
            *near_held,
            output_first,
            mlp_gain,
            up_weight,
            down_weight,
            second_gain,
            key_second,
            value_second,
        ),
        [near(2, width, width), near(picked_count, width)]
        + attention_work(picked_count)
        + [near(picked_count, width), pltpu.VMEM((2, picked_count, part), F32)]
        + [near(2, picked_count, part), pltpu.VMEM((picked_count, width), F32)],
        far=(14, 15),
        copies=2,
        flops=row_flops * picked_count,
        name="layer_of_picked",
    )
    seconds = [picked_second]

    def rest_attention(held):
        made["mixed"], held = local_call(
            functools.partial(rest_attention_kernel, heads=heads),
            [near(rest_count, width)],
            (
                made["rest"],
                query_peaks,
                made["rest_early"],
                keyval,
                keyval_far,
                made["turned"],
                turned,
                peaks,
            ),
            attention_work(rest_count),
            relay=held,
            flops=4 * 256 * KEYS * heads * rest_count,
            name="rest_attention",
        )
        return held

    half = hidden // 4 * 3

    def rest_up(held):
        made["first"], made["normed"], made["inner"], held = local_call(
            rest_up_kernel,
            [near(rest_count, width), near(rest_count, width), near(rest_count, half)],
            (rows, made["mixed"], output_first, mlp_gain, up_weight),
            [pltpu.VMEM((2, rest_count, part), F32)],
            relay=held,
            flops=2 * width * (half + width) * rest_count,
            name="rest_up",
        )
        return held

    def rest_down(held):
        result, held = local_call(
            rest_down_kernel,
            [near(rest_count, width)],
            (made["first"], made["normed"], made["inner"], up_weight, down_weight),
            [pltpu.VMEM((1, rest_count, part), F32), near(rest_count, hidden - half)],
            relay=held,
            flops=2 * width * (2 * hidden - half) * rest_count,
            name="rest_down",
        )
        seconds.append(result)
        return held

    def picked_query(held):
        made["picked_two"], made["picked_peaks"], held = local_call(
            functools.partial(picked_query_kernel, heads=heads),
            [near(picked_count, width), pltpu.VMEM((1, 128), F32)],
            (picked_normed, query_second),
            [],
            relay=held,
            flops=2 * picked_count * width * width,
            name="picked_query",
        )
        return held

    def rest_query(held):
        made["query_two"], made["peaks_two"], held = local_call(
            functools.partial(rest_query_kernel, heads=heads),
            [near(count, width), pltpu.VMEM((1, 128), F32)],
            (made["picked_two"], made["picked_peaks"], seconds[1], second_gain, query_second),
            [near(rest_count, width)],
            relay=held,
            flops=2 * rest_count * width * width,
            name="rest_query",
        )
        return held

    tasks = [[rest_attention, picked_query], [rest_up], [rest_down], [rest_query]]
    levels = seq_count.bit_length() - 1

    def beside_second(level, held):
        for work in tasks[len(tasks) * level // levels : len(tasks) * (level + 1) // levels]:
            for task in work:
                held = task(held)
        return held

    keyval_two, keyval_two_far = exchange(keyval_two, seq_count, beside_second)
    (encoded,) = local_call(
        functools.partial(second_kernel, heads=heads, parts=len(seconds)),
        [jax.ShapeDtypeStruct((count, width), BF16)],
        (
            made["back"],
            *seconds,
            made["query_two"],
            made["peaks_two"],
            keyval_two,
            keyval_two_far,
            output_second,
        ),
        held_shapes[:1] * 2
        + [near(1, width, width)]
        + [near(count, width)] * 3
        + attention_work(count),
        far=(len(seconds) + 5,),
        out_near=False,
        copies=1 + count // chunk,
        flops=count * (2 * width * width + 4 * 256 * KEYS * heads),
        name="second_attention",
    )
    return encoded


def solution(mesh):
    placed = (
        P(("slides", "seq", "mp"), None),
        P(),
        P(None, "mp"),
        P(None, "mp"),
        P(None, "mp"),
        P("mp", None),
        P(),
        P(None, "mp"),
        P("mp", None),
        P(),
        P(None, "mp"),
        P(None, "mp"),
        P(None, "mp"),
        P("mp", None),
        P("mp"),
        P("mp"),
    )
    fits = mesh.shape["mp"] == 1 and mesh.shape["seq"] in (2, 4, 8, 16)
    return jax.shard_map(
        whole_body if fits else split_body,
        mesh=mesh,
        in_specs=placed,
        out_specs=P(("slides", "seq", "mp"), None),
        check_vma=False,
    )
```

```python
import functools
import math

import jax
import jax.numpy as jnp
from jax import lax
from jax.experimental import pallas as pl
from jax.experimental.pallas import tpu as pltpu
from jax.sharding import PartitionSpec as P

KEYS = 256
SEG_MAX = 16
ROWS = 256
LOG2E = 1.4426950408889634
BF16 = jnp.bfloat16
F32 = jnp.float32
VMEM_LIMIT = 22 * 1024 * 1024


def swapped(x, axis, apart):
    return lax.ppermute(x, axis, [(i, i ^ 1 << apart) for i in range(lax.axis_size(axis))])


def norm_rows(values, gain):
    center = values - jnp.mean(values, axis=-1, keepdims=True)
    spread = jnp.mean(center * center, axis=-1, keepdims=True)
    return (center * lax.rsqrt(spread + 1e-05) * gain).astype(jnp.bfloat16)


def pick_keys(hidden, offsets, stride, key_weight, value_weight):
    token_count, width = hidden.shape
    head_count = offsets.shape[0]
    head_size = key_weight.shape[1] // head_count
    grouped_rows = hidden.reshape(token_count // stride, stride, width)
    dilation_selector = (
        lax.broadcasted_iota(jnp.int32, (stride, head_count), 0) == offsets[None, :]
    ).astype(jnp.bfloat16)
    chosen = jnp.einsum(
        "nof,oj->njf", grouped_rows, dilation_selector, preferred_element_type=jnp.float32
    ).astype(jnp.bfloat16)
    key_heads = jnp.einsum(
        "xkr,rkf->xkf",
        chosen,
        key_weight.reshape(width, head_count, head_size),
        preferred_element_type=jnp.float32,
    ).astype(jnp.bfloat16)
    value_heads = jnp.einsum(
        "xkr,rkf->xkf",
        chosen,
        value_weight.reshape(width, head_count, head_size),
        preferred_element_type=jnp.float32,
    ).astype(jnp.bfloat16)
    picked = token_count // stride
    return jnp.stack(
        [
            key_heads.reshape(picked, head_count * head_size),
            value_heads.reshape(picked, head_count * head_size),
        ]
    )


def attend_local(query, keyval, head_count):
    token_count, width = query.shape
    head_size = width // head_count
    query_heads = query.reshape(token_count, head_count, head_size)
    key_heads = keyval[0].reshape(-1, head_count, head_size)
    value_heads = keyval[1].reshape(-1, head_count, head_size)
    scores = jnp.einsum(
        "thd,khd->htk", query_heads, key_heads, preferred_element_type=jnp.float32
    ) * head_size ** (-0.5)
    highest = jnp.max(scores, axis=-1, keepdims=True)
    weights = jnp.exp(scores - highest)
    weights = (weights / jnp.sum(weights, axis=-1, keepdims=True)).astype(jnp.bfloat16)
    mixed = jnp.einsum(
        "htk,khd->thd", weights, value_heads, preferred_element_type=jnp.float32
    ).astype(jnp.bfloat16)
    return mixed.reshape(token_count, width)


def merge_branch_pair(mine, other, level, token_position):
    lower = token_position >> level & 1 == 0
    return jnp.where(
        lower, jnp.concatenate((mine, other), axis=1), jnp.concatenate((other, mine), axis=1)
    )


def spread_segment(keyval, seg_span, token_position):
    for level in range(seg_span.bit_length() - 1):
        partner = swapped(keyval, "seq", level)
        keyval = merge_branch_pair(keyval, partner, level, token_position)
    return keyval


def spread_global(keyval_two):
    keyval_two = lax.all_gather(keyval_two, "seq", axis=1, tiled=True)
    return keyval_two


def combine(partial_value, residual_full, need_full):
    row_count = residual_full.shape[0] // lax.axis_size("mp")
    row_start = lax.axis_index("mp") * row_count
    share = lax.psum_scatter(partial_value, "mp", scatter_dimension=0, tiled=True)
    own_rows = lax.dynamic_slice_in_dim(residual_full, row_start, row_count, 0)
    own_rows = (own_rows.astype(jnp.float32) + share).astype(jnp.bfloat16)
    full_rows = lax.all_gather(own_rows, "mp", axis=0, tiled=True) if need_full else own_rows
    return (own_rows, full_rows)


def split_body(
    tokens,
    attn_gain,
    query_first,
    key_first,
    segment_value,
    output_first,
    mlp_gain,
    up_weight,
    down_weight,
    second_gain,
    query_second,
    key_second,
    value_second,
    output_second,
    segment_offset,
    global_offset,
):
    seq_count = lax.axis_size("seq")
    token_position = lax.axis_index("seq")
    seg_span = min(SEG_MAX, seq_count)
    head_count = segment_offset.shape[0]
    full_rows = lax.all_gather(tokens, "mp", axis=0, tiled=True)
    token_count = full_rows.shape[0]
    hidden = norm_rows(full_rows.astype(jnp.float32), attn_gain)
    query = jnp.dot(hidden, query_first, preferred_element_type=jnp.float32).astype(jnp.bfloat16)
    seg_stride = token_count // (KEYS // seg_span)
    keyval = pick_keys(hidden, segment_offset, seg_stride, key_first, segment_value)
    keyval = spread_segment(keyval, seg_span, token_position)
    mixed = attend_local(query, keyval, head_count)
    partial_value = jnp.dot(mixed, output_first, preferred_element_type=jnp.float32)
    own_rows, first_rows = combine(partial_value, full_rows, True)
    normed = norm_rows(first_rows.astype(jnp.float32), mlp_gain)
    inner = jax.nn.gelu(
        jnp.dot(normed, up_weight, preferred_element_type=jnp.float32), approximate=True
    ).astype(jnp.bfloat16)
    partial_value = jnp.dot(inner, down_weight, preferred_element_type=jnp.float32)
    own_rows, second_rows = combine(partial_value, first_rows, True)
    hidden_two = norm_rows(second_rows.astype(jnp.float32), second_gain)
    query_two = jnp.dot(hidden_two, query_second, preferred_element_type=jnp.float32).astype(
        jnp.bfloat16
    )
    glob_stride = token_count // (KEYS // seq_count)
    keyval_two = pick_keys(hidden_two, global_offset, glob_stride, key_second, value_second)
    keyval_two = spread_global(keyval_two)
    mixed_two = attend_local(query_two, keyval_two, head_count)
    partial_value = jnp.dot(mixed_two, output_second, preferred_element_type=jnp.float32)
    own_rows, unused_rows = combine(partial_value, second_rows, False)
    return own_rows


def one_hot(condition):
    return jnp.where(condition, 1.0, 0.0).astype(BF16)


def dot(left, right):
    return jnp.dot(left, right, preferred_element_type=F32)


def pieces(count, size):
    size = size if count % size == 0 else count
    return [slice(start, start + size) for start in range(0, count, size)]


def norm_into(out, start, source, gain, count):
    for span in pieces(count, 64):
        out[start + span.start : start + span.stop, :] = norm_rows(
            source[span, :].astype(F32), gain
        )


def bring(source, target, sem):
    copy = pltpu.make_async_copy(source, target, sem)
    copy.start()
    return copy


def pick_matrix(offsets, heads, groups, stride):
    count = groups * stride
    place = lax.broadcasted_iota(jnp.int32, (groups, count), 1)
    place = place - lax.broadcasted_iota(jnp.int32, (groups, count), 0) * stride
    return jnp.concatenate([one_hot(place == offsets[h]) for h in range(heads)], axis=0)


def project_keys(chosen, heads, weights, keyval_ref):
    rows, width = chosen.shape
    groups, head_size = rows // heads, width // heads
    for slot, weight in enumerate(weights):
        held = weight()
        for span in pieces(width, 256):
            first, last = span.start // head_size, (span.stop - 1) // head_size + 1
            wide = dot(chosen[first * groups : last * groups], held[:, span])
            column = lax.broadcasted_iota(jnp.int32, (groups, span.stop - span.start), 1)
            total = wide[:groups]
            for h in range(first + 1, last):
                row = (h - first) * groups
                own = column >= h * head_size - span.start
                total = jnp.where(own, wide[row : row + groups], total)
            total = total.astype(BF16)
            for copy in range(keyval_ref.shape[0]):
                keyval_ref[copy, slot, :, span] = total


def ranks(offsets, chunk, stride, share, axis):
    heads = offsets.shape[0]

    def places(way):
        shape = (1, chunk) if way else (chunk, 1)
        place = lax.broadcasted_iota(jnp.int32, shape, way)
        inside = lax.rem(place, stride)
        taken = inside == offsets[0]
        for h in range(1, heads):
            taken = taken | (inside == offsets[h])
        return place, inside, jnp.where(taken, inside, inside + stride)

    place, inside, order = places(axis)
    other_place, _, other_order = places(1 - axis)
    ahead = (other_order < order) & (lax.div(other_place, stride) == lax.div(place, stride))
    rank = jnp.sum(jnp.where(ahead, 1, 0), axis=1 - axis, keepdims=True)
    group = lax.div(place, stride)
    return jnp.where(
        rank < heads, group * heads + rank, share + group * (stride - heads) + rank - heads
    )


def slots_of(offsets, heads):
    values = [offsets[h] for h in range(heads)]
    fresh = []
    for h in range(heads):
        seen = jnp.int32(1)
        for earlier in values[:h]:
            seen = jnp.where(earlier == values[h], 0, seen)
        fresh.append(seen)
    slots = []
    for h in range(heads):
        slot = jnp.int32(0)
        for other in range(heads):
            slot = slot + jnp.where(values[other] < values[h], fresh[other], 0)
        slots.append(slot)
    return slots


def first_keys_kernel(
    offsets, tokens, gain, key_weight, value_weight, keyval, rows, wide, picks, scale, sems, *, stride
):
    spans = pieces(tokens.shape[0], tokens.shape[0] // 4)
    copies = [
        bring(offsets, picks, sems.at[0]),
        bring(gain, scale, sems.at[1]),
        *[bring(tokens.at[x], rows.at[x], sems.at[4 + i]) for i, x in enumerate(spans)],
        bring(key_weight, wide.at[0], sems.at[2]),
        bring(value_weight, wide.at[1], sems.at[3]),
    ]
    heads = offsets.shape[0]
    copies[0].wait()
    chooser = pick_matrix(picks, heads, rows.shape[0] // stride, stride)
    copies[1].wait()
    chosen = None
    for copy, span in zip(copies[2:-2], spans):
        copy.wait()
        part = dot(chooser[:, span], rows[span, :])
        chosen = part if chosen is None else chosen + part
    chosen = norm_rows(chosen, scale[...])

    def weight(slot):
        copies[slot - 2].wait()
        return wide[slot]

    project_keys(
        chosen, heads, [functools.partial(weight, slot) for slot in range(2)], keyval
    )


def order_kernel(
    offsets,
    tokens,
    gain,
    moved_rows,
    normed,
    chooser,
    back,
    rows,
    picks,
    scale,
    sems,
    *,
    stride,
    chunk,
):
    copies = [
        bring(offsets, picks, sems.at[0]),
        bring(tokens, rows, sems.at[1]),
        bring(gain, scale, sems.at[2]),
    ]
    count = tokens.shape[0]
    share = chunk // stride * offsets.shape[0]
    rest = chunk - share
    picked = count // chunk * share
    copies[0].wait()
    mover = one_hot(
        lax.broadcasted_iota(jnp.int32, (chunk, chunk), 0)
        == ranks(picks, chunk, stride, share, 1)
    )
    heads = offsets.shape[0]
    chooser[...] = pick_matrix(slots_of(picks, heads), heads, picked // heads, heads)
    back[...] = one_hot(
        lax.broadcasted_iota(jnp.int32, (chunk, chunk), 1)
        == ranks(picks, chunk, stride, share, 0)
    )
    copies[1].wait()
    copies[2].wait()
    for c in range(count // chunk):
        moved = dot(mover, rows[c * chunk : (c + 1) * chunk, :]).astype(BF16)
        moved_rows[c * share : (c + 1) * share, :] = moved[:share]
        moved_rows[picked + c * rest : picked + (c + 1) * rest, :] = moved[share:]
    norm_into(normed, 0, moved_rows, scale[...], count)


def score_scale(head_size):
    return head_size ** (-0.5) * LOG2E


def project_rows(normed, span, weight, out, peak):
    query = dot(normed[span, :], weight[...])
    out[...] = query.astype(BF16)
    for part in pieces(query.shape[0], 64):
        square = query[part] * query[part]
        peak = square if peak is None else jnp.maximum(peak, square)
    return peak


def project_query(normed, weight, outs, heads, peaks):
    peak = None
    for out, row in outs:
        for span in pieces(out.shape[0], 512 if out.shape[0] % 512 == 0 else 256):
            place = slice(row + span.start, row + span.stop)
            peak = project_rows(normed, place, weight, out.at[span], peak)
    peaks[...] = summed_peaks(peak.astype(BF16), heads)


def first_query_kernel(normed, weight, picked, rest, peaks, sems, *, heads):
    del sems
    project_query(normed, weight, [(picked, 0), (rest, picked.shape[0])], heads, peaks)


def head_windows(head_size, width):
    period = min(width, math.lcm(head_size, 128))
    windows = []
    for h in range(period // head_size):
        start = h * head_size // 128 * 128
        stop = min(period, -(-(h + 1) * head_size // 128) * 128)
        windows.append((start, stop - start))
    return period, windows


def summed_peaks(peak, heads):
    width = peak.shape[1]
    column = lax.broadcasted_iota(jnp.int32, (width, 128), 0)
    head = lax.broadcasted_iota(jnp.int32, (width, 128), 1)
    low = head * (width // heads)
    sums = one_hot((column >= low) & (column < low + width // heads))
    return jnp.max(dot(peak, sums), axis=0, keepdims=True)


def load_keys(keyval, turned):
    keys = jnp.concatenate([keyval[i, 0] for i in range(keyval.shape[0])], axis=0)
    turned[...] = keys.T
    return keys * keys


def small_scores(query_peaks, key_peaks, head_size):
    scale = score_scale(head_size)
    return jnp.max(query_peaks[...] * key_peaks[...]) < 9000.0 / (scale * scale)


def reciprocal(x):
    guess = pl.reciprocal(x, approx=True)
    return guess * (2.0 - x * guess)


def padded_keys(turned, base, head, head_size, start, size):
    low = base + head * head_size
    rows = pl.ds(low if isinstance(low, int) else pl.multiple_of(low, 16), head_size)
    own = jnp.concatenate([part[rows, :] for part in turned], axis=1)
    low = head * head_size - start
    parts = [own]
    if low:
        parts.insert(0, jnp.zeros((low, own.shape[1]), BF16))
    if low + head_size < size:
        parts.append(jnp.zeros((size - low - head_size, own.shape[1]), BF16))
    return jnp.concatenate(parts, axis=0)


def score_pair(query, span, base, head, head_size, windows, turned):
    start = windows[head][0]
    size = windows[head + 1][0] + windows[head + 1][1] - start
    keys = [padded_keys([turned], base, head + i, head_size, start, size) for i in range(2)]
    return dot(query[span, pl.ds(base + start, size)], jnp.concatenate(keys, axis=1))


def near_weights_kernel(
    picked, rest, keyval, picked_early, rest_early, turned, peaks, scores_ref, sems, *, heads
):
    del sems
    peaks[...] = summed_peaks(load_keys(keyval, turned), heads)
    width = picked.shape[1]
    head_size = width // heads
    scale = score_scale(head_size)
    key_count = turned.shape[1]
    period, windows = head_windows(head_size, width)
    jobs = [
        (query, early, head)
        for query, early in ((picked, picked_early), (rest, rest_early))
        for head in range(0, len(windows), 2)
    ]

    @pl.loop(0, width // period)
    def _(turn):
        base = pl.multiple_of(turn * period, 128)

        def score(i):
            query, _, head = jobs[i]
            rows = query.shape[0]
            scores_ref[i % 2, :rows] = score_pair(
                query, slice(0, rows), base, head, head_size, windows, turned
            )

        score(0)
        for i, (query, early, head) in enumerate(jobs):
            if i + 1 < len(jobs):
                score(i + 1)
            for part in pieces(query.shape[0], 64):
                weights = jnp.exp2(scores_ref[i % 2, part, :] * scale).astype(BF16)
                for j in range(2):
                    early[turn * len(windows) + head + j, part, :] = weights[
                        :, j * key_count : (j + 1) * key_count
                    ]


def attend_rows(
    query, first_row, rows, heads, turned, keyvals, mixed_ref, mixed_row, work, plain, early=None
):
    scores_ref, weights_ref = work
    width = query.shape[1]
    key_count = sum(part.shape[1] for part in turned)
    head_size = width // heads
    period, windows = head_windows(head_size, width)
    span = pl.ds(first_row, rows)
    out_span = pl.ds(mixed_row, rows)
    scale = score_scale(head_size)
    lane = lax.broadcasted_iota(jnp.int32, (1, 128), 1)
    step = 2 if early is not None else 1
    piece = max(64, min(256, rows // 512 * 128))

    def take_turn(turn):
        base = turn * period if plain else pl.multiple_of(turn * period, 128)
        sums = {}

        def score(i):
            if early is not None:
                scores = score_pair(query, span, base, 2 * i, head_size, windows, turned[1])
            else:
                start, size = windows[i]
                scores = dot(
                    query[span, pl.ds(base + start, size)],
                    padded_keys(turned, base, i, head_size, start, size),
                )
            scores_ref[i % 2, :rows] = scores

        def weigh(h):
            for part in pieces(rows, piece):
                scores = scores_ref[h % 2, part, :]
                if not plain:
                    scores = scores - jnp.max(scores, axis=1, keepdims=True)
                weights_ref[h % 2, part, :] = jnp.exp2(scores * scale).astype(BF16)

        def mix(h):
            start, size = windows[h]
            low = h * head_size - start
            values = jnp.concatenate(
                [
                    x[i, 1, :, pl.ds(base + start, size)]
                    for x in keyvals
                    for i in range(x.shape[0])
                ],
                axis=0,
            )
            column = lax.broadcasted_iota(jnp.int32, (key_count, size), 1)
            own = (column >= low) & (column < low + head_size)
            values = jnp.where(own, values, jnp.ones((), BF16))
            if early is not None:
                half = key_count // 2
                far = weights_ref[h // 2 % 2, :rows, h % 2 * half : (h % 2 + 1) * half]
                near = early[turn * len(windows) + h, span, :]
                weights = jnp.concatenate([near, far], axis=1)
            else:
                weights = weights_ref[h % 2, :rows]
            mixed = dot(weights, values)
            for offset in range(0, size, 128):
                own = mixed[:, offset : offset + 128]
                total = pltpu.roll(own, 64, 1)
                at = start + offset
                if at in sums:
                    mine = lane >= h * head_size - at
                    own = jnp.where(mine, own, sums[at][0])
                    total = jnp.where(mine, total, sums[at][1])
                sums[at] = own, total
                if (h + 1) * head_size >= at + 128:
                    own, total = sums.pop(at)
                    mixed_ref[out_span, pl.ds(base + at, 128)] = (
                        own * reciprocal(total)
                    ).astype(BF16)

        count = len(windows) // step
        score(0)
        for i in range(count):
            if i:
                for h in range((i - 1) * step, i * step):
                    mix(h)
            if i + 1 < count:
                score(i + 1)
            weigh(i)
        for h in range((count - 1) * step, count * step):
            mix(h)

    if plain:
        for turn in range(width // period):
            take_turn(turn)
    else:
        pl.loop(0, width // period)(take_turn)


def attend(query, rows, heads, turned, keyvals, mixed_ref, work, small, early=None):
    size = math.gcd(rows, ROWS)

    @pl.when(small)
    def _():
        attend_rows(query, 0, rows, heads, turned, keyvals, mixed_ref, 0, work, True, early)

    @pl.when(jnp.logical_not(small))
    def _():
        @pl.loop(0, rows // size)
        def _(step):
            row = pl.multiple_of(step * size, size)
            attend_rows(
                query,
                row,
                size,
                heads,
                turned,
                keyvals,
                mixed_ref,
                row,
                work,
                False,
            )


def gelu(x):
    half = 0.5 * x
    return half + half * jnp.tanh(x * (0.7978845608028654 + 0.035677408136300125 * (x * x)))


def widen(normed, up_weight, low, wide_ref, inner):
    rows = normed.shape[0]
    spans = pieces(inner.shape[1], wide_ref.shape[2])

    def product(i):
        columns = slice(low + spans[i].start, low + spans[i].stop)
        wide_ref[i % 2] = dot(normed[...], up_weight[:, columns])

    product(0)
    for i, span in enumerate(spans):
        if i + 1 < len(spans):
            product(i + 1)
        for part in pieces(rows, 32):
            inner[part, span] = gelu(wide_ref[i % 2, part, :]).astype(BF16)


def feed_forward(normed, up_weight, down_weight, total, wide_ref, inner):
    rows = normed.shape[0]
    spans = pieces(up_weight.shape[1], wide_ref.shape[2])

    def product(i):
        wide_ref[i % 2] = dot(normed[...], up_weight[:, spans[i]])

    product(0)
    for i, span in enumerate(spans):
        if i + 1 < len(spans):
            product(i + 1)
        for part in pieces(rows, 32):
            inner[i % 2, part, :] = gelu(wide_ref[i % 2, part, :]).astype(BF16)
        total[...] += dot(inner[i % 2], down_weight[span, :])


def narrow(inners, down_weight, first, second, size):
    for span in pieces(second.shape[1], size):
        total = first[:, span].astype(F32)
        low = 0
        for inner in inners:
            high = low + inner.shape[1]
            total = total + dot(inner[...], down_weight[low:high, span])
            low = high
        second[:, span] = total.astype(BF16)


def add_heads(tokens, first_row, mixed, out_weight, gain, first, normed):
    before = None
    for span in pieces(mixed.shape[0], 256):
        total = dot(mixed[span, :], out_weight[...])
        rows = tokens[first_row + span.start : first_row + span.stop, :]
        first[span, :] = (rows.astype(F32) + total).astype(BF16)
        if before is not None:
            norm_into(normed, before.start, first.at[before], gain, before.stop - before.start)
        before = span
    norm_into(normed, before.start, first.at[before], gain, before.stop - before.start)


def picked_kernel(
    chooser,
    tokens,
    query,
    query_peaks,
    early,
    keyval,
    keyval_far,
    turned_near,
    peaks_near,
    out_weight,
    mlp_gain,
    up_weight,
    down_weight,
    gain,
    key_weight,
    value_weight,
    second,
    normed,
    keyval_two,
    turned,
    peaks,
    held,
    mixed,
    scores,
    weights,
    first,
    wide,
    inner,
    total,
    sems,
    *,
    heads,
):
    copies = [
        bring(x, held.at[i], sems.at[i]) for i, x in enumerate((key_weight, value_weight))
    ]
    rows = second.shape[0]
    keyvals = (keyval, keyval_far)
    squares = load_keys(keyval_far, turned)
    peaks[...] = jnp.maximum(peaks_near[...], summed_peaks(squares, heads))
    small = small_scores(query_peaks, peaks, query.shape[1] // heads)
    attend(
        query,
        rows,
        heads,
        (turned_near, turned),
        keyvals,
        mixed,
        (scores, weights),
        small,
        early,
    )
    add_heads(tokens, 0, mixed, out_weight, mlp_gain[...], first, normed)
    total[...] = first[...].astype(F32)
    feed_forward(normed, up_weight, down_weight, total, wide, inner)
    second[...] = total[...].astype(BF16)
    norm_into(normed, 0, second, gain[...], rows)
    chosen = dot(chooser[...], normed[...]).astype(BF16)

    def weight(slot):
        copies[slot].wait()
        return held[slot]

    project_keys(
        chosen, heads, [functools.partial(weight, slot) for slot in range(2)], keyval_two
    )


def rest_attention_kernel(
    query,
    query_peaks,
    early,
    keyval,
    keyval_far,
    turned_near,
    turned,
    peaks,
    mixed,
    scores,
    weights,
    sems,
    *,
    heads,
):
    del sems
    attend(
        query,
        mixed.shape[0],
        heads,
        (turned_near, turned),
        (keyval, keyval_far),
        mixed,
        (scores, weights),
        small_scores(query_peaks, peaks, query.shape[1] // heads),
        early,
    )


def rest_up_kernel(
    tokens, mixed, out_weight, gain, up_weight, first, normed, inner, wide, sems
):
    del sems
    add_heads(
        tokens, tokens.shape[0] - mixed.shape[0], mixed, out_weight, gain[...], first, normed
    )
    widen(normed, up_weight, 0, wide, inner)


def rest_down_kernel(
    first, normed, inner, up_weight, down_weight, second, wide, inner_more, sems
):
    del sems
    widen(normed, up_weight, inner.shape[1], wide, inner_more)
    narrow([inner, inner_more], down_weight, first, second, 256)


def picked_query_kernel(normed, weight, query, peaks, sems, *, heads):
    del sems
    project_query(normed, weight, [(query, 0)], heads, peaks)


def rest_query_kernel(
    picked, picked_peaks, rows, gain, weight, query, peaks, normed, sems, *, heads
):
    del sems
    start = picked.shape[0]
    query[:start, :] = picked[...]
    norm_into(normed, 0, rows, gain[...], rows.shape[0])
    out = query.at[pl.ds(start, rows.shape[0])]
    project_query(normed, weight, [(out, 0)], heads, peaks)
    peaks[...] = jnp.maximum(peaks[...], picked_peaks[...])


def second_kernel(*refs, heads, parts):
    back, *rows = refs[: 1 + parts]
    query, query_peaks, keyval, keyval_far, out_weight, encoded = refs[1 + parts : 7 + parts]
    turned_near, turned, held, mixed = refs[7 + parts : 11 + parts]
    result, ready, scores, weights, sems = refs[11 + parts :]
    copy = bring(out_weight, held.at[0], sems.at[0])
    keyvals = (keyval, keyval_far)
    squares = jnp.maximum(load_keys(keyval, turned_near), load_keys(keyval_far, turned))
    count = query.shape[0]
    small = small_scores(query_peaks, summed_peaks(squares, heads), query.shape[1] // heads)
    attend(
        query, count, heads, (turned_near, turned), keyvals, mixed, (scores, weights), small
    )
    chunk = back.shape[0]
    share = rows[0].shape[0] * chunk // count
    rest_share = chunk - share
    copy.wait()
    start = 0
    for part in rows:
        span = slice(start, start + part.shape[0])
        total = part[...].astype(F32) + dot(mixed[span, :], held[0])
        result[span, :] = total.astype(BF16)
        start += part.shape[0]
    start = count // chunk * share
    copies = []
    for c in range(count // chunk):
        far = start + c * rest_share
        blend = jnp.concatenate(
            [result[c * share : (c + 1) * share, :], result[far : far + rest_share, :]], axis=0
        )
        span = pl.ds(c * chunk, chunk)
        ready[span, :] = dot(back[...], blend).astype(BF16)
        copies.append(bring(ready.at[span], encoded.at[span], sems.at[1 + c]))
    for copy in copies:
        copy.wait()


def relaying(kernel, ins, outs, *refs):
    end = ins + 1 + outs
    refs[end][...] = refs[ins][...]
    kernel(*refs[:ins], *refs[ins + 1 : end], *refs[end + 1 :])


def local_call(kernel, outs, inputs, scratch, scalars=0, far=(), relay=None, out_near=True, copies=1, flops=0, name=None):
    outs, inputs = list(outs), list(inputs)
    if relay is not None:
        kernel = functools.partial(relaying, kernel, len(inputs), len(outs))
        inputs.append(relay)
        outs.append(pltpu.VMEM(relay.shape, relay.dtype))
    specs, placed = [], []
    for i, x in enumerate(inputs):
        if i < scalars:
            specs.append(pl.BlockSpec(memory_space=pltpu.SMEM))
        elif i in far:
            specs.append(pl.BlockSpec(memory_space=pltpu.HBM))
            x = pltpu.with_memory_space_constraint(x, pltpu.HBM)
        else:
            specs.append(pl.BlockSpec(memory_space=pltpu.VMEM))
            x = pltpu.with_memory_space_constraint(x, pltpu.VMEM)
        placed.append(x)
    return pl.pallas_call(
        kernel,
        out_shape=outs,
        in_specs=specs,
        out_specs=[
            pl.BlockSpec(memory_space=pltpu.VMEM if out_near else pltpu.HBM)
        ] * len(outs),
        scratch_shapes=list(scratch) + [pltpu.SemaphoreType.DMA((copies,))],
        compiler_params=pltpu.CompilerParams(vmem_limit_bytes=VMEM_LIMIT),
        cost_estimate=pl.CostEstimate(
            flops=int(flops),
            transcendentals=0,
            bytes_accessed=sum(inputs[i].size * inputs[i].dtype.itemsize for i in far),
        ),
        name=name,
    )(*placed)


def exchange(keyval, span, beside):
    size = lax.axis_size("seq")
    levels = span.bit_length() - 1
    even = list(range(levels - 1, 0, -1))
    orders = (even, even[-1:] + even[:-1])
    for step in range(levels - 1):
        pairs = [(i, i ^ 1 << orders[i % 2][step]) for i in range(size)]
        partner = lax.ppermute(keyval, "seq", pairs)
        keyval = jnp.concatenate([beside(step, keyval), partner], axis=0)
    far = swapped(keyval, "seq", 0)
    return beside(levels - 1, keyval), far


def early_exchange(keyval, span, beside):
    levels = span.bit_length() - 1
    crossed, fresh = [], keyval
    for level in range(levels - 1, 1, -1):
        crossed.append(swapped(fresh, "seq", 1))
        partner = swapped(keyval, "seq", level)
        keyval = jnp.concatenate([beside(levels - 1 - level, keyval), partner], axis=0)
        fresh = partner
    if levels > 1:
        crossed.append(swapped(fresh, "seq", 1))
        keyval = jnp.concatenate([beside(levels - 2, keyval), *crossed], axis=0)
    far = swapped(keyval, "seq", 0)
    return beside(levels - 1, keyval), far


def whole_body(
    tokens,
    attn_gain,
    query_first,
    key_first,
    segment_value,
    output_first,
    mlp_gain,
    up_weight,
    down_weight,
    second_gain,
    query_second,
    key_second,
    value_second,
    output_second,
    segment_offset,
    global_offset,
):
    seq_count = lax.axis_size("seq")
    seg_span = min(SEG_MAX, seq_count)
    heads = segment_offset.shape[0]
    count, width = tokens.shape
    head_size = width // heads
    hidden = up_weight.shape[1]
    stride = count // (KEYS // seg_span)
    stride_two = count // (KEYS // seq_count)
    groups, groups_two = count // stride, count // stride_two
    chunk = max(ROWS, stride_two)
    picked_count = groups_two * heads
    rest_count = count - picked_count
    part = hidden // 4
    wide = hidden // 3 if hidden % 768 == 0 else part

    def near(*shape):
        return pltpu.VMEM(shape, BF16)

    def attention_work(rows):
        return [pltpu.VMEM((2, rows, KEYS), F32), near(2, rows, KEYS)]

    held_shapes = [near(width, KEYS // 2), pltpu.VMEM((1, 128), F32)]
    small_work = [pltpu.SMEM((heads,), jnp.int32), pltpu.VMEM((width,), F32)]

    (keyval,) = local_call(
        functools.partial(first_keys_kernel, stride=stride),
        [near(1, 2, groups, width)],
        (segment_offset, tokens, attn_gain, key_first, segment_value),
        [near(count, width), near(2, width, width)] + small_work,
        far=(0, 1, 2, 3, 4),
        copies=8,
        flops=2 * heads * groups * width * (count + 2 * width),
        name="first_keys",
    )
    made = {}

    def beside_first(level, held):
        if level == 0:
            made["rows"], made["normed"], made["chooser"], made["back"], held = local_call(
                functools.partial(order_kernel, stride=stride_two, chunk=chunk),
                [
                    near(count, width),
                    near(count, width),
                    near(picked_count, picked_count),
                    near(chunk, chunk),
                ],
                (global_offset, tokens, attn_gain),
                [near(count, width)] + small_work,
                far=(0, 1, 2),
                copies=3,
                relay=held,
                flops=2 * count * width * chunk,
                name="order",
            )
        if level == min(1, seg_span.bit_length() - 2):
            made["picked"], made["rest"], made["peaks"], held = local_call(
                functools.partial(first_query_kernel, heads=heads),
                [near(picked_count, width), near(rest_count, width), pltpu.VMEM((1, 128), F32)],
                (made["normed"], query_first),
                [],
                relay=held,
                flops=2 * count * width * width,
                name="first_query",
            )
        if level == seg_span.bit_length() - 2:
            made["picked_early"], made["rest_early"], made["turned"], made["key_peaks"] = local_call(
                functools.partial(near_weights_kernel, heads=heads),
                [near(heads, picked_count, KEYS // 2), near(heads, rest_count, KEYS // 2)]
                + held_shapes,
                (made["picked"], made["rest"], held),
                [pltpu.VMEM((2, rest_count, KEYS), F32)],
                flops=2 * 256 * KEYS // 2 * heads * count,
                name="near_weights",
            )
        return held

    keyval, keyval_far = early_exchange(keyval, seg_span, beside_first)
    rows = made["rows"]
    query_peaks, near_held = made["peaks"], (made["turned"], made["key_peaks"])
    row_flops = 2 * width * (2 * hidden + width) + 4 * 256 * KEYS * heads
    picked_second, picked_normed, keyval_two, turned, peaks = local_call(
        functools.partial(picked_kernel, heads=heads),
        [
            near(picked_count, width),
            near(picked_count, width),
            near(1, 2, groups_two, width),
        ]
        + held_shapes,
        (
            made["chooser"],
            rows,
            made["picked"],
            query_peaks,
            made["picked_early"],
            keyval,
            keyval_far,
            *near_held,
            output_first,
            mlp_gain,
            up_weight,
            down_weight,
            second_gain,
            key_second,
            value_second,
        ),
        [near(2, width, width), near(picked_count, width)]
        + attention_work(picked_count)
        + [near(picked_count, width), pltpu.VMEM((2, picked_count, wide), F32)]
        + [near(2, picked_count, wide), pltpu.VMEM((picked_count, width), F32)],
        far=(14, 15),
        copies=2,
        flops=row_flops * picked_count,
        name="layer_of_picked",
    )
    seconds = [picked_second]

    def rest_attention(held):
        made["mixed"], held = local_call(
            functools.partial(rest_attention_kernel, heads=heads),
            [near(rest_count, width)],
            (
                made["rest"],
                query_peaks,
                made["rest_early"],
                keyval,
                keyval_far,
                made["turned"],
                turned,
                peaks,
            ),
            attention_work(rest_count),
            relay=held,
            flops=4 * 256 * KEYS * heads * rest_count,
            name="rest_attention",
        )
        return held

    half = hidden // 4 * 3

    def rest_up(held):
        made["first"], made["normed"], made["inner"], held = local_call(
            rest_up_kernel,
            [near(rest_count, width), near(rest_count, width), near(rest_count, half)],
            (rows, made["mixed"], output_first, mlp_gain, up_weight),
            [pltpu.VMEM((2, rest_count, part), F32)],
            relay=held,
            flops=2 * width * (half + width) * rest_count,
            name="rest_up",
        )
        return held

    def rest_down(held):
        result, held = local_call(
            rest_down_kernel,
            [near(rest_count, width)],
            (made["first"], made["normed"], made["inner"], up_weight, down_weight),
            [pltpu.VMEM((1, rest_count, part), F32), near(rest_count, hidden - half)],
            relay=held,
            flops=2 * width * (2 * hidden - half) * rest_count,
            name="rest_down",
        )
        seconds.append(result)
        return held

    def picked_query(held):
        made["picked_two"], made["picked_peaks"], held = local_call(
            functools.partial(picked_query_kernel, heads=heads),
            [near(picked_count, width), pltpu.VMEM((1, 128), F32)],
            (picked_normed, query_second),
            [],
            relay=held,
            flops=2 * picked_count * width * width,
            name="picked_query",
        )
        return held

    def rest_query(held):
        made["query_two"], made["peaks_two"], held = local_call(
            functools.partial(rest_query_kernel, heads=heads),
            [near(count, width), pltpu.VMEM((1, 128), F32)],
            (made["picked_two"], made["picked_peaks"], seconds[1], second_gain, query_second),
            [near(rest_count, width)],
            relay=held,
            flops=2 * rest_count * width * width,
            name="rest_query",
        )
        return held

    tasks = [[rest_attention, picked_query], [rest_up], [rest_down], [rest_query]]
    levels = seq_count.bit_length() - 1

    def beside_second(level, held):
        for work in tasks[len(tasks) * level // levels : len(tasks) * (level + 1) // levels]:
            for task in work:
                held = task(held)
        return held

    keyval_two, keyval_two_far = exchange(keyval_two, seq_count, beside_second)
    (encoded,) = local_call(
        functools.partial(second_kernel, heads=heads, parts=len(seconds)),
        [jax.ShapeDtypeStruct((count, width), BF16)],
        (
            made["back"],
            *seconds,
            made["query_two"],
            made["peaks_two"],
            keyval_two,
            keyval_two_far,
            output_second,
        ),
        held_shapes[:1] * 2
        + [near(1, width, width)]
        + [near(count, width)] * 3
        + attention_work(count),
        far=(len(seconds) + 5,),
        out_near=False,
        copies=1 + count // chunk,
        flops=count * (2 * width * width + 4 * 256 * KEYS * heads),
        name="second_attention",
    )
    return encoded


def solution(mesh):
    placed = (
        P(("slides", "seq", "mp"), None),
        P(),
        P(None, "mp"),
        P(None, "mp"),
        P(None, "mp"),
        P("mp", None),
        P(),
        P(None, "mp"),
        P("mp", None),
        P(),
        P(None, "mp"),
        P(None, "mp"),
        P(None, "mp"),
        P("mp", None),
        P("mp"),
        P("mp"),
    )
    fits = mesh.shape["mp"] == 1 and mesh.shape["seq"] in (2, 4, 8, 16)
    return jax.shard_map(
        whole_body if fits else split_body,
        mesh=mesh,
        in_specs=placed,
        out_specs=P(("slides", "seq", "mp"), None),
        check_vma=False,
    )
```

```python
import functools
import math

import jax
import jax.numpy as jnp
from jax import lax
from jax.experimental import pallas as pl
from jax.experimental.pallas import tpu as pltpu
from jax.sharding import PartitionSpec as P

KEYS = 256
SEG_MAX = 16
ROWS = 256
LOG2E = 1.4426950408889634
BF16 = jnp.bfloat16
F32 = jnp.float32
VMEM_LIMIT = 22 * 1024 * 1024


def swapped(x, axis, apart):
    return lax.ppermute(x, axis, [(i, i ^ 1 << apart) for i in range(lax.axis_size(axis))])


def norm_rows(values, gain):
    center = values - jnp.mean(values, axis=-1, keepdims=True)
    spread = jnp.mean(center * center, axis=-1, keepdims=True)
    return (center * lax.rsqrt(spread + 1e-05) * gain).astype(jnp.bfloat16)


def pick_keys(hidden, offsets, stride, key_weight, value_weight):
    token_count, width = hidden.shape
    head_count = offsets.shape[0]
    head_size = key_weight.shape[1] // head_count
    grouped_rows = hidden.reshape(token_count // stride, stride, width)
    dilation_selector = (
        lax.broadcasted_iota(jnp.int32, (stride, head_count), 0) == offsets[None, :]
    ).astype(jnp.bfloat16)
    chosen = jnp.einsum(
        "nof,oj->njf", grouped_rows, dilation_selector, preferred_element_type=jnp.float32
    ).astype(jnp.bfloat16)
    key_heads = jnp.einsum(
        "xkr,rkf->xkf",
        chosen,
        key_weight.reshape(width, head_count, head_size),
        preferred_element_type=jnp.float32,
    ).astype(jnp.bfloat16)
    value_heads = jnp.einsum(
        "xkr,rkf->xkf",
        chosen,
        value_weight.reshape(width, head_count, head_size),
        preferred_element_type=jnp.float32,
    ).astype(jnp.bfloat16)
    picked = token_count // stride
    return jnp.stack(
        [
            key_heads.reshape(picked, head_count * head_size),
            value_heads.reshape(picked, head_count * head_size),
        ]
    )


def attend_local(query, keyval, head_count):
    token_count, width = query.shape
    head_size = width // head_count
    query_heads = query.reshape(token_count, head_count, head_size)
    key_heads = keyval[0].reshape(-1, head_count, head_size)
    value_heads = keyval[1].reshape(-1, head_count, head_size)
    scores = jnp.einsum(
        "thd,khd->htk", query_heads, key_heads, preferred_element_type=jnp.float32
    ) * head_size ** (-0.5)
    highest = jnp.max(scores, axis=-1, keepdims=True)
    weights = jnp.exp(scores - highest)
    weights = (weights / jnp.sum(weights, axis=-1, keepdims=True)).astype(jnp.bfloat16)
    mixed = jnp.einsum(
        "htk,khd->thd", weights, value_heads, preferred_element_type=jnp.float32
    ).astype(jnp.bfloat16)
    return mixed.reshape(token_count, width)


def merge_branch_pair(mine, other, level, token_position):
    lower = token_position >> level & 1 == 0
    return jnp.where(
        lower, jnp.concatenate((mine, other), axis=1), jnp.concatenate((other, mine), axis=1)
    )


def spread_segment(keyval, seg_span, token_position):
    for level in range(seg_span.bit_length() - 1):
        partner = swapped(keyval, "seq", level)
        keyval = merge_branch_pair(keyval, partner, level, token_position)
    return keyval


def spread_global(keyval_two):
    keyval_two = lax.all_gather(keyval_two, "seq", axis=1, tiled=True)
    return keyval_two


def combine(partial_value, residual_full, need_full):
    row_count = residual_full.shape[0] // lax.axis_size("mp")
    row_start = lax.axis_index("mp") * row_count
    share = lax.psum_scatter(partial_value, "mp", scatter_dimension=0, tiled=True)
    own_rows = lax.dynamic_slice_in_dim(residual_full, row_start, row_count, 0)
    own_rows = (own_rows.astype(jnp.float32) + share).astype(jnp.bfloat16)
    full_rows = lax.all_gather(own_rows, "mp", axis=0, tiled=True) if need_full else own_rows
    return (own_rows, full_rows)


def split_body(
    tokens,
    attn_gain,
    query_first,
    key_first,
    segment_value,
    output_first,
    mlp_gain,
    up_weight,
    down_weight,
    second_gain,
    query_second,
    key_second,
    value_second,
    output_second,
    segment_offset,
    global_offset,
):
    seq_count = lax.axis_size("seq")
    token_position = lax.axis_index("seq")
    seg_span = min(SEG_MAX, seq_count)
    head_count = segment_offset.shape[0]
    full_rows = lax.all_gather(tokens, "mp", axis=0, tiled=True)
    token_count = full_rows.shape[0]
    hidden = norm_rows(full_rows.astype(jnp.float32), attn_gain)
    query = jnp.dot(hidden, query_first, preferred_element_type=jnp.float32).astype(jnp.bfloat16)
    seg_stride = token_count // (KEYS // seg_span)
    keyval = pick_keys(hidden, segment_offset, seg_stride, key_first, segment_value)
    keyval = spread_segment(keyval, seg_span, token_position)
    mixed = attend_local(query, keyval, head_count)
    partial_value = jnp.dot(mixed, output_first, preferred_element_type=jnp.float32)
    own_rows, first_rows = combine(partial_value, full_rows, True)
    normed = norm_rows(first_rows.astype(jnp.float32), mlp_gain)
    inner = jax.nn.gelu(
        jnp.dot(normed, up_weight, preferred_element_type=jnp.float32), approximate=True
    ).astype(jnp.bfloat16)
    partial_value = jnp.dot(inner, down_weight, preferred_element_type=jnp.float32)
    own_rows, second_rows = combine(partial_value, first_rows, True)
    hidden_two = norm_rows(second_rows.astype(jnp.float32), second_gain)
    query_two = jnp.dot(hidden_two, query_second, preferred_element_type=jnp.float32).astype(
        jnp.bfloat16
    )
    glob_stride = token_count // (KEYS // seq_count)
    keyval_two = pick_keys(hidden_two, global_offset, glob_stride, key_second, value_second)
    keyval_two = spread_global(keyval_two)
    mixed_two = attend_local(query_two, keyval_two, head_count)
    partial_value = jnp.dot(mixed_two, output_second, preferred_element_type=jnp.float32)
    own_rows, unused_rows = combine(partial_value, second_rows, False)
    return own_rows


def one_hot(condition):
    return jnp.where(condition, 1.0, 0.0).astype(BF16)


def dot(left, right):
    return jnp.dot(left, right, preferred_element_type=F32)


def pieces(count, size):
    size = size if count % size == 0 else count
    return [slice(start, start + size) for start in range(0, count, size)]


def norm_into(out, start, source, gain, count):
    for span in pieces(count, 64):
        out[start + span.start : start + span.stop, :] = norm_rows(
            source[span, :].astype(F32), gain
        )


def bring(source, target, sem):
    copy = pltpu.make_async_copy(source, target, sem)
    copy.start()
    return copy


def pick_matrix(offsets, heads, groups, stride):
    count = groups * stride
    place = lax.broadcasted_iota(jnp.int32, (groups, count), 1)
    place = place - lax.broadcasted_iota(jnp.int32, (groups, count), 0) * stride
    return jnp.concatenate([one_hot(place == offsets[h]) for h in range(heads)], axis=0)


def project_keys(chosen, heads, weights, keyval_ref):
    rows, width = chosen.shape
    groups, head_size = rows // heads, width // heads
    for slot, weight in enumerate(weights):
        held = weight()
        for span in pieces(width, 256):
            first, last = span.start // head_size, (span.stop - 1) // head_size + 1
            wide = dot(chosen[first * groups : last * groups], held[:, span])
            column = lax.broadcasted_iota(jnp.int32, (groups, span.stop - span.start), 1)
            total = wide[:groups]
            for h in range(first + 1, last):
                row = (h - first) * groups
                own = column >= h * head_size - span.start
                total = jnp.where(own, wide[row : row + groups], total)
            total = total.astype(BF16)
            for copy in range(keyval_ref.shape[0]):
                keyval_ref[copy, slot, :, span] = total


def ranks(offsets, chunk, stride, share, axis):
    heads = offsets.shape[0]

    def places(way):
        shape = (1, chunk) if way else (chunk, 1)
        place = lax.broadcasted_iota(jnp.int32, shape, way)
        inside = lax.rem(place, stride)
        taken = inside == offsets[0]
        for h in range(1, heads):
            taken = taken | (inside == offsets[h])
        return place, inside, jnp.where(taken, inside, inside + stride)

    place, inside, order = places(axis)
    other_place, _, other_order = places(1 - axis)
    ahead = (other_order < order) & (lax.div(other_place, stride) == lax.div(place, stride))
    rank = jnp.sum(jnp.where(ahead, 1, 0), axis=1 - axis, keepdims=True)
    group = lax.div(place, stride)
    return jnp.where(
        rank < heads, group * heads + rank, share + group * (stride - heads) + rank - heads
    )


def slots_of(offsets, heads):
    values = [offsets[h] for h in range(heads)]
    fresh = []
    for h in range(heads):
        seen = jnp.int32(1)
        for earlier in values[:h]:
            seen = jnp.where(earlier == values[h], 0, seen)
        fresh.append(seen)
    slots = []
    for h in range(heads):
        slot = jnp.int32(0)
        for other in range(heads):
            slot = slot + jnp.where(values[other] < values[h], fresh[other], 0)
        slots.append(slot)
    return slots


def first_keys_kernel(
    offsets, tokens, gain, key_weight, value_weight, keyval, rows, wide, picks, scale, sems, *, stride
):
    spans = pieces(tokens.shape[0], tokens.shape[0] // 4)
    copies = [
        bring(offsets, picks, sems.at[0]),
        bring(gain, scale, sems.at[1]),
        *[bring(tokens.at[x], rows.at[x], sems.at[4 + i]) for i, x in enumerate(spans)],
        bring(key_weight, wide.at[0], sems.at[2]),
        bring(value_weight, wide.at[1], sems.at[3]),
    ]
    heads = offsets.shape[0]
    copies[0].wait()
    chooser = pick_matrix(picks, heads, rows.shape[0] // stride, stride)
    copies[1].wait()
    chosen = None
    for copy, span in zip(copies[2:-2], spans):
        copy.wait()
        part = dot(chooser[:, span], rows[span, :])
        chosen = part if chosen is None else chosen + part
    chosen = norm_rows(chosen, scale[...])

    def weight(slot):
        copies[slot - 2].wait()
        return wide[slot]

    project_keys(
        chosen, heads, [functools.partial(weight, slot) for slot in range(2)], keyval
    )


def order_kernel(
    offsets,
    tokens,
    gain,
    moved_rows,
    normed,
    chooser,
    back,
    rows,
    picks,
    scale,
    sems,
    *,
    stride,
    chunk,
):
    copies = [
        bring(offsets, picks, sems.at[0]),
        bring(tokens, rows, sems.at[1]),
        bring(gain, scale, sems.at[2]),
    ]
    count = tokens.shape[0]
    share = chunk // stride * offsets.shape[0]
    rest = chunk - share
    picked = count // chunk * share
    copies[0].wait()
    mover = one_hot(
        lax.broadcasted_iota(jnp.int32, (chunk, chunk), 0)
        == ranks(picks, chunk, stride, share, 1)
    )
    heads = offsets.shape[0]
    chooser[...] = pick_matrix(slots_of(picks, heads), heads, picked // heads, heads)
    back[...] = one_hot(
        lax.broadcasted_iota(jnp.int32, (chunk, chunk), 1)
        == ranks(picks, chunk, stride, share, 0)
    )
    copies[1].wait()
    copies[2].wait()
    for c in range(count // chunk):
        moved = dot(mover, rows[c * chunk : (c + 1) * chunk, :]).astype(BF16)
        moved_rows[c * share : (c + 1) * share, :] = moved[:share]
        moved_rows[picked + c * rest : picked + (c + 1) * rest, :] = moved[share:]
    norm_into(normed, 0, moved_rows, scale[...], count)


def score_scale(head_size):
    return head_size ** (-0.5) * LOG2E


def project_rows(normed, span, weight, out, peak):
    query = dot(normed[span, :], weight[...])
    out[...] = query.astype(BF16)
    for part in pieces(query.shape[0], 64):
        square = query[part] * query[part]
        peak = square if peak is None else jnp.maximum(peak, square)
    return peak


def project_query(normed, weight, outs, heads, peaks):
    peak = None
    for out, row in outs:
        for span in pieces(out.shape[0], 512 if out.shape[0] % 512 == 0 else 256):
            place = slice(row + span.start, row + span.stop)
            peak = project_rows(normed, place, weight, out.at[span], peak)
    peaks[...] = summed_peaks(peak.astype(BF16), heads)


def first_query_kernel(normed, weight, picked, rest, peaks, sems, *, heads):
    del sems
    project_query(normed, weight, [(picked, 0), (rest, picked.shape[0])], heads, peaks)


def head_windows(head_size, width):
    period = min(width, math.lcm(head_size, 128))
    windows = []
    for h in range(period // head_size):
        start = h * head_size // 128 * 128
        stop = min(period, -(-(h + 1) * head_size // 128) * 128)
        windows.append((start, stop - start))
    return period, windows


def summed_peaks(peak, heads):
    width = peak.shape[1]
    column = lax.broadcasted_iota(jnp.int32, (width, 128), 0)
    head = lax.broadcasted_iota(jnp.int32, (width, 128), 1)
    low = head * (width // heads)
    sums = one_hot((column >= low) & (column < low + width // heads))
    return jnp.max(dot(peak, sums), axis=0, keepdims=True)


def load_keys(keyval, turned):
    keys = jnp.concatenate([keyval[i, 0] for i in range(keyval.shape[0])], axis=0)
    turned[...] = keys.T
    return keys * keys


def small_scores(query_peaks, key_peaks, head_size):
    scale = score_scale(head_size)
    return jnp.max(query_peaks[...] * key_peaks[...]) < 9000.0 / (scale * scale)


def reciprocal(x):
    guess = pl.reciprocal(x, approx=True)
    return guess * (2.0 - x * guess)


def padded_keys(turned, base, head, head_size, start, size):
    low = base + head * head_size
    rows = pl.ds(low if isinstance(low, int) else pl.multiple_of(low, 16), head_size)
    own = jnp.concatenate([part[rows, :] for part in turned], axis=1)
    low = head * head_size - start
    parts = [own]
    if low:
        parts.insert(0, jnp.zeros((low, own.shape[1]), BF16))
    if low + head_size < size:
        parts.append(jnp.zeros((size - low - head_size, own.shape[1]), BF16))
    return jnp.concatenate(parts, axis=0)


def score_pair(query, span, base, head, head_size, windows, turned):
    start = windows[head][0]
    size = windows[head + 1][0] + windows[head + 1][1] - start
    keys = [padded_keys([turned], base, head + i, head_size, start, size) for i in range(2)]
    return dot(query[span, pl.ds(base + start, size)], jnp.concatenate(keys, axis=1))


def near_weights_kernel(
    picked, rest, keyval, picked_early, rest_early, turned, peaks, scores_ref, sems, *, heads
):
    del sems
    peaks[...] = summed_peaks(load_keys(keyval, turned), heads)
    width = picked.shape[1]
    head_size = width // heads
    scale = score_scale(head_size)
    key_count = turned.shape[1]
    period, windows = head_windows(head_size, width)
    jobs = [
        (query, early, head)
        for query, early in ((picked, picked_early), (rest, rest_early))
        for head in range(0, len(windows), 2)
    ]

    @pl.loop(0, width // period)
    def _(turn):
        base = pl.multiple_of(turn * period, 128)

        def score(i):
            query, _, head = jobs[i]
            rows = query.shape[0]
            scores_ref[i % 2, :rows] = score_pair(
                query, slice(0, rows), base, head, head_size, windows, turned
            )

        score(0)
        for i, (query, early, head) in enumerate(jobs):
            if i + 1 < len(jobs):
                score(i + 1)
            for part in pieces(query.shape[0], 64):
                weights = jnp.exp2(scores_ref[i % 2, part, :] * scale).astype(BF16)
                for j in range(2):
                    early[turn * len(windows) + head + j, part, :] = weights[
                        :, j * key_count : (j + 1) * key_count
                    ]


def attend_rows(
    query, first_row, rows, heads, turned, keyvals, mixed_ref, mixed_row, work, plain, early=None
):
    scores_ref, weights_ref = work
    width = query.shape[1]
    key_count = sum(part.shape[1] for part in turned)
    head_size = width // heads
    period, windows = head_windows(head_size, width)
    span = pl.ds(first_row, rows)
    out_span = pl.ds(mixed_row, rows)
    scale = score_scale(head_size)
    lane = lax.broadcasted_iota(jnp.int32, (1, 128), 1)
    step = 2 if early is not None else 1
    piece = 64

    def take_turn(turn):
        base = turn * period if plain else pl.multiple_of(turn * period, 128)
        sums = {}

        def score(i):
            if early is not None:
                scores = score_pair(query, span, base, 2 * i, head_size, windows, turned[1])
            else:
                start, size = windows[i]
                scores = dot(
                    query[span, pl.ds(base + start, size)],
                    padded_keys(turned, base, i, head_size, start, size),
                )
            scores_ref[i % 2, :rows] = scores

        def weigh(h):
            for part in pieces(rows, piece):
                scores = scores_ref[h % 2, part, :]
                if not plain:
                    scores = scores - jnp.max(scores, axis=1, keepdims=True)
                weights_ref[h % 2, part, :] = jnp.exp2(scores * scale).astype(BF16)

        def mix(h):
            start, size = windows[h]
            low = h * head_size - start
            values = jnp.concatenate(
                [
                    x[i, 1, :, pl.ds(base + start, size)]
                    for x in keyvals
                    for i in range(x.shape[0])
                ],
                axis=0,
            )
            column = lax.broadcasted_iota(jnp.int32, (key_count, size), 1)
            own = (column >= low) & (column < low + head_size)
            values = jnp.where(own, values, jnp.ones((), BF16))
            if early is not None:
                half = key_count // 2
                far = weights_ref[h // 2 % 2, :rows, h % 2 * half : (h % 2 + 1) * half]
                near = early[turn * len(windows) + h, span, :]
                weights = jnp.concatenate([near, far], axis=1)
            else:
                weights = weights_ref[h % 2, :rows]
            mixed = dot(weights, values)
            for offset in range(0, size, 128):
                own = mixed[:, offset : offset + 128]
                total = pltpu.roll(own, 64, 1)
                at = start + offset
                if at in sums:
                    mine = lane >= h * head_size - at
                    own = jnp.where(mine, own, sums[at][0])
                    total = jnp.where(mine, total, sums[at][1])
                sums[at] = own, total
                if (h + 1) * head_size >= at + 128:
                    own, total = sums.pop(at)
                    mixed_ref[out_span, pl.ds(base + at, 128)] = (
                        own * reciprocal(total)
                    ).astype(BF16)

        count = len(windows) // step
        score(0)
        for i in range(count):
            if i:
                for h in range((i - 1) * step, i * step):
                    mix(h)
            if i + 1 < count:
                score(i + 1)
            weigh(i)
        for h in range((count - 1) * step, count * step):
            mix(h)

    if plain:
        for turn in range(width // period):
            take_turn(turn)
    else:
        pl.loop(0, width // period)(take_turn)


def attend(query, rows, heads, turned, keyvals, mixed_ref, work, small, early=None):
    size = math.gcd(rows, ROWS)

    @pl.when(small)
    def _():
        attend_rows(query, 0, rows, heads, turned, keyvals, mixed_ref, 0, work, True, early)

    @pl.when(jnp.logical_not(small))
    def _():
        @pl.loop(0, rows // size)
        def _(step):
            row = pl.multiple_of(step * size, size)
            attend_rows(
                query,
                row,
                size,
                heads,
                turned,
                keyvals,
                mixed_ref,
                row,
                work,
                False,
            )


def gelu(x):
    half = 0.5 * x
    return half + half * jnp.tanh(x * (0.7978845608028654 + 0.035677408136300125 * (x * x)))


def widen(normed, up_weight, low, wide_ref, inner):
    rows = normed.shape[0]
    spans = pieces(inner.shape[1], wide_ref.shape[2])

    def product(i):
        columns = slice(low + spans[i].start, low + spans[i].stop)
        wide_ref[i % 2] = dot(normed[...], up_weight[:, columns])

    product(0)
    for i, span in enumerate(spans):
        if i + 1 < len(spans):
            product(i + 1)
        for part in pieces(rows, 32):
            inner[part, span] = gelu(wide_ref[i % 2, part, :]).astype(BF16)


def feed_forward(normed, up_weight, down_weight, total, wide_ref, inner):
    rows = normed.shape[0]
    spans = pieces(up_weight.shape[1], wide_ref.shape[2])

    def product(i):
        wide_ref[i % 2] = dot(normed[...], up_weight[:, spans[i]])

    product(0)
    for i, span in enumerate(spans):
        if i + 1 < len(spans):
            product(i + 1)
        for part in pieces(rows, 32):
            inner[i % 2, part, :] = gelu(wide_ref[i % 2, part, :]).astype(BF16)
        total[...] += dot(inner[i % 2], down_weight[span, :])


def narrow(inners, down_weight, first, second, size):
    for span in pieces(second.shape[1], size):
        total = first[:, span].astype(F32)
        low = 0
        for inner in inners:
            high = low + inner.shape[1]
            total = total + dot(inner[...], down_weight[low:high, span])
            low = high
        second[:, span] = total.astype(BF16)


def add_heads(tokens, first_row, mixed, out_weight, gain, first, normed):
    before = None
    for span in pieces(mixed.shape[0], 256):
        total = dot(mixed[span, :], out_weight[...])
        rows = tokens[first_row + span.start : first_row + span.stop, :]
        first[span, :] = (rows.astype(F32) + total).astype(BF16)
        if before is not None:
            norm_into(normed, before.start, first.at[before], gain, before.stop - before.start)
        before = span
    norm_into(normed, before.start, first.at[before], gain, before.stop - before.start)


def picked_kernel(
    chooser,
    tokens,
    query,
    query_peaks,
    early,
    keyval,
    keyval_far,
    turned_near,
    peaks_near,
    out_weight,
    mlp_gain,
    up_weight,
    down_weight,
    gain,
    key_weight,
    value_weight,
    second,
    normed,
    keyval_two,
    turned,
    peaks,
    held,
    mixed,
    scores,
    weights,
    first,
    wide,
    inner,
    total,
    sems,
    *,
    heads,
):
    copies = [
        bring(x, held.at[i], sems.at[i]) for i, x in enumerate((key_weight, value_weight))
    ]
    rows = second.shape[0]
    keyvals = (keyval, keyval_far)
    squares = load_keys(keyval_far, turned)
    peaks[...] = jnp.maximum(peaks_near[...], summed_peaks(squares, heads))
    small = small_scores(query_peaks, peaks, query.shape[1] // heads)
    attend(
        query,
        rows,
        heads,
        (turned_near, turned),
        keyvals,
        mixed,
        (scores, weights),
        small,
        early,
    )
    add_heads(tokens, 0, mixed, out_weight, mlp_gain[...], first, normed)
    total[...] = first[...].astype(F32)
    feed_forward(normed, up_weight, down_weight, total, wide, inner)
    second[...] = total[...].astype(BF16)
    norm_into(normed, 0, second, gain[...], rows)
    chosen = dot(chooser[...], normed[...]).astype(BF16)

    def weight(slot):
        copies[slot].wait()
        return held[slot]

    project_keys(
        chosen, heads, [functools.partial(weight, slot) for slot in range(2)], keyval_two
    )


def rest_attention_kernel(
    query,
    query_peaks,
    early,
    keyval,
    keyval_far,
    turned_near,
    turned,
    peaks,
    mixed,
    scores,
    weights,
    sems,
    *,
    heads,
):
    del sems
    attend(
        query,
        mixed.shape[0],
        heads,
        (turned_near, turned),
        (keyval, keyval_far),
        mixed,
        (scores, weights),
        small_scores(query_peaks, peaks, query.shape[1] // heads),
        early,
    )


def rest_up_kernel(
    tokens, mixed, out_weight, gain, up_weight, first, normed, inner, wide, sems
):
    del sems
    add_heads(
        tokens, tokens.shape[0] - mixed.shape[0], mixed, out_weight, gain[...], first, normed
    )
    widen(normed, up_weight, 0, wide, inner)


def rest_down_kernel(
    first, normed, inner, up_weight, down_weight, second, wide, inner_more, sems
):
    del sems
    widen(normed, up_weight, inner.shape[1], wide, inner_more)
    narrow([inner, inner_more], down_weight, first, second, 256)


def picked_query_kernel(normed, weight, query, peaks, sems, *, heads):
    del sems
    project_query(normed, weight, [(query, 0)], heads, peaks)


def rest_query_kernel(
    picked, picked_peaks, rows, gain, weight, query, peaks, normed, sems, *, heads
):
    del sems
    start = picked.shape[0]
    query[:start, :] = picked[...]
    norm_into(normed, 0, rows, gain[...], rows.shape[0])
    out = query.at[pl.ds(start, rows.shape[0])]
    project_query(normed, weight, [(out, 0)], heads, peaks)
    peaks[...] = jnp.maximum(peaks[...], picked_peaks[...])


def second_kernel(*refs, heads, parts):
    back, *rows = refs[: 1 + parts]
    query, query_peaks, keyval, keyval_far, out_weight, encoded = refs[1 + parts : 7 + parts]
    turned_near, turned, held, mixed = refs[7 + parts : 11 + parts]
    result, ready, scores, weights, sems = refs[11 + parts :]
    copy = bring(out_weight, held.at[0], sems.at[0])
    keyvals = (keyval, keyval_far)
    squares = jnp.maximum(load_keys(keyval, turned_near), load_keys(keyval_far, turned))
    count = query.shape[0]
    small = small_scores(query_peaks, summed_peaks(squares, heads), query.shape[1] // heads)
    attend(
        query, count, heads, (turned_near, turned), keyvals, mixed, (scores, weights), small
    )
    chunk = back.shape[0]
    share = rows[0].shape[0] * chunk // count
    rest_share = chunk - share
    copy.wait()
    start = 0
    for part in rows:
        span = slice(start, start + part.shape[0])
        total = part[...].astype(F32) + dot(mixed[span, :], held[0])
        result[span, :] = total.astype(BF16)
        start += part.shape[0]
    start = count // chunk * share
    copies = []
    for c in range(count // chunk):
        far = start + c * rest_share
        blend = jnp.concatenate(
            [result[c * share : (c + 1) * share, :], result[far : far + rest_share, :]], axis=0
        )
        span = pl.ds(c * chunk, chunk)
        ready[span, :] = dot(back[...], blend).astype(BF16)
        copies.append(bring(ready.at[span], encoded.at[span], sems.at[1 + c]))
    for copy in copies:
        copy.wait()


def relaying(kernel, ins, outs, *refs):
    end = ins + 1 + outs
    refs[end][...] = refs[ins][...]
    kernel(*refs[:ins], *refs[ins + 1 : end], *refs[end + 1 :])


def local_call(kernel, outs, inputs, scratch, scalars=0, far=(), relay=None, out_near=True, copies=1, flops=0, name=None):
    outs, inputs = list(outs), list(inputs)
    if relay is not None:
        kernel = functools.partial(relaying, kernel, len(inputs), len(outs))
        inputs.append(relay)
        outs.append(pltpu.VMEM(relay.shape, relay.dtype))
    specs, placed = [], []
    for i, x in enumerate(inputs):
        if i < scalars:
            specs.append(pl.BlockSpec(memory_space=pltpu.SMEM))
        elif i in far:
            specs.append(pl.BlockSpec(memory_space=pltpu.HBM))
            x = pltpu.with_memory_space_constraint(x, pltpu.HBM)
        else:
            specs.append(pl.BlockSpec(memory_space=pltpu.VMEM))
            x = pltpu.with_memory_space_constraint(x, pltpu.VMEM)
        placed.append(x)
    return pl.pallas_call(
        kernel,
        out_shape=outs,
        in_specs=specs,
        out_specs=[
            pl.BlockSpec(memory_space=pltpu.VMEM if out_near else pltpu.HBM)
        ] * len(outs),
        scratch_shapes=list(scratch) + [pltpu.SemaphoreType.DMA((copies,))],
        compiler_params=pltpu.CompilerParams(vmem_limit_bytes=VMEM_LIMIT),
        cost_estimate=pl.CostEstimate(
            flops=int(flops),
            transcendentals=0,
            bytes_accessed=sum(inputs[i].size * inputs[i].dtype.itemsize for i in far),
        ),
        name=name,
    )(*placed)


def exchange(keyval, span, beside):
    size = lax.axis_size("seq")
    levels = span.bit_length() - 1
    even = list(range(levels - 1, 0, -1))
    orders = (even, even[-1:] + even[:-1])
    for step in range(levels - 1):
        pairs = [(i, i ^ 1 << orders[i % 2][step]) for i in range(size)]
        partner = lax.ppermute(keyval, "seq", pairs)
        keyval = jnp.concatenate([beside(step, keyval), partner], axis=0)
    far = swapped(keyval, "seq", 0)
    return beside(levels - 1, keyval), far


def early_exchange(keyval, span, beside):
    levels = span.bit_length() - 1
    crossed, fresh = [], keyval
    for level in range(levels - 1, 1, -1):
        crossed.append(swapped(fresh, "seq", 1))
        partner = swapped(keyval, "seq", level)
        keyval = jnp.concatenate([beside(levels - 1 - level, keyval), partner], axis=0)
        fresh = partner
    if levels > 1:
        crossed.append(swapped(fresh, "seq", 1))
        keyval = jnp.concatenate([beside(levels - 2, keyval), *crossed], axis=0)
    far = swapped(keyval, "seq", 0)
    return beside(levels - 1, keyval), far


def whole_body(
    tokens,
    attn_gain,
    query_first,
    key_first,
    segment_value,
    output_first,
    mlp_gain,
    up_weight,
    down_weight,
    second_gain,
    query_second,
    key_second,
    value_second,
    output_second,
    segment_offset,
    global_offset,
):
    seq_count = lax.axis_size("seq")
    seg_span = min(SEG_MAX, seq_count)
    heads = segment_offset.shape[0]
    count, width = tokens.shape
    head_size = width // heads
    hidden = up_weight.shape[1]
    stride = count // (KEYS // seg_span)
    stride_two = count // (KEYS // seq_count)
    groups, groups_two = count // stride, count // stride_two
    chunk = max(ROWS, stride_two)
    picked_count = groups_two * heads
    rest_count = count - picked_count
    part = hidden // 4
    wide = hidden // 6 if hidden % 768 == 0 else part

    def near(*shape):
        return pltpu.VMEM(shape, BF16)

    def attention_work(rows):
        return [pltpu.VMEM((2, rows, KEYS), F32), near(2, rows, KEYS)]

    held_shapes = [near(width, KEYS // 2), pltpu.VMEM((1, 128), F32)]
    small_work = [pltpu.SMEM((heads,), jnp.int32), pltpu.VMEM((width,), F32)]

    (keyval,) = local_call(
        functools.partial(first_keys_kernel, stride=stride),
        [near(1, 2, groups, width)],
        (segment_offset, tokens, attn_gain, key_first, segment_value),
        [near(count, width), near(2, width, width)] + small_work,
        far=(0, 1, 2, 3, 4),
        copies=8,
        flops=2 * heads * groups * width * (count + 2 * width),
        name="first_keys",
    )
    made = {}

    def beside_first(level, held):
        if level == 0:
            made["rows"], made["normed"], made["chooser"], made["back"], held = local_call(
                functools.partial(order_kernel, stride=stride_two, chunk=chunk),
                [
                    near(count, width),
                    near(count, width),
                    near(picked_count, picked_count),
                    near(chunk, chunk),
                ],
                (global_offset, tokens, attn_gain),
                [near(count, width)] + small_work,
                far=(0, 1, 2),
                copies=3,
                relay=held,
                flops=2 * count * width * chunk,
                name="order",
            )
        if level == min(1, seg_span.bit_length() - 2):
            made["picked"], made["rest"], made["peaks"], held = local_call(
                functools.partial(first_query_kernel, heads=heads),
                [near(picked_count, width), near(rest_count, width), pltpu.VMEM((1, 128), F32)],
                (made["normed"], query_first),
                [],
                relay=held,
                flops=2 * count * width * width,
                name="first_query",
            )
        if level == seg_span.bit_length() - 2:
            made["picked_early"], made["rest_early"], made["turned"], made["key_peaks"] = local_call(
                functools.partial(near_weights_kernel, heads=heads),
                [near(heads, picked_count, KEYS // 2), near(heads, rest_count, KEYS // 2)]
                + held_shapes,
                (made["picked"], made["rest"], held),
                [pltpu.VMEM((2, rest_count, KEYS), F32)],
                flops=2 * 256 * KEYS // 2 * heads * count,
                name="near_weights",
            )
        return held

    keyval, keyval_far = early_exchange(keyval, seg_span, beside_first)
    rows = made["rows"]
    query_peaks, near_held = made["peaks"], (made["turned"], made["key_peaks"])
    row_flops = 2 * width * (2 * hidden + width) + 4 * 256 * KEYS * heads
    picked_second, picked_normed, keyval_two, turned, peaks = local_call(
        functools.partial(picked_kernel, heads=heads),
        [
            near(picked_count, width),
            near(picked_count, width),
            near(1, 2, groups_two, width),
        ]
        + held_shapes,
        (
            made["chooser"],
            rows,
            made["picked"],
            query_peaks,
            made["picked_early"],
            keyval,
            keyval_far,
            *near_held,
            output_first,
            mlp_gain,
            up_weight,
            down_weight,
            second_gain,
            key_second,
            value_second,
        ),
        [near(2, width, width), near(picked_count, width)]
        + attention_work(picked_count)
        + [near(picked_count, width), pltpu.VMEM((2, picked_count, wide), F32)]
        + [near(2, picked_count, wide), pltpu.VMEM((picked_count, width), F32)],
        far=(14, 15),
        copies=2,
        flops=row_flops * picked_count,
        name="layer_of_picked",
    )
    seconds = [picked_second]

    def rest_attention(held):
        made["mixed"], held = local_call(
            functools.partial(rest_attention_kernel, heads=heads),
            [near(rest_count, width)],
            (
                made["rest"],
                query_peaks,
                made["rest_early"],
                keyval,
                keyval_far,
                made["turned"],
                turned,
                peaks,
            ),
            attention_work(rest_count),
            relay=held,
            flops=4 * 256 * KEYS * heads * rest_count,
            name="rest_attention",
        )
        return held

    half = hidden // 4 * 3

    def rest_up(held):
        made["first"], made["normed"], made["inner"], held = local_call(
            rest_up_kernel,
            [near(rest_count, width), near(rest_count, width), near(rest_count, half)],
            (rows, made["mixed"], output_first, mlp_gain, up_weight),
            [pltpu.VMEM((2, rest_count, part), F32)],
            relay=held,
            flops=2 * width * (half + width) * rest_count,
            name="rest_up",
        )
        return held

    def rest_down(held):
        result, held = local_call(
            rest_down_kernel,
            [near(rest_count, width)],
            (made["first"], made["normed"], made["inner"], up_weight, down_weight),
            [pltpu.VMEM((1, rest_count, part), F32), near(rest_count, hidden - half)],
            relay=held,
            flops=2 * width * (2 * hidden - half) * rest_count,
            name="rest_down",
        )
        seconds.append(result)
        return held

    def picked_query(held):
        made["picked_two"], made["picked_peaks"], held = local_call(
            functools.partial(picked_query_kernel, heads=heads),
            [near(picked_count, width), pltpu.VMEM((1, 128), F32)],
            (picked_normed, query_second),
            [],
            relay=held,
            flops=2 * picked_count * width * width,
            name="picked_query",
        )
        return held

    def rest_query(held):
        made["query_two"], made["peaks_two"], held = local_call(
            functools.partial(rest_query_kernel, heads=heads),
            [near(count, width), pltpu.VMEM((1, 128), F32)],
            (made["picked_two"], made["picked_peaks"], seconds[1], second_gain, query_second),
            [near(rest_count, width)],
            relay=held,
            flops=2 * rest_count * width * width,
            name="rest_query",
        )
        return held

    tasks = [[rest_attention, picked_query], [rest_up], [rest_down], [rest_query]]
    levels = seq_count.bit_length() - 1

    def beside_second(level, held):
        for work in tasks[len(tasks) * level // levels : len(tasks) * (level + 1) // levels]:
            for task in work:
                held = task(held)
        return held

    keyval_two, keyval_two_far = exchange(keyval_two, seq_count, beside_second)
    (encoded,) = local_call(
        functools.partial(second_kernel, heads=heads, parts=len(seconds)),
        [jax.ShapeDtypeStruct((count, width), BF16)],
        (
            made["back"],
            *seconds,
            made["query_two"],
            made["peaks_two"],
            keyval_two,
            keyval_two_far,
            output_second,
        ),
        held_shapes[:1] * 2
        + [near(1, width, width)]
        + [near(count, width)] * 3
        + attention_work(count),
        far=(len(seconds) + 5,),
        out_near=False,
        copies=1 + count // chunk,
        flops=count * (2 * width * width + 4 * 256 * KEYS * heads),
        name="second_attention",
    )
    return encoded


def solution(mesh):
    placed = (
        P(("slides", "seq", "mp"), None),
        P(),
        P(None, "mp"),
        P(None, "mp"),
        P(None, "mp"),
        P("mp", None),
        P(),
        P(None, "mp"),
        P("mp", None),
        P(),
        P(None, "mp"),
        P(None, "mp"),
        P(None, "mp"),
        P("mp", None),
        P("mp"),
        P("mp"),
    )
    fits = mesh.shape["mp"] == 1 and mesh.shape["seq"] in (2, 4, 8, 16)
    return jax.shard_map(
        whole_body if fits else split_body,
        mesh=mesh,
        in_specs=placed,
        out_specs=P(("slides", "seq", "mp"), None),
        check_vma=False,
    )
```

```python
import functools
import math

import jax
import jax.numpy as jnp
from jax import lax
from jax.experimental import pallas as pl
from jax.experimental.pallas import tpu as pltpu
from jax.sharding import PartitionSpec as P

KEYS = 256
SEG_MAX = 16
ROWS = 256
LOG2E = 1.4426950408889634
BF16 = jnp.bfloat16
F32 = jnp.float32
VMEM_LIMIT = 22 * 1024 * 1024


def swapped(x, axis, apart):
    return lax.ppermute(x, axis, [(i, i ^ 1 << apart) for i in range(lax.axis_size(axis))])


def norm_rows(values, gain):
    center = values - jnp.mean(values, axis=-1, keepdims=True)
    spread = jnp.mean(center * center, axis=-1, keepdims=True)
    return (center * lax.rsqrt(spread + 1e-05) * gain).astype(jnp.bfloat16)


def pick_keys(hidden, offsets, stride, key_weight, value_weight):
    token_count, width = hidden.shape
    head_count = offsets.shape[0]
    head_size = key_weight.shape[1] // head_count
    grouped_rows = hidden.reshape(token_count // stride, stride, width)
    dilation_selector = (
        lax.broadcasted_iota(jnp.int32, (stride, head_count), 0) == offsets[None, :]
    ).astype(jnp.bfloat16)
    chosen = jnp.einsum(
        "nof,oj->njf", grouped_rows, dilation_selector, preferred_element_type=jnp.float32
    ).astype(jnp.bfloat16)
    key_heads = jnp.einsum(
        "xkr,rkf->xkf",
        chosen,
        key_weight.reshape(width, head_count, head_size),
        preferred_element_type=jnp.float32,
    ).astype(jnp.bfloat16)
    value_heads = jnp.einsum(
        "xkr,rkf->xkf",
        chosen,
        value_weight.reshape(width, head_count, head_size),
        preferred_element_type=jnp.float32,
    ).astype(jnp.bfloat16)
    picked = token_count // stride
    return jnp.stack(
        [
            key_heads.reshape(picked, head_count * head_size),
            value_heads.reshape(picked, head_count * head_size),
        ]
    )


def attend_local(query, keyval, head_count):
    token_count, width = query.shape
    head_size = width // head_count
    query_heads = query.reshape(token_count, head_count, head_size)
    key_heads = keyval[0].reshape(-1, head_count, head_size)
    value_heads = keyval[1].reshape(-1, head_count, head_size)
    scores = jnp.einsum(
        "thd,khd->htk", query_heads, key_heads, preferred_element_type=jnp.float32
    ) * head_size ** (-0.5)
    highest = jnp.max(scores, axis=-1, keepdims=True)
    weights = jnp.exp(scores - highest)
    weights = (weights / jnp.sum(weights, axis=-1, keepdims=True)).astype(jnp.bfloat16)
    mixed = jnp.einsum(
        "htk,khd->thd", weights, value_heads, preferred_element_type=jnp.float32
    ).astype(jnp.bfloat16)
    return mixed.reshape(token_count, width)


def merge_branch_pair(mine, other, level, token_position):
    lower = token_position >> level & 1 == 0
    return jnp.where(
        lower, jnp.concatenate((mine, other), axis=1), jnp.concatenate((other, mine), axis=1)
    )


def spread_segment(keyval, seg_span, token_position):
    for level in range(seg_span.bit_length() - 1):
        partner = swapped(keyval, "seq", level)
        keyval = merge_branch_pair(keyval, partner, level, token_position)
    return keyval


def spread_global(keyval_two):
    keyval_two = lax.all_gather(keyval_two, "seq", axis=1, tiled=True)
    return keyval_two


def combine(partial_value, residual_full, need_full):
    row_count = residual_full.shape[0] // lax.axis_size("mp")
    row_start = lax.axis_index("mp") * row_count
    share = lax.psum_scatter(partial_value, "mp", scatter_dimension=0, tiled=True)
    own_rows = lax.dynamic_slice_in_dim(residual_full, row_start, row_count, 0)
    own_rows = (own_rows.astype(jnp.float32) + share).astype(jnp.bfloat16)
    full_rows = lax.all_gather(own_rows, "mp", axis=0, tiled=True) if need_full else own_rows
    return (own_rows, full_rows)


def split_body(
    tokens,
    attn_gain,
    query_first,
    key_first,
    segment_value,
    output_first,
    mlp_gain,
    up_weight,
    down_weight,
    second_gain,
    query_second,
    key_second,
    value_second,
    output_second,
    segment_offset,
    global_offset,
):
    seq_count = lax.axis_size("seq")
    token_position = lax.axis_index("seq")
    seg_span = min(SEG_MAX, seq_count)
    head_count = segment_offset.shape[0]
    full_rows = lax.all_gather(tokens, "mp", axis=0, tiled=True)
    token_count = full_rows.shape[0]
    hidden = norm_rows(full_rows.astype(jnp.float32), attn_gain)
    query = jnp.dot(hidden, query_first, preferred_element_type=jnp.float32).astype(jnp.bfloat16)
    seg_stride = token_count // (KEYS // seg_span)
    keyval = pick_keys(hidden, segment_offset, seg_stride, key_first, segment_value)
    keyval = spread_segment(keyval, seg_span, token_position)
    mixed = attend_local(query, keyval, head_count)
    partial_value = jnp.dot(mixed, output_first, preferred_element_type=jnp.float32)
    own_rows, first_rows = combine(partial_value, full_rows, True)
    normed = norm_rows(first_rows.astype(jnp.float32), mlp_gain)
    inner = jax.nn.gelu(
        jnp.dot(normed, up_weight, preferred_element_type=jnp.float32), approximate=True
    ).astype(jnp.bfloat16)
    partial_value = jnp.dot(inner, down_weight, preferred_element_type=jnp.float32)
    own_rows, second_rows = combine(partial_value, first_rows, True)
    hidden_two = norm_rows(second_rows.astype(jnp.float32), second_gain)
    query_two = jnp.dot(hidden_two, query_second, preferred_element_type=jnp.float32).astype(
        jnp.bfloat16
    )
    glob_stride = token_count // (KEYS // seq_count)
    keyval_two = pick_keys(hidden_two, global_offset, glob_stride, key_second, value_second)
    keyval_two = spread_global(keyval_two)
    mixed_two = attend_local(query_two, keyval_two, head_count)
    partial_value = jnp.dot(mixed_two, output_second, preferred_element_type=jnp.float32)
    own_rows, unused_rows = combine(partial_value, second_rows, False)
    return own_rows


def one_hot(condition):
    return jnp.where(condition, 1.0, 0.0).astype(BF16)


def dot(left, right):
    return jnp.dot(left, right, preferred_element_type=F32)


def pieces(count, size):
    size = size if count % size == 0 else count
    return [slice(start, start + size) for start in range(0, count, size)]


def norm_into(out, start, source, gain, count):
    for span in pieces(count, 64):
        out[start + span.start : start + span.stop, :] = norm_rows(
            source[span, :].astype(F32), gain
        )


def bring(source, target, sem):
    copy = pltpu.make_async_copy(source, target, sem)
    copy.start()
    return copy


def pick_matrix(offsets, heads, groups, stride):
    count = groups * stride
    place = lax.broadcasted_iota(jnp.int32, (groups, count), 1)
    place = place - lax.broadcasted_iota(jnp.int32, (groups, count), 0) * stride
    return jnp.concatenate([one_hot(place == offsets[h]) for h in range(heads)], axis=0)


def project_keys(chosen, heads, weights, keyval_ref):
    rows, width = chosen.shape
    groups, head_size = rows // heads, width // heads
    for slot, weight in enumerate(weights):
        held = weight()
        for span in pieces(width, 256):
            first, last = span.start // head_size, (span.stop - 1) // head_size + 1
            wide = dot(chosen[first * groups : last * groups], held[:, span])
            column = lax.broadcasted_iota(jnp.int32, (groups, span.stop - span.start), 1)
            total = wide[:groups]
            for h in range(first + 1, last):
                row = (h - first) * groups
                own = column >= h * head_size - span.start
                total = jnp.where(own, wide[row : row + groups], total)
            total = total.astype(BF16)
            for copy in range(keyval_ref.shape[0]):
                keyval_ref[copy, slot, :, span] = total


def ranks(offsets, chunk, stride, share, axis):
    heads = offsets.shape[0]

    def places(way):
        shape = (1, chunk) if way else (chunk, 1)
        place = lax.broadcasted_iota(jnp.int32, shape, way)
        inside = lax.rem(place, stride)
        taken = inside == offsets[0]
        for h in range(1, heads):
            taken = taken | (inside == offsets[h])
        return place, inside, jnp.where(taken, inside, inside + stride)

    place, inside, order = places(axis)
    other_place, _, other_order = places(1 - axis)
    ahead = (other_order < order) & (lax.div(other_place, stride) == lax.div(place, stride))
    rank = jnp.sum(jnp.where(ahead, 1, 0), axis=1 - axis, keepdims=True)
    group = lax.div(place, stride)
    return jnp.where(
        rank < heads, group * heads + rank, share + group * (stride - heads) + rank - heads
    )


def slots_of(offsets, heads):
    values = [offsets[h] for h in range(heads)]
    fresh = []
    for h in range(heads):
        seen = jnp.int32(1)
        for earlier in values[:h]:
            seen = jnp.where(earlier == values[h], 0, seen)
        fresh.append(seen)
    slots = []
    for h in range(heads):
        slot = jnp.int32(0)
        for other in range(heads):
            slot = slot + jnp.where(values[other] < values[h], fresh[other], 0)
        slots.append(slot)
    return slots


def first_keys_kernel(
    offsets, tokens, gain, key_weight, value_weight, keyval, rows, wide, picks, scale, sems, *, stride
):
    spans = pieces(tokens.shape[0], tokens.shape[0] // 4)
    copies = [
        bring(offsets, picks, sems.at[0]),
        bring(gain, scale, sems.at[1]),
        *[bring(tokens.at[x], rows.at[x], sems.at[4 + i]) for i, x in enumerate(spans)],
        bring(key_weight, wide.at[0], sems.at[2]),
        bring(value_weight, wide.at[1], sems.at[3]),
    ]
    heads = offsets.shape[0]
    copies[0].wait()
    chooser = pick_matrix(picks, heads, rows.shape[0] // stride, stride)
    copies[1].wait()
    chosen = None
    for copy, span in zip(copies[2:-2], spans):
        copy.wait()
        part = dot(chooser[:, span], rows[span, :])
        chosen = part if chosen is None else chosen + part
    chosen = norm_rows(chosen, scale[...])

    def weight(slot):
        copies[slot - 2].wait()
        return wide[slot]

    project_keys(
        chosen, heads, [functools.partial(weight, slot) for slot in range(2)], keyval
    )


def order_kernel(
    offsets,
    tokens,
    gain,
    moved_rows,
    normed,
    chooser,
    back,
    rows,
    picks,
    scale,
    sems,
    *,
    stride,
    chunk,
):
    copies = [
        bring(offsets, picks, sems.at[0]),
        bring(tokens, rows, sems.at[1]),
        bring(gain, scale, sems.at[2]),
    ]
    count = tokens.shape[0]
    share = chunk // stride * offsets.shape[0]
    rest = chunk - share
    picked = count // chunk * share
    copies[0].wait()
    mover = one_hot(
        lax.broadcasted_iota(jnp.int32, (chunk, chunk), 0)
        == ranks(picks, chunk, stride, share, 1)
    )
    heads = offsets.shape[0]
    chooser[...] = pick_matrix(slots_of(picks, heads), heads, picked // heads, heads)
    back[...] = one_hot(
        lax.broadcasted_iota(jnp.int32, (chunk, chunk), 1)
        == ranks(picks, chunk, stride, share, 0)
    )
    copies[1].wait()
    copies[2].wait()
    for c in range(count // chunk):
        moved = dot(mover, rows[c * chunk : (c + 1) * chunk, :]).astype(BF16)
        moved_rows[c * share : (c + 1) * share, :] = moved[:share]
        moved_rows[picked + c * rest : picked + (c + 1) * rest, :] = moved[share:]
    norm_into(normed, 0, moved_rows, scale[...], count)


def score_scale(head_size):
    return head_size ** (-0.5) * LOG2E


def project_rows(normed, span, weight, out, peak):
    query = dot(normed[span, :], weight[...])
    out[...] = query.astype(BF16)
    for part in pieces(query.shape[0], 64):
        square = query[part] * query[part]
        peak = square if peak is None else jnp.maximum(peak, square)
    return peak


def project_query(normed, weight, outs, heads, peaks):
    peak = None
    for out, row in outs:
        for span in pieces(out.shape[0], 768):
            place = slice(row + span.start, row + span.stop)
            peak = project_rows(normed, place, weight, out.at[span], peak)
    peaks[...] = summed_peaks(peak.astype(BF16), heads)


def first_query_kernel(normed, weight, picked, rest, peaks, sems, *, heads):
    del sems
    project_query(normed, weight, [(picked, 0), (rest, picked.shape[0])], heads, peaks)


def head_windows(head_size, width):
    period = min(width, math.lcm(head_size, 128))
    windows = []
    for h in range(period // head_size):
        start = h * head_size // 128 * 128
        stop = min(period, -(-(h + 1) * head_size // 128) * 128)
        windows.append((start, stop - start))
    return period, windows


def summed_peaks(peak, heads):
    width = peak.shape[1]
    column = lax.broadcasted_iota(jnp.int32, (width, 128), 0)
    head = lax.broadcasted_iota(jnp.int32, (width, 128), 1)
    low = head * (width // heads)
    sums = one_hot((column >= low) & (column < low + width // heads))
    return jnp.max(dot(peak, sums), axis=0, keepdims=True)


def load_keys(keyval, turned):
    keys = jnp.concatenate([keyval[i, 0] for i in range(keyval.shape[0])], axis=0)
    turned[...] = keys.T
    return keys * keys


def small_scores(query_peaks, key_peaks, head_size):
    scale = score_scale(head_size)
    return jnp.max(query_peaks[...] * key_peaks[...]) < 9000.0 / (scale * scale)


def reciprocal(x):
    guess = pl.reciprocal(x, approx=True)
    return guess * (2.0 - x * guess)


def padded_keys(turned, base, head, head_size, start, size):
    low = base + head * head_size
    rows = pl.ds(low if isinstance(low, int) else pl.multiple_of(low, 16), head_size)
    own = jnp.concatenate([part[rows, :] for part in turned], axis=1)
    low = head * head_size - start
    parts = [own]
    if low:
        parts.insert(0, jnp.zeros((low, own.shape[1]), BF16))
    if low + head_size < size:
        parts.append(jnp.zeros((size - low - head_size, own.shape[1]), BF16))
    return jnp.concatenate(parts, axis=0)


def score_pair(query, span, base, head, head_size, windows, turned):
    start = windows[head][0]
    size = windows[head + 1][0] + windows[head + 1][1] - start
    keys = [padded_keys([turned], base, head + i, head_size, start, size) for i in range(2)]
    return dot(query[span, pl.ds(base + start, size)], jnp.concatenate(keys, axis=1))


def near_weights_kernel(
    picked, rest, keyval, picked_early, rest_early, turned, peaks, scores_ref, sems, *, heads
):
    del sems
    peaks[...] = summed_peaks(load_keys(keyval, turned), heads)
    width = picked.shape[1]
    head_size = width // heads
    scale = score_scale(head_size)
    key_count = turned.shape[1]
    period, windows = head_windows(head_size, width)
    jobs = [
        (query, early, head)
        for query, early in ((picked, picked_early), (rest, rest_early))
        for head in range(0, len(windows), 2)
    ]

    @pl.loop(0, width // period)
    def _(turn):
        base = pl.multiple_of(turn * period, 128)

        def score(i):
            query, _, head = jobs[i]
            rows = query.shape[0]
            scores_ref[i % 2, :rows] = score_pair(
                query, slice(0, rows), base, head, head_size, windows, turned
            )

        score(0)
        for i, (query, early, head) in enumerate(jobs):
            if i + 1 < len(jobs):
                score(i + 1)
            for part in pieces(query.shape[0], 64):
                weights = jnp.exp2(scores_ref[i % 2, part, :] * scale).astype(BF16)
                for j in range(2):
                    early[turn * len(windows) + head + j, part, :] = weights[
                        :, j * key_count : (j + 1) * key_count
                    ]


def attend_rows(
    query, first_row, rows, heads, turned, keyvals, mixed_ref, mixed_row, work, plain, early=None
):
    scores_ref, weights_ref = work
    width = query.shape[1]
    key_count = sum(part.shape[1] for part in turned)
    head_size = width // heads
    period, windows = head_windows(head_size, width)
    span = pl.ds(first_row, rows)
    out_span = pl.ds(mixed_row, rows)
    scale = score_scale(head_size)
    lane = lax.broadcasted_iota(jnp.int32, (1, 128), 1)
    step = 2 if early is not None else 1
    piece = 64

    def take_turn(turn):
        base = turn * period if plain else pl.multiple_of(turn * period, 128)
        sums = {}

        def score(i):
            if early is not None:
                scores = score_pair(query, span, base, 2 * i, head_size, windows, turned[1])
            else:
                start, size = windows[i]
                scores = dot(
                    query[span, pl.ds(base + start, size)],
                    padded_keys(turned, base, i, head_size, start, size),
                )
            scores_ref[i % 2, :rows] = scores

        def weigh(h):
            for part in pieces(rows, piece):
                scores = scores_ref[h % 2, part, :]
                if not plain:
                    scores = scores - jnp.max(scores, axis=1, keepdims=True)
                weights_ref[h % 2, part, :] = jnp.exp2(scores * scale).astype(BF16)

        def mix(h):
            start, size = windows[h]
            low = h * head_size - start
            values = jnp.concatenate(
                [
                    x[i, 1, :, pl.ds(base + start, size)]
                    for x in keyvals
                    for i in range(x.shape[0])
                ],
                axis=0,
            )
            column = lax.broadcasted_iota(jnp.int32, (key_count, size), 1)
            own = (column >= low) & (column < low + head_size)
            values = jnp.where(own, values, jnp.ones((), BF16))
            if early is not None:
                half = key_count // 2
                far = weights_ref[h // 2 % 2, :rows, h % 2 * half : (h % 2 + 1) * half]
                near = early[turn * len(windows) + h, span, :]
                weights = jnp.concatenate([near, far], axis=1)
            else:
                weights = weights_ref[h % 2, :rows]
            mixed = dot(weights, values)
            for offset in range(0, size, 128):
                own = mixed[:, offset : offset + 128]
                total = pltpu.roll(own, 64, 1)
                at = start + offset
                if at in sums:
                    mine = lane >= h * head_size - at
                    own = jnp.where(mine, own, sums[at][0])
                    total = jnp.where(mine, total, sums[at][1])
                sums[at] = own, total
                if (h + 1) * head_size >= at + 128:
                    own, total = sums.pop(at)
                    mixed_ref[out_span, pl.ds(base + at, 128)] = (
                        own * reciprocal(total)
                    ).astype(BF16)

        count = len(windows) // step
        score(0)
        for i in range(count):
            if i:
                for h in range((i - 1) * step, i * step):
                    mix(h)
            if i + 1 < count:
                score(i + 1)
            weigh(i)
        for h in range((count - 1) * step, count * step):
            mix(h)

    if plain:
        for turn in range(width // period):
            take_turn(turn)
    else:
        pl.loop(0, width // period)(take_turn)


def attend(query, rows, heads, turned, keyvals, mixed_ref, work, small, early=None):
    size = math.gcd(rows, ROWS)

    @pl.when(small)
    def _():
        attend_rows(query, 0, rows, heads, turned, keyvals, mixed_ref, 0, work, True, early)

    @pl.when(jnp.logical_not(small))
    def _():
        @pl.loop(0, rows // size)
        def _(step):
            row = pl.multiple_of(step * size, size)
            attend_rows(
                query,
                row,
                size,
                heads,
                turned,
                keyvals,
                mixed_ref,
                row,
                work,
                False,
            )


def gelu(x):
    half = 0.5 * x
    return half + half * jnp.tanh(x * (0.7978845608028654 + 0.035677408136300125 * (x * x)))


def widen(normed, up_weight, low, wide_ref, inner):
    rows = normed.shape[0]
    spans = pieces(inner.shape[1], wide_ref.shape[2])

    def product(i):
        columns = slice(low + spans[i].start, low + spans[i].stop)
        wide_ref[i % 2] = dot(normed[...], up_weight[:, columns])

    product(0)
    for i, span in enumerate(spans):
        if i + 1 < len(spans):
            product(i + 1)
        for part in pieces(rows, 32):
            inner[part, span] = gelu(wide_ref[i % 2, part, :]).astype(BF16)


def feed_forward(normed, up_weight, down_weight, total, wide_ref, inner):
    rows = normed.shape[0]
    spans = pieces(up_weight.shape[1], wide_ref.shape[2])

    def product(i):
        wide_ref[i % 2] = dot(normed[...], up_weight[:, spans[i]])

    product(0)
    for i, span in enumerate(spans):
        if i + 1 < len(spans):
            product(i + 1)
        for part in pieces(rows, 32):
            inner[i % 2, part, :] = gelu(wide_ref[i % 2, part, :]).astype(BF16)
        total[...] += dot(inner[i % 2], down_weight[span, :])


def narrow(inners, down_weight, first, second, size):
    for span in pieces(second.shape[1], size):
        total = first[:, span].astype(F32)
        low = 0
        for inner in inners:
            high = low + inner.shape[1]
            total = total + dot(inner[...], down_weight[low:high, span])
            low = high
        second[:, span] = total.astype(BF16)


def add_heads(tokens, first_row, mixed, out_weight, gain, first, normed):
    before = None
    for span in pieces(mixed.shape[0], 256):
        total = dot(mixed[span, :], out_weight[...])
        rows = tokens[first_row + span.start : first_row + span.stop, :]
        first[span, :] = (rows.astype(F32) + total).astype(BF16)
        if before is not None:
            norm_into(normed, before.start, first.at[before], gain, before.stop - before.start)
        before = span
    norm_into(normed, before.start, first.at[before], gain, before.stop - before.start)


def picked_kernel(
    chooser,
    tokens,
    query,
    query_peaks,
    early,
    keyval,
    keyval_far,
    turned_near,
    peaks_near,
    out_weight,
    mlp_gain,
    up_weight,
    down_weight,
    gain,
    key_weight,
    value_weight,
    second,
    normed,
    keyval_two,
    turned,
    peaks,
    held,
    mixed,
    scores,
    weights,
    first,
    wide,
    inner,
    total,
    sems,
    *,
    heads,
):
    copies = [
        bring(x, held.at[i], sems.at[i]) for i, x in enumerate((key_weight, value_weight))
    ]
    rows = second.shape[0]
    keyvals = (keyval, keyval_far)
    squares = load_keys(keyval_far, turned)
    peaks[...] = jnp.maximum(peaks_near[...], summed_peaks(squares, heads))
    small = small_scores(query_peaks, peaks, query.shape[1] // heads)
    attend(
        query,
        rows,
        heads,
        (turned_near, turned),
        keyvals,
        mixed,
        (scores, weights),
        small,
        early,
    )
    add_heads(tokens, 0, mixed, out_weight, mlp_gain[...], first, normed)
    total[...] = first[...].astype(F32)
    feed_forward(normed, up_weight, down_weight, total, wide, inner)
    second[...] = total[...].astype(BF16)
    norm_into(normed, 0, second, gain[...], rows)
    chosen = dot(chooser[...], normed[...]).astype(BF16)

    def weight(slot):
        copies[slot].wait()
        return held[slot]

    project_keys(
        chosen, heads, [functools.partial(weight, slot) for slot in range(2)], keyval_two
    )


def rest_attention_kernel(
    query,
    query_peaks,
    early,
    keyval,
    keyval_far,
    turned_near,
    turned,
    peaks,
    mixed,
    scores,
    weights,
    sems,
    *,
    heads,
):
    del sems
    attend(
        query,
        mixed.shape[0],
        heads,
        (turned_near, turned),
        (keyval, keyval_far),
        mixed,
        (scores, weights),
        small_scores(query_peaks, peaks, query.shape[1] // heads),
        early,
    )


def rest_up_kernel(
    tokens, mixed, out_weight, gain, up_weight, first, normed, inner, wide, sems
):
    del sems
    add_heads(
        tokens, tokens.shape[0] - mixed.shape[0], mixed, out_weight, gain[...], first, normed
    )
    widen(normed, up_weight, 0, wide, inner)


def rest_down_kernel(
    first, normed, inner, up_weight, down_weight, second, wide, inner_more, sems
):
    del sems
    widen(normed, up_weight, inner.shape[1], wide, inner_more)
    narrow([inner, inner_more], down_weight, first, second, 256)


def picked_query_kernel(normed, weight, query, peaks, sems, *, heads):
    del sems
    project_query(normed, weight, [(query, 0)], heads, peaks)


def rest_query_kernel(
    picked, picked_peaks, rows, gain, weight, query, peaks, normed, sems, *, heads
):
    del sems
    start = picked.shape[0]
    query[:start, :] = picked[...]
    norm_into(normed, 0, rows, gain[...], rows.shape[0])
    out = query.at[pl.ds(start, rows.shape[0])]
    project_query(normed, weight, [(out, 0)], heads, peaks)
    peaks[...] = jnp.maximum(peaks[...], picked_peaks[...])


def second_kernel(*refs, heads, parts):
    back, *rows = refs[: 1 + parts]
    query, query_peaks, keyval, keyval_far, out_weight, encoded = refs[1 + parts : 7 + parts]
    turned_near, turned, held, mixed = refs[7 + parts : 11 + parts]
    result, ready, scores, weights, sems = refs[11 + parts :]
    copy = bring(out_weight, held.at[0], sems.at[0])
    keyvals = (keyval, keyval_far)
    squares = jnp.maximum(load_keys(keyval, turned_near), load_keys(keyval_far, turned))
    count = query.shape[0]
    small = small_scores(query_peaks, summed_peaks(squares, heads), query.shape[1] // heads)
    attend(
        query, count, heads, (turned_near, turned), keyvals, mixed, (scores, weights), small
    )
    chunk = back.shape[0]
    share = rows[0].shape[0] * chunk // count
    rest_share = chunk - share
    copy.wait()
    start = 0
    total = dot(mixed[...], held[0])
    for part in rows:
        span = slice(start, start + part.shape[0])
        result[span, :] = (part[...].astype(F32) + total[span]).astype(BF16)
        start += part.shape[0]
    start = count // chunk * share
    copies = []
    for c in range(count // chunk):
        far = start + c * rest_share
        blend = jnp.concatenate(
            [result[c * share : (c + 1) * share, :], result[far : far + rest_share, :]], axis=0
        )
        span = pl.ds(c * chunk, chunk)
        ready[span, :] = dot(back[...], blend).astype(BF16)
        copies.append(bring(ready.at[span], encoded.at[span], sems.at[1 + c]))
    for copy in copies:
        copy.wait()


def relaying(kernel, ins, outs, *refs):
    end = ins + 1 + outs
    refs[end][...] = refs[ins][...]
    kernel(*refs[:ins], *refs[ins + 1 : end], *refs[end + 1 :])


def local_call(kernel, outs, inputs, scratch, scalars=0, far=(), relay=None, out_near=True, copies=1, flops=0, name=None):
    outs, inputs = list(outs), list(inputs)
    if relay is not None:
        kernel = functools.partial(relaying, kernel, len(inputs), len(outs))
        inputs.append(relay)
        outs.append(pltpu.VMEM(relay.shape, relay.dtype))
    specs, placed = [], []
    for i, x in enumerate(inputs):
        if i < scalars:
            specs.append(pl.BlockSpec(memory_space=pltpu.SMEM))
        elif i in far:
            specs.append(pl.BlockSpec(memory_space=pltpu.HBM))
            x = pltpu.with_memory_space_constraint(x, pltpu.HBM)
        else:
            specs.append(pl.BlockSpec(memory_space=pltpu.VMEM))
            x = pltpu.with_memory_space_constraint(x, pltpu.VMEM)
        placed.append(x)
    return pl.pallas_call(
        kernel,
        out_shape=outs,
        in_specs=specs,
        out_specs=[
            pl.BlockSpec(memory_space=pltpu.VMEM if out_near else pltpu.HBM)
        ] * len(outs),
        scratch_shapes=list(scratch) + [pltpu.SemaphoreType.DMA((copies,))],
        compiler_params=pltpu.CompilerParams(vmem_limit_bytes=VMEM_LIMIT),
        cost_estimate=pl.CostEstimate(
            flops=int(flops),
            transcendentals=0,
            bytes_accessed=sum(inputs[i].size * inputs[i].dtype.itemsize for i in far),
        ),
        name=name,
    )(*placed)


def exchange(keyval, span, beside):
    size = lax.axis_size("seq")
    levels = span.bit_length() - 1
    even = list(range(levels - 1, 0, -1))
    orders = (even, even[-1:] + even[:-1])
    for step in range(levels - 1):
        pairs = [(i, i ^ 1 << orders[i % 2][step]) for i in range(size)]
        partner = lax.ppermute(keyval, "seq", pairs)
        keyval = jnp.concatenate([beside(step, keyval), partner], axis=0)
    far = swapped(keyval, "seq", 0)
    return beside(levels - 1, keyval), far


def early_exchange(keyval, span, beside):
    levels = span.bit_length() - 1
    crossed, fresh = [], keyval
    for level in range(levels - 1, 1, -1):
        crossed.append(swapped(fresh, "seq", 1))
        partner = swapped(keyval, "seq", level)
        keyval = jnp.concatenate([beside(levels - 1 - level, keyval), partner], axis=0)
        fresh = partner
    if levels > 1:
        crossed.append(swapped(fresh, "seq", 1))
        keyval = jnp.concatenate([beside(levels - 2, keyval), *crossed], axis=0)
    far = swapped(keyval, "seq", 0)
    return beside(levels - 1, keyval), far


def whole_body(
    tokens,
    attn_gain,
    query_first,
    key_first,
    segment_value,
    output_first,
    mlp_gain,
    up_weight,
    down_weight,
    second_gain,
    query_second,
    key_second,
    value_second,
    output_second,
    segment_offset,
    global_offset,
):
    seq_count = lax.axis_size("seq")
    seg_span = min(SEG_MAX, seq_count)
    heads = segment_offset.shape[0]
    count, width = tokens.shape
    head_size = width // heads
    hidden = up_weight.shape[1]
    stride = count // (KEYS // seg_span)
    stride_two = count // (KEYS // seq_count)
    groups, groups_two = count // stride, count // stride_two
    chunk = max(ROWS, stride_two)
    picked_count = groups_two * heads
    rest_count = count - picked_count
    part = hidden // 4
    wide = hidden // 6 if hidden % 768 == 0 else part

    def near(*shape):
        return pltpu.VMEM(shape, BF16)

    def attention_work(rows):
        return [pltpu.VMEM((2, rows, KEYS), F32), near(2, rows, KEYS)]

    held_shapes = [near(width, KEYS // 2), pltpu.VMEM((1, 128), F32)]
    small_work = [pltpu.SMEM((heads,), jnp.int32), pltpu.VMEM((width,), F32)]

    (keyval,) = local_call(
        functools.partial(first_keys_kernel, stride=stride),
        [near(1, 2, groups, width)],
        (segment_offset, tokens, attn_gain, key_first, segment_value),
        [near(count, width), near(2, width, width)] + small_work,
        far=(0, 1, 2, 3, 4),
        copies=8,
        flops=2 * heads * groups * width * (count + 2 * width),
        name="first_keys",
    )
    made = {}

    def beside_first(level, held):
        if level == 0:
            made["rows"], made["normed"], made["chooser"], made["back"], held = local_call(
                functools.partial(order_kernel, stride=stride_two, chunk=chunk),
                [
                    near(count, width),
                    near(count, width),
                    near(picked_count, picked_count),
                    near(chunk, chunk),
                ],
                (global_offset, tokens, attn_gain),
                [near(count, width)] + small_work,
                far=(0, 1, 2),
                copies=3,
                relay=held,
                flops=2 * count * width * chunk,
                name="order",
            )
        if level == min(1, seg_span.bit_length() - 2):
            made["picked"], made["rest"], made["peaks"], held = local_call(
                functools.partial(first_query_kernel, heads=heads),
                [near(picked_count, width), near(rest_count, width), pltpu.VMEM((1, 128), F32)],
                (made["normed"], query_first),
                [],
                relay=held,
                flops=2 * count * width * width,
                name="first_query",
            )
        if level == seg_span.bit_length() - 2:
            made["picked_early"], made["rest_early"], made["turned"], made["key_peaks"] = local_call(
                functools.partial(near_weights_kernel, heads=heads),
                [near(heads, picked_count, KEYS // 2), near(heads, rest_count, KEYS // 2)]
                + held_shapes,
                (made["picked"], made["rest"], held),
                [pltpu.VMEM((2, rest_count, KEYS), F32)],
                flops=2 * 256 * KEYS // 2 * heads * count,
                name="near_weights",
            )
        return held

    keyval, keyval_far = early_exchange(keyval, seg_span, beside_first)
    rows = made["rows"]
    query_peaks, near_held = made["peaks"], (made["turned"], made["key_peaks"])
    row_flops = 2 * width * (2 * hidden + width) + 4 * 256 * KEYS * heads
    picked_second, picked_normed, keyval_two, turned, peaks = local_call(
        functools.partial(picked_kernel, heads=heads),
        [
            near(picked_count, width),
            near(picked_count, width),
            near(1, 2, groups_two, width),
        ]
        + held_shapes,
        (
            made["chooser"],
            rows,
            made["picked"],
            query_peaks,
            made["picked_early"],
            keyval,
            keyval_far,
            *near_held,
            output_first,
            mlp_gain,
            up_weight,
            down_weight,
            second_gain,
            key_second,
            value_second,
        ),
        [near(2, width, width), near(picked_count, width)]
        + attention_work(picked_count)
        + [near(picked_count, width), pltpu.VMEM((2, picked_count, wide), F32)]
        + [near(2, picked_count, wide), pltpu.VMEM((picked_count, width), F32)],
        far=(14, 15),
        copies=2,
        flops=row_flops * picked_count,
        name="layer_of_picked",
    )
    seconds = [picked_second]

    def rest_attention(held):
        made["mixed"], held = local_call(
            functools.partial(rest_attention_kernel, heads=heads),
            [near(rest_count, width)],
            (
                made["rest"],
                query_peaks,
                made["rest_early"],
                keyval,
                keyval_far,
                made["turned"],
                turned,
                peaks,
            ),
            attention_work(rest_count),
            relay=held,
            flops=4 * 256 * KEYS * heads * rest_count,
            name="rest_attention",
        )
        return held

    half = hidden // 4 * 3

    def rest_up(held):
        made["first"], made["normed"], made["inner"], held = local_call(
            rest_up_kernel,
            [near(rest_count, width), near(rest_count, width), near(rest_count, half)],
            (rows, made["mixed"], output_first, mlp_gain, up_weight),
            [pltpu.VMEM((2, rest_count, part), F32)],
            relay=held,
            flops=2 * width * (half + width) * rest_count,
            name="rest_up",
        )
        return held

    def rest_down(held):
        result, held = local_call(
            rest_down_kernel,
            [near(rest_count, width)],
            (made["first"], made["normed"], made["inner"], up_weight, down_weight),
            [pltpu.VMEM((1, rest_count, part), F32), near(rest_count, hidden - half)],
            relay=held,
            flops=2 * width * (2 * hidden - half) * rest_count,
            name="rest_down",
        )
        seconds.append(result)
        return held

    def picked_query(held):
        made["picked_two"], made["picked_peaks"], held = local_call(
            functools.partial(picked_query_kernel, heads=heads),
            [near(picked_count, width), pltpu.VMEM((1, 128), F32)],
            (picked_normed, query_second),
            [],
            relay=held,
            flops=2 * picked_count * width * width,
            name="picked_query",
        )
        return held

    def rest_query(held):
        made["query_two"], made["peaks_two"], held = local_call(
            functools.partial(rest_query_kernel, heads=heads),
            [near(count, width), pltpu.VMEM((1, 128), F32)],
            (made["picked_two"], made["picked_peaks"], seconds[1], second_gain, query_second),
            [near(rest_count, width)],
            relay=held,
            flops=2 * rest_count * width * width,
            name="rest_query",
        )
        return held

    tasks = [[rest_attention, picked_query], [rest_up], [rest_down], [rest_query]]
    levels = seq_count.bit_length() - 1

    def beside_second(level, held):
        for work in tasks[len(tasks) * level // levels : len(tasks) * (level + 1) // levels]:
            for task in work:
                held = task(held)
        return held

    keyval_two, keyval_two_far = exchange(keyval_two, seq_count, beside_second)
    (encoded,) = local_call(
        functools.partial(second_kernel, heads=heads, parts=len(seconds)),
        [jax.ShapeDtypeStruct((count, width), BF16)],
        (
            made["back"],
            *seconds,
            made["query_two"],
            made["peaks_two"],
            keyval_two,
            keyval_two_far,
            output_second,
        ),
        held_shapes[:1] * 2
        + [near(1, width, width)]
        + [near(count, width)] * 3
        + attention_work(count),
        far=(len(seconds) + 5,),
        out_near=False,
        copies=1 + count // chunk,
        flops=count * (2 * width * width + 4 * 256 * KEYS * heads),
        name="second_attention",
    )
    return encoded


def solution(mesh):
    placed = (
        P(("slides", "seq", "mp"), None),
        P(),
        P(None, "mp"),
        P(None, "mp"),
        P(None, "mp"),
        P("mp", None),
        P(),
        P(None, "mp"),
        P("mp", None),
        P(),
        P(None, "mp"),
        P(None, "mp"),
        P(None, "mp"),
        P("mp", None),
        P("mp"),
        P("mp"),
    )
    fits = mesh.shape["mp"] == 1 and mesh.shape["seq"] in (2, 4, 8, 16)
    return jax.shard_map(
        whole_body if fits else split_body,
        mesh=mesh,
        in_specs=placed,
        out_specs=P(("slides", "seq", "mp"), None),
        check_vma=False,
    )
```
